32 devices in a mesh: dp: 16 (over z, x, core), mp: 2 (over y).
Axes of the slice: x: 2, y: 2, z: 4, core: 2. Of those that a mesh axis runs over, the one named last changes fastest.
Arguments:
- tokens: bfloat16 [32768, 768], P('dp'), may hold values from -6 to 6
- lengths: int32 [128], P('dp'), may hold values from 64 to 256, as said below
- queries: bfloat16 [192, 768], P('dp'), may hold values from -0.4375 to 0.4375
- positives: int32 [192], replicated, may hold values from 0 to 127
- w_qkv: bfloat16 [3, 768, 768], P(None, None, 'mp'), may hold values from -0.21875 to 0.21875
- b_qv: bfloat16 [2, 768], P(None, 'mp'), may hold values from -1.796875 to 1.796875
- w_out: bfloat16 [768, 768], P('mp'), may hold values from -1.75 to 1.75
- b_out: bfloat16 [768], replicated, may hold values from -1.796875 to 1.796875
- gain_one: bfloat16 [768], replicated, may hold values from 0.5 to 1.5
- shift_one: bfloat16 [768], replicated, may hold values from -1.796875 to 1.796875
- w_in: bfloat16 [768, 3072], P(None, 'mp'), may hold values from -0.21875 to 0.21875
- b_in: bfloat16 [3072], P('mp'), may hold values from -3 to 3
- w_back: bfloat16 [3072, 768], P('mp'), may hold values from -0.109375 to 0.109375
- b_back: bfloat16 [768], replicated, may hold values from -1.796875 to 1.796875
- gain_two: bfloat16 [768], replicated, may hold values from 0.5 to 1.5
Outputs:
- activations: bfloat16 [32768, 768], P('dp', 'mp')
- query_loss: float32 [192], P('dp')
- input_grad: float32 [32768, 768], P('dp', 'mp')
- query_grad: float32 [192, 768], P('dp')
- grad_qkv: float32 [3, 768, 768], P(None, 'dp', 'mp')
- grad_bias_qv: float32 [2, 768], P(None, ('mp', 'dp'))
- grad_out: float32 [768, 768], P('mp', 'dp')
- grad_bias_out: float32 [768], P('dp')
- grad_gain_one: float32 [768], P('dp')
- grad_shift_one: float32 [768], P('dp')
- grad_in: float32 [768, 3072], P('dp', 'mp')
- grad_bias_in: float32 [3072], P(('mp', 'dp'))
- grad_back: float32 [3072, 768], P('mp', 'dp')
- grad_bias_back: float32 [768], P('dp')
- grad_gain_two: float32 [768], P('dp')
The draws below stay inside these ranges and needn't reach their ends.
Inputs may be any that keep to these rules, and one draw needn't show every extreme that they name: `lengths`: each passage has 64 or 256 tokens, both occur in every draw; the rest of its slot is padding.
All inputs are finite; a program needn't handle non-finite values.
Results may differ from the reference program's by a relative error of at most 0.029.
Values may be sent and summed in bfloat16 or wider, within the bound.
A program may use at most 192 MiB of HBM per device.

```python
import math
import jax
import jax.numpy as jnp
from jax import lax

D = 768
HEADS = 12
HEAD = 64
FF = 3072
SLOT = 256
SHORT = 64
PASSAGES = 128
QUERIES = 192
ROWS = 32768
N_MP = 2


def draw_lengths(key, part):
    key = jax.random.fold_in(key, 7)
    picks = jax.random.randint(key, (PASSAGES,), 0, 11)
    lengths = jnp.where(picks < 3, SLOT, SHORT).astype(jnp.int32)
    return lengths.at[0].set(SLOT).at[1].set(SHORT)


def with_ends(array, own_key, least, top_value):
    longest = array.shape.index(max(array.shape))
    spots = []
    for shift in (0, 1):
        where = [jax.random.randint(jax.random.fold_in(own_key, axis), (), 0, length) for axis, length in enumerate(array.shape)]
        where[longest] = (where[longest] + shift) % array.shape[longest]
        spots.append(tuple(where))
    return array.at[spots[0]].set(least).at[spots[1]].set(top_value)


def block_scale(own_key, shape, pieces, smallest, high):
    loudness = 1.0
    for axis_at, parts in pieces:
        heights = jax.random.uniform(jax.random.fold_in(jax.random.fold_in(own_key, 6), axis_at), (parts,), jnp.float32, smallest / len(pieces), high / len(pieces))
        loudness = loudness * jnp.repeat(jnp.exp(heights), shape[axis_at] // parts).reshape((-1,) + (1,) * (len(shape) - 1 - axis_at))
    return loudness


def gaussian(rng, shape, scale, most, split=(), dtype=jnp.bfloat16):
    drawn = jax.random.normal(rng, shape, jnp.float32) * scale
    if len(split) > 0:
        drawn = block_scale(rng, shape, split, -0.22, 0.18) * drawn
    return jnp.clip(drawn, min=-most, max=most).astype(dtype)


def setup_inputs(seed: int = 0) -> dict:
    splits = jax.random.split(jax.random.key(seed), 16)
    tokens = gaussian(splits[0], (ROWS, D), 1.0, 6.0, ((0, 16),))
    lengths = draw_lengths(jax.random.fold_in(splits[15], 71), 0)
    queries = gaussian(splits[2], (QUERIES, D), (D // 4) ** -0.5, 0.4375, ((0, 16),))
    positives = with_ends(jax.random.randint(splits[3], (QUERIES,), 0, PASSAGES), jax.random.fold_in(splits[3], 1), 0, PASSAGES - 1).astype(jnp.int32)
    w_qkv = gaussian(splits[4], (3, D, D), D ** -0.5, 0.21875, ((2, 2),))
    b_qv = gaussian(splits[5], (2, D), 0.3, 1.796875, ((1, 2),))
    w_out = gaussian(splits[6], (D, D), (D // 64) ** -0.5, 1.75, ((0, 2),))
    b_out = gaussian(splits[7], (D,), 0.3, 1.796875)
    gain_one = jnp.clip(1.0 + 0.1 * jax.random.normal(splits[8], (D,), jnp.float32), 0.5, 1.5).astype(jnp.bfloat16)
    shift_one = gaussian(splits[9], (D,), 0.3, 1.796875)
    w_in = gaussian(splits[10], (D, FF), D ** -0.5, 0.21875, ((1, 2),))
    b_in = gaussian(splits[11], (FF,), 0.5, 3.0, ((0, 2),))
    w_back = gaussian(splits[12], (FF, D), FF ** -0.5, 0.109375, ((0, 2),))
    b_back = gaussian(splits[13], (D,), 0.3, 1.796875)
    gain_two = jnp.clip(1.0 + 0.1 * jax.random.normal(splits[14], (D,), jnp.float32), 0.5, 1.5).astype(jnp.bfloat16)
    return {"tokens": tokens, "lengths": lengths, "queries": queries, "positives": positives, "w_qkv": w_qkv, "b_qv": b_qv, "w_out": w_out, "b_out": b_out, "gain_one": gain_one, "shift_one": shift_one, "w_in": w_in, "b_in": b_in, "w_back": w_back, "b_back": b_back, "gain_two": gain_two}


@jax.custom_vjp
def low(v):
    return lax.optimization_barrier(v.astype(jnp.bfloat16)).astype(jnp.float32)

@jax.custom_vjp
def low_back(v):
    return v

def low_keep(v):
    return (low(v), None)

def low_pass(kept, grad):
    return (grad,)

def back_keep(v):
    return (v, None)

def back_low(kept, grad):
    return (low(grad),)
low.defvjp(low_keep, low_pass)
low_back.defvjp(back_keep, back_low)
epsilon = 1e-05
masked = -1e+30

def product(left, right):
    return jnp.dot(left, right, precision=lax.Precision.HIGHEST)

def layer_norm(rows, gain, shift):
    center = lax.optimization_barrier(jnp.mean(rows, axis=-1, keepdims=True))
    spread = rows - center
    second = lax.optimization_barrier(jnp.mean(spread * spread, axis=-1, keepdims=True))
    return spread * lax.rsqrt(second + epsilon) * gain + shift

def scaled_norm(rows, gain):
    center = lax.optimization_barrier(jnp.mean(rows, axis=-1, keepdims=True))
    spread = rows - center
    second = lax.optimization_barrier(jnp.mean(spread * spread, axis=-1, keepdims=True))
    return spread * lax.rsqrt(second + epsilon) * gain

def passage_group(tokens, lengths, w_qkv, b_qv, w_out, b_out, gain_one, shift_one, w_in, b_in, w_back, b_back, gain_two):
    count = lengths.shape[0]
    rows = tokens.shape[0]
    scale = 1.0 / math.sqrt(HEAD)
    query = low(low_back(product(tokens, w_qkv[0])) + b_qv[0])
    keyed = low(low_back(product(tokens, w_qkv[1])))
    value = low(low_back(product(tokens, w_qkv[2])) + b_qv[1])
    shaped = (count, SLOT, HEADS, HEAD)
    scores = jnp.einsum('pqhd,pkhd->phqk', query.reshape(shaped), keyed.reshape(shaped), precision=lax.Precision.HIGHEST) * scale
    scores = low_back(scores)
    valid = lax.broadcasted_iota(jnp.int32, (count, SLOT), 1) < lengths[:, None]
    scores = jnp.where(valid[:, None, None, :], scores, masked)
    top = lax.optimization_barrier(jnp.max(scores, axis=-1, keepdims=True))
    raised = jnp.exp(scores - top)
    chance = low(raised / lax.optimization_barrier(jnp.sum(raised, axis=-1, keepdims=True)))
    context = jnp.einsum('phqk,pkhd->pqhd', chance, value.reshape(shaped), precision=lax.Precision.HIGHEST).reshape(rows, D)
    context = low_back(low(context))
    group = D // N_MP
    attended = jnp.zeros((rows, D), jnp.float32)
    for part in range(N_MP):
        attended = attended + low(product(context[:, part * group:(part + 1) * group], w_out[part * group:(part + 1) * group]))
    attended = low_back(attended) + b_out
    resid_one = tokens + attended
    norm_one = layer_norm(resid_one, gain_one, shift_one)
    inner = low_back(product(low(norm_one), w_in)) + b_in
    active = low(jax.nn.gelu(inner, approximate=False))
    units = FF // N_MP
    feed = jnp.zeros((rows, D), jnp.float32)
    for part in range(N_MP):
        feed = feed + low(product(active[:, part * units:(part + 1) * units], w_back[part * units:(part + 1) * units]))
    resid_two = norm_one + low_back(feed) + b_back
    return scaled_norm(resid_two, gain_two)

def reference(tokens, lengths, queries, positives, w_qkv, b_qv, w_out, b_out, gain_one, shift_one, w_in, b_in, w_back, b_back, gain_two):
    group = min(PASSAGES, max(1, 4096 // SLOT))
    blocks = PASSAGES // group
    params = tuple((arr.astype(jnp.float32) for arr in (w_qkv, b_qv, w_out, b_out, gain_one, shift_one, w_in, b_in, w_back, b_back, gain_two)))
    token_wide = tokens.astype(jnp.float32)
    query_wide = queries.astype(jnp.float32)
    length_blocks = lengths.reshape(blocks, group)

    def forward(token_in, query_in, *weights):

        def one_block(inputs):
            token_block, length_block = inputs
            return passage_group(token_block, length_block, *weights)
        outputs = lax.map(jax.checkpoint(one_block), (token_in.reshape(blocks, group * SLOT, D), length_blocks))
        output = outputs.reshape(ROWS, D)
        cls = low(output.reshape(PASSAGES, SLOT, D)[:, 0])
        similar = product(query_in, cls.T)
        top = lax.optimization_barrier(jnp.max(similar, axis=1, keepdims=True))
        log_sum = top[:, 0] + jnp.log(lax.optimization_barrier(jnp.sum(jnp.exp(similar - top), axis=1)))
        picked = jnp.take_along_axis(similar, positives[:, None].astype(jnp.int32), axis=1)[:, 0]
        return (output, log_sum - picked)
    (output, query_loss), pull = jax.vjp(forward, token_wide, query_wide, *params)
    grads = pull((jnp.zeros_like(output), jnp.full((QUERIES,), 1.0 / QUERIES, jnp.float32)))
    return (output.astype(jnp.bfloat16), query_loss, grads[0], grads[1], grads[2], grads[3], grads[4], grads[5], grads[6], grads[7], grads[8], grads[9], grads[10], grads[11], grads[12])
```

```python
import functools
import math

import jax
import jax.numpy as jnp
from jax import lax
from jax.experimental import pallas as pl
from jax.experimental.pallas import tpu as pltpu
from jax.sharding import PartitionSpec as P

HEAD = 64
EPS = 1e-05
MASKED = -1e30
MESH = pl.DeviceIdType.MESH
BF = jnp.bfloat16
F32 = jnp.float32
MIB = 2**20


def nn(a, b):
    return jnp.dot(a, b, preferred_element_type=F32)


def nt(a, b):
    return lax.dot_general(a, b, (((1,), (1,)), ((), ())), preferred_element_type=F32)


def tn(a, b):
    return lax.dot_general(a, b, (((0,), (0,)), ((), ())), preferred_element_type=F32)


def gelu(h):
    return 0.5 * h * (1.0 + lax.erf(h * math.sqrt(0.5)))


def gelu_slope(h):
    bell = jnp.exp(-0.5 * h * h) * (1.0 / math.sqrt(2.0 * math.pi))
    return 0.5 * (1.0 + lax.erf(h * math.sqrt(0.5))) + h * bell


def standard(rows):
    center = jnp.mean(rows, axis=-1, keepdims=True)
    spread = rows - center
    second = jnp.mean(spread * spread, axis=-1, keepdims=True)
    inverse = lax.rsqrt(second + EPS)
    return spread * inverse, inverse


def norm_back(grad, scaled, inverse):
    first = jnp.mean(grad, axis=-1, keepdims=True)
    second = jnp.mean(grad * scaled, axis=-1, keepdims=True)
    return inverse * (grad - first - scaled * second)


def flip(index, bit):
    return index + bit * (1 - 2 * lax.rem(lax.div(index, bit), 2))


def mult(value, step):
    return pl.multiple_of(value, step)


def tower(
    nd,
    query_total,
    lengths,
    tokens,
    queries,
    positives,
    w_qkv,
    b_qv,
    w_out,
    b_out,
    gain_one,
    shift_one,
    w_in,
    b_in,
    w_back,
    b_back,
    gain_two,
    out_act,
    o_coef,
    o_rank,
    o_factor,
    o_dquery,
    o_active,
    o_inner,
    o_context,
    o_qcls,
    o_dctx,
    o_norm,
    o_ffn,
    o_attn,
    o_tok,
    o_sums,
    o_sums_in,
    o_loss,
    o_qgrad,
    tok,
    wq,
    wo,
    wi,
    wb,
    keyb,
    valb,
    ctx,
    ctx_send,
    norm_low,
    acc,
    act_far,
    obuf,
    chance,
    factor,
    stage,
    tcls,
    pack,
    gath,
    ctx_all,
    tok_all,
    q_all,
    xh1_all,
    norm_all,
    inner_all,
    act_all,
    low_all,
    dc_all,
    qc_all,
    d1_all,
    dq_rows,
    rank_f,
    coef_own,
    coef_far,
    rank_own,
    rank_send,
    rank_far,
    fac_send,
    fac_all,
    dq_send,
    dq_all,
    loc_sem,
    ysend,
    yrecv,
    w_send,
    w_recv,
    c_send,
    c_recv,
    o_send,
    o_recv,
    o_loc,
    g_send,
    g_recv,
    gs_send,
    gs_recv,
    f_send,
    f_recv,
    q_send,
    q_recv,
    m_send,
    m_recv,
    b_send,
    b_recv,
    bin_own,
    bin_far,
):
    dp = lax.axis_index("dp")
    mp = lax.axis_index("mp")
    far = 1 - mp
    chips = nd // 2
    core = lax.rem(dp, 2)
    chip = lax.div(dp, 2)
    bit_a = lax.rem(lax.div(dp, 2), 2)
    bit_b = lax.rem(lax.div(dp, 4), 2)
    quarter = bit_a + 2 * bit_b
    quarter_x = flip(quarter, 1)
    quarter_z = flip(quarter, 2)
    quarter_d = 3 - quarter
    pair = (dp, far)
    sibling = (flip(dp, 1), mp)
    near_x = (flip(dp, 2), mp)
    near_z = (flip(dp, 4), mp)

    rows, width = tok.shape
    count = lengths.shape[0]
    slot = rows // count
    own = count // 2
    half = width // 2
    own_rows = own * slot
    passages = nd * count
    blocks, unit = wi.shape[1], wi.shape[3]
    m_col = mult(mp * half, 128)
    f_col = mult(far * half, 128)

    barrier = pltpu.get_barrier_semaphore()

    def greet(i, carry):
        other = lax.rem(dp * 2 + mp + i, 2 * nd)
        pl.semaphore_signal(
            barrier,
            inc=1,
            device_id=(lax.div(other, 2), lax.rem(other, 2)),
            device_id_type=MESH,
        )
        return carry

    lax.fori_loop(1, 2 * nd, greet, 0)

    def local(src, dst, k):
        return pltpu.make_async_copy(src, dst, loc_sem.at[k])

    loads = [local(tokens, tok, 0)]
    loads += [local(w_qkv.at[j], wq.at[:, pl.ds(j * half, half)], 1 + j) for j in range(3)]
    loads.append(local(w_out, wo.at[pl.ds(mult(mp * half, 128), half), :], 4))
    loads += [
        local(w_in.at[:, pl.ds(u * unit, unit)], wi.at[mp, u], 5 + u) for u in range(blocks)
    ]
    loads += [
        local(w_back.at[pl.ds(u * unit, unit), :], wb.at[mp, u], 5 + blocks + u)
        for u in range(blocks)
    ]
    for copy in loads:
        copy.start()

    chunks = 1 + 2 * blocks

    def piece(k, q, c, which, side=None):
        if k == 0:
            size = half // 8
            at = mult(which * half + (c * 4 + q) * size, 16)
            cols = pl.ds(0, width) if side is None else pl.ds(side * half, half)
            return wo.at[pl.ds(at, size), cols]
        if k <= blocks:
            size = width // 8
            at = (c * 4 + q) * size
            if side is not None:
                size = size // 2
                at = at + side * size
            return wi.at[which, k - 1, pl.ds(mult(at, 16), size), :]
        size = unit // 8
        cols = pl.ds(0, width) if side is None else pl.ds(side * half, half)
        return wb.at[which, k - 1 - blocks, pl.ds(mult((c * 4 + q) * size, 16), size), cols]

    def source(k):
        if k == 0:
            size = half // 8
            return w_out.at[pl.ds(mult((core * 4 + quarter) * size, 16), size), :]
        if k <= blocks:
            size = width // 8
            at = mult((core * 4 + quarter) * size, 16)
            return w_in.at[pl.ds(at, size), pl.ds((k - 1) * unit, unit)]
        size = unit // 8
        at = mult((k - 1 - blocks) * unit + (core * 4 + quarter) * size, 16)
        return w_back.at[pl.ds(at, size), :]

    def remote(src, dst, ss, rs, device):
        return pltpu.make_async_remote_copy(
            src_ref=src,
            dst_ref=dst,
            send_sem=ss,
            recv_sem=rs,
            device_id=device,
            device_id_type=MESH,
        )

    def cross(k):
        return remote(
            source(k), piece(k, quarter, core, mp), ysend.at[k], yrecv.at[k], pair
        )

    def send(k, lane, q, c, side, device):
        ref = piece(k, q, c, far, side)
        return remote(ref, ref, w_send.at[k, lane], w_recv.at[k, lane], device)

    def lane(k, n):
        q = (quarter, quarter, quarter_z, quarter_x, quarter, quarter_x, quarter_z, quarter_d)[n]
        side = (None, None, 0, 1, None, None, None, None)[n]
        return send(k, n, q, core, side, (near_x, near_z, near_x, near_z)[n] if n < 4 else sibling)

    def arrival(k, n):
        q = (quarter_x, quarter_z, quarter_d, quarter_d, quarter, quarter_x, quarter_z, quarter_d)[n]
        side = (None, None, 0, 1, None, None, None, None)[n]
        c = core if n < 4 else 1 - core
        return send(k, n, q, c, side, (near_x, near_z, near_x, near_z)[n] if n < 4 else sibling)

    def step_one(k):
        remote(
            source(k), piece(k, quarter, core, far), ysend.at[k], yrecv.at[k], pair
        ).wait_recv()
        for n in (0, 1, 4):
            lane(k, n).start()

    def step_two(k):
        arrival(k, 1).wait_recv()
        lane(k, 2).start()
        arrival(k, 0).wait_recv()
        for n in (3, 5, 6):
            lane(k, n).start()

    def step_three(k):
        arrival(k, 2).wait_recv()
        arrival(k, 3).wait_recv()
        lane(k, 7).start()

    def complete(k):
        for n in range(4, 8):
            arrival(k, n).wait_recv()

    def tick(i):
        if i < chunks:
            step_one(i)
        if 0 <= i - 1 < chunks:
            step_two(i - 1)
        if 0 <= i - 2 < chunks:
            step_three(i - 2)

    for copy in loads[:4]:
        copy.wait()
    pl.semaphore_wait(barrier, 2 * nd - 1)
    bin_own[...] = jnp.zeros_like(bin_own)
    bin_own[0:blocks, :] = b_in[...].astype(F32)
    bias_copy = remote(bin_own, bin_far, b_send, b_recv, pair)
    bias_copy.start()
    for k in range(chunks):
        cross(k).start()

    lane_pair = lax.broadcasted_iota(jnp.int32, (slot, 128), 1)
    key_place = lax.broadcasted_iota(jnp.int32, (1, slot), 1)
    head_rows = lax.broadcasted_iota(jnp.int32, (8, half), 0)
    head_mask = head_rows == lax.div(lax.broadcasted_iota(jnp.int32, (8, half), 1), HEAD)
    heads = half // HEAD
    live = lax.broadcasted_iota(jnp.int32, (8, 1), 0) < heads
    bias_q = b_qv[0:1, :].astype(F32)
    bias_v = b_qv[1:2, :].astype(F32)
    ones = jnp.ones((slot, 128), BF)
    row_place = lax.broadcasted_iota(jnp.int32, (8, slot), 0)
    first_key = (lax.broadcasted_iota(jnp.int32, (8, slot), 1) == 0).astype(F32)

    def ctx_copy(i):
        there = ctx.at[pl.ds(mult(i * slot, 16), slot), pl.ds(m_col, half)]
        return remote(
            ctx_send.at[pl.ds(mult(i * slot, 16), slot), :], there, c_send.at[i], c_recv.at[i], pair
        )

    def ctx_came(i):
        here = ctx.at[pl.ds(mult(i * slot, 16), slot), pl.ds(f_col, half)]
        return remote(
            ctx_send.at[pl.ds(mult(i * slot, 16), slot), :], here, c_send.at[i], c_recv.at[i], pair
        )

    def attend(i, carry):
        theirs = i < own
        side = jnp.where(theirs, far, mp)
        place = lax.rem(i, own)
        p = side * own + place
        at = mult(p * slot, slot)
        x = tok[pl.ds(at, slot), :]
        made = nn(x, wq[...])
        query = ((made[:, :half] + bias_q).astype(BF).astype(F32) * 0.125).astype(BF)
        keyed = made[:, half : 2 * half].astype(BF)
        value = (made[:, 2 * half :] + bias_v).astype(BF)
        keyb[pl.ds(at, slot), :] = keyed
        valb[pl.ds(at, slot), :] = value
        length = lengths[p]
        bias = jnp.where(key_place < length, 0.0, MASKED)
        done = []
        for t in range(half // 128):
            q2 = query[:, 128 * t : 128 * t + 128]
            k2 = keyed[:, 128 * t : 128 * t + 128]
            v2 = jnp.concatenate([value[:, 128 * t : 128 * t + 128], ones], axis=1)
            parts = []
            for hx in range(2):
                mask = (lane_pair < HEAD) if hx == 0 else (lane_pair >= HEAD)
                s = nt(jnp.where(mask, q2, jnp.zeros_like(q2)), k2) + bias
                e = jnp.exp(s - jnp.max(s, axis=1, keepdims=True)).astype(BF)
                o = nn(e, v2)
                parts.append(o[:, :128] / o[:, 128:])
            done.append(jnp.where(lane_pair < HEAD, parts[0], parts[1]))
        mixed = jnp.concatenate(done, axis=1)
        low = mixed.astype(BF)
        stage[pl.ds(p, 1), :] = mixed[0:1, :]
        tcls[pl.ds(p, 1), :] = x[0:16, :].astype(F32)[0:1, :]
        q_row = query[0:16, :].astype(F32)[0:1, :]
        q_heads = jnp.where(head_mask, q_row, 0.0).astype(BF)
        s = nt(q_heads, keyed) + bias
        e = jnp.exp(s - jnp.max(s, axis=1, keepdims=True))
        c = jnp.where(live, e / jnp.sum(e, axis=1, keepdims=True), 0.0)
        chance[p] = c
        c_low = c.astype(BF)
        coef_own[pl.ds(mult(p * 16, 16), 8), :] = jnp.where(row_place == heads, first_key, c)
        factor[pl.ds(mult(p * 8, 8), 8), :] = nn(c_low, x)

        @pl.when(theirs)
        def _():
            ctx_send[pl.ds(mult(place * slot, 16), slot), :] = low
            ctx_copy(place).start()

        @pl.when(i >= own)
        def _():
            ctx[pl.ds(mult(place * slot, 16), slot), pl.ds(m_col, half)] = low

        @pl.when(i == own)
        def _():
            tick(0)

        @pl.when(i == own + 2)
        def _():
            tick(1)

        return carry

    lax.fori_loop(0, count, attend, 0)

    pack[0:8, :] = stage[...]
    pack[8:16, :] = tcls[:, pl.ds(m_col, half)]
    pack[16:32, :] = jnp.zeros((16, half), F32)
    q_rows = queries.shape[0]
    pack[16 : 16 + q_rows, :] = queries[:, pl.ds(m_col, half)].astype(F32)
    gath[chip, core, mp] = pack[...].astype(BF)

    def gather_copy(i, mine):
        me = chip * 2 + mp
        there = lax.rem(me + i, 2 * chips)
        t_chip, t_mp = lax.div(there, 2), lax.rem(there, 2)
        holder = gath.at[chip, core, mp] if mine else gath.at[t_chip, core, t_mp]
        return remote(
            gath.at[chip, core, mp],
            holder,
            g_send.at[i],
            g_recv.at[me if mine else there],
            (t_chip * 2 + core, t_mp),
        )

    def gather_start(i, carry):
        gather_copy(i, True).start()
        return carry

    def gather_wait(i, carry):
        gather_copy(i, False).wait_recv()
        return carry

    def gather_sent(i, carry):
        gather_copy(i, True).wait_send()
        return carry

    lax.fori_loop(1, 2 * chips, gather_start, 0)

    for copy in loads[4:]:
        copy.wait()
    tick(2)
    tick(3)
    complete(0)
    bo = b_out[0:1, :].astype(F32)
    g1 = gain_one[0:1, :].astype(F32)
    s1 = shift_one[0:1, :].astype(F32)
    g2 = gain_two[0:1, :].astype(F32)
    bb = b_back[0:1, :].astype(F32)

    def feed_own(i, carry):
        ctx_came(i).wait_recv()
        at = mult(i * slot, slot)
        here = pl.ds(at, slot)
        x = tok[pl.ds(mult(mp * own_rows + i * slot, slot), slot), :].astype(F32)
        resid = x + nn(ctx[here, :], wo[...]) + bo
        scaled, _ = standard(resid)
        norm = scaled * g1 + s1
        low = norm.astype(BF)
        norm_low[here, :] = low
        total = norm + bb
        for u in range(blocks):
            inner = nn(low, wi[mp, u]) + bin_own[u : u + 1, :]
            total = total + nn(gelu(inner).astype(BF), wb[mp, u])
        acc[here, :] = total

        for j in range(own):

            @pl.when(i == j)
            def _():
                if j + 4 < chunks + 2:
                    tick(j + 4)

        return carry

    lax.fori_loop(0, own, feed_own, 0)
    for i in range(own + 4, chunks + 2):
        tick(i)

    lax.fori_loop(1, 2 * chips, gather_wait, 0)
    to_sibling = remote(gath.at[:, core], gath.at[:, core], gs_send, gs_recv, sibling)
    to_sibling.start()

    bias_copy.wait_recv()
    for u in range(blocks):
        complete(1 + u)

        def feed_far_in(i, carry, u=u):
            here = pl.ds(mult(i * slot, slot), slot)
            inner = nn(norm_low[here, :], wi[far, u]) + bin_far[u : u + 1, :]
            act_far[u, here, :] = gelu(inner).astype(BF)
            return carry

        lax.fori_loop(0, own, feed_far_in, 0)

    for u in range(blocks - 1):
        complete(1 + blocks + u)

        def feed_far_back(i, carry, u=u):
            here = pl.ds(mult(i * slot, slot), slot)
            acc[here, :] += nn(act_far[u, here, :], wb[far, u])
            return carry

        lax.fori_loop(0, own, feed_far_back, 0)

    complete(chunks - 1)

    def out_copy(i, mine):
        side = mp if mine else far
        there = out_act.at[pl.ds(mult(side * own_rows + i * slot, 16), slot), :]
        return remote(
            obuf.at[1, pl.ds(mult(i * slot, 16), slot), :], there, o_send.at[i], o_recv.at[i], pair
        )

    def out_local(i):
        there = out_act.at[pl.ds(mult(mp * own_rows + i * slot, 16), slot), :]
        return pltpu.make_async_copy(
            obuf.at[0, pl.ds(mult(i * slot, 16), slot), :], there, o_loc.at[i]
        )

    def finish(i, carry):
        here = pl.ds(mult(i * slot, slot), slot)
        total = acc[here, :] + nn(act_far[blocks - 1, here, :], wb[far, blocks - 1])
        scaled, _ = standard(total)
        acc[here, :] = scaled * g2
        obuf[0, here, :] = acc[here, pl.ds(m_col, half)].astype(BF)
        obuf[1, here, :] = acc[here, pl.ds(f_col, half)].astype(BF)
        out_copy(i, True).start()
        out_local(i).start()
        return carry

    lax.fori_loop(0, own, finish, 0)

    remote(
        gath.at[:, 1 - core], gath.at[:, 1 - core], gs_send, gs_recv, sibling
    ).wait_recv()
    q_pad = nd * 16
    for h in range(2):
        cols = slice(h * half, (h + 1) * half)
        block = gath[:, :, h].astype(F32)
        ctx_all[:, cols] = block[:, :, 0:8].reshape(passages, half).astype(BF)
        tok_all[:, cols] = block[:, :, 8:16].reshape(passages, half).astype(BF)
        q_all[:, cols] = block[:, :, 16:32].reshape(q_pad, half).astype(BF)

    resid = tok_all[...].astype(F32) + nn(ctx_all[...], wo[...]) + bo
    scaled, inverse1 = standard(resid)
    xh1_all[...] = scaled
    norm = scaled * g1 + s1
    low = norm.astype(BF)
    norm_all[...] = low
    total = norm + bb
    for h in range(2):
        for u in range(blocks):
            bias = jnp.where(mp == h, bin_own[u : u + 1, :], bin_far[u : u + 1, :])
            inner = nn(low, wi[h, u]) + bias
            inner_all[h, u] = inner
            active = gelu(inner).astype(BF)
            act_all[h, u] = active
            total = total + nn(active, wb[h, u])
    xh2, inverse2 = standard(total)
    cls = (xh2 * g2).astype(BF)
    similar = nt(cls, q_all[...])
    top = jnp.max(similar, axis=0, keepdims=True)
    log_sum = top + jnp.log(jnp.sum(jnp.exp(similar - top), axis=0, keepdims=True))
    target = lax.broadcasted_iota(jnp.int32, similar.shape, 0) == positives[0:1, :]
    picked = jnp.sum(jnp.where(target, similar, 0.0), axis=0, keepdims=True)
    o_loss[...] = jnp.broadcast_to(log_sum - picked, o_loss.shape)
    slopes = (jnp.exp(similar - log_sum) - target.astype(F32)) * (1.0 / query_total)
    slope_high = slopes.astype(BF)
    slope_low = (slopes - slope_high.astype(F32)).astype(BF)
    cls_grad = nn(slope_high, q_all[...]) + nn(slope_low, q_all[...])
    pick = (
        lax.broadcasted_iota(jnp.int32, (16, q_pad), 1)
        == lax.broadcasted_iota(jnp.int32, (16, q_pad), 0) + dp * 16
    ).astype(BF)
    o_qgrad[...] = nn(nt(pick, slope_high).astype(BF), cls) + nn(
        nt(pick, slope_low).astype(BF), cls
    )
    d_two = norm_back(g2 * cls_grad, xh2, inverse2)
    o_sums[0:1, :] = jnp.sum(cls_grad * xh2, axis=0, keepdims=True)
    o_sums[1:2, :] = jnp.sum(d_two, axis=0, keepdims=True)
    ffn_low = d_two.astype(BF)
    o_ffn[...] = ffn_low
    back = d_two
    for h in range(2):
        for u in range(blocks):
            d_active = nt(ffn_low, wb[h, u])
            d_inner = d_active * gelu_slope(inner_all[h, u])
            inner_all[h, u, 0:8, :] = jnp.broadcast_to(
                jnp.sum(d_inner, axis=0, keepdims=True), (8, unit)
            )
            inner_low = d_inner.astype(BF)
            low_all[h, u] = inner_low
            back = back + nt(inner_low, wi[h, u])
    for u in range(blocks):
        o_active[u] = act_all[mp, u]
        o_inner[u] = low_all[mp, u]
        o_sums_in[u : u + 1, :] = inner_all[mp, u, 0:1, :]
    xh1 = xh1_all[...]
    d_one = norm_back(g1 * back, xh1, inverse1)
    d1_all[...] = d_one
    o_sums[2:3, :] = jnp.sum(back * xh1, axis=0, keepdims=True)
    o_sums[3:4, :] = jnp.sum(back, axis=0, keepdims=True)
    o_sums[4:5, :] = jnp.sum(d_one, axis=0, keepdims=True)
    attn_low = d_one.astype(BF)
    o_attn[...] = attn_low
    o_norm[...] = norm_all[...]
    o_tok[...] = tok_all[...]
    d_ctx = nt(attn_low, wo[pl.ds(mult(mp * half, 128), half), :]).astype(BF)
    o_dctx[...] = d_ctx
    dc_all[...] = d_ctx.astype(F32)
    q_cls = (nn(tok_all[...], wq[:, 0:half]) + bias_q).astype(BF)
    o_qcls[...] = q_cls
    qc_all[...] = q_cls.astype(F32) * 0.125
    o_context[...] = ctx_all[:, pl.ds(m_col, half)]
    o_sums[5:6, 0:half] = jnp.sum(dc_all[...], axis=0, keepdims=True)

    base = mult(dp * count, 8)
    fkind = count * 8

    def attend_back(p, carry):
        at = mult(p * slot, slot)
        d_row = dc_all[pl.ds(base + p, 1), :]
        q_row = qc_all[pl.ds(base + p, 1), :]
        d_heads = jnp.where(head_mask, d_row, 0.0)
        q_heads = jnp.where(head_mask, q_row, 0.0)
        c = chance[p]
        d_chance = nt(d_heads.astype(BF), valb[pl.ds(at, slot), :])
        d_scores = c * (d_chance - jnp.sum(c * d_chance, axis=1, keepdims=True))
        s_low = d_scores.astype(BF)
        mark = jnp.logical_or(row_place == heads, row_place == heads + 1)
        coef_own[pl.ds(mult(p * 16 + 8, 8), 8), :] = jnp.where(mark, first_key, d_scores)
        factor[pl.ds(mult(fkind + p * 8, 8), 8), :] = nn(s_low, tok[pl.ds(at, slot), :])
        spread = nn(s_low, keyb[pl.ds(at, slot), :])
        dq_rows[pl.ds(p, 1), :] = 0.125 * jnp.sum(
            jnp.where(head_mask, spread, 0.0), axis=0, keepdims=True
        )
        rank_f[pl.ds(mult(p * 16, 8), 8), 0:half] = d_heads
        rank_f[pl.ds(mult(p * 16 + 8, 8), 8), 0:half] = q_heads
        return carry

    lax.fori_loop(0, count, attend_back, 0)

    turned = jnp.transpose(factor[...]).astype(BF)
    fac_send[...] = turned
    dq = dq_rows[...]
    for b in range(half // 128):
        pack[b * 8 : b * 8 + 8, 0:128] = dq[:, b * 128 : b * 128 + 128]
    pack[half // 16 : 32, 0:128] = jnp.zeros((32 - half // 16, 128), F32)
    dq_send[...] = pack[:, 0:128].astype(BF)
    share = width // nd
    fac_all[dp] = fac_send[pl.ds(mult(dp * share, 16), share), :]
    dq_all[dp] = dq_send[...]

    def factor_copy(i, mine):
        there = lax.rem(dp + i, nd)
        holder = fac_all.at[dp] if mine else fac_all.at[there]
        rows_out = fac_send.at[pl.ds(mult(there * share, 16), share), :]
        return remote(
            rows_out, holder, f_send.at[i], f_recv.at[dp if mine else there], (there, mp)
        )

    def dq_copy(i, mine):
        there = lax.rem(dp + i, nd)
        holder = dq_all.at[dp] if mine else dq_all.at[there]
        return remote(
            dq_send, holder, q_send.at[i], q_recv.at[dp if mine else there], (there, mp)
        )

    def factor_start(i, carry):
        factor_copy(i, True).start()
        dq_copy(i, True).start()
        return carry

    lax.fori_loop(1, nd, factor_start, 0)

    kept = rank_f[:, 0:half].astype(BF)
    even = lax.rem(lax.div(lax.broadcasted_iota(jnp.int32, (count * 16, 1), 0), 8), 2) == 0
    rank_v = nt(kept, wq[:, 2 * half :])
    rank_k = nt(kept, wq[:, half : 2 * half])
    rank_f[...] = jnp.where(even, rank_v, rank_k)
    back_q = nt(dq.astype(BF), wq[:, 0:half])
    for p in range(count):
        rank_f[p * 16 + heads : p * 16 + heads + 1, :] = back_q[p : p + 1, :]
        rank_f[p * 16 + heads + 1 : p * 16 + 8, :] = jnp.zeros((7 - heads, width), F32)
        rank_f[p * 16 + 8 + heads : p * 16 + 16, :] = jnp.zeros((8 - heads, width), F32)
    rank_send[...] = rank_f[:, pl.ds(f_col, half)].astype(BF)
    coef_low = coef_own[...].astype(BF)
    o_coef[0] = coef_low
    coef_far_copy = remote(o_coef.at[0], coef_far, m_send.at[0], m_recv.at[0], pair)
    coef_far_copy.start()
    rank_copy = remote(rank_send, rank_far, m_send.at[1], m_recv.at[1], pair)
    rank_copy.start()
    d1_rows = d1_all[pl.ds(base, count), pl.ds(m_col, half)]
    d1_high = d1_rows.astype(BF).astype(F32)
    d1_low = d1_rows - d1_high
    for p in range(count):
        rank_f[p * 16 + 8 + heads : p * 16 + 9 + heads, pl.ds(m_col, half)] = d1_high[p : p + 1]
        rank_f[p * 16 + 9 + heads : p * 16 + 10 + heads, pl.ds(m_col, half)] = d1_low[p : p + 1]
    o_rank[0] = rank_f[:, pl.ds(m_col, half)].astype(BF)

    coef_far_copy.wait_recv()
    rank_copy.wait_recv()
    o_coef[1] = coef_far[...]
    o_rank[1] = rank_far[...]

    def factor_wait(i, carry):
        factor_copy(i, False).wait_recv()
        dq_copy(i, False).wait_recv()
        return carry

    lax.fori_loop(1, nd, factor_wait, 0)
    o_factor[...] = fac_all[...]
    o_dquery[...] = dq_all[...]

    def factor_sent(i, carry):
        factor_copy(i, True).wait_send()
        dq_copy(i, True).wait_send()
        return carry

    lax.fori_loop(1, nd, factor_sent, 0)
    coef_far_copy.wait_send()
    rank_copy.wait_send()
    bias_copy.wait_send()
    lax.fori_loop(1, 2 * chips, gather_sent, 0)
    to_sibling.wait_send()
    for k in range(chunks):
        cross(k).wait_send()
        for n in range(8):
            lane(k, n).wait_send()

    def drain(i, carry):
        ctx_copy(i).wait_send()
        out_copy(i, True).wait_send()
        out_copy(i, False).wait_recv()
        out_local(i).wait()
        return carry

    lax.fori_loop(0, own, drain, 0)


def gradients(
    nd,
    act_in,
    coef,
    rank,
    factor,
    dquery,
    active,
    inner,
    context,
    qcls,
    dctx,
    norm,
    ffn,
    attn,
    tok,
    sums,
    sums_in,
    loss,
    act_out,
    input_grad,
    grad_qkv,
    grad_out,
    grad_in,
    grad_back,
    small,
    act_sem,
    wide,
    rhs,
):
    dp = lax.axis_index("dp")
    mp = lax.axis_index("mp")
    copy = pltpu.make_async_copy(act_in, act_out, act_sem)
    copy.start()
    passages, width = ffn.shape
    half = width // 2
    heads = half // HEAD
    share = width // nd
    count = passages // nd
    slot = coef.shape[2]

    def input_rows(p, carry):
        rows16 = pl.ds(mult(p * 16, 16), 16)
        at = pl.ds(mult(p * slot, slot), slot)
        both = jnp.concatenate([coef[0, rows16, :], coef[1, rows16, :]], axis=0)
        right = jnp.concatenate([rank[0, rows16, :], rank[1, rows16, :]], axis=0)
        input_grad[at, :] = tn(both, right)
        return carry

    lax.fori_loop(0, count, input_rows, 0)

    own = lax.broadcasted_iota(jnp.int32, (width, share), 0)
    pick = (own == lax.broadcasted_iota(jnp.int32, (width, share), 1) + dp * share).astype(BF)
    own_t = lax.broadcasted_iota(jnp.int32, (share, width), 1)
    pick_t = (own_t == lax.broadcasted_iota(jnp.int32, (share, width), 0) + dp * share).astype(BF)
    ffn_own = nn(ffn[...], pick).astype(BF)
    attn_own = nn(attn[...], pick).astype(BF)
    norm_own = nt(pick_t, norm[...]).astype(BF)
    tok_own = nt(pick_t, tok[...]).astype(BF)
    grad_out[...] = tn(context[...], attn_own)
    unit = active.shape[2]
    for u in range(active.shape[0]):
        grad_back[u * unit : (u + 1) * unit, :] = tn(active[u], ffn_own)
        grad_in[:, u * unit : (u + 1) * unit] = nn(norm_own, inner[u])

    spread = lax.broadcasted_iota(jnp.int32, (8, half), 0) == lax.div(
        lax.broadcasted_iota(jnp.int32, (8, half), 1), HEAD
    )
    fkind = count * 8

    def build(s, carry):
        wide[...] = qcls[pl.ds(mult(s * count, 8), count), :].astype(F32) * 0.125
        d_rows = dctx[pl.ds(mult(s * count, 8), count), :].astype(F32)
        q_rows = wide[...]
        k_blocks = [
            jnp.where(spread, q_rows[p : p + 1, :], 0.0) for p in range(count)
        ]
        v_blocks = [
            jnp.where(spread, d_rows[p : p + 1, :], 0.0) for p in range(count)
        ]
        rhs[pl.ds(mult(s * fkind, 16), fkind), 0:half] = jnp.concatenate(k_blocks, 0).astype(BF)
        rhs[pl.ds(mult(s * fkind, 16), fkind), half:] = jnp.concatenate(v_blocks, 0).astype(BF)
        return carry

    lax.fori_loop(0, nd, build, 0)
    grad_k = jnp.zeros((share, half), F32)
    grad_v = jnp.zeros((share, half), F32)
    for s in range(0, nd, 4):
        left_v = jnp.concatenate([factor[s + t][:, 0:fkind] for t in range(4)], axis=1)
        left_k = jnp.concatenate([factor[s + t][:, fkind:] for t in range(4)], axis=1)
        grad_k = grad_k + nn(left_k, rhs[s * fkind : (s + 4) * fkind, 0:half])
        grad_v = grad_v + nn(left_v, rhs[s * fkind : (s + 4) * fkind, half:])
    grad_qkv[1] = grad_k
    grad_qkv[2] = grad_v
    dq_sum = []
    grad_q = []
    for b in range(half // 128):
        cols = dquery[:, pl.ds(0, 32), :].astype(F32)[:, b * 8 : b * 8 + 8, :]
        cols = cols.reshape(passages, 128)
        dq_sum.append(jnp.sum(cols, axis=0, keepdims=True))
        grad_qkv[0, :, b * 128 : b * 128 + 128] = nn(tok_own, cols.astype(BF))
    small[0:8, :] = sums[...]
    small[8:9, 0:half] = jnp.concatenate(dq_sum, axis=1)
    small[9:16, :] = jnp.zeros((7, width), F32)
    copy.wait()


def per_device(nd, *arrays):
    (
        tokens,
        lengths,
        queries,
        positives,
        w_qkv,
        b_qv,
        w_out,
        b_out,
        gain_one,
        shift_one,
        w_in,
        b_in,
        w_back,
        b_back,
        gain_two,
    ) = arrays
    rows, width = tokens.shape
    count = lengths.shape[0]
    slot = rows // count
    half = w_qkv.shape[2]
    units = w_in.shape[1]
    unit = 512
    blocks = units // unit
    chunks = 1 + 2 * blocks
    own_rows = rows // 2
    passages = nd * count
    chips = nd // 2
    q_rows = queries.shape[0]
    q_pad = nd * 16
    share = width // nd
    dp = lax.axis_index("dp")
    mp = lax.axis_index("mp")

    places = jnp.pad(positives.reshape(nd, q_rows), ((0, 0), (0, 16 - q_rows)), constant_values=-1)
    vmem = pl.BlockSpec(memory_space=pltpu.VMEM)
    hbm = pl.BlockSpec(memory_space=pl.ANY)
    smem = pl.BlockSpec(memory_space=pltpu.SMEM)
    in_specs = [smem, hbm, vmem, vmem, hbm, vmem, hbm, vmem, vmem, vmem, hbm, vmem, hbm, vmem, vmem]
    shape = jax.ShapeDtypeStruct
    outs = [
        (shape((rows, half), BF), hbm),
        (shape((2, count * 16, slot), BF), vmem),
        (shape((2, count * 16, half), BF), vmem),
        (shape((nd, share, 128), BF), vmem),
        (shape((nd, 32, 128), BF), vmem),
        (shape((blocks, passages, unit), BF), vmem),
        (shape((blocks, passages, unit), BF), vmem),
        (shape((passages, half), BF), vmem),
        (shape((passages, half), BF), vmem),
        (shape((passages, half), BF), vmem),
        (shape((passages, width), BF), vmem),
        (shape((passages, width), BF), vmem),
        (shape((passages, width), BF), vmem),
        (shape((passages, width), BF), vmem),
        (shape((8, width), F32), vmem),
        (shape((8, unit), F32), vmem),
        (shape((8, q_pad), F32), vmem),
        (shape((16, width), F32), vmem),
    ]
    dma = pltpu.SemaphoreType.DMA
    scratch = [
        pltpu.VMEM((rows, width), BF),
        pltpu.VMEM((width, 3 * half), BF),
        pltpu.VMEM((width, width), BF),
        pltpu.VMEM((2, blocks, width, unit), BF),
        pltpu.VMEM((2, blocks, unit, width), BF),
        pltpu.VMEM((rows, half), BF),
        pltpu.VMEM((rows, half), BF),
        pltpu.VMEM((own_rows, width), BF),
        pltpu.VMEM((own_rows, half), BF),
        pltpu.VMEM((own_rows, width), BF),
        pltpu.VMEM((own_rows, width), F32),
        pltpu.VMEM((blocks, own_rows, unit), BF),
        pltpu.VMEM((2, own_rows, half), BF),
        pltpu.VMEM((count, 8, slot), F32),
        pltpu.VMEM((2 * count * 8, width), F32),
        pltpu.VMEM((8, half), F32),
        pltpu.VMEM((8, width), F32),
        pltpu.VMEM((32, half), F32),
        pltpu.VMEM((chips, 2, 2, 32, half), BF),
        pltpu.VMEM((passages, width), BF),
        pltpu.VMEM((passages, width), BF),
        pltpu.VMEM((q_pad, width), BF),
        pltpu.VMEM((passages, width), F32),
        pltpu.VMEM((passages, width), BF),
        pltpu.VMEM((2, blocks, passages, unit), F32),
        pltpu.VMEM((2, blocks, passages, unit), BF),
        pltpu.VMEM((2, blocks, passages, unit), BF),
        pltpu.VMEM((passages, half), F32),
        pltpu.VMEM((passages, half), F32),
        pltpu.VMEM((passages, width), F32),
        pltpu.VMEM((8, half), F32),
        pltpu.VMEM((count * 16, width), F32),
        pltpu.VMEM((count * 16, slot), F32),
        pltpu.VMEM((count * 16, slot), BF),
        pltpu.VMEM((count * 16, half), BF),
        pltpu.VMEM((count * 16, half), BF),
        pltpu.VMEM((count * 16, half), BF),
        pltpu.VMEM((width, 128), BF),
        pltpu.VMEM((nd, share, 128), BF),
        pltpu.VMEM((32, 128), BF),
        pltpu.VMEM((nd, 32, 128), BF),
        dma((5 + 2 * blocks,)),
        dma((chunks,)),
        dma((chunks,)),
        dma((chunks, 8)),
        dma((chunks, 8)),
        dma((count // 2,)),
        dma((count // 2,)),
        dma((count // 2,)),
        dma((count // 2,)),
        dma((count // 2,)),
        dma((2 * chips,)),
        dma((2 * chips,)),
        dma,
        dma,
        dma((nd,)),
        dma((nd,)),
        dma((nd,)),
        dma((nd,)),
        dma((2,)),
        dma((2,)),
        dma,
        dma,
        pltpu.VMEM((8, unit), F32),
        pltpu.VMEM((8, unit), F32),
    ]
    made = pl.pallas_call(
        functools.partial(tower, nd, nd * q_rows),
        out_shape=[o[0] for o in outs],
        in_specs=in_specs,
        out_specs=[o[1] for o in outs],
        scratch_shapes=scratch,
        compiler_params=pltpu.CompilerParams(
            collective_id=0, has_side_effects=True, vmem_limit_bytes=60 * MIB
        ),
        name="tower",
    )(
        lengths,
        tokens,
        queries,
        places.reshape(1, q_pad),
        w_qkv,
        b_qv,
        w_out,
        b_out.reshape(1, width),
        gain_one.reshape(1, width),
        shift_one.reshape(1, width),
        w_in,
        b_in.reshape(blocks, unit),
        w_back,
        b_back.reshape(1, width),
        gain_two.reshape(1, width),
    )
    sums, sums_in, loss, q_grad = made[14:18]
    g_outs = [
        (shape((rows, half), BF), hbm),
        (shape((rows, half), F32), vmem),
        (shape((3, share, half), F32), vmem),
        (shape((half, share), F32), vmem),
        (shape((share, units), F32), vmem),
        (shape((units, share), F32), vmem),
        (shape((16, width), F32), vmem),
    ]
    grads = pl.pallas_call(
        functools.partial(gradients, nd),
        out_shape=[o[0] for o in g_outs],
        in_specs=[hbm] + [vmem] * 16,
        out_specs=[o[1] for o in g_outs],
        scratch_shapes=[
            dma,
            pltpu.VMEM((count, half), F32),
            pltpu.VMEM((nd * count * 8, width), BF),
        ],
        compiler_params=pltpu.CompilerParams(vmem_limit_bytes=48 * MIB),
        name="gradients",
    )(*made[:17])
    activations, input_grad, grad_qkv, grad_out, grad_in, grad_back, small = grads

    def own_part(row, size):
        return lax.dynamic_slice(small, (row, dp * size), (1, size))[0]

    bias_share = half // nd
    grad_bias_qv = jnp.stack([own_part(8, bias_share), own_part(5, bias_share)])
    in_share = units // nd
    grad_bias_in = lax.dynamic_slice(sums_in[:blocks].reshape(units), (dp * in_share,), (in_share,))
    query_loss = lax.dynamic_slice(loss[0], (dp * 16,), (q_rows,))
    return (
        activations,
        query_loss,
        input_grad,
        q_grad[:q_rows],
        grad_qkv,
        grad_bias_qv,
        grad_out,
        own_part(4, share),
        own_part(2, share),
        own_part(3, share),
        grad_in,
        grad_bias_in,
        grad_back,
        own_part(1, share),
        own_part(0, share),
    )


def layer_norm(rows, gain, shift):
    center = jnp.mean(rows, axis=-1, keepdims=True)
    spread = rows - center
    second = jnp.mean(spread * spread, axis=-1, keepdims=True)
    return spread * lax.rsqrt(second + EPS) * gain + shift


def scaled_norm(rows, gain):
    center = jnp.mean(rows, axis=-1, keepdims=True)
    spread = rows - center
    second = jnp.mean(spread * spread, axis=-1, keepdims=True)
    return spread * lax.rsqrt(second + EPS) * gain


def gelu_exact(values):
    return jax.nn.gelu(values, approximate=False)


def first_rows(values, count):
    return values.reshape((count, values.shape[0] // count) + values.shape[1:])[:, 0]


def by_collectives(
    tokens,
    lengths,
    queries,
    positives,
    w_qkv,
    b_qv,
    w_out,
    b_out,
    gain_one,
    shift_one,
    w_in,
    b_in,
    w_back,
    b_back,
    gain_two,
):
    rows, width = tokens.shape
    count = lengths.shape[0]
    slot = rows // count
    local = w_qkv.shape[2]
    heads_here = local // HEAD
    scale = 1.0 / math.sqrt(HEAD)
    projected = jnp.einsum("rd,jdc->jrc", tokens, w_qkv, preferred_element_type=F32)
    bias_qv = b_qv.astype(F32)
    query = (projected[0] + bias_qv[0]).astype(BF)
    keyed = projected[1].astype(BF)
    value = (projected[2] + bias_qv[1]).astype(BF)
    block = min(count, max(1, 512 // slot))
    blocks = count // block
    valid = lax.broadcasted_iota(jnp.int32, (count, slot), 1) < lengths[:, None]
    split_shape = (blocks, block, slot, heads_here, HEAD)

    def attend(inputs):
        query_part, keyed_part, value_part, valid_part = inputs
        scores = (
            jnp.einsum(
                "pqhd,pkhd->phqk", query_part, keyed_part, preferred_element_type=F32
            )
            * scale
        )
        scores = jnp.where(valid_part[:, None, None, :], scores, MASKED)
        top = jnp.max(scores, axis=-1, keepdims=True)
        raised = jnp.exp(scores - top)
        total = jnp.sum(raised, axis=-1, keepdims=True)
        chance_low = (raised / total).astype(BF)
        mixed = jnp.einsum(
            "phqk,pkhd->pqhd", chance_low, value_part, preferred_element_type=F32
        )
        return (mixed.astype(BF), (top + jnp.log(total))[:, :, 0, 0])

    context, log_total = lax.map(
        attend,
        (
            query.reshape(split_shape),
            keyed.reshape(split_shape),
            value.reshape(split_shape),
            valid.reshape(blocks, block, slot),
        ),
    )
    context = context.reshape(rows, local)
    log_total = log_total.reshape(count, heads_here)
    partial_attn = jnp.dot(context, w_out, preferred_element_type=F32).astype(BF)
    attended = lax.psum(partial_attn, "mp").astype(F32) + b_out.astype(F32)
    resid_one = tokens.astype(F32) + attended
    gain_one_w = gain_one.astype(F32)
    shift_one_w = shift_one.astype(F32)
    gain_two_w = gain_two.astype(F32)
    norm_one = layer_norm(resid_one, gain_one_w, shift_one_w)
    norm_low = norm_one.astype(BF)
    inner = jnp.dot(norm_low, w_in, preferred_element_type=F32) + b_in.astype(F32)
    active = gelu_exact(inner).astype(BF)
    partial_ffn = jnp.dot(active, w_back, preferred_element_type=F32).astype(BF)
    resid_two = (
        norm_one + lax.psum(partial_ffn, "mp").astype(F32) + b_back.astype(F32)
    )
    output = scaled_norm(resid_two, gain_two_w)
    column = lax.axis_index("mp") * local
    activations = lax.dynamic_slice_in_dim(output, column, local, 1).astype(BF)
    cls_low = first_rows(output, count).astype(BF)
    query_rows = queries.shape[0]
    members = lax.axis_size("dp")
    query_total = query_rows * members
    own_query = lax.axis_index("dp") * query_rows
    gathered = lax.all_gather(cls_low, "dp", axis=0, tiled=True)
    similar = jnp.einsum("qd,pd->qp", queries, gathered, preferred_element_type=F32)
    mine = lax.dynamic_slice_in_dim(positives, own_query, query_rows)
    target = lax.broadcasted_iota(jnp.int32, similar.shape, 1) == mine[:, None]
    top = jnp.max(similar, axis=1, keepdims=True)
    log_sum = top[:, 0] + jnp.log(jnp.sum(jnp.exp(similar - top), axis=1))
    picked = jnp.sum(jnp.where(target, similar, 0.0), axis=1)
    query_loss = log_sum - picked
    slopes = (jnp.exp(similar - log_sum[:, None]) - target.astype(F32)) / query_total
    query_grad = jnp.dot(slopes, gathered.astype(F32), precision=lax.Precision.HIGHEST)
    queries_wide = queries.astype(F32)
    cls_grad = lax.psum_scatter(
        jnp.einsum("qp,qd->pd", slopes, queries_wide, precision=lax.Precision.HIGHEST),
        "dp",
        scatter_dimension=0,
        tiled=True,
    )
    _, norm_two_pull = jax.vjp(scaled_norm, first_rows(resid_two, count), gain_two_w)
    d_resid_two, grad_gain_two = norm_two_pull(cls_grad)
    grad_bias_back = jnp.sum(d_resid_two, axis=0)
    ffn_low = d_resid_two.astype(BF)
    grad_back = jnp.einsum(
        "pf,pd->fd", first_rows(active, count), ffn_low, preferred_element_type=F32
    )
    d_active = jnp.einsum("pd,fd->pf", ffn_low, w_back, preferred_element_type=F32)
    _, gelu_pull = jax.vjp(gelu_exact, first_rows(inner, count))
    d_inner = gelu_pull(d_active)[0]
    grad_bias_in = jnp.sum(d_inner, axis=0)
    inner_low = d_inner.astype(BF)
    grad_in = jnp.einsum(
        "pd,pf->df", first_rows(norm_low, count), inner_low, preferred_element_type=F32
    )
    back_norm = jnp.einsum("pf,df->pd", inner_low, w_in, preferred_element_type=F32)
    d_norm_one = d_resid_two + lax.psum(back_norm, "mp")
    _, norm_one_pull = jax.vjp(layer_norm, first_rows(resid_one, count), gain_one_w, shift_one_w)
    d_resid_one, grad_gain_one, grad_shift_one = norm_one_pull(d_norm_one)
    grad_bias_out = jnp.sum(d_resid_one, axis=0)
    attn_low = d_resid_one.astype(BF)
    grad_out = jnp.einsum(
        "pc,pd->cd", first_rows(context, count), attn_low, preferred_element_type=F32
    )
    d_context = jnp.einsum("pd,cd->pc", attn_low, w_out, preferred_element_type=F32).astype(
        BF
    )
    d_context = d_context.reshape(count, heads_here, HEAD)
    query_cls = first_rows(query, count).reshape(count, heads_here, HEAD)
    keyed_heads = keyed.reshape(count, slot, heads_here, HEAD)
    value_heads = value.reshape(count, slot, heads_here, HEAD)
    scores_cls = (
        jnp.einsum("phd,pkhd->phk", query_cls, keyed_heads, preferred_element_type=F32)
        * scale
    )
    scores_cls = jnp.where(valid[:, None, :], scores_cls, MASKED)
    chance = jnp.exp(scores_cls - log_total[:, :, None])
    d_chance = jnp.einsum(
        "phd,pkhd->phk", d_context, value_heads, preferred_element_type=F32
    )
    d_value = jnp.einsum(
        "phk,phd->pkhd", chance.astype(BF), d_context, preferred_element_type=F32
    )
    d_scores = chance * (d_chance - jnp.sum(chance * d_chance, axis=-1, keepdims=True))
    scores_low = d_scores.astype(BF)
    d_query = (
        jnp.einsum("phk,pkhd->phd", scores_low, keyed_heads, preferred_element_type=F32)
        * scale
    )
    d_keyed = (
        jnp.einsum("phk,phd->pkhd", scores_low, query_cls, preferred_element_type=F32)
        * scale
    )
    d_query = d_query.reshape(count, local)
    d_value = d_value.reshape(rows, local)
    query_low = d_query.astype(BF)
    keyed_value_low = jnp.stack(
        [d_keyed.reshape(rows, local).astype(BF), d_value.astype(BF)]
    )
    grad_bias_qv = jnp.stack([jnp.sum(d_query, axis=0), jnp.sum(d_value, axis=0)])
    grad_query_w = jnp.einsum(
        "pd,pc->dc", first_rows(tokens, count), query_low, preferred_element_type=F32
    )
    grad_kv = jnp.einsum("rd,jrc->jdc", tokens, keyed_value_low, preferred_element_type=F32)
    grad_qkv = jnp.concatenate([grad_query_w[None], grad_kv], axis=0)
    own_half = lax.dynamic_slice_in_dim(d_resid_one, column, local, 1)
    back_kv = jnp.einsum(
        "jrc,jdc->rd", keyed_value_low, w_qkv[1:], preferred_element_type=F32
    )
    back_query = jnp.einsum("pc,dc->pd", query_low, w_qkv[0], preferred_element_type=F32)
    back_all = back_kv.reshape(count, slot, width).at[:, 0].add(back_query).reshape(rows, width)
    input_grad = lax.psum_scatter(
        back_all.astype(BF), "mp", scatter_dimension=1, tiled=True
    ).astype(F32)
    input_grad = input_grad.reshape(count, slot, local).at[:, 0].add(own_half).reshape(rows, local)
    summed = (
        lax.psum_scatter(grad_qkv, "dp", scatter_dimension=1, tiled=True),
        lax.psum_scatter(grad_bias_qv, "dp", scatter_dimension=1, tiled=True),
        lax.psum_scatter(grad_out, "dp", scatter_dimension=1, tiled=True),
        lax.psum_scatter(grad_bias_out, "dp", scatter_dimension=0, tiled=True),
        lax.psum_scatter(grad_gain_one, "dp", scatter_dimension=0, tiled=True),
        lax.psum_scatter(grad_shift_one, "dp", scatter_dimension=0, tiled=True),
        lax.psum_scatter(grad_in, "dp", scatter_dimension=0, tiled=True),
        lax.psum_scatter(grad_bias_in, "dp", scatter_dimension=0, tiled=True),
        lax.psum_scatter(grad_back, "dp", scatter_dimension=1, tiled=True),
        lax.psum_scatter(grad_bias_back, "dp", scatter_dimension=0, tiled=True),
        lax.psum_scatter(grad_gain_two, "dp", scatter_dimension=0, tiled=True),
    )
    return (
        activations,
        query_loss,
        input_grad,
        query_grad,
        summed[0],
        summed[1],
        summed[2],
        summed[3],
        summed[4],
        summed[5],
        summed[6],
        summed[7],
        summed[8],
        summed[9],
        summed[10],
    )


def solution(mesh):
    in_specs = (
        P("dp", None),
        P("dp"),
        P("dp", None),
        P(),
        P(None, None, "mp"),
        P(None, "mp"),
        P("mp", None),
        P(),
        P(),
        P(),
        P(None, "mp"),
        P("mp"),
        P("mp", None),
        P(),
        P(),
    )
    out_specs = (
        P("dp", "mp"),
        P("dp"),
        P("dp", "mp"),
        P("dp", None),
        P(None, "dp", "mp"),
        P(None, ("mp", "dp")),
        P("mp", "dp"),
        P("dp"),
        P("dp"),
        P("dp"),
        P("dp", "mp"),
        P(("mp", "dp")),
        P("mp", "dp"),
        P("dp"),
        P("dp"),
    )
    groups = mesh.shape["dp"]
    fits = groups <= 16 and mesh.shape["mp"] == 2
    return jax.shard_map(
        functools.partial(per_device, groups) if fits else by_collectives,
        mesh=mesh,
        in_specs=in_specs,
        out_specs=out_specs,
        check_vma=False,
    )
```

```python
import functools
import math

import jax
import jax.numpy as jnp
from jax import lax
from jax.experimental import pallas as pl
from jax.experimental.pallas import tpu as pltpu
from jax.sharding import PartitionSpec as P

HEAD = 64
EPS = 1e-05
MASKED = -1e30
MESH = pl.DeviceIdType.MESH
BF = jnp.bfloat16
F32 = jnp.float32
MIB = 2**20


def nn(a, b):
    return jnp.dot(a, b, preferred_element_type=F32)


def nt(a, b):
    return lax.dot_general(a, b, (((1,), (1,)), ((), ())), preferred_element_type=F32)


def tn(a, b):
    return lax.dot_general(a, b, (((0,), (0,)), ((), ())), preferred_element_type=F32)


def gelu(h):
    return 0.5 * h * (1.0 + lax.erf(h * math.sqrt(0.5)))


def gelu_slope(h):
    bell = jnp.exp(-0.5 * h * h) * (1.0 / math.sqrt(2.0 * math.pi))
    return 0.5 * (1.0 + lax.erf(h * math.sqrt(0.5))) + h * bell


def row_of(vector):
    return vector[None, :].astype(F32)


def exact(a, b):
    return jnp.dot(a, b, preferred_element_type=F32, precision=lax.Precision.HIGHEST)


def one_hot(shape, shift, dtype=F32):
    row = lax.broadcasted_iota(jnp.int32, shape, 0)
    column = lax.broadcasted_iota(jnp.int32, shape, 1)
    return (row == column + shift).astype(dtype)


def standard(rows):
    center = jnp.mean(rows, axis=-1, keepdims=True)
    spread = rows - center
    second = jnp.mean(spread * spread, axis=-1, keepdims=True)
    inverse = lax.rsqrt(second + EPS)
    return spread * inverse, inverse


def norm_back(grad, scaled, inverse):
    first = jnp.mean(grad, axis=-1, keepdims=True)
    second = jnp.mean(grad * scaled, axis=-1, keepdims=True)
    return inverse * (grad - first - scaled * second)


def flip(index, bit):
    return index + bit * (1 - 2 * lax.rem(lax.div(index, bit), 2))


def mult(value, step):
    return pl.multiple_of(value, step)


def tower(
    nd,
    query_total,
    lengths,
    tokens,
    queries,
    positives,
    w_qkv,
    b_qv,
    w_out,
    b_out,
    gain_one,
    shift_one,
    w_in,
    b_in,
    w_back,
    b_back,
    gain_two,
    out_act,
    o_coef,
    o_rank,
    o_factor,
    o_dquery,
    o_active,
    o_inner,
    o_context,
    o_qcls,
    o_dctx,
    o_norm,
    o_ffn,
    o_attn,
    o_tok,
    o_sums,
    o_sums_in,
    o_loss,
    o_qgrad,
    tok,
    wq,
    wo,
    wi,
    wb,
    keyb,
    valb,
    ctx,
    ctx_send,
    norm_low,
    acc,
    act_far,
    obuf,
    chance,
    factor,
    stage,
    tcls,
    pack,
    gath,
    ctx_all,
    tok_all,
    q_all,
    xh1_all,
    norm_all,
    inner_all,
    act_all,
    low_all,
    dc_all,
    qc_all,
    d1_all,
    dq_rows,
    rank_f,
    coef_own,
    coef_far,
    rank_own,
    rank_send,
    rank_far,
    fac_send,
    fac_all,
    dq_send,
    dq_all,
    loc_sem,
    ysend,
    yrecv,
    w_send,
    w_recv,
    c_send,
    c_recv,
    o_send,
    o_recv,
    o_loc,
    g_send,
    g_recv,
    gs_send,
    gs_recv,
    f_send,
    f_recv,
    q_send,
    q_recv,
    m_send,
    m_recv,
    b_send,
    b_recv,
    bin_own,
    bin_far,
):
    dp = lax.axis_index("dp")
    mp = lax.axis_index("mp")
    far = 1 - mp
    chips = nd // 2
    core = lax.rem(dp, 2)
    chip = lax.div(dp, 2)
    bit_a = lax.rem(lax.div(dp, 2), 2)
    bit_b = lax.rem(lax.div(dp, 4), 2)
    quarter = bit_a + 2 * bit_b
    quarter_x = flip(quarter, 1)
    quarter_z = flip(quarter, 2)
    quarter_d = 3 - quarter
    pair = (dp, far)
    sibling = (flip(dp, 1), mp)
    near_x = (flip(dp, 2), mp)
    near_z = (flip(dp, 4), mp)

    rows, width = tok.shape
    count = lengths.shape[0]
    slot = rows // count
    own = count // 2
    half = width // 2
    own_rows = own * slot
    passages = nd * count
    blocks, unit = wi.shape[1], wi.shape[3]
    m_col = mult(mp * half, 128)
    f_col = mult(far * half, 128)

    barrier = pltpu.get_barrier_semaphore()

    def greet(i, carry):
        other = lax.rem(dp * 2 + mp + i, 2 * nd)
        pl.semaphore_signal(
            barrier,
            inc=1,
            device_id=(lax.div(other, 2), lax.rem(other, 2)),
            device_id_type=MESH,
        )
        return carry

    lax.fori_loop(1, 2 * nd, greet, 0)

    def local(src, dst, k):
        return pltpu.make_async_copy(src, dst, loc_sem.at[k])

    loads = [local(tokens, tok, 0)]
    loads += [local(w_qkv.at[j], wq.at[:, pl.ds(j * half, half)], 1 + j) for j in range(3)]
    loads.append(local(w_out, wo.at[pl.ds(mult(mp * half, 128), half), :], 4))
    loads += [
        local(w_in.at[:, pl.ds(u * unit, unit)], wi.at[mp, u], 5 + u) for u in range(blocks)
    ]
    loads += [
        local(w_back.at[pl.ds(u * unit, unit), :], wb.at[mp, u], 5 + blocks + u)
        for u in range(blocks)
    ]
    for copy in loads:
        copy.start()

    chunks = 1 + 2 * blocks

    def piece(k, q, c, which, side=None):
        if k == 0:
            size = half // 8
            at = mult(which * half + (c * 4 + q) * size, 16)
            cols = pl.ds(0, width) if side is None else pl.ds(side * half, half)
            return wo.at[pl.ds(at, size), cols]
        if k <= blocks:
            size = width // 8
            at = (c * 4 + q) * size
            if side is not None:
                size = size // 2
                at = at + side * size
            return wi.at[which, k - 1, pl.ds(mult(at, 16), size), :]
        size = unit // 8
        cols = pl.ds(0, width) if side is None else pl.ds(side * half, half)
        return wb.at[which, k - 1 - blocks, pl.ds(mult((c * 4 + q) * size, 16), size), cols]

    def source(k):
        if k == 0:
            size = half // 8
            return w_out.at[pl.ds(mult((core * 4 + quarter) * size, 16), size), :]
        if k <= blocks:
            size = width // 8
            at = mult((core * 4 + quarter) * size, 16)
            return w_in.at[pl.ds(at, size), pl.ds((k - 1) * unit, unit)]
        size = unit // 8
        at = mult((k - 1 - blocks) * unit + (core * 4 + quarter) * size, 16)
        return w_back.at[pl.ds(at, size), :]

    def remote(src, dst, ss, rs, device):
        return pltpu.make_async_remote_copy(
            src_ref=src,
            dst_ref=dst,
            send_sem=ss,
            recv_sem=rs,
            device_id=device,
            device_id_type=MESH,
        )

    def cross(k):
        return remote(
            source(k), piece(k, quarter, core, mp), ysend.at[k], yrecv.at[k], pair
        )

    def send(k, lane, q, c, side, device):
        ref = piece(k, q, c, far, side)
        return remote(ref, ref, w_send.at[k, lane], w_recv.at[k, lane], device)

    def lane(k, n):
        q = (quarter, quarter, quarter_z, quarter_x, quarter, quarter_x, quarter_z, quarter_d)[n]
        side = (None, None, 0, 1, None, None, None, None)[n]
        return send(k, n, q, core, side, (near_x, near_z, near_x, near_z)[n] if n < 4 else sibling)

    def arrival(k, n):
        q = (quarter_x, quarter_z, quarter_d, quarter_d, quarter, quarter_x, quarter_z, quarter_d)[n]
        side = (None, None, 0, 1, None, None, None, None)[n]
        c = core if n < 4 else 1 - core
        return send(k, n, q, c, side, (near_x, near_z, near_x, near_z)[n] if n < 4 else sibling)

    def step_one(k):
        remote(
            source(k), piece(k, quarter, core, far), ysend.at[k], yrecv.at[k], pair
        ).wait_recv()
        for n in (0, 1, 4):
            lane(k, n).start()

    def step_two(k):
        arrival(k, 1).wait_recv()
        lane(k, 2).start()
        arrival(k, 0).wait_recv()
        for n in (3, 5, 6):
            lane(k, n).start()

    def step_three(k):
        arrival(k, 2).wait_recv()
        arrival(k, 3).wait_recv()
        lane(k, 7).start()

    def complete(k):
        for n in range(4, 8):
            arrival(k, n).wait_recv()

    def tick(i):
        if i < chunks:
            step_one(i)
        if 0 <= i - 1 < chunks:
            step_two(i - 1)
        if 0 <= i - 2 < chunks:
            step_three(i - 2)

    for copy in loads[:4]:
        copy.wait()
    pl.semaphore_wait(barrier, 2 * nd - 1)
    bin_own[...] = jnp.zeros_like(bin_own)
    for u in range(blocks):
        bin_own[u : u + 1, :] = row_of(b_in[pl.ds(u * unit, unit)])
    bias_copy = remote(bin_own, bin_far, b_send, b_recv, pair)
    bias_copy.start()
    for k in range(chunks):
        cross(k).start()

    lane_pair = lax.broadcasted_iota(jnp.int32, (slot, 128), 1)
    key_place = lax.broadcasted_iota(jnp.int32, (1, slot), 1)
    head_rows = lax.broadcasted_iota(jnp.int32, (8, half), 0)
    head_mask = head_rows == lax.div(lax.broadcasted_iota(jnp.int32, (8, half), 1), HEAD)
    heads = half // HEAD
    live = lax.broadcasted_iota(jnp.int32, (8, 1), 0) < heads
    bias_q = b_qv[0:1, :].astype(F32)
    bias_v = b_qv[1:2, :].astype(F32)
    ones = jnp.ones((slot, 128), BF)
    row_place = lax.broadcasted_iota(jnp.int32, (8, slot), 0)
    first_key = (lax.broadcasted_iota(jnp.int32, (8, slot), 1) == 0).astype(F32)

    def ctx_copy(i):
        there = ctx.at[pl.ds(mult(i * slot, 16), slot), pl.ds(m_col, half)]
        return remote(
            ctx_send.at[pl.ds(mult(i * slot, 16), slot), :], there, c_send.at[i], c_recv.at[i], pair
        )

    def ctx_came(i):
        here = ctx.at[pl.ds(mult(i * slot, 16), slot), pl.ds(f_col, half)]
        return remote(
            ctx_send.at[pl.ds(mult(i * slot, 16), slot), :], here, c_send.at[i], c_recv.at[i], pair
        )

    def attend(i, carry):
        theirs = i < own
        side = jnp.where(theirs, far, mp)
        place = lax.rem(i, own)
        p = side * own + place
        at = mult(p * slot, slot)
        x = tok[pl.ds(at, slot), :]
        made = nn(x, wq[...])
        query = ((made[:, :half] + bias_q).astype(BF).astype(F32) * 0.125).astype(BF)
        keyed = made[:, half : 2 * half].astype(BF)
        value = (made[:, 2 * half :] + bias_v).astype(BF)
        keyb[pl.ds(at, slot), :] = keyed
        valb[pl.ds(at, slot), :] = value
        length = lengths[p]
        bias = jnp.where(key_place < length, 0.0, MASKED)
        done = []
        for t in range(half // 128):
            q2 = query[:, 128 * t : 128 * t + 128]
            k2 = keyed[:, 128 * t : 128 * t + 128]
            v2 = jnp.concatenate([value[:, 128 * t : 128 * t + 128], ones], axis=1)
            parts = []
            for hx in range(2):
                mask = (lane_pair < HEAD) if hx == 0 else (lane_pair >= HEAD)
                s = nt(jnp.where(mask, q2, jnp.zeros_like(q2)), k2) + bias
                e = jnp.exp(s - jnp.max(s, axis=1, keepdims=True)).astype(BF)
                o = nn(e, v2)
                parts.append(o[:, :128] / o[:, 128:])
            done.append(jnp.where(lane_pair < HEAD, parts[0], parts[1]))
        mixed = jnp.concatenate(done, axis=1)
        low = mixed.astype(BF)
        stage[pl.ds(p, 1), :] = mixed[0:1, :]
        tcls[pl.ds(p, 1), :] = x[0:16, :].astype(F32)[0:1, :]
        q_row = query[0:16, :].astype(F32)[0:1, :]
        q_heads = jnp.where(head_mask, q_row, 0.0).astype(BF)
        s = nt(q_heads, keyed) + bias
        e = jnp.exp(s - jnp.max(s, axis=1, keepdims=True))
        c = jnp.where(live, e / jnp.sum(e, axis=1, keepdims=True), 0.0)
        chance[p] = c
        c_low = c.astype(BF)
        coef_own[pl.ds(mult(p * 16, 16), 8), :] = jnp.where(row_place == heads, first_key, c)
        factor[pl.ds(mult(p * 8, 8), 8), :] = nn(c_low, x)

        @pl.when(theirs)
        def _():
            ctx_send[pl.ds(mult(place * slot, 16), slot), :] = low
            ctx_copy(place).start()

        @pl.when(i >= own)
        def _():
            ctx[pl.ds(mult(place * slot, 16), slot), pl.ds(m_col, half)] = low

        @pl.when(i == own)
        def _():
            tick(0)

        @pl.when(i == own + 2)
        def _():
            tick(1)

        return carry

    lax.fori_loop(0, count, attend, 0)

    pack[0:8, :] = stage[...]
    pack[8:16, :] = tcls[:, pl.ds(m_col, half)]
    pack[16:32, :] = jnp.zeros((16, half), F32)
    q_rows = queries.shape[0]
    pack[16 : 16 + q_rows, :] = queries[:, pl.ds(m_col, half)].astype(F32)
    gath[chip, core, mp] = pack[...].astype(BF)

    def gather_copy(i, mine):
        me = chip * 2 + mp
        there = lax.rem(me + i, 2 * chips)
        t_chip, t_mp = lax.div(there, 2), lax.rem(there, 2)
        holder = gath.at[chip, core, mp] if mine else gath.at[t_chip, core, t_mp]
        return remote(
            gath.at[chip, core, mp],
            holder,
            g_send.at[i],
            g_recv.at[me if mine else there],
            (t_chip * 2 + core, t_mp),
        )

    def gather_start(i, carry):
        gather_copy(i, True).start()
        return carry

    def gather_wait(i, carry):
        gather_copy(i, False).wait_recv()
        return carry

    def gather_sent(i, carry):
        gather_copy(i, True).wait_send()
        return carry

    lax.fori_loop(1, 2 * chips, gather_start, 0)

    for copy in loads[4:]:
        copy.wait()
    tick(2)
    tick(3)
    complete(0)
    bo = row_of(b_out[...])
    g1 = row_of(gain_one[...])
    s1 = row_of(shift_one[...])
    g2 = row_of(gain_two[...])
    bb = row_of(b_back[...])

    def feed_own(i, carry):
        ctx_came(i).wait_recv()
        at = mult(i * slot, slot)
        here = pl.ds(at, slot)
        x = tok[pl.ds(mult(mp * own_rows + i * slot, slot), slot), :].astype(F32)
        resid = x + nn(ctx[here, :], wo[...]) + bo
        scaled, _ = standard(resid)
        norm = scaled * g1 + s1
        low = norm.astype(BF)
        norm_low[here, :] = low
        total = norm + bb
        for u in range(blocks):
            inner = nn(low, wi[mp, u]) + bin_own[u : u + 1, :]
            total = total + nn(gelu(inner).astype(BF), wb[mp, u])
        acc[here, :] = total

        for j in range(own):

            @pl.when(i == j)
            def _():
                if j + 4 < chunks + 2:
                    tick(j + 4)

        return carry

    lax.fori_loop(0, own, feed_own, 0)
    for i in range(own + 4, chunks + 2):
        tick(i)

    lax.fori_loop(1, 2 * chips, gather_wait, 0)
    to_sibling = remote(gath.at[:, core], gath.at[:, core], gs_send, gs_recv, sibling)
    to_sibling.start()

    bias_copy.wait_recv()
    for u in range(blocks):
        complete(1 + u)

        def feed_far_in(i, carry, u=u):
            here = pl.ds(mult(i * slot, slot), slot)
            inner = nn(norm_low[here, :], wi[far, u]) + bin_far[u : u + 1, :]
            act_far[u, here, :] = gelu(inner).astype(BF)
            return carry

        lax.fori_loop(0, own, feed_far_in, 0)

    for u in range(blocks - 1):
        complete(1 + blocks + u)

        def feed_far_back(i, carry, u=u):
            here = pl.ds(mult(i * slot, slot), slot)
            acc[here, :] += nn(act_far[u, here, :], wb[far, u])
            return carry

        lax.fori_loop(0, own, feed_far_back, 0)

    complete(chunks - 1)

    def out_copy(i, mine):
        side = mp if mine else far
        there = out_act.at[pl.ds(mult(side * own_rows + i * slot, 16), slot), :]
        return remote(
            obuf.at[1, pl.ds(mult(i * slot, 16), slot), :], there, o_send.at[i], o_recv.at[i], pair
        )

    def out_local(i):
        there = out_act.at[pl.ds(mult(mp * own_rows + i * slot, 16), slot), :]
        return pltpu.make_async_copy(
            obuf.at[0, pl.ds(mult(i * slot, 16), slot), :], there, o_loc.at[i]
        )

    def finish(i, carry):
        here = pl.ds(mult(i * slot, slot), slot)
        total = acc[here, :] + nn(act_far[blocks - 1, here, :], wb[far, blocks - 1])
        scaled, _ = standard(total)
        acc[here, :] = scaled * g2
        obuf[0, here, :] = acc[here, pl.ds(m_col, half)].astype(BF)
        obuf[1, here, :] = acc[here, pl.ds(f_col, half)].astype(BF)
        out_copy(i, True).start()
        out_local(i).start()
        return carry

    lax.fori_loop(0, own, finish, 0)

    remote(
        gath.at[:, 1 - core], gath.at[:, 1 - core], gs_send, gs_recv, sibling
    ).wait_recv()
    q_pad = nd * 16
    for h in range(2):
        cols = slice(h * half, (h + 1) * half)
        block = gath[:, :, h].astype(F32)
        ctx_all[:, cols] = block[:, :, 0:8].reshape(passages, half).astype(BF)
        tok_all[:, cols] = block[:, :, 8:16].reshape(passages, half).astype(BF)
        q_all[:, cols] = block[:, :, 16:32].reshape(q_pad, half).astype(BF)

    resid = tok_all[...].astype(F32) + nn(ctx_all[...], wo[...]) + bo
    scaled, inverse1 = standard(resid)
    xh1_all[...] = scaled
    norm = scaled * g1 + s1
    low = norm.astype(BF)
    norm_all[...] = low
    total = norm + bb
    for h in range(2):
        for u in range(blocks):
            bias = jnp.where(mp == h, bin_own[u : u + 1, :], bin_far[u : u + 1, :])
            inner = nn(low, wi[h, u]) + bias
            inner_all[h, u] = inner
            active = gelu(inner).astype(BF)
            act_all[h, u] = active
            total = total + nn(active, wb[h, u])
    xh2, inverse2 = standard(total)
    cls = (xh2 * g2).astype(BF)
    similar = nt(cls, q_all[...])
    top = jnp.max(similar, axis=0, keepdims=True)
    log_sum = top + jnp.log(jnp.sum(jnp.exp(similar - top), axis=0, keepdims=True))
    q_count = query_total // nd
    from_q = lax.broadcasted_iota(jnp.int32, (query_total, q_pad), 0)
    to_q = lax.broadcasted_iota(jnp.int32, (query_total, q_pad), 1)
    spot = lax.div(from_q, q_count) * 16 + lax.rem(from_q, q_count)
    wanted = jnp.broadcast_to(row_of(positives[...]), (8, query_total)) + 1.0
    place = exact(wanted, (spot == to_q).astype(F32))[0:1, :] - 1.0
    target = lax.broadcasted_iota(jnp.int32, similar.shape, 0).astype(F32) == place
    picked = jnp.sum(jnp.where(target, similar, 0.0), axis=0, keepdims=True)
    o_loss[...] = jnp.broadcast_to(log_sum - picked, o_loss.shape)
    slopes = (jnp.exp(similar - log_sum) - target.astype(F32)) * (1.0 / query_total)
    slope_high = slopes.astype(BF)
    slope_low = (slopes - slope_high.astype(F32)).astype(BF)
    cls_grad = nn(slope_high, q_all[...]) + nn(slope_low, q_all[...])
    pick = (
        lax.broadcasted_iota(jnp.int32, (16, q_pad), 1)
        == lax.broadcasted_iota(jnp.int32, (16, q_pad), 0) + dp * 16
    ).astype(BF)
    o_qgrad[...] = nn(nt(pick, slope_high).astype(BF), cls) + nn(
        nt(pick, slope_low).astype(BF), cls
    )
    d_two = norm_back(g2 * cls_grad, xh2, inverse2)
    o_sums[0:1, :] = jnp.sum(cls_grad * xh2, axis=0, keepdims=True)
    o_sums[1:2, :] = jnp.sum(d_two, axis=0, keepdims=True)
    ffn_low = d_two.astype(BF)
    o_ffn[...] = ffn_low
    back = d_two
    for h in range(2):
        for u in range(blocks):
            d_active = nt(ffn_low, wb[h, u])
            d_inner = d_active * gelu_slope(inner_all[h, u])
            inner_all[h, u, 0:8, :] = jnp.broadcast_to(
                jnp.sum(d_inner, axis=0, keepdims=True), (8, unit)
            )
            inner_low = d_inner.astype(BF)
            low_all[h, u] = inner_low
            back = back + nt(inner_low, wi[h, u])
    for u in range(blocks):
        o_active[u] = act_all[mp, u]
        o_inner[u] = low_all[mp, u]
        o_sums_in[u : u + 1, :] = inner_all[mp, u, 0:1, :]
    xh1 = xh1_all[...]
    d_one = norm_back(g1 * back, xh1, inverse1)
    d1_all[...] = d_one
    o_sums[2:3, :] = jnp.sum(back * xh1, axis=0, keepdims=True)
    o_sums[3:4, :] = jnp.sum(back, axis=0, keepdims=True)
    o_sums[4:5, :] = jnp.sum(d_one, axis=0, keepdims=True)
    attn_low = d_one.astype(BF)
    o_attn[...] = attn_low
    o_norm[...] = norm_all[...]
    o_tok[...] = tok_all[...]
    d_ctx = nt(attn_low, wo[pl.ds(mult(mp * half, 128), half), :]).astype(BF)
    o_dctx[...] = d_ctx
    dc_all[...] = d_ctx.astype(F32)
    q_cls = (nn(tok_all[...], wq[:, 0:half]) + bias_q).astype(BF)
    o_qcls[...] = q_cls
    qc_all[...] = q_cls.astype(F32) * 0.125
    o_context[...] = ctx_all[:, pl.ds(m_col, half)]
    o_sums[5:6, 0:half] = jnp.sum(dc_all[...], axis=0, keepdims=True)

    base = mult(dp * count, 8)
    fkind = count * 8

    def attend_back(p, carry):
        at = mult(p * slot, slot)
        d_row = dc_all[pl.ds(base + p, 1), :]
        q_row = qc_all[pl.ds(base + p, 1), :]
        d_heads = jnp.where(head_mask, d_row, 0.0)
        q_heads = jnp.where(head_mask, q_row, 0.0)
        c = chance[p]
        d_chance = nt(d_heads.astype(BF), valb[pl.ds(at, slot), :])
        d_scores = c * (d_chance - jnp.sum(c * d_chance, axis=1, keepdims=True))
        s_low = d_scores.astype(BF)
        mark = jnp.logical_or(row_place == heads, row_place == heads + 1)
        coef_own[pl.ds(mult(p * 16 + 8, 8), 8), :] = jnp.where(mark, first_key, d_scores)
        factor[pl.ds(mult(fkind + p * 8, 8), 8), :] = nn(s_low, tok[pl.ds(at, slot), :])
        spread = nn(s_low, keyb[pl.ds(at, slot), :])
        dq_rows[pl.ds(p, 1), :] = 0.125 * jnp.sum(
            jnp.where(head_mask, spread, 0.0), axis=0, keepdims=True
        )
        rank_f[pl.ds(mult(p * 16, 8), 8), 0:half] = d_heads
        rank_f[pl.ds(mult(p * 16 + 8, 8), 8), 0:half] = q_heads
        return carry

    lax.fori_loop(0, count, attend_back, 0)

    turned = jnp.transpose(factor[...]).astype(BF)
    fac_send[...] = turned
    dq = dq_rows[...]
    for b in range(half // 128):
        pack[b * 8 : b * 8 + 8, 0:128] = dq[:, b * 128 : b * 128 + 128]
    pack[half // 16 : 32, 0:128] = jnp.zeros((32 - half // 16, 128), F32)
    dq_send[...] = pack[:, 0:128].astype(BF)
    share = width // nd
    fac_all[dp] = fac_send[pl.ds(mult(dp * share, 16), share), :]
    dq_all[dp] = dq_send[...]

    def factor_copy(i, mine):
        there = lax.rem(dp + i, nd)
        holder = fac_all.at[dp] if mine else fac_all.at[there]
        rows_out = fac_send.at[pl.ds(mult(there * share, 16), share), :]
        return remote(
            rows_out, holder, f_send.at[i], f_recv.at[dp if mine else there], (there, mp)
        )

    def dq_copy(i, mine):
        there = lax.rem(dp + i, nd)
        holder = dq_all.at[dp] if mine else dq_all.at[there]
        return remote(
            dq_send, holder, q_send.at[i], q_recv.at[dp if mine else there], (there, mp)
        )

    def factor_start(i, carry):
        factor_copy(i, True).start()
        dq_copy(i, True).start()
        return carry

    lax.fori_loop(1, nd, factor_start, 0)

    kept = rank_f[:, 0:half].astype(BF)
    even = lax.rem(lax.div(lax.broadcasted_iota(jnp.int32, (count * 16, 1), 0), 8), 2) == 0
    rank_v = nt(kept, wq[:, 2 * half :])
    rank_k = nt(kept, wq[:, half : 2 * half])
    rank_f[...] = jnp.where(even, rank_v, rank_k)
    back_q = nt(dq.astype(BF), wq[:, 0:half])
    for p in range(count):
        rank_f[p * 16 + heads : p * 16 + heads + 1, :] = back_q[p : p + 1, :]
        rank_f[p * 16 + heads + 1 : p * 16 + 8, :] = jnp.zeros((7 - heads, width), F32)
        rank_f[p * 16 + 8 + heads : p * 16 + 16, :] = jnp.zeros((8 - heads, width), F32)
    rank_send[...] = rank_f[:, pl.ds(f_col, half)].astype(BF)
    coef_low = coef_own[...].astype(BF)
    o_coef[0] = coef_low
    coef_far_copy = remote(o_coef.at[0], coef_far, m_send.at[0], m_recv.at[0], pair)
    coef_far_copy.start()
    rank_copy = remote(rank_send, rank_far, m_send.at[1], m_recv.at[1], pair)
    rank_copy.start()
    d1_rows = d1_all[pl.ds(base, count), pl.ds(m_col, half)]
    d1_high = d1_rows.astype(BF).astype(F32)
    d1_low = d1_rows - d1_high
    for p in range(count):
        rank_f[p * 16 + 8 + heads : p * 16 + 9 + heads, pl.ds(m_col, half)] = d1_high[p : p + 1]
        rank_f[p * 16 + 9 + heads : p * 16 + 10 + heads, pl.ds(m_col, half)] = d1_low[p : p + 1]
    o_rank[0] = rank_f[:, pl.ds(m_col, half)].astype(BF)

    coef_far_copy.wait_recv()
    rank_copy.wait_recv()
    o_coef[1] = coef_far[...]
    o_rank[1] = rank_far[...]

    def factor_wait(i, carry):
        factor_copy(i, False).wait_recv()
        dq_copy(i, False).wait_recv()
        return carry

    lax.fori_loop(1, nd, factor_wait, 0)
    o_factor[...] = fac_all[...]
    o_dquery[...] = dq_all[...]

    def factor_sent(i, carry):
        factor_copy(i, True).wait_send()
        dq_copy(i, True).wait_send()
        return carry

    lax.fori_loop(1, nd, factor_sent, 0)
    coef_far_copy.wait_send()
    rank_copy.wait_send()
    bias_copy.wait_send()
    lax.fori_loop(1, 2 * chips, gather_sent, 0)
    to_sibling.wait_send()
    for k in range(chunks):
        cross(k).wait_send()
        for n in range(8):
            lane(k, n).wait_send()

    def drain(i, carry):
        ctx_copy(i).wait_send()
        out_copy(i, True).wait_send()
        out_copy(i, False).wait_recv()
        out_local(i).wait()
        return carry

    lax.fori_loop(0, own, drain, 0)


def gradients(
    nd,
    act_in,
    coef_in,
    rank_in,
    factor_in,
    dquery_in,
    active_in,
    inner_in,
    context_in,
    qcls_in,
    dctx_in,
    norm_in,
    ffn_in,
    attn_in,
    tok_in,
    sums_in,
    sums_units_in,
    loss_in,
    qgrad_in,
    act_out,
    query_loss,
    input_grad,
    query_grad,
    grad_qkv,
    grad_bias_qv,
    grad_out,
    grad_bias_out,
    grad_gain_one,
    grad_shift_one,
    grad_in,
    grad_bias_in,
    grad_back,
    grad_bias_back,
    grad_gain_two,
    coef,
    rank,
    factor,
    dquery,
    active,
    inner,
    context,
    qcls,
    dctx,
    norm,
    ffn,
    attn,
    tok,
    sums,
    sums_units,
    loss,
    qgrad,
    sems,
    act_sem,
    act_buf,
    in_buf,
    in_sems,
    rhs,
):
    dp = lax.axis_index("dp")
    act_load = pltpu.make_async_copy(act_in, act_buf, act_sem.at[0])
    act_store = pltpu.make_async_copy(act_buf, act_out, act_sem.at[1])
    act_load.start()
    pairs = (
        (coef_in, coef),
        (rank_in, rank),
        (factor_in, factor),
        (dquery_in, dquery),
        (qcls_in, qcls),
        (dctx_in, dctx),
        (active_in, active),
        (inner_in, inner),
        (context_in, context),
        (norm_in, norm),
        (ffn_in, ffn),
        (attn_in, attn),
        (tok_in, tok),
        (sums_in, sums),
        (sums_units_in, sums_units),
        (loss_in, loss),
        (qgrad_in, qgrad),
    )
    loads = [pltpu.make_async_copy(src, dst, sems.at[i]) for i, (src, dst) in enumerate(pairs)]
    for load in loads:
        load.start()
    passages, width = ffn.shape
    half = width // 2
    share = width // nd
    count = passages // nd
    slot = coef.shape[2]
    for load in loads[:2]:
        load.wait()

    def input_copy(p):
        at = pl.ds(mult(p * slot, slot), slot)
        return pltpu.make_async_copy(in_buf.at[at, :], input_grad.at[at, :], in_sems.at[p])

    def input_rows(p, carry):
        rows16 = pl.ds(mult(p * 16, 16), 16)
        both = jnp.concatenate([coef[0, rows16, :], coef[1, rows16, :]], axis=0)
        right = jnp.concatenate([rank[0, rows16, :], rank[1, rows16, :]], axis=0)
        in_buf[pl.ds(mult(p * slot, slot), slot), :] = tn(both, right)
        input_copy(p).start()
        return carry

    lax.fori_loop(0, count, input_rows, 0)
    act_load.wait()
    act_store.start()
    for load in loads[2:]:
        load.wait()

    spread = lax.broadcasted_iota(jnp.int32, (8, half), 0) == lax.div(
        lax.broadcasted_iota(jnp.int32, (8, half), 1), HEAD
    )
    fkind = count * 8

    def build(s, carry):
        d_rows = dctx[pl.ds(mult(s * 2 * count, 16), 2 * count), :].astype(F32)
        q_rows = qcls[pl.ds(mult(s * 2 * count, 16), 2 * count), :].astype(F32) * 0.125
        k_blocks = [jnp.where(spread, q_rows[p : p + 1, :], 0.0) for p in range(2 * count)]
        v_blocks = [jnp.where(spread, d_rows[p : p + 1, :], 0.0) for p in range(2 * count)]
        here = pl.ds(mult(s * 2 * fkind, 16), 2 * fkind)
        rhs[here, 0:half] = jnp.concatenate(k_blocks, 0).astype(BF)
        rhs[here, half:] = jnp.concatenate(v_blocks, 0).astype(BF)
        return carry

    lax.fori_loop(0, nd // 2, build, 0)
    grad_k = jnp.zeros((share, half), F32)
    grad_v = jnp.zeros((share, half), F32)
    for s in range(0, nd, 4):
        left_v = jnp.concatenate([factor[s + t][:, 0:fkind] for t in range(4)], axis=1)
        left_k = jnp.concatenate([factor[s + t][:, fkind:] for t in range(4)], axis=1)
        grad_k = grad_k + nn(left_k, rhs[s * fkind : (s + 4) * fkind, 0:half])
        grad_v = grad_v + nn(left_v, rhs[s * fkind : (s + 4) * fkind, half:])
    grad_qkv[1] = grad_k
    grad_qkv[2] = grad_v

    pick = one_hot((width, share), dp * share)
    pick_low = pick.astype(BF)
    row = lax.broadcasted_iota(jnp.int32, (share, width), 0)
    column = lax.broadcasted_iota(jnp.int32, (share, width), 1)
    pick_t = (column == row + dp * share).astype(BF)
    ffn_own = nt(pick_t, ffn[...]).astype(BF)
    attn_own = nt(pick_t, attn[...]).astype(BF)
    norm_own = nt(pick_t, norm[...]).astype(BF)
    tok_own = nt(pick_t, tok[...]).astype(BF)
    grad_out[...] = nn(attn_own, context[...])
    unit = active.shape[2]
    blocks = active.shape[0]
    for u in range(blocks):
        cols = slice(u * unit, (u + 1) * unit)
        grad_back[:, cols] = nn(ffn_own, active[u])
        grad_in[:, cols] = nn(norm_own, inner[u])
    dq_sum = []
    for b in range(half // 128):
        cols = dquery[...].astype(F32)[:, b * 8 : b * 8 + 8, :].reshape(passages, 128)
        dq_sum.append(jnp.sum(cols, axis=0, keepdims=True))
        grad_qkv[0, :, b * 128 : b * 128 + 128] = nn(tok_own, cols.astype(BF))

    mine = exact(sums[...], pick)
    grad_gain_two[...] = mine[0:1, :].reshape(share)
    grad_bias_back[...] = mine[1:2, :].reshape(share)
    grad_gain_one[...] = mine[2:3, :].reshape(share)
    grad_shift_one[...] = mine[3:4, :].reshape(share)
    grad_bias_out[...] = mine[4:5, :].reshape(share)
    part = half // nd
    both = jnp.concatenate([jnp.concatenate(dq_sum, axis=1), sums[5:6, 0:half]], axis=0)
    wide = jnp.concatenate([both, jnp.zeros((6, half), F32)], axis=0)
    grad_bias_qv[...] = exact(wide, one_hot((half, part), dp * part))[0:2, :]
    in_share = grad_bias_in.shape[0]
    total = jnp.zeros((8, in_share), F32)
    for u in range(blocks):
        total = total + exact(
            jnp.broadcast_to(sums_units[u : u + 1, :], (8, unit)),
            one_hot((unit, in_share), dp * in_share - u * unit),
        )
    grad_bias_in[...] = total[0:1, :].reshape(in_share)
    q_rows = query_loss.shape[0]
    query_loss[...] = exact(loss[...], one_hot((loss.shape[1], q_rows), dp * 16))[0:1, :].reshape(q_rows)
    query_grad[...] = qgrad[0:q_rows, :]

    def input_wait(p, carry):
        input_copy(p).wait()
        return carry

    lax.fori_loop(0, count, input_wait, 0)
    act_store.wait()


def per_device(nd, *arrays):
    (
        tokens,
        lengths,
        queries,
        positives,
        w_qkv,
        b_qv,
        w_out,
        b_out,
        gain_one,
        shift_one,
        w_in,
        b_in,
        w_back,
        b_back,
        gain_two,
    ) = arrays
    rows, width = tokens.shape
    count = lengths.shape[0]
    slot = rows // count
    half = w_qkv.shape[2]
    units = w_in.shape[1]
    unit = 512
    blocks = units // unit
    chunks = 1 + 2 * blocks
    own_rows = rows // 2
    passages = nd * count
    chips = nd // 2
    q_rows = queries.shape[0]
    q_pad = nd * 16
    share = width // nd
    vmem = pl.BlockSpec(memory_space=pltpu.VMEM)
    hbm = pl.BlockSpec(memory_space=pl.ANY)
    smem = pl.BlockSpec(memory_space=pltpu.SMEM)
    in_specs = [smem, hbm, vmem, vmem, hbm, vmem, hbm, vmem, vmem, vmem, hbm, vmem, hbm, vmem, vmem]
    shape = jax.ShapeDtypeStruct
    outs = [
        (shape((rows, half), BF), hbm),
        (shape((2, count * 16, slot), BF), vmem),
        (shape((2, count * 16, half), BF), vmem),
        (shape((nd, share, 128), BF), vmem),
        (shape((nd, 32, 128), BF), vmem),
        (shape((blocks, passages, unit), BF), vmem),
        (shape((blocks, passages, unit), BF), vmem),
        (shape((passages, half), BF), vmem),
        (shape((passages, half), BF), vmem),
        (shape((passages, half), BF), vmem),
        (shape((passages, width), BF), vmem),
        (shape((passages, width), BF), vmem),
        (shape((passages, width), BF), vmem),
        (shape((passages, width), BF), vmem),
        (shape((8, width), F32), vmem),
        (shape((8, unit), F32), vmem),
        (shape((8, q_pad), F32), vmem),
        (shape((16, width), F32), vmem),
    ]
    dma = pltpu.SemaphoreType.DMA
    scratch = [
        pltpu.VMEM((rows, width), BF),
        pltpu.VMEM((width, 3 * half), BF),
        pltpu.VMEM((width, width), BF),
        pltpu.VMEM((2, blocks, width, unit), BF),
        pltpu.VMEM((2, blocks, unit, width), BF),
        pltpu.VMEM((rows, half), BF),
        pltpu.VMEM((rows, half), BF),
        pltpu.VMEM((own_rows, width), BF),
        pltpu.VMEM((own_rows, half), BF),
        pltpu.VMEM((own_rows, width), BF),
        pltpu.VMEM((own_rows, width), F32),
        pltpu.VMEM((blocks, own_rows, unit), BF),
        pltpu.VMEM((2, own_rows, half), BF),
        pltpu.VMEM((count, 8, slot), F32),
        pltpu.VMEM((2 * count * 8, width), F32),
        pltpu.VMEM((8, half), F32),
        pltpu.VMEM((8, width), F32),
        pltpu.VMEM((32, half), F32),
        pltpu.VMEM((chips, 2, 2, 32, half), BF),
        pltpu.VMEM((passages, width), BF),
        pltpu.VMEM((passages, width), BF),
        pltpu.VMEM((q_pad, width), BF),
        pltpu.VMEM((passages, width), F32),
        pltpu.VMEM((passages, width), BF),
        pltpu.VMEM((2, blocks, passages, unit), F32),
        pltpu.VMEM((2, blocks, passages, unit), BF),
        pltpu.VMEM((2, blocks, passages, unit), BF),
        pltpu.VMEM((passages, half), F32),
        pltpu.VMEM((passages, half), F32),
        pltpu.VMEM((passages, width), F32),
        pltpu.VMEM((8, half), F32),
        pltpu.VMEM((count * 16, width), F32),
        pltpu.VMEM((count * 16, slot), F32),
        pltpu.VMEM((count * 16, slot), BF),
        pltpu.VMEM((count * 16, half), BF),
        pltpu.VMEM((count * 16, half), BF),
        pltpu.VMEM((count * 16, half), BF),
        pltpu.VMEM((width, 128), BF),
        pltpu.VMEM((nd, share, 128), BF),
        pltpu.VMEM((32, 128), BF),
        pltpu.VMEM((nd, 32, 128), BF),
        dma((5 + 2 * blocks,)),
        dma((chunks,)),
        dma((chunks,)),
        dma((chunks, 8)),
        dma((chunks, 8)),
        dma((count // 2,)),
        dma((count // 2,)),
        dma((count // 2,)),
        dma((count // 2,)),
        dma((count // 2,)),
        dma((2 * chips,)),
        dma((2 * chips,)),
        dma,
        dma,
        dma((nd,)),
        dma((nd,)),
        dma((nd,)),
        dma((nd,)),
        dma((2,)),
        dma((2,)),
        dma,
        dma,
        pltpu.VMEM((8, unit), F32),
        pltpu.VMEM((8, unit), F32),
    ]
    made = pl.pallas_call(
        functools.partial(tower, nd, nd * q_rows),
        out_shape=[o[0] for o in outs],
        in_specs=in_specs,
        out_specs=[o[1] for o in outs],
        scratch_shapes=scratch,
        compiler_params=pltpu.CompilerParams(
            collective_id=0, has_side_effects=True, vmem_limit_bytes=60 * MIB
        ),
        name="tower",
    )(
        lengths,
        tokens,
        queries,
        positives,
        w_qkv,
        b_qv,
        w_out,
        b_out,
        gain_one,
        shift_one,
        w_in,
        b_in,
        w_back,
        b_back,
        gain_two,
    )
    g_outs = [
        (shape((rows, half), BF), hbm),
        (shape((q_rows,), F32), vmem),
        (shape((rows, half), F32), hbm),
        (shape((q_rows, width), F32), vmem),
        (shape((3, share, half), F32), vmem),
        (shape((2, half // nd), F32), vmem),
        (shape((share, half), F32), vmem),
        (shape((share,), F32), vmem),
        (shape((share,), F32), vmem),
        (shape((share,), F32), vmem),
        (shape((share, units), F32), vmem),
        (shape((units // nd,), F32), vmem),
        (shape((share, units), F32), vmem),
        (shape((share,), F32), vmem),
        (shape((share,), F32), vmem),
    ]
    grads = pl.pallas_call(
        functools.partial(gradients, nd),
        out_shape=[o[0] for o in g_outs],
        in_specs=[hbm] * len(outs),
        out_specs=[o[1] for o in g_outs],
        scratch_shapes=[pltpu.VMEM(o[0].shape, o[0].dtype) for o in outs[1:]]
        + [
            dma((len(outs) - 1,)),
            dma((2,)),
            pltpu.VMEM((rows, half), BF),
            pltpu.VMEM((rows, half), F32),
            dma((count,)),
            pltpu.VMEM((nd * count * 8, width), BF),
        ],
        compiler_params=pltpu.CompilerParams(vmem_limit_bytes=62 * MIB),
        name="gradients",
    )(*made)
    grads = list(grads)
    grads[6] = grads[6].T
    grads[12] = grads[12].T
    return tuple(grads)


def layer_norm(rows, gain, shift):
    center = jnp.mean(rows, axis=-1, keepdims=True)
    spread = rows - center
    second = jnp.mean(spread * spread, axis=-1, keepdims=True)
    return spread * lax.rsqrt(second + EPS) * gain + shift


def scaled_norm(rows, gain):
    center = jnp.mean(rows, axis=-1, keepdims=True)
    spread = rows - center
    second = jnp.mean(spread * spread, axis=-1, keepdims=True)
    return spread * lax.rsqrt(second + EPS) * gain


def gelu_exact(values):
    return jax.nn.gelu(values, approximate=False)


def first_rows(values, count):
    return values.reshape((count, values.shape[0] // count) + values.shape[1:])[:, 0]


def by_collectives(
    tokens,
    lengths,
    queries,
    positives,
    w_qkv,
    b_qv,
    w_out,
    b_out,
    gain_one,
    shift_one,
    w_in,
    b_in,
    w_back,
    b_back,
    gain_two,
):
    rows, width = tokens.shape
    count = lengths.shape[0]
    slot = rows // count
    local = w_qkv.shape[2]
    heads_here = local // HEAD
    scale = 1.0 / math.sqrt(HEAD)
    projected = jnp.einsum("rd,jdc->jrc", tokens, w_qkv, preferred_element_type=F32)
    bias_qv = b_qv.astype(F32)
    query = (projected[0] + bias_qv[0]).astype(BF)
    keyed = projected[1].astype(BF)
    value = (projected[2] + bias_qv[1]).astype(BF)
    block = min(count, max(1, 512 // slot))
    blocks = count // block
    valid = lax.broadcasted_iota(jnp.int32, (count, slot), 1) < lengths[:, None]
    split_shape = (blocks, block, slot, heads_here, HEAD)

    def attend(inputs):
        query_part, keyed_part, value_part, valid_part = inputs
        scores = (
            jnp.einsum(
                "pqhd,pkhd->phqk", query_part, keyed_part, preferred_element_type=F32
            )
            * scale
        )
        scores = jnp.where(valid_part[:, None, None, :], scores, MASKED)
        top = jnp.max(scores, axis=-1, keepdims=True)
        raised = jnp.exp(scores - top)
        total = jnp.sum(raised, axis=-1, keepdims=True)
        chance_low = (raised / total).astype(BF)
        mixed = jnp.einsum(
            "phqk,pkhd->pqhd", chance_low, value_part, preferred_element_type=F32
        )
        return (mixed.astype(BF), (top + jnp.log(total))[:, :, 0, 0])

    context, log_total = lax.map(
        attend,
        (
            query.reshape(split_shape),
            keyed.reshape(split_shape),
            value.reshape(split_shape),
            valid.reshape(blocks, block, slot),
        ),
    )
    context = context.reshape(rows, local)
    log_total = log_total.reshape(count, heads_here)
    partial_attn = jnp.dot(context, w_out, preferred_element_type=F32).astype(BF)
    attended = lax.psum(partial_attn, "mp").astype(F32) + b_out.astype(F32)
    resid_one = tokens.astype(F32) + attended
    gain_one_w = gain_one.astype(F32)
    shift_one_w = shift_one.astype(F32)
    gain_two_w = gain_two.astype(F32)
    norm_one = layer_norm(resid_one, gain_one_w, shift_one_w)
    norm_low = norm_one.astype(BF)
    inner = jnp.dot(norm_low, w_in, preferred_element_type=F32) + b_in.astype(F32)
    active = gelu_exact(inner).astype(BF)
    partial_ffn = jnp.dot(active, w_back, preferred_element_type=F32).astype(BF)
    resid_two = (
        norm_one + lax.psum(partial_ffn, "mp").astype(F32) + b_back.astype(F32)
    )
    output = scaled_norm(resid_two, gain_two_w)
    column = lax.axis_index("mp") * local
    activations = lax.dynamic_slice_in_dim(output, column, local, 1).astype(BF)
    cls_low = first_rows(output, count).astype(BF)
    query_rows = queries.shape[0]
    members = lax.axis_size("dp")
    query_total = query_rows * members
    own_query = lax.axis_index("dp") * query_rows
    gathered = lax.all_gather(cls_low, "dp", axis=0, tiled=True)
    similar = jnp.einsum("qd,pd->qp", queries, gathered, preferred_element_type=F32)
    mine = lax.dynamic_slice_in_dim(positives, own_query, query_rows)
    target = lax.broadcasted_iota(jnp.int32, similar.shape, 1) == mine[:, None]
    top = jnp.max(similar, axis=1, keepdims=True)
    log_sum = top[:, 0] + jnp.log(jnp.sum(jnp.exp(similar - top), axis=1))
    picked = jnp.sum(jnp.where(target, similar, 0.0), axis=1)
    query_loss = log_sum - picked
    slopes = (jnp.exp(similar - log_sum[:, None]) - target.astype(F32)) / query_total
    query_grad = jnp.dot(slopes, gathered.astype(F32), precision=lax.Precision.HIGHEST)
    queries_wide = queries.astype(F32)
    cls_grad = lax.psum_scatter(
        jnp.einsum("qp,qd->pd", slopes, queries_wide, precision=lax.Precision.HIGHEST),
        "dp",
        scatter_dimension=0,
        tiled=True,
    )
    _, norm_two_pull = jax.vjp(scaled_norm, first_rows(resid_two, count), gain_two_w)
    d_resid_two, grad_gain_two = norm_two_pull(cls_grad)
    grad_bias_back = jnp.sum(d_resid_two, axis=0)
    ffn_low = d_resid_two.astype(BF)
    grad_back = jnp.einsum(
        "pf,pd->fd", first_rows(active, count), ffn_low, preferred_element_type=F32
    )
    d_active = jnp.einsum("pd,fd->pf", ffn_low, w_back, preferred_element_type=F32)
    _, gelu_pull = jax.vjp(gelu_exact, first_rows(inner, count))
    d_inner = gelu_pull(d_active)[0]
    grad_bias_in = jnp.sum(d_inner, axis=0)
    inner_low = d_inner.astype(BF)
    grad_in = jnp.einsum(
        "pd,pf->df", first_rows(norm_low, count), inner_low, preferred_element_type=F32
    )
    back_norm = jnp.einsum("pf,df->pd", inner_low, w_in, preferred_element_type=F32)
    d_norm_one = d_resid_two + lax.psum(back_norm, "mp")
    _, norm_one_pull = jax.vjp(layer_norm, first_rows(resid_one, count), gain_one_w, shift_one_w)
    d_resid_one, grad_gain_one, grad_shift_one = norm_one_pull(d_norm_one)
    grad_bias_out = jnp.sum(d_resid_one, axis=0)
    attn_low = d_resid_one.astype(BF)
    grad_out = jnp.einsum(
        "pc,pd->cd", first_rows(context, count), attn_low, preferred_element_type=F32
    )
    d_context = jnp.einsum("pd,cd->pc", attn_low, w_out, preferred_element_type=F32).astype(
        BF
    )
    d_context = d_context.reshape(count, heads_here, HEAD)
    query_cls = first_rows(query, count).reshape(count, heads_here, HEAD)
    keyed_heads = keyed.reshape(count, slot, heads_here, HEAD)
    value_heads = value.reshape(count, slot, heads_here, HEAD)
    scores_cls = (
        jnp.einsum("phd,pkhd->phk", query_cls, keyed_heads, preferred_element_type=F32)
        * scale
    )
    scores_cls = jnp.where(valid[:, None, :], scores_cls, MASKED)
    chance = jnp.exp(scores_cls - log_total[:, :, None])
    d_chance = jnp.einsum(
        "phd,pkhd->phk", d_context, value_heads, preferred_element_type=F32
    )
    d_value = jnp.einsum(
        "phk,phd->pkhd", chance.astype(BF), d_context, preferred_element_type=F32
    )
    d_scores = chance * (d_chance - jnp.sum(chance * d_chance, axis=-1, keepdims=True))
    scores_low = d_scores.astype(BF)
    d_query = (
        jnp.einsum("phk,pkhd->phd", scores_low, keyed_heads, preferred_element_type=F32)
        * scale
    )
    d_keyed = (
        jnp.einsum("phk,phd->pkhd", scores_low, query_cls, preferred_element_type=F32)
        * scale
    )
    d_query = d_query.reshape(count, local)
    d_value = d_value.reshape(rows, local)
    query_low = d_query.astype(BF)
    keyed_value_low = jnp.stack(
        [d_keyed.reshape(rows, local).astype(BF), d_value.astype(BF)]
    )
    grad_bias_qv = jnp.stack([jnp.sum(d_query, axis=0), jnp.sum(d_value, axis=0)])
    grad_query_w = jnp.einsum(
        "pd,pc->dc", first_rows(tokens, count), query_low, preferred_element_type=F32
    )
    grad_kv = jnp.einsum("rd,jrc->jdc", tokens, keyed_value_low, preferred_element_type=F32)
    grad_qkv = jnp.concatenate([grad_query_w[None], grad_kv], axis=0)
    own_half = lax.dynamic_slice_in_dim(d_resid_one, column, local, 1)
    back_kv = jnp.einsum(
        "jrc,jdc->rd", keyed_value_low, w_qkv[1:], preferred_element_type=F32
    )
    back_query = jnp.einsum("pc,dc->pd", query_low, w_qkv[0], preferred_element_type=F32)
    back_all = back_kv.reshape(count, slot, width).at[:, 0].add(back_query).reshape(rows, width)
    input_grad = lax.psum_scatter(
        back_all.astype(BF), "mp", scatter_dimension=1, tiled=True
    ).astype(F32)
    input_grad = input_grad.reshape(count, slot, local).at[:, 0].add(own_half).reshape(rows, local)
    summed = (
        lax.psum_scatter(grad_qkv, "dp", scatter_dimension=1, tiled=True),
        lax.psum_scatter(grad_bias_qv, "dp", scatter_dimension=1, tiled=True),
        lax.psum_scatter(grad_out, "dp", scatter_dimension=1, tiled=True),
        lax.psum_scatter(grad_bias_out, "dp", scatter_dimension=0, tiled=True),
        lax.psum_scatter(grad_gain_one, "dp", scatter_dimension=0, tiled=True),
        lax.psum_scatter(grad_shift_one, "dp", scatter_dimension=0, tiled=True),
        lax.psum_scatter(grad_in, "dp", scatter_dimension=0, tiled=True),
        lax.psum_scatter(grad_bias_in, "dp", scatter_dimension=0, tiled=True),
        lax.psum_scatter(grad_back, "dp", scatter_dimension=1, tiled=True),
        lax.psum_scatter(grad_bias_back, "dp", scatter_dimension=0, tiled=True),
        lax.psum_scatter(grad_gain_two, "dp", scatter_dimension=0, tiled=True),
    )
    return (
        activations,
        query_loss,
        input_grad,
        query_grad,
        summed[0],
        summed[1],
        summed[2],
        summed[3],
        summed[4],
        summed[5],
        summed[6],
        summed[7],
        summed[8],
        summed[9],
        summed[10],
    )


def solution(mesh):
    in_specs = (
        P("dp", None),
        P("dp"),
        P("dp", None),
        P(),
        P(None, None, "mp"),
        P(None, "mp"),
        P("mp", None),
        P(),
        P(),
        P(),
        P(None, "mp"),
        P("mp"),
        P("mp", None),
        P(),
        P(),
    )
    out_specs = (
        P("dp", "mp"),
        P("dp"),
        P("dp", "mp"),
        P("dp", None),
        P(None, "dp", "mp"),
        P(None, ("mp", "dp")),
        P("mp", "dp"),
        P("dp"),
        P("dp"),
        P("dp"),
        P("dp", "mp"),
        P(("mp", "dp")),
        P("mp", "dp"),
        P("dp"),
        P("dp"),
    )
    groups = mesh.shape["dp"]
    fits = groups <= 16 and mesh.shape["mp"] == 2
    return jax.shard_map(
        functools.partial(per_device, groups) if fits else by_collectives,
        mesh=mesh,
        in_specs=in_specs,
        out_specs=out_specs,
        check_vma=False,
    )
```

```python
import functools
import math

import jax
import jax.numpy as jnp
from jax import lax
from jax.experimental import pallas as pl
from jax.experimental.pallas import tpu as pltpu
from jax.sharding import PartitionSpec as P

HEAD = 64
EPS = 1e-05
MASKED = -1e30
MESH = pl.DeviceIdType.MESH
BF = jnp.bfloat16
F32 = jnp.float32
MIB = 2**20


def nn(a, b):
    return jnp.dot(a, b, preferred_element_type=F32)


def nt(a, b):
    return lax.dot_general(a, b, (((1,), (1,)), ((), ())), preferred_element_type=F32)


def tn(a, b):
    return lax.dot_general(a, b, (((0,), (0,)), ((), ())), preferred_element_type=F32)


def gelu(h):
    return 0.5 * h * (1.0 + lax.erf(h * math.sqrt(0.5)))


def gelu_slope(h):
    bell = jnp.exp(-0.5 * h * h) * (1.0 / math.sqrt(2.0 * math.pi))
    return 0.5 * (1.0 + lax.erf(h * math.sqrt(0.5))) + h * bell


def row_of(vector):
    return vector[None, :].astype(F32)


def exact(a, b):
    return jnp.dot(a, b, preferred_element_type=F32, precision=lax.Precision.HIGHEST)


def one_hot(shape, shift, dtype=F32):
    row = lax.broadcasted_iota(jnp.int32, shape, 0)
    column = lax.broadcasted_iota(jnp.int32, shape, 1)
    return (row == column + shift).astype(dtype)


def standard(rows):
    center = jnp.mean(rows, axis=-1, keepdims=True)
    spread = rows - center
    second = jnp.mean(spread * spread, axis=-1, keepdims=True)
    inverse = lax.rsqrt(second + EPS)
    return spread * inverse, inverse


def norm_back(grad, scaled, inverse):
    first = jnp.mean(grad, axis=-1, keepdims=True)
    second = jnp.mean(grad * scaled, axis=-1, keepdims=True)
    return inverse * (grad - first - scaled * second)


def flip(index, bit):
    return index + bit * (1 - 2 * lax.rem(lax.div(index, bit), 2))


def mult(value, step):
    return pl.multiple_of(value, step)


def tower(
    nd,
    query_total,
    lengths,
    tokens,
    queries,
    positives,
    w_qkv,
    b_qv,
    w_out,
    b_out,
    gain_one,
    shift_one,
    w_in,
    b_in,
    w_back,
    b_back,
    gain_two,
    out_act,
    h_coef,
    h_rank,
    h_factor,
    h_active,
    h_inner,
    h_context,
    h_qcls,
    h_dctx,
    h_norm,
    h_ffn,
    h_attn,
    h_tok,
    h_sums,
    h_sums_in,
    h_loss,
    h_qgrad,
    tok,
    wq,
    wq_far,
    wo,
    wi,
    wb,
    keyb,
    valb,
    ctx,
    norm_low,
    acc,
    act_far,
    obuf,
    chance,
    factor,
    stage,
    tcls,
    pack,
    gath,
    ctx_all,
    tok_all,
    q_all,
    xh1_all,
    norm_all,
    inner_all,
    act_all,
    low_all,
    dc_all,
    qc_all,
    d1_all,
    dq_rows,
    rank_f,
    coef_own,
    coef_far,
    rank_own,
    rank_send,
    rank_far,
    fac_send,
    loc_sem,
    ysend,
    yrecv,
    w_send,
    w_recv,
    o_send,
    o_recv,
    o_loc,
    g_send,
    g_recv,
    gs_send,
    gs_recv,
    f_send,
    f_recv,
    m_send,
    m_recv,
    b_send,
    b_recv,
    bin_own,
    bin_far,
    out_sem,
    o_coef,
    o_rank,
    o_factor,
    o_active,
    o_inner,
    o_context,
    o_qcls,
    o_dctx,
    o_norm,
    o_ffn,
    o_attn,
    o_tok,
    o_sums,
    o_sums_in,
    o_loss,
    o_qgrad,
):
    dp = lax.axis_index("dp")
    mp = lax.axis_index("mp")
    far = 1 - mp
    chips = nd // 2
    core = lax.rem(dp, 2)
    chip = lax.div(dp, 2)
    bit_a = lax.rem(lax.div(dp, 2), 2)
    bit_b = lax.rem(lax.div(dp, 4), 2)
    quarter = bit_a + 2 * bit_b
    quarter_x = flip(quarter, 1)
    quarter_z = flip(quarter, 2)
    quarter_d = 3 - quarter
    pair = (dp, far)
    sibling = (flip(dp, 1), mp)
    near_x = (flip(dp, 2), mp)
    near_z = (flip(dp, 4), mp)

    rows, width = tok.shape
    count = lengths.shape[0]
    slot = rows // count
    own = count // 2
    half = width // 2
    own_rows = own * slot
    passages = nd * count
    blocks, unit = wi.shape[1], wi.shape[3]
    m_col = mult(mp * half, 128)
    f_col = mult(far * half, 128)

    barrier = pltpu.get_barrier_semaphore()

    def greet(i, carry):
        other = lax.rem(dp * 2 + mp + i, 2 * nd)
        pl.semaphore_signal(
            barrier,
            inc=1,
            device_id=(lax.div(other, 2), lax.rem(other, 2)),
            device_id_type=MESH,
        )
        return carry

    lax.fori_loop(1, 2 * nd, greet, 0)

    def local(src, dst, k):
        return pltpu.make_async_copy(src, dst, loc_sem.at[k])

    loads = [local(tokens, tok, 0)]
    loads += [local(w_qkv.at[j], wq.at[:, pl.ds(j * half, half)], 1 + j) for j in range(3)]
    loads.append(local(w_out, wo.at[pl.ds(mult(mp * half, 128), half), :], 4))
    loads += [
        local(w_in.at[:, pl.ds(u * unit, unit)], wi.at[mp, u], 5 + u) for u in range(blocks)
    ]
    loads += [
        local(w_back.at[pl.ds(u * unit, unit), :], wb.at[mp, u], 5 + blocks + u)
        for u in range(blocks)
    ]
    for copy in loads:
        copy.start()

    first_in = 4
    first_back = 4 + blocks
    chunks = 4 + 2 * blocks
    direct = (3, chunks - 1)

    def piece(k, q, c, which, side=None):
        if k < 3 or first_in <= k < first_back:
            size = width // 8
            at = (c * 4 if q is None else c * 4 + q) * size
            size = 4 * size if q is None else size
            if side is not None:
                size = size // 2
                at = at + side * size
            here = pl.ds(mult(at, 16), size)
            return wq_far.at[here, pl.ds(k * half, half)] if k < 3 else wi.at[which, k - 4, here, :]
        cols = pl.ds(0, width) if side is None else pl.ds(side * half, half)
        if k == 3:
            size = half // 2
            return wo.at[pl.ds(mult(which * half + c * size, 16), size), cols]
        whole = k in direct or q is None
        size = unit // 2 if whole else unit // 8
        at = c * size if whole else (c * 4 + q) * size
        return wb.at[which, k - first_back, pl.ds(mult(at, 16), size), cols]

    def sent_bytes(k):
        if k < 3:
            return wq_far.at[pl.ds(0, 7 * width // 8), pl.ds(k * half, half)]
        if k == 3:
            return piece(k, None, core, far)
        if k < first_back:
            return wi.at[far, k - 4, pl.ds(0, 7 * width // 8), :]
        return wb.at[far, k - first_back, pl.ds(0, unit // 2 if k in direct else 7 * unit // 8), :]

    def source(k):
        if k < 3 or first_in <= k < first_back:
            size = width // 8
            here = pl.ds(mult((core * 4 + quarter) * size, 16), size)
            return w_qkv.at[k, here, :] if k < 3 else w_in.at[here, pl.ds((k - 4) * unit, unit)]
        if k == 3:
            return w_out.at[pl.ds(mult(core * (half // 2), 16), half // 2), :]
        size = unit // 2 if k in direct else unit // 8
        at = core * size if k in direct else (core * 4 + quarter) * size
        return w_back.at[pl.ds(mult((k - first_back) * unit + at, 16), size), :]

    def remote(src, dst, ss, rs, device):
        return pltpu.make_async_remote_copy(
            src_ref=src,
            dst_ref=dst,
            send_sem=ss,
            recv_sem=rs,
            device_id=device,
            device_id_type=MESH,
        )

    def cross(k):
        return remote(
            source(k), piece(k, quarter, core, mp), ysend.at[k], yrecv.at[k], pair
        )

    def send(k, lane, q, c, side, device):
        ref = piece(k, q, c, far, side)
        return remote(ref, ref, w_send.at[k], w_recv.at[k, lane], device)

    def lane(k, n):
        q = (quarter, quarter, quarter_z, quarter_x, None)[n]
        side = (None, None, 0, 1, None)[n]
        return send(k, n, q, core, side, (near_x, near_z, near_x, near_z, sibling)[n])

    def arrival(k, n):
        q = (quarter_x, quarter_z, quarter_d, quarter_d, None)[n]
        side = (None, None, 0, 1, None)[n]
        c = core if n < 4 else 1 - core
        return send(k, n, q, c, side, (near_x, near_z, near_x, near_z, sibling)[n])

    def step_one(k):
        remote(
            source(k), piece(k, quarter, core, far), ysend.at[k], yrecv.at[k], pair
        ).wait_recv()
        for n in (4,) if k in direct else (0, 1):
            lane(k, n).start()

    def step_two(k):
        arrival(k, 1).wait_recv()
        lane(k, 2).start()
        arrival(k, 0).wait_recv()
        lane(k, 3).start()

    def step_three(k):
        arrival(k, 2).wait_recv()
        arrival(k, 3).wait_recv()
        lane(k, 4).start()

    def complete(k):
        arrival(k, 4).wait_recv()

    def spent(window, sem):
        pltpu.make_async_copy(window, window, sem).wait()

    def advance(*steps):
        for stage_of, k in steps:
            (step_one, step_two, step_three)[stage_of - 1](k)

    for copy in loads[:4]:
        copy.wait()
    bin_own[...] = jnp.zeros_like(bin_own)
    for u in range(blocks):
        bin_own[u : u + 1, :] = row_of(b_in[pl.ds(u * unit, unit)])
    bin_own[6:8, 0:half] = b_qv[...].astype(F32)
    bias_copy = remote(bin_own, bin_far, b_send, b_recv, pair)

    lane_pair = lax.broadcasted_iota(jnp.int32, (slot, 128), 1)
    key_place = lax.broadcasted_iota(jnp.int32, (1, slot), 1)
    head_rows = lax.broadcasted_iota(jnp.int32, (8, half), 0)
    head_mask = head_rows == lax.div(lax.broadcasted_iota(jnp.int32, (8, half), 1), HEAD)
    heads = half // HEAD
    live = lax.broadcasted_iota(jnp.int32, (8, 1), 0) < heads
    bias_q = b_qv[0:1, :].astype(F32)
    bias_v = b_qv[1:2, :].astype(F32)
    ones = jnp.ones((slot, 128), BF)
    row_place = lax.broadcasted_iota(jnp.int32, (8, slot), 0)
    first_key = (lax.broadcasted_iota(jnp.int32, (8, slot), 1) == 0).astype(F32)

    def mix(query, keyed, value, bias):
        done = []
        for t in range(half // 128):
            q2 = query[:, 128 * t : 128 * t + 128]
            k2 = keyed[:, 128 * t : 128 * t + 128]
            v2 = jnp.concatenate([value[:, 128 * t : 128 * t + 128], ones], axis=1)
            parts = []
            for hx in range(2):
                mask = (lane_pair < HEAD) if hx == 0 else (lane_pair >= HEAD)
                s = nt(jnp.where(mask, q2, jnp.zeros_like(q2)), k2) + bias
                e = jnp.exp(s - jnp.max(s, axis=1, keepdims=True)).astype(BF)
                o = nn(e, v2)
                parts.append(o[:, :128] / o[:, 128:])
            done.append(jnp.where(lane_pair < HEAD, parts[0], parts[1]))
        return jnp.concatenate(done, axis=1).astype(BF)

    def first_row(p, x, query, keyed, value, bias):
        tcls[pl.ds(p, 1), :] = x[0:16, :].astype(F32)[0:1, :]
        q_heads = jnp.where(head_mask, query.astype(F32)[0:1, :], 0.0).astype(BF)
        s = nt(q_heads, keyed) + bias
        e = jnp.exp(s - jnp.max(s, axis=1, keepdims=True))
        c = jnp.where(live, e / jnp.sum(e, axis=1, keepdims=True), 0.0)
        chance[p] = c
        c_low = c.astype(BF)
        mixed = jnp.where(head_mask, nn(c_low, value), 0.0)
        stage[pl.ds(p, 1), :] = jnp.sum(mixed, axis=0, keepdims=True)
        coef_own[pl.ds(mult(p * 16, 16), 8), :] = jnp.where(row_place == heads, first_key, c)
        factor[pl.ds(mult(p * 8, 8), 8), :] = nn(c_low, x)

    theirs_plan = (((1, 0),), (), ((1, 1),), ())
    gap_plan = ((1, 2), (2, 0), (2, 1), (2, 2), (3, 0), (3, 1), (1, 3), (3, 2))
    far_plan = ((), ((1, 4),), (), ((1, 5),))
    feed_plan = ((), ((2, 4), (1, 7)), ((2, 5), (1, 8)), ((3, 4),))
    feed_mid_plan = (((1, 6),), (), ((2, 6),), ((2, 7),))
    in_plan = (
        (((3, 5),), ()),
        (((2, 8), (1, 9)), ((3, 6),)),
        (((3, 7),), ((3, 8),)),
    )

    def move_on(i, plan):
        for j, steps in enumerate(plan):
            if steps:

                @pl.when(i == j)
                def _():
                    advance(*steps)

    def key_bias(p):
        return jnp.where(key_place < lengths[p], 0.0, MASKED)

    def attend_theirs(i, carry):
        move_on(i, theirs_plan)
        p = far * own + i
        at = mult(p * slot, slot)
        x = tok[pl.ds(at, slot), :]
        made = nn(x, wq[:, half:])
        keyed = made[:, :half].astype(BF)
        value = (made[:, half:] + bias_v).astype(BF)
        keyb[pl.ds(at, slot), :] = keyed
        valb[pl.ds(at, slot), :] = value
        query = ((nn(x[0:16, :], wq[:, :half]) + bias_q).astype(BF).astype(F32) * 0.125).astype(BF)
        first_row(p, x, query, keyed, value, key_bias(p))
        return carry

    def attend_own(i, carry):
        @pl.when(i == 1)
        def _():
            pl.semaphore_wait(barrier, 2 * nd - 1)
            for k in (0, 1, 2, 3, 4):
                cross(k).start()
            bias_copy.start()

        p = mp * own + i
        at = mult(p * slot, slot)
        x = tok[pl.ds(at, slot), :]
        made = nn(x, wq[...])
        query = ((made[:, :half] + bias_q).astype(BF).astype(F32) * 0.125).astype(BF)
        keyed = made[:, half : 2 * half].astype(BF)
        value = (made[:, 2 * half :] + bias_v).astype(BF)
        keyb[pl.ds(at, slot), :] = keyed
        valb[pl.ds(at, slot), :] = value
        bias = key_bias(p)
        ctx[pl.ds(mult(i * slot, slot), slot), pl.ds(m_col, half)] = mix(query, keyed, value, bias)
        first_row(p, x, query[0:16, :], keyed, value, bias)
        return carry

    def attend_far(i, carry):
        move_on(i, far_plan)
        p = mp * own + i
        x = tok[pl.ds(mult(p * slot, slot), slot), :]
        made = nn(x, wq_far[...])
        bias_far = bin_far[6:8, 0:half]
        query = ((made[:, :half] + bias_far[0:1, :]).astype(BF).astype(F32) * 0.125).astype(BF)
        keyed = made[:, half : 2 * half].astype(BF)
        value = (made[:, 2 * half :] + bias_far[1:2, :]).astype(BF)
        ctx[pl.ds(mult(i * slot, slot), slot), pl.ds(f_col, half)] = mix(
            query, keyed, value, key_bias(p)
        )
        return carry

    lax.fori_loop(0, own, attend_own, 0)
    lax.fori_loop(0, own, attend_theirs, 0)

    advance(*gap_plan)
    bias_copy.wait_recv()
    for k in range(3):
        complete(k)
    for k in range(5, chunks):
        cross(k).start()

    pack[0:8, :] = stage[...]
    pack[8:16, :] = tcls[:, pl.ds(m_col, half)]
    pack[16:32, :] = jnp.zeros((16, half), F32)
    q_rows = queries.shape[0]
    pack[16 : 16 + q_rows, :] = queries[:, pl.ds(m_col, half)].astype(F32)
    gath[chip, core, mp] = pack[...].astype(BF)

    def gather_start(i, carry):
        there = lax.rem(chip * 2 + mp + i, 2 * chips)
        here = gath.at[chip, core, mp]
        remote(
            here, here, g_send, g_recv, (lax.div(there, 2) * 2 + core, lax.rem(there, 2))
        ).start()
        return carry

    gather_window = tok.at[pl.ds(0, (2 * chips - 1) * 16), :]

    lax.fori_loop(1, 2 * chips, gather_start, 0)

    lax.fori_loop(0, own, attend_far, 0)

    for copy in loads[4:]:
        copy.wait()
    complete(3)
    bo = row_of(b_out[...])
    g1 = row_of(gain_one[...])
    s1 = row_of(shift_one[...])
    g2 = row_of(gain_two[...])
    bb = row_of(b_back[...])

    def feed_own(i, carry):
        move_on(i, feed_plan)
        at = mult(i * slot, slot)
        here = pl.ds(at, slot)
        x = tok[pl.ds(mult(mp * own_rows + i * slot, slot), slot), :].astype(F32)
        resid = x + nn(ctx[here, :], wo[...]) + bo
        scaled, _ = standard(resid)
        norm = scaled * g1 + s1
        low = norm.astype(BF)
        norm_low[here, :] = low
        total = norm + bb
        for u in range(blocks):
            if u == 1:
                move_on(i, feed_mid_plan)
            inner = nn(low, wi[mp, u]) + bin_own[u : u + 1, :]
            total = total + nn(gelu(inner).astype(BF), wb[mp, u])
        acc[here, :] = total

        return carry

    lax.fori_loop(0, own, feed_own, 0)

    spent(gather_window, g_recv)
    to_sibling = remote(gath.at[:, core], gath.at[:, core], gs_send, gs_recv, sibling)
    to_sibling.start()

    for u in range(blocks):
        complete(first_in + u)

        def feed_far_in(i, carry, u=u):
            move_on(i, in_plan[u])
            here = pl.ds(mult(i * 2 * slot, slot), 2 * slot)
            inner = nn(norm_low[here, :], wi[far, u]) + bin_far[u : u + 1, :]
            act_far[u, here, :] = gelu(inner).astype(BF)
            return carry

        lax.fori_loop(0, own // 2, feed_far_in, 0)

    for u in range(blocks):
        complete(first_back + u)

    def out_copy(i, mine):
        side = mp if mine else far
        there = out_act.at[pl.ds(mult(side * own_rows + i * slot, 16), slot), :]
        return remote(
            obuf.at[1, pl.ds(mult(i * slot, 16), slot), :], there, o_send.at[i], o_recv.at[i], pair
        )

    def out_local(i):
        there = out_act.at[pl.ds(mult(mp * own_rows + i * slot, 16), slot), :]
        return pltpu.make_async_copy(
            obuf.at[0, pl.ds(mult(i * slot, 16), slot), :], there, o_loc.at[i]
        )

    def finish(i, carry):
        here = pl.ds(mult(i * slot, slot), slot)
        total = acc[here, :]
        for u in range(blocks):
            total = total + nn(act_far[u, here, :], wb[far, u])
        scaled, _ = standard(total)
        acc[here, :] = scaled * g2
        obuf[0, here, :] = acc[here, pl.ds(m_col, half)].astype(BF)
        obuf[1, here, :] = acc[here, pl.ds(f_col, half)].astype(BF)
        out_copy(i, True).start()
        out_local(i).start()
        return carry

    lax.fori_loop(0, own, finish, 0)

    remote(
        gath.at[:, 1 - core], gath.at[:, 1 - core], gs_send, gs_recv, sibling
    ).wait_recv()
    q_pad = nd * 16
    for h in range(2):
        cols = slice(h * half, (h + 1) * half)
        block = gath[:, :, h].astype(F32)
        ctx_all[:, cols] = block[:, :, 0:8].reshape(passages, half).astype(BF)
        tok_all[:, cols] = block[:, :, 8:16].reshape(passages, half).astype(BF)
        q_all[:, cols] = block[:, :, 16:32].reshape(q_pad, half).astype(BF)

    resid = tok_all[...].astype(F32) + nn(ctx_all[...], wo[...]) + bo
    scaled, inverse1 = standard(resid)
    xh1_all[...] = scaled
    norm = scaled * g1 + s1
    low = norm.astype(BF)
    norm_all[...] = low
    total = norm + bb
    for h in range(2):
        for u in range(blocks):
            bias = jnp.where(mp == h, bin_own[u : u + 1, :], bin_far[u : u + 1, :])
            inner = nn(low, wi[h, u]) + bias
            inner_all[h, u] = inner
            active = gelu(inner).astype(BF)
            act_all[h, u] = active
            total = total + nn(active, wb[h, u])
    xh2, inverse2 = standard(total)
    cls = (xh2 * g2).astype(BF)
    similar = nt(cls, q_all[...])
    top = jnp.max(similar, axis=0, keepdims=True)
    log_sum = top + jnp.log(jnp.sum(jnp.exp(similar - top), axis=0, keepdims=True))
    q_count = query_total // nd
    from_q = lax.broadcasted_iota(jnp.int32, (query_total, q_pad), 0)
    to_q = lax.broadcasted_iota(jnp.int32, (query_total, q_pad), 1)
    spot = lax.div(from_q, q_count) * 16 + lax.rem(from_q, q_count)
    wanted = jnp.broadcast_to(row_of(positives[...]), (8, query_total)) + 1.0
    place = exact(wanted, (spot == to_q).astype(F32))[0:1, :] - 1.0
    target = lax.broadcasted_iota(jnp.int32, similar.shape, 0).astype(F32) == place
    picked = jnp.sum(jnp.where(target, similar, 0.0), axis=0, keepdims=True)
    o_loss[...] = jnp.broadcast_to(log_sum - picked, o_loss.shape)
    slopes = (jnp.exp(similar - log_sum) - target.astype(F32)) * (1.0 / query_total)
    slope_high = slopes.astype(BF)
    slope_low = (slopes - slope_high.astype(F32)).astype(BF)
    cls_grad = nn(slope_high, q_all[...]) + nn(slope_low, q_all[...])
    pick = (
        lax.broadcasted_iota(jnp.int32, (16, q_pad), 1)
        == lax.broadcasted_iota(jnp.int32, (16, q_pad), 0) + dp * 16
    ).astype(BF)
    o_qgrad[...] = nn(nt(pick, slope_high).astype(BF), cls) + nn(
        nt(pick, slope_low).astype(BF), cls
    )
    d_two = norm_back(g2 * cls_grad, xh2, inverse2)
    o_sums[0:1, :] = jnp.sum(cls_grad * xh2, axis=0, keepdims=True)
    o_sums[1:2, :] = jnp.sum(d_two, axis=0, keepdims=True)
    ffn_low = d_two.astype(BF)
    o_ffn[...] = ffn_low
    back = d_two
    for h in range(2):
        for u in range(blocks):
            d_active = nt(ffn_low, wb[h, u])
            d_inner = d_active * gelu_slope(inner_all[h, u])
            inner_all[h, u, 0:8, :] = jnp.broadcast_to(
                jnp.sum(d_inner, axis=0, keepdims=True), (8, unit)
            )
            inner_low = d_inner.astype(BF)
            low_all[h, u] = inner_low
            back = back + nt(inner_low, wi[h, u])
    for u in range(blocks):
        o_active[u] = act_all[mp, u]
        o_inner[u] = low_all[mp, u]
        o_sums_in[u : u + 1, :] = inner_all[mp, u, 0:1, :]
    xh1 = xh1_all[...]
    d_one = norm_back(g1 * back, xh1, inverse1)
    d1_all[...] = d_one
    o_sums[2:3, :] = jnp.sum(back * xh1, axis=0, keepdims=True)
    o_sums[3:4, :] = jnp.sum(back, axis=0, keepdims=True)
    o_sums[4:5, :] = jnp.sum(d_one, axis=0, keepdims=True)
    attn_low = d_one.astype(BF)
    o_attn[...] = attn_low
    o_norm[...] = norm_all[...]
    o_tok[...] = tok_all[...]
    d_ctx = nt(attn_low, wo[pl.ds(mult(mp * half, 128), half), :]).astype(BF)
    o_dctx[...] = d_ctx
    dc_all[...] = d_ctx.astype(F32)
    q_cls = (nn(tok_all[...], wq[:, 0:half]) + bias_q).astype(BF)
    o_qcls[...] = q_cls
    qc_all[...] = q_cls.astype(F32) * 0.125
    o_context[...] = ctx_all[:, pl.ds(m_col, half)]
    o_sums[5:6, 0:half] = jnp.sum(dc_all[...], axis=0, keepdims=True)

    def stored(src, dst, k):
        return pltpu.make_async_copy(src, dst, out_sem.at[k])

    early = [
        stored(src, dst, k)
        for k, (src, dst) in enumerate(
            (
                (o_active, h_active),
                (o_inner, h_inner),
                (o_context, h_context),
                (o_qcls, h_qcls),
                (o_dctx, h_dctx),
                (o_norm, h_norm),
                (o_ffn, h_ffn),
                (o_attn, h_attn),
                (o_tok, h_tok),
                (o_sums, h_sums),
                (o_sums_in, h_sums_in),
                (o_loss, h_loss),
                (o_qgrad, h_qgrad),
            )
        )
    ]
    for copy in early:
        copy.start()

    base = mult(dp * count, 8)
    fkind = count * 8

    mark = jnp.logical_or(row_place == heads, row_place == heads + 1)
    for p in range(count):
        d_row = dc_all[pl.ds(base + p, 1), :]
        q_row = qc_all[pl.ds(base + p, 1), :]
        rank_f[p * 16 : p * 16 + 8, 0:half] = jnp.where(head_mask, d_row, 0.0)
        rank_f[p * 16 + 8 : p * 16 + 16, 0:half] = jnp.where(head_mask, q_row, 0.0)
    kept = rank_f[:, 0:half].astype(BF)
    group = 4
    for first in range(0, count, group):
        d_scores = []
        for p in range(first, first + group):
            c = chance[p]
            d_chance = nt(kept[p * 16 : p * 16 + 16, :], valb[p * slot : (p + 1) * slot, :])[0:8, :]
            d_scores.append(c * (d_chance - jnp.sum(c * d_chance, axis=1, keepdims=True)))
        for p, d in zip(range(first, first + group), d_scores):
            s_low = d.astype(BF)
            at = slice(p * slot, (p + 1) * slot)
            coef_own[p * 16 + 8 : p * 16 + 16, :] = jnp.where(mark, first_key, d)
            factor[fkind + p * 8 : fkind + p * 8 + 8, :] = nn(s_low, tok[at, :])
            spread = nn(s_low, keyb[at, :])
            dq_rows[p : p + 1, :] = 0.125 * jnp.sum(
                jnp.where(head_mask, spread, 0.0), axis=0, keepdims=True
            )

    turned = jnp.transpose(factor[...]).astype(BF)
    dq = dq_rows[...]
    for b in range(half // 128):
        pack[b * 8 : b * 8 + 8, 0:128] = dq[:, b * 128 : b * 128 + 128]
    pack[half // 16 : 32, 0:128] = jnp.zeros((32 - half // 16, 128), F32)
    dq_low = pack[:, 0:128].astype(BF)
    share = width // nd
    for j in range(nd):
        fac_send[j, 0:share, :] = turned[j * share : (j + 1) * share, :]
        fac_send[j, share:, :] = dq_low
    o_factor[dp] = fac_send[dp]

    def factor_start(i, carry):
        there = lax.rem(dp + i, nd)
        remote(fac_send.at[there], o_factor.at[dp], f_send, f_recv, (there, mp)).start()
        return carry

    lax.fori_loop(1, nd, factor_start, 0)

    even = lax.rem(lax.div(lax.broadcasted_iota(jnp.int32, (count * 16, 1), 0), 8), 2) == 0
    rank_v = nt(kept, wq[:, 2 * half :])
    rank_k = nt(kept, wq[:, half : 2 * half])
    rank_f[...] = jnp.where(even, rank_v, rank_k)
    back_q = nt(dq.astype(BF), wq[:, 0:half])
    for p in range(count):
        rank_f[p * 16 + heads : p * 16 + heads + 1, :] = back_q[p : p + 1, :]
        rank_f[p * 16 + heads + 1 : p * 16 + 8, :] = jnp.zeros((7 - heads, width), F32)
        rank_f[p * 16 + 8 + heads : p * 16 + 16, :] = jnp.zeros((8 - heads, width), F32)
    rank_send[...] = rank_f[:, pl.ds(f_col, half)].astype(BF)
    coef_low = coef_own[...].astype(BF)
    o_coef[0] = coef_low
    coef_far_copy = remote(o_coef.at[0], coef_far, m_send.at[0], m_recv.at[0], pair)
    coef_far_copy.start()
    rank_copy = remote(rank_send, rank_far, m_send.at[1], m_recv.at[1], pair)
    rank_copy.start()
    d1_rows = d1_all[pl.ds(base, count), pl.ds(m_col, half)]
    d1_high = d1_rows.astype(BF).astype(F32)
    d1_low = d1_rows - d1_high
    for p in range(count):
        rank_f[p * 16 + 8 + heads : p * 16 + 9 + heads, pl.ds(m_col, half)] = d1_high[p : p + 1]
        rank_f[p * 16 + 9 + heads : p * 16 + 10 + heads, pl.ds(m_col, half)] = d1_low[p : p + 1]
    o_rank[0] = rank_f[:, pl.ds(m_col, half)].astype(BF)

    coef_far_copy.wait_recv()
    rank_copy.wait_recv()
    o_coef[1] = coef_far[...]
    o_rank[1] = rank_far[...]

    factor_window = fac_send.at[pl.ds(0, nd - 1)]
    spent(factor_window, f_recv)
    last = [stored(o_factor, h_factor, 15), stored(o_coef, h_coef, 13), stored(o_rank, h_rank, 14)]
    for copy in last:
        copy.start()
    spent(factor_window, f_send)
    coef_far_copy.wait_send()
    rank_copy.wait_send()
    bias_copy.wait_send()
    spent(gather_window, g_send)
    to_sibling.wait_send()
    for k in range(chunks):
        cross(k).wait_send()
        spent(sent_bytes(k), w_send.at[k])

    def drain(i, carry):
        out_copy(i, True).wait_send()
        out_copy(i, False).wait_recv()
        out_local(i).wait()
        return carry

    lax.fori_loop(0, own, drain, 0)
    for copy in early + last:
        copy.wait()


def gradients(
    nd,
    act_in,
    coef_in,
    rank_in,
    factor_in,
    active_in,
    inner_in,
    context_in,
    qcls_in,
    dctx_in,
    norm_in,
    ffn_in,
    attn_in,
    tok_in,
    sums_in,
    sums_units_in,
    loss_in,
    qgrad_in,
    act_out,
    query_loss,
    input_grad,
    query_grad,
    grad_qkv,
    grad_bias_qv,
    grad_out,
    grad_bias_out,
    grad_gain_one,
    grad_shift_one,
    grad_in,
    grad_bias_in,
    grad_back,
    grad_bias_back,
    grad_gain_two,
    coef,
    rank,
    factor,
    active,
    inner,
    context,
    qcls,
    dctx,
    norm,
    ffn,
    attn,
    tok,
    sums,
    sums_units,
    loss,
    qgrad,
    sems,
    act_sem,
    act_buf,
    in_buf,
    in_sems,
    rhs,
):
    dp = lax.axis_index("dp")
    act_load = pltpu.make_async_copy(act_in, act_buf, act_sem.at[0])
    act_store = pltpu.make_async_copy(act_buf, act_out, act_sem.at[1])
    act_load.start()
    pairs = (
        (coef_in, coef),
        (rank_in, rank),
        (factor_in, factor),
        (qcls_in, qcls),
        (dctx_in, dctx),
        (active_in, active),
        (inner_in, inner),
        (context_in, context),
        (norm_in, norm),
        (ffn_in, ffn),
        (attn_in, attn),
        (tok_in, tok),
        (sums_in, sums),
        (sums_units_in, sums_units),
        (loss_in, loss),
        (qgrad_in, qgrad),
    )
    loads = [pltpu.make_async_copy(src, dst, sems.at[i]) for i, (src, dst) in enumerate(pairs)]
    for load in loads:
        load.start()
    passages, width = ffn.shape
    half = width // 2
    share = width // nd
    count = passages // nd
    slot = coef.shape[2]
    for load in loads[:2]:
        load.wait()

    def input_copy(p):
        at = pl.ds(mult(p * slot, slot), slot)
        return pltpu.make_async_copy(in_buf.at[at, :], input_grad.at[at, :], in_sems.at[p])

    def input_rows(p, carry):
        rows16 = pl.ds(mult(p * 16, 16), 16)
        both = jnp.concatenate([coef[0, rows16, :], coef[1, rows16, :]], axis=0)
        right = jnp.concatenate([rank[0, rows16, :], rank[1, rows16, :]], axis=0)
        in_buf[pl.ds(mult(p * slot, slot), slot), :] = tn(both, right)
        input_copy(p).start()
        return carry

    lax.fori_loop(0, count, input_rows, 0)
    act_load.wait()
    act_store.start()
    for load in loads[2:]:
        load.wait()

    spread = lax.broadcasted_iota(jnp.int32, (8, half), 0) == lax.div(
        lax.broadcasted_iota(jnp.int32, (8, half), 1), HEAD
    )
    fkind = count * 8

    def build(s, carry):
        d_rows = dctx[pl.ds(mult(s * 2 * count, 16), 2 * count), :].astype(F32)
        q_rows = qcls[pl.ds(mult(s * 2 * count, 16), 2 * count), :].astype(F32) * 0.125
        k_blocks = [jnp.where(spread, q_rows[p : p + 1, :], 0.0) for p in range(2 * count)]
        v_blocks = [jnp.where(spread, d_rows[p : p + 1, :], 0.0) for p in range(2 * count)]
        here = pl.ds(mult(s * 2 * fkind, 16), 2 * fkind)
        rhs[here, 0:half] = jnp.concatenate(k_blocks, 0).astype(BF)
        rhs[here, half:] = jnp.concatenate(v_blocks, 0).astype(BF)
        return carry

    lax.fori_loop(0, nd // 2, build, 0)
    grad_k = jnp.zeros((share, half), F32)
    grad_v = jnp.zeros((share, half), F32)
    for s in range(0, nd, 4):
        left_v = jnp.concatenate([factor[s + t, 0:share, :][:, 0:fkind] for t in range(4)], axis=1)
        left_k = jnp.concatenate([factor[s + t, 0:share, :][:, fkind:] for t in range(4)], axis=1)
        grad_k = grad_k + nn(left_k, rhs[s * fkind : (s + 4) * fkind, 0:half])
        grad_v = grad_v + nn(left_v, rhs[s * fkind : (s + 4) * fkind, half:])
    grad_qkv[1] = grad_k
    grad_qkv[2] = grad_v

    pick = one_hot((width, share), dp * share)
    pick_low = pick.astype(BF)
    row = lax.broadcasted_iota(jnp.int32, (share, width), 0)
    column = lax.broadcasted_iota(jnp.int32, (share, width), 1)
    pick_t = (column == row + dp * share).astype(BF)
    ffn_own = nt(pick_t, ffn[...]).astype(BF)
    attn_own = nt(pick_t, attn[...]).astype(BF)
    norm_own = nt(pick_t, norm[...]).astype(BF)
    tok_own = nt(pick_t, tok[...]).astype(BF)
    grad_out[...] = nn(attn_own, context[...])
    unit = active.shape[2]
    blocks = active.shape[0]
    for u in range(blocks):
        cols = slice(u * unit, (u + 1) * unit)
        grad_back[:, cols] = nn(ffn_own, active[u])
        grad_in[:, cols] = nn(norm_own, inner[u])
    dq_sum = []
    for b in range(half // 128):
        cols = factor[:, share:, :].astype(F32)[:, b * 8 : b * 8 + 8, :].reshape(passages, 128)
        dq_sum.append(jnp.sum(cols, axis=0, keepdims=True))
        grad_qkv[0, :, b * 128 : b * 128 + 128] = nn(tok_own, cols.astype(BF))

    mine = exact(sums[...], pick)
    grad_gain_two[...] = mine[0:1, :].reshape(share)
    grad_bias_back[...] = mine[1:2, :].reshape(share)
    grad_gain_one[...] = mine[2:3, :].reshape(share)
    grad_shift_one[...] = mine[3:4, :].reshape(share)
    grad_bias_out[...] = mine[4:5, :].reshape(share)
    part = half // nd
    both = jnp.concatenate([jnp.concatenate(dq_sum, axis=1), sums[5:6, 0:half]], axis=0)
    wide = jnp.concatenate([both, jnp.zeros((6, half), F32)], axis=0)
    grad_bias_qv[...] = exact(wide, one_hot((half, part), dp * part))[0:2, :]
    in_share = grad_bias_in.shape[0]
    total = jnp.zeros((8, in_share), F32)
    for u in range(blocks):
        total = total + exact(
            jnp.broadcast_to(sums_units[u : u + 1, :], (8, unit)),
            one_hot((unit, in_share), dp * in_share - u * unit),
        )
    grad_bias_in[...] = total[0:1, :].reshape(in_share)
    q_rows = query_loss.shape[0]
    query_loss[...] = exact(loss[...], one_hot((loss.shape[1], q_rows), dp * 16))[0:1, :].reshape(q_rows)
    query_grad[...] = qgrad[0:q_rows, :]

    def input_wait(p, carry):
        input_copy(p).wait()
        return carry

    lax.fori_loop(0, count, input_wait, 0)
    act_store.wait()


def per_device(nd, *arrays):
    (
        tokens,
        lengths,
        queries,
        positives,
        w_qkv,
        b_qv,
        w_out,
        b_out,
        gain_one,
        shift_one,
        w_in,
        b_in,
        w_back,
        b_back,
        gain_two,
    ) = arrays
    rows, width = tokens.shape
    count = lengths.shape[0]
    slot = rows // count
    half = w_qkv.shape[2]
    units = w_in.shape[1]
    unit = 512
    blocks = units // unit
    chunks = 4 + 2 * blocks
    own_rows = rows // 2
    passages = nd * count
    chips = nd // 2
    q_rows = queries.shape[0]
    q_pad = nd * 16
    share = width // nd
    vmem = pl.BlockSpec(memory_space=pltpu.VMEM)
    hbm = pl.BlockSpec(memory_space=pl.ANY)
    smem = pl.BlockSpec(memory_space=pltpu.SMEM)
    in_specs = [smem, hbm, vmem, vmem, hbm, vmem, hbm, vmem, vmem, vmem, hbm, vmem, hbm, vmem, vmem]
    shape = jax.ShapeDtypeStruct
    outs = [
        (shape((rows, half), BF), hbm),
        (shape((2, count * 16, slot), BF), hbm),
        (shape((2, count * 16, half), BF), hbm),
        (shape((nd, share + 32, 128), BF), hbm),
        (shape((blocks, passages, unit), BF), hbm),
        (shape((blocks, passages, unit), BF), hbm),
        (shape((passages, half), BF), hbm),
        (shape((passages, half), BF), hbm),
        (shape((passages, half), BF), hbm),
        (shape((passages, width), BF), hbm),
        (shape((passages, width), BF), hbm),
        (shape((passages, width), BF), hbm),
        (shape((passages, width), BF), hbm),
        (shape((8, width), F32), hbm),
        (shape((8, unit), F32), hbm),
        (shape((8, q_pad), F32), hbm),
        (shape((16, width), F32), hbm),
    ]
    dma = pltpu.SemaphoreType.DMA
    scratch = [
        pltpu.VMEM((rows, width), BF),
        pltpu.VMEM((width, 3 * half), BF),
        pltpu.VMEM((width, 3 * half), BF),
        pltpu.VMEM((width, width), BF),
        pltpu.VMEM((2, blocks, width, unit), BF),
        pltpu.VMEM((2, blocks, unit, width), BF),
        pltpu.VMEM((rows, half), BF),
        pltpu.VMEM((rows, half), BF),
        pltpu.VMEM((own_rows, width), BF),
        pltpu.VMEM((own_rows, width), BF),
        pltpu.VMEM((own_rows, width), F32),
        pltpu.VMEM((blocks, own_rows, unit), BF),
        pltpu.VMEM((2, own_rows, half), BF),
        pltpu.VMEM((count, 8, slot), F32),
        pltpu.VMEM((2 * count * 8, width), F32),
        pltpu.VMEM((8, half), F32),
        pltpu.VMEM((8, width), F32),
        pltpu.VMEM((32, half), F32),
        pltpu.VMEM((chips, 2, 2, 32, half), BF),
        pltpu.VMEM((passages, width), BF),
        pltpu.VMEM((passages, width), BF),
        pltpu.VMEM((q_pad, width), BF),
        pltpu.VMEM((passages, width), F32),
        pltpu.VMEM((passages, width), BF),
        pltpu.VMEM((2, blocks, passages, unit), F32),
        pltpu.VMEM((2, blocks, passages, unit), BF),
        pltpu.VMEM((2, blocks, passages, unit), BF),
        pltpu.VMEM((passages, half), F32),
        pltpu.VMEM((passages, half), F32),
        pltpu.VMEM((passages, width), F32),
        pltpu.VMEM((8, half), F32),
        pltpu.VMEM((count * 16, width), F32),
        pltpu.VMEM((count * 16, slot), F32),
        pltpu.VMEM((count * 16, slot), BF),
        pltpu.VMEM((count * 16, half), BF),
        pltpu.VMEM((count * 16, half), BF),
        pltpu.VMEM((count * 16, half), BF),
        pltpu.VMEM((nd, share + 32, 128), BF),
        dma((5 + 2 * blocks,)),
        dma((chunks,)),
        dma((chunks,)),
        dma((chunks,)),
        dma((chunks, 5)),
        dma((count // 2,)),
        dma((count // 2,)),
        dma((count // 2,)),
        dma,
        dma,
        dma,
        dma,
        dma,
        dma,
        dma((2,)),
        dma((2,)),
        dma,
        dma,
        pltpu.VMEM((8, unit), F32),
        pltpu.VMEM((8, unit), F32),
        dma((16,)),
    ] + [pltpu.VMEM(o[0].shape, o[0].dtype) for o in outs[1:]]
    made = pl.pallas_call(
        functools.partial(tower, nd, nd * q_rows),
        out_shape=[o[0] for o in outs],
        in_specs=in_specs,
        out_specs=[o[1] for o in outs],
        scratch_shapes=scratch,
        compiler_params=pltpu.CompilerParams(
            collective_id=0, has_side_effects=True, vmem_limit_bytes=60 * MIB
        ),
        name="tower",
    )(
        lengths,
        tokens,
        queries,
        positives,
        w_qkv,
        b_qv,
        w_out,
        b_out,
        gain_one,
        shift_one,
        w_in,
        b_in,
        w_back,
        b_back,
        gain_two,
    )
    g_outs = [
        (shape((rows, half), BF), hbm),
        (shape((q_rows,), F32), vmem),
        (shape((rows, half), F32), hbm),
        (shape((q_rows, width), F32), vmem),
        (shape((3, share, half), F32), vmem),
        (shape((2, half // nd), F32), vmem),
        (shape((share, half), F32), vmem),
        (shape((share,), F32), vmem),
        (shape((share,), F32), vmem),
        (shape((share,), F32), vmem),
        (shape((share, units), F32), vmem),
        (shape((units // nd,), F32), vmem),
        (shape((share, units), F32), vmem),
        (shape((share,), F32), vmem),
        (shape((share,), F32), vmem),
    ]
    grads = pl.pallas_call(
        functools.partial(gradients, nd),
        out_shape=[o[0] for o in g_outs],
        in_specs=[hbm] * len(outs),
        out_specs=[o[1] for o in g_outs],
        scratch_shapes=[pltpu.VMEM(o[0].shape, o[0].dtype) for o in outs[1:]]
        + [
            dma((len(outs) - 1,)),
            dma((2,)),
            pltpu.VMEM((rows, half), BF),
            pltpu.VMEM((rows, half), F32),
            dma((count,)),
            pltpu.VMEM((nd * count * 8, width), BF),
        ],
        compiler_params=pltpu.CompilerParams(vmem_limit_bytes=62 * MIB),
        name="gradients",
    )(*made)
    grads = list(grads)
    grads[6] = grads[6].T
    grads[12] = grads[12].T
    return tuple(grads)


def layer_norm(rows, gain, shift):
    center = jnp.mean(rows, axis=-1, keepdims=True)
    spread = rows - center
    second = jnp.mean(spread * spread, axis=-1, keepdims=True)
    return spread * lax.rsqrt(second + EPS) * gain + shift


def scaled_norm(rows, gain):
    center = jnp.mean(rows, axis=-1, keepdims=True)
    spread = rows - center
    second = jnp.mean(spread * spread, axis=-1, keepdims=True)
    return spread * lax.rsqrt(second + EPS) * gain


def gelu_exact(values):
    return jax.nn.gelu(values, approximate=False)


def first_rows(values, count):
    return values.reshape((count, values.shape[0] // count) + values.shape[1:])[:, 0]


def by_collectives(
    tokens,
    lengths,
    queries,
    positives,
    w_qkv,
    b_qv,
    w_out,
    b_out,
    gain_one,
    shift_one,
    w_in,
    b_in,
    w_back,
    b_back,
    gain_two,
):
    rows, width = tokens.shape
    count = lengths.shape[0]
    slot = rows // count
    local = w_qkv.shape[2]
    heads_here = local // HEAD
    scale = 1.0 / math.sqrt(HEAD)
    projected = jnp.einsum("rd,jdc->jrc", tokens, w_qkv, preferred_element_type=F32)
    bias_qv = b_qv.astype(F32)
    query = (projected[0] + bias_qv[0]).astype(BF)
    keyed = projected[1].astype(BF)
    value = (projected[2] + bias_qv[1]).astype(BF)
    block = min(count, max(1, 512 // slot))
    blocks = count // block
    valid = lax.broadcasted_iota(jnp.int32, (count, slot), 1) < lengths[:, None]
    split_shape = (blocks, block, slot, heads_here, HEAD)

    def attend(inputs):
        query_part, keyed_part, value_part, valid_part = inputs
        scores = (
            jnp.einsum(
                "pqhd,pkhd->phqk", query_part, keyed_part, preferred_element_type=F32
            )
            * scale
        )
        scores = jnp.where(valid_part[:, None, None, :], scores, MASKED)
        top = jnp.max(scores, axis=-1, keepdims=True)
        raised = jnp.exp(scores - top)
        total = jnp.sum(raised, axis=-1, keepdims=True)
        chance_low = (raised / total).astype(BF)
        mixed = jnp.einsum(
            "phqk,pkhd->pqhd", chance_low, value_part, preferred_element_type=F32
        )
        return (mixed.astype(BF), (top + jnp.log(total))[:, :, 0, 0])

    context, log_total = lax.map(
        attend,
        (
            query.reshape(split_shape),
            keyed.reshape(split_shape),
            value.reshape(split_shape),
            valid.reshape(blocks, block, slot),
        ),
    )
    context = context.reshape(rows, local)
    log_total = log_total.reshape(count, heads_here)
    partial_attn = jnp.dot(context, w_out, preferred_element_type=F32).astype(BF)
    attended = lax.psum(partial_attn, "mp").astype(F32) + b_out.astype(F32)
    resid_one = tokens.astype(F32) + attended
    gain_one_w = gain_one.astype(F32)
    shift_one_w = shift_one.astype(F32)
    gain_two_w = gain_two.astype(F32)
    norm_one = layer_norm(resid_one, gain_one_w, shift_one_w)
    norm_low = norm_one.astype(BF)
    inner = jnp.dot(norm_low, w_in, preferred_element_type=F32) + b_in.astype(F32)
    active = gelu_exact(inner).astype(BF)
    partial_ffn = jnp.dot(active, w_back, preferred_element_type=F32).astype(BF)
    resid_two = (
        norm_one + lax.psum(partial_ffn, "mp").astype(F32) + b_back.astype(F32)
    )
    output = scaled_norm(resid_two, gain_two_w)
    column = lax.axis_index("mp") * local
    activations = lax.dynamic_slice_in_dim(output, column, local, 1).astype(BF)
    cls_low = first_rows(output, count).astype(BF)
    query_rows = queries.shape[0]
    members = lax.axis_size("dp")
    query_total = query_rows * members
    own_query = lax.axis_index("dp") * query_rows
    gathered = lax.all_gather(cls_low, "dp", axis=0, tiled=True)
    similar = jnp.einsum("qd,pd->qp", queries, gathered, preferred_element_type=F32)
    mine = lax.dynamic_slice_in_dim(positives, own_query, query_rows)
    target = lax.broadcasted_iota(jnp.int32, similar.shape, 1) == mine[:, None]
    top = jnp.max(similar, axis=1, keepdims=True)
    log_sum = top[:, 0] + jnp.log(jnp.sum(jnp.exp(similar - top), axis=1))
    picked = jnp.sum(jnp.where(target, similar, 0.0), axis=1)
    query_loss = log_sum - picked
    slopes = (jnp.exp(similar - log_sum[:, None]) - target.astype(F32)) / query_total
    query_grad = jnp.dot(slopes, gathered.astype(F32), precision=lax.Precision.HIGHEST)
    queries_wide = queries.astype(F32)
    cls_grad = lax.psum_scatter(
        jnp.einsum("qp,qd->pd", slopes, queries_wide, precision=lax.Precision.HIGHEST),
        "dp",
        scatter_dimension=0,
        tiled=True,
    )
    _, norm_two_pull = jax.vjp(scaled_norm, first_rows(resid_two, count), gain_two_w)
    d_resid_two, grad_gain_two = norm_two_pull(cls_grad)
    grad_bias_back = jnp.sum(d_resid_two, axis=0)
    ffn_low = d_resid_two.astype(BF)
    grad_back = jnp.einsum(
        "pf,pd->fd", first_rows(active, count), ffn_low, preferred_element_type=F32
    )
    d_active = jnp.einsum("pd,fd->pf", ffn_low, w_back, preferred_element_type=F32)
    _, gelu_pull = jax.vjp(gelu_exact, first_rows(inner, count))
    d_inner = gelu_pull(d_active)[0]
    grad_bias_in = jnp.sum(d_inner, axis=0)
    inner_low = d_inner.astype(BF)
    grad_in = jnp.einsum(
        "pd,pf->df", first_rows(norm_low, count), inner_low, preferred_element_type=F32
    )
    back_norm = jnp.einsum("pf,df->pd", inner_low, w_in, preferred_element_type=F32)
    d_norm_one = d_resid_two + lax.psum(back_norm, "mp")
    _, norm_one_pull = jax.vjp(layer_norm, first_rows(resid_one, count), gain_one_w, shift_one_w)
    d_resid_one, grad_gain_one, grad_shift_one = norm_one_pull(d_norm_one)
    grad_bias_out = jnp.sum(d_resid_one, axis=0)
    attn_low = d_resid_one.astype(BF)
    grad_out = jnp.einsum(
        "pc,pd->cd", first_rows(context, count), attn_low, preferred_element_type=F32
    )
    d_context = jnp.einsum("pd,cd->pc", attn_low, w_out, preferred_element_type=F32).astype(
        BF
    )
    d_context = d_context.reshape(count, heads_here, HEAD)
    query_cls = first_rows(query, count).reshape(count, heads_here, HEAD)
    keyed_heads = keyed.reshape(count, slot, heads_here, HEAD)
    value_heads = value.reshape(count, slot, heads_here, HEAD)
    scores_cls = (
        jnp.einsum("phd,pkhd->phk", query_cls, keyed_heads, preferred_element_type=F32)
        * scale
    )
    scores_cls = jnp.where(valid[:, None, :], scores_cls, MASKED)
    chance = jnp.exp(scores_cls - log_total[:, :, None])
    d_chance = jnp.einsum(
        "phd,pkhd->phk", d_context, value_heads, preferred_element_type=F32
    )
    d_value = jnp.einsum(
        "phk,phd->pkhd", chance.astype(BF), d_context, preferred_element_type=F32
    )
    d_scores = chance * (d_chance - jnp.sum(chance * d_chance, axis=-1, keepdims=True))
    scores_low = d_scores.astype(BF)
    d_query = (
        jnp.einsum("phk,pkhd->phd", scores_low, keyed_heads, preferred_element_type=F32)
        * scale
    )
    d_keyed = (
        jnp.einsum("phk,phd->pkhd", scores_low, query_cls, preferred_element_type=F32)
        * scale
    )
    d_query = d_query.reshape(count, local)
    d_value = d_value.reshape(rows, local)
    query_low = d_query.astype(BF)
    keyed_value_low = jnp.stack(
        [d_keyed.reshape(rows, local).astype(BF), d_value.astype(BF)]
    )
    grad_bias_qv = jnp.stack([jnp.sum(d_query, axis=0), jnp.sum(d_value, axis=0)])
    grad_query_w = jnp.einsum(
        "pd,pc->dc", first_rows(tokens, count), query_low, preferred_element_type=F32
    )
    grad_kv = jnp.einsum("rd,jrc->jdc", tokens, keyed_value_low, preferred_element_type=F32)
    grad_qkv = jnp.concatenate([grad_query_w[None], grad_kv], axis=0)
    own_half = lax.dynamic_slice_in_dim(d_resid_one, column, local, 1)
    back_kv = jnp.einsum(
        "jrc,jdc->rd", keyed_value_low, w_qkv[1:], preferred_element_type=F32
    )
    back_query = jnp.einsum("pc,dc->pd", query_low, w_qkv[0], preferred_element_type=F32)
    back_all = back_kv.reshape(count, slot, width).at[:, 0].add(back_query).reshape(rows, width)
    input_grad = lax.psum_scatter(
        back_all.astype(BF), "mp", scatter_dimension=1, tiled=True
    ).astype(F32)
    input_grad = input_grad.reshape(count, slot, local).at[:, 0].add(own_half).reshape(rows, local)
    summed = (
        lax.psum_scatter(grad_qkv, "dp", scatter_dimension=1, tiled=True),
        lax.psum_scatter(grad_bias_qv, "dp", scatter_dimension=1, tiled=True),
        lax.psum_scatter(grad_out, "dp", scatter_dimension=1, tiled=True),
        lax.psum_scatter(grad_bias_out, "dp", scatter_dimension=0, tiled=True),
        lax.psum_scatter(grad_gain_one, "dp", scatter_dimension=0, tiled=True),
        lax.psum_scatter(grad_shift_one, "dp", scatter_dimension=0, tiled=True),
        lax.psum_scatter(grad_in, "dp", scatter_dimension=0, tiled=True),
        lax.psum_scatter(grad_bias_in, "dp", scatter_dimension=0, tiled=True),
        lax.psum_scatter(grad_back, "dp", scatter_dimension=1, tiled=True),
        lax.psum_scatter(grad_bias_back, "dp", scatter_dimension=0, tiled=True),
        lax.psum_scatter(grad_gain_two, "dp", scatter_dimension=0, tiled=True),
    )
    return (
        activations,
        query_loss,
        input_grad,
        query_grad,
        summed[0],
        summed[1],
        summed[2],
        summed[3],
        summed[4],
        summed[5],
        summed[6],
        summed[7],
        summed[8],
        summed[9],
        summed[10],
    )


def solution(mesh):
    in_specs = (
        P("dp", None),
        P("dp"),
        P("dp", None),
        P(),
        P(None, None, "mp"),
        P(None, "mp"),
        P("mp", None),
        P(),
        P(),
        P(),
        P(None, "mp"),
        P("mp"),
        P("mp", None),
        P(),
        P(),
    )
    out_specs = (
        P("dp", "mp"),
        P("dp"),
        P("dp", "mp"),
        P("dp", None),
        P(None, "dp", "mp"),
        P(None, ("mp", "dp")),
        P("mp", "dp"),
        P("dp"),
        P("dp"),
        P("dp"),
        P("dp", "mp"),
        P(("mp", "dp")),
        P("mp", "dp"),
        P("dp"),
        P("dp"),
    )
    groups = mesh.shape["dp"]
    fits = groups <= 16 and mesh.shape["mp"] == 2
    return jax.shard_map(
        functools.partial(per_device, groups) if fits else by_collectives,
        mesh=mesh,
        in_specs=in_specs,
        out_specs=out_specs,
        check_vma=False,
    )
```

```python
import functools
import math

import jax
import jax.numpy as jnp
from jax import lax
from jax.experimental import pallas as pl
from jax.experimental.pallas import tpu as pltpu
from jax.sharding import PartitionSpec as P

HEAD = 64
EPS = 1e-05
MASKED = -1e30
MESH = pl.DeviceIdType.MESH
BF = jnp.bfloat16
F32 = jnp.float32
MIB = 2**20


def nn(a, b):
    return jnp.dot(a, b, preferred_element_type=F32)


def nt(a, b):
    return lax.dot_general(a, b, (((1,), (1,)), ((), ())), preferred_element_type=F32)


def tn(a, b):
    return lax.dot_general(a, b, (((0,), (0,)), ((), ())), preferred_element_type=F32)


def gelu(h):
    return 0.5 * h * (1.0 + lax.erf(h * math.sqrt(0.5)))


def gelu_slope(h):
    bell = jnp.exp(-0.5 * h * h) * (1.0 / math.sqrt(2.0 * math.pi))
    return 0.5 * (1.0 + lax.erf(h * math.sqrt(0.5))) + h * bell


def row_of(vector):
    return vector[None, :].astype(F32)


def exact(a, b):
    return jnp.dot(a, b, preferred_element_type=F32, precision=lax.Precision.HIGHEST)


def one_hot(shape, shift, dtype=F32):
    row = lax.broadcasted_iota(jnp.int32, shape, 0)
    column = lax.broadcasted_iota(jnp.int32, shape, 1)
    return (row == column + shift).astype(dtype)


def standard(rows):
    center = jnp.mean(rows, axis=-1, keepdims=True)
    spread = rows - center
    second = jnp.mean(spread * spread, axis=-1, keepdims=True)
    inverse = lax.rsqrt(second + EPS)
    return spread * inverse, inverse


def norm_back(grad, scaled, inverse):
    first = jnp.mean(grad, axis=-1, keepdims=True)
    second = jnp.mean(grad * scaled, axis=-1, keepdims=True)
    return inverse * (grad - first - scaled * second)


def flip(index, bit):
    return index + bit * (1 - 2 * lax.rem(lax.div(index, bit), 2))


def mult(value, step):
    return pl.multiple_of(value, step)


def tower(
    nd,
    query_total,
    lengths,
    tokens,
    queries,
    positives,
    w_qkv,
    b_qv,
    w_out,
    b_out,
    gain_one,
    shift_one,
    w_in,
    b_in,
    w_back,
    b_back,
    gain_two,
    out_act,
    h_coef,
    h_rank,
    h_factor,
    h_active,
    h_inner,
    h_context,
    h_qcls,
    h_dctx,
    h_norm,
    h_ffn,
    h_attn,
    h_tok,
    h_sums,
    h_sums_in,
    h_loss,
    h_qgrad,
    tok,
    wq,
    wq_far,
    wo,
    wi,
    wb,
    keyb,
    valb,
    ctx,
    norm_low,
    acc,
    act_far,
    obuf,
    chance,
    factor,
    stage,
    tcls,
    pack,
    gath,
    ctx_all,
    tok_all,
    q_all,
    xh1_all,
    norm_all,
    inner_all,
    act_all,
    low_all,
    dc_all,
    qc_all,
    d1_all,
    dq_rows,
    rank_f,
    coef_own,
    coef_far,
    dq_far,
    fac_send,
    loc_sem,
    ysend,
    yrecv,
    w_send,
    w_recv,
    o_send,
    o_recv,
    o_loc,
    g_send,
    g_recv,
    gs_send,
    gs_recv,
    f_send,
    f_recv,
    m_send,
    m_recv,
    b_send,
    b_recv,
    bin_own,
    bin_far,
    out_sem,
    o_coef,
    o_rank,
    o_factor,
    o_active,
    o_inner,
    o_context,
    o_qcls,
    o_dctx,
    o_norm,
    o_ffn,
    o_attn,
    o_tok,
    o_sums,
    o_sums_in,
    o_loss,
    o_qgrad,
):
    dp = lax.axis_index("dp")
    mp = lax.axis_index("mp")
    far = 1 - mp
    chips = nd // 2
    core = lax.rem(dp, 2)
    chip = lax.div(dp, 2)
    bit_a = lax.rem(lax.div(dp, 2), 2)
    bit_b = lax.rem(lax.div(dp, 4), 2)
    quarter = bit_a + 2 * bit_b
    quarter_x = flip(quarter, 1)
    quarter_z = flip(quarter, 2)
    quarter_d = 3 - quarter
    pair = (dp, far)
    sibling = (flip(dp, 1), mp)
    near_x = (flip(dp, 2), mp)
    near_z = (flip(dp, 4), mp)

    rows, width = tok.shape
    count = lengths.shape[0]
    slot = rows // count
    own = count // 2
    half = width // 2
    own_rows = own * slot
    passages = nd * count
    blocks, unit = wi.shape[1], wi.shape[3]
    m_col = mult(mp * half, 128)
    f_col = mult(far * half, 128)

    barrier = pltpu.get_barrier_semaphore()

    def greet(i, carry):
        other = lax.rem(dp * 2 + mp + i, 2 * nd)
        pl.semaphore_signal(
            barrier,
            inc=1,
            device_id=(lax.div(other, 2), lax.rem(other, 2)),
            device_id_type=MESH,
        )
        return carry

    lax.fori_loop(1, 2 * nd, greet, 0)

    def local(src, dst, k):
        return pltpu.make_async_copy(src, dst, loc_sem.at[k])

    loads = [local(tokens, tok, 0)]
    loads += [local(w_qkv.at[j], wq.at[:, pl.ds(j * half, half)], 1 + j) for j in range(3)]
    loads.append(local(w_out, wo.at[pl.ds(mult(mp * half, 128), half), :], 4))
    loads += [
        local(w_in.at[:, pl.ds(u * unit, unit)], wi.at[mp, u], 5 + u) for u in range(blocks)
    ]
    loads += [
        local(w_back.at[pl.ds(u * unit, unit), :], wb.at[mp, u], 5 + blocks + u)
        for u in range(blocks)
    ]
    for copy in loads:
        copy.start()

    first_in = 4
    first_back = 4 + blocks
    chunks = 4 + 2 * blocks
    direct = (3, chunks - 1)

    def piece(k, q, c, which, side=None):
        if k < 3 or first_in <= k < first_back:
            size = width // 8
            at = (c * 4 if q is None else c * 4 + q) * size
            size = 4 * size if q is None else size
            if side is not None:
                size = size // 2
                at = at + side * size
            here = pl.ds(mult(at, 16), size)
            return wq_far.at[here, pl.ds(k * half, half)] if k < 3 else wi.at[which, k - 4, here, :]
        cols = pl.ds(0, width) if side is None else pl.ds(side * half, half)
        if k == 3:
            size = half // 2
            return wo.at[pl.ds(mult(which * half + c * size, 16), size), cols]
        whole = k in direct or q is None
        size = unit // 2 if whole else unit // 8
        at = c * size if whole else (c * 4 + q) * size
        return wb.at[which, k - first_back, pl.ds(mult(at, 16), size), cols]

    def sent_bytes(k):
        if k < 3:
            return wq_far.at[pl.ds(0, 7 * width // 8), pl.ds(k * half, half)]
        if k == 3:
            return piece(k, None, core, far)
        if k < first_back:
            return wi.at[far, k - 4, pl.ds(0, 7 * width // 8), :]
        return wb.at[far, k - first_back, pl.ds(0, unit // 2 if k in direct else 7 * unit // 8), :]

    def source(k):
        if k < 3 or first_in <= k < first_back:
            size = width // 8
            here = pl.ds(mult((core * 4 + quarter) * size, 16), size)
            return w_qkv.at[k, here, :] if k < 3 else w_in.at[here, pl.ds((k - 4) * unit, unit)]
        if k == 3:
            return w_out.at[pl.ds(mult(core * (half // 2), 16), half // 2), :]
        size = unit // 2 if k in direct else unit // 8
        at = core * size if k in direct else (core * 4 + quarter) * size
        return w_back.at[pl.ds(mult((k - first_back) * unit + at, 16), size), :]

    def remote(src, dst, ss, rs, device):
        return pltpu.make_async_remote_copy(
            src_ref=src,
            dst_ref=dst,
            send_sem=ss,
            recv_sem=rs,
            device_id=device,
            device_id_type=MESH,
        )

    def cross(k):
        return remote(
            source(k), piece(k, quarter, core, mp), ysend.at[k], yrecv.at[k], pair
        )

    def send(k, lane, q, c, side, device):
        ref = piece(k, q, c, far, side)
        return remote(ref, ref, w_send.at[k], w_recv.at[k, lane], device)

    def lane(k, n):
        q = (quarter, quarter, quarter_z, quarter_x, None)[n]
        side = (None, None, 0, 1, None)[n]
        return send(k, n, q, core, side, (near_x, near_z, near_x, near_z, sibling)[n])

    def arrival(k, n):
        q = (quarter_x, quarter_z, quarter_d, quarter_d, None)[n]
        side = (None, None, 0, 1, None)[n]
        c = core if n < 4 else 1 - core
        return send(k, n, q, c, side, (near_x, near_z, near_x, near_z, sibling)[n])

    def step_one(k):
        remote(
            source(k), piece(k, quarter, core, far), ysend.at[k], yrecv.at[k], pair
        ).wait_recv()
        for n in (4,) if k in direct else (0, 1):
            lane(k, n).start()

    def step_two(k):
        arrival(k, 1).wait_recv()
        lane(k, 2).start()
        arrival(k, 0).wait_recv()
        lane(k, 3).start()

    def step_three(k):
        arrival(k, 2).wait_recv()
        arrival(k, 3).wait_recv()
        lane(k, 4).start()

    def complete(k):
        arrival(k, 4).wait_recv()

    def spent(window, sem):
        pltpu.make_async_copy(window, window, sem).wait()

    def advance(*steps):
        for stage_of, k in steps:
            (step_one, step_two, step_three)[stage_of - 1](k)

    for copy in loads[:4]:
        copy.wait()
    bin_own[...] = jnp.zeros_like(bin_own)
    for u in range(blocks):
        bin_own[u : u + 1, :] = row_of(b_in[pl.ds(u * unit, unit)])
    bin_own[6:8, 0:half] = b_qv[...].astype(F32)
    bias_copy = remote(bin_own, bin_far, b_send, b_recv, pair)

    lane_pair = lax.broadcasted_iota(jnp.int32, (slot, 128), 1)
    key_place = lax.broadcasted_iota(jnp.int32, (1, slot), 1)
    head_rows = lax.broadcasted_iota(jnp.int32, (8, half), 0)
    head_mask = head_rows == lax.div(lax.broadcasted_iota(jnp.int32, (8, half), 1), HEAD)
    heads = half // HEAD
    live = lax.broadcasted_iota(jnp.int32, (8, 1), 0) < heads
    bias_q = b_qv[0:1, :].astype(F32)
    bias_v = b_qv[1:2, :].astype(F32)
    ones = jnp.ones((slot, 128), BF)
    row_place = lax.broadcasted_iota(jnp.int32, (8, slot), 0)
    first_key = (lax.broadcasted_iota(jnp.int32, (8, slot), 1) == 0).astype(F32)

    def mix(query, keyed, value, bias):
        done = []
        for t in range(half // 128):
            q2 = query[:, 128 * t : 128 * t + 128]
            k2 = keyed[:, 128 * t : 128 * t + 128]
            v2 = jnp.concatenate([value[:, 128 * t : 128 * t + 128], ones], axis=1)
            parts = []
            for hx in range(2):
                mask = (lane_pair < HEAD) if hx == 0 else (lane_pair >= HEAD)
                s = nt(jnp.where(mask, q2, jnp.zeros_like(q2)), k2) + bias
                e = jnp.exp(s - jnp.max(s, axis=1, keepdims=True)).astype(BF)
                o = nn(e, v2)
                parts.append(o[:, :128] / o[:, 128:])
            done.append(jnp.where(lane_pair < HEAD, parts[0], parts[1]))
        return jnp.concatenate(done, axis=1).astype(BF)

    def first_row(p, x, query, keyed, value, bias):
        tcls[pl.ds(p, 1), :] = x[0:16, :].astype(F32)[0:1, :]
        q_heads = jnp.where(head_mask, query.astype(F32)[0:1, :], 0.0).astype(BF)
        s = nt(q_heads, keyed) + bias
        e = jnp.exp(s - jnp.max(s, axis=1, keepdims=True))
        c = jnp.where(live, e / jnp.sum(e, axis=1, keepdims=True), 0.0)
        chance[p] = c
        c_low = c.astype(BF)
        mixed = jnp.where(head_mask, nn(c_low, value), 0.0)
        stage[pl.ds(p, 1), :] = jnp.sum(mixed, axis=0, keepdims=True)
        coef_own[pl.ds(mult(p * 16, 16), 8), :] = jnp.where(row_place == heads, first_key, c)
        factor[pl.ds(mult(p * 8, 8), 8), :] = nn(c_low, x)

    theirs_plan = (((1, 0),), (), ((1, 1),), ())
    gap_plan = (
        (1, 2), (2, 0), (1, 4), (2, 1), (2, 2), (3, 0), (2, 4), (3, 1), (1, 3), (3, 2)
    )
    far_plan = ((), ((3, 4), (1, 5)), (), ((1, 6),))
    feed_plan = (
        ((), ((2, 5), (1, 8)), (), ()),
        (((1, 7),), (), ((2, 7),), ()),
        ((), ((2, 6),), ((3, 5),), ((2, 8),)),
    )
    in_plan = ((((3, 6), (1, 9)), ((3, 7),)), ((), ()), (((3, 8),), ()))

    def move_on(i, plan):
        for j, steps in enumerate(plan):
            if steps:

                @pl.when(i == j)
                def _():
                    advance(*steps)

    def key_bias(p):
        return jnp.where(key_place < lengths[p], 0.0, MASKED)

    def attend_theirs(i, carry):
        move_on(i, theirs_plan)
        p = far * own + i
        at = mult(p * slot, slot)
        x = tok[pl.ds(at, slot), :]
        made = nn(x, wq[:, half:])
        keyed = made[:, :half].astype(BF)
        value = (made[:, half:] + bias_v).astype(BF)
        keyb[pl.ds(at, slot), :] = keyed
        valb[pl.ds(at, slot), :] = value
        query = ((nn(x[0:16, :], wq[:, :half]) + bias_q).astype(BF).astype(F32) * 0.125).astype(BF)
        first_row(p, x, query, keyed, value, key_bias(p))
        return carry

    def attend_own(i, carry):
        @pl.when(i == 1)
        def _():
            pl.semaphore_wait(barrier, 2 * nd - 1)
            for k in (0, 1, 2, 4, 3, 5):
                cross(k).start()
            bias_copy.start()

        p = mp * own + i
        at = mult(p * slot, slot)
        x = tok[pl.ds(at, slot), :]
        made = nn(x, wq[...])
        query = ((made[:, :half] + bias_q).astype(BF).astype(F32) * 0.125).astype(BF)
        keyed = made[:, half : 2 * half].astype(BF)
        value = (made[:, 2 * half :] + bias_v).astype(BF)
        keyb[pl.ds(at, slot), :] = keyed
        valb[pl.ds(at, slot), :] = value
        bias = key_bias(p)
        ctx[pl.ds(mult(i * slot, slot), slot), pl.ds(m_col, half)] = mix(query, keyed, value, bias)
        first_row(p, x, query[0:16, :], keyed, value, bias)
        return carry

    def attend_far(i, carry):
        move_on(i, far_plan)
        p = mp * own + i
        x = tok[pl.ds(mult(p * slot, slot), slot), :]
        made = nn(x, wq_far[...])
        bias_far = bin_far[6:8, 0:half]
        query = ((made[:, :half] + bias_far[0:1, :]).astype(BF).astype(F32) * 0.125).astype(BF)
        keyed = made[:, half : 2 * half].astype(BF)
        value = (made[:, 2 * half :] + bias_far[1:2, :]).astype(BF)
        ctx[pl.ds(mult(i * slot, slot), slot), pl.ds(f_col, half)] = mix(
            query, keyed, value, key_bias(p)
        )
        return carry

    lax.fori_loop(0, own, attend_own, 0)
    lax.fori_loop(0, own, attend_theirs, 0)

    pack[0:8, :] = stage[...]
    pack[8:16, :] = tcls[:, pl.ds(m_col, half)]
    pack[16:32, :] = jnp.zeros((16, half), F32)
    q_rows = queries.shape[0]
    pack[16 : 16 + q_rows, :] = queries[:, pl.ds(m_col, half)].astype(F32)
    gath[chip, core, mp] = pack[...].astype(BF)

    here = gath.at[chip, core, mp]
    to_pair = remote(here, here, gs_send.at[0], gs_recv.at[0], pair)
    to_pair.start()
    advance(*gap_plan)
    bias_copy.wait_recv()
    for k in range(3):
        complete(k)
    remote(
        here, gath.at[chip, core, far], gs_send.at[0], gs_recv.at[0], pair
    ).wait_recv()

    def gather_start(i, carry):
        both = gath.at[chip, core]
        there = lax.rem(chip + i, chips) * 2 + core
        remote(both, both, g_send, g_recv, (there, mp)).start()
        return carry

    lax.fori_loop(1, chips, gather_start, 0)
    gather_window = tok.at[pl.ds(0, (chips - 1) * 32), :]
    for k in range(6, chunks):
        cross(k).start()

    lax.fori_loop(0, own, attend_far, 0)

    for copy in loads[4:]:
        copy.wait()
    complete(3)
    bo = row_of(b_out[...])
    g1 = row_of(gain_one[...])
    s1 = row_of(shift_one[...])
    g2 = row_of(gain_two[...])
    bb = row_of(b_back[...])

    def feed_own(i, carry):
        move_on(i, feed_plan[0])
        at = mult(i * slot, slot)
        here = pl.ds(at, slot)
        x = tok[pl.ds(mult(mp * own_rows + i * slot, slot), slot), :].astype(F32)
        resid = x + nn(ctx[here, :], wo[...]) + bo
        scaled, _ = standard(resid)
        norm = scaled * g1 + s1
        low = norm.astype(BF)
        norm_low[here, :] = low
        total = norm + bb
        for u in range(blocks):
            if u > 0:
                move_on(i, feed_plan[u])
            inner = nn(low, wi[mp, u]) + bin_own[u : u + 1, :]
            total = total + nn(gelu(inner).astype(BF), wb[mp, u])
        acc[here, :] = total

        return carry

    lax.fori_loop(0, own, feed_own, 0)

    for u in range(blocks):
        complete(first_in + u)

        def feed_far_in(i, carry, u=u):
            move_on(i, in_plan[u])
            here = pl.ds(mult(i * 2 * slot, slot), 2 * slot)
            inner = nn(norm_low[here, :], wi[far, u]) + bin_far[u : u + 1, :]
            act_far[u, here, :] = gelu(inner).astype(BF)
            return carry

        lax.fori_loop(0, own // 2, feed_far_in, 0)

    spent(gather_window, g_recv)
    to_sibling = remote(
        gath.at[:, core], gath.at[:, core], gs_send.at[1], gs_recv.at[1], sibling
    )
    to_sibling.start()

    def feed_far_back(u):
        def feed(i, carry):
            here = pl.ds(mult(i * 2 * slot, slot), 2 * slot)
            acc[here, :] += nn(act_far[u, here, :], wb[far, u])
            return carry

        lax.fori_loop(0, own // 2, feed, 0)

    complete(first_back)
    feed_far_back(0)

    remote(
        gath.at[:, 1 - core], gath.at[:, 1 - core], gs_send.at[1], gs_recv.at[1], sibling
    ).wait_recv()
    q_pad = nd * 16
    for h in range(2):
        cols = slice(h * half, (h + 1) * half)
        block = gath[:, :, h].astype(F32)
        ctx_all[:, cols] = block[:, :, 0:8].reshape(passages, half).astype(BF)
        tok_all[:, cols] = block[:, :, 8:16].reshape(passages, half).astype(BF)
        q_all[:, cols] = block[:, :, 16:32].reshape(q_pad, half).astype(BF)
    resid = tok_all[...].astype(F32) + nn(ctx_all[...], wo[...]) + bo
    scaled, inverse1 = standard(resid)
    xh1_all[...] = scaled
    norm = scaled * g1 + s1
    low = norm.astype(BF)
    norm_all[...] = low
    total = norm + bb
    for which, bias in ((mp, bin_own), (far, bin_far)):
        for u in range(blocks):
            inner = nn(low, wi[which, u]) + bias[u : u + 1, :]
            inner_all[which, u] = inner
            active = gelu(inner).astype(BF)
            act_all[which, u] = active
    for u in range(blocks):
        total = total + nn(act_all[mp, u], wb[mp, u])
    total = total + nn(act_all[far, 0], wb[far, 0])
    for u in range(1, blocks - 1):
        complete(first_back + u)
        feed_far_back(u)
        total = total + nn(act_all[far, u], wb[far, u])
    complete(chunks - 1)

    def out_copy(i, mine):
        side = mp if mine else far
        there = out_act.at[pl.ds(mult(side * own_rows + i * slot, 16), slot), :]
        return remote(
            obuf.at[1, pl.ds(mult(i * slot, 16), slot), :], there, o_send.at[i], o_recv.at[i], pair
        )

    def out_local(i):
        there = out_act.at[pl.ds(mult(mp * own_rows + i * slot, 16), slot), :]
        return pltpu.make_async_copy(
            obuf.at[0, pl.ds(mult(i * slot, 16), slot), :], there, o_loc.at[i]
        )

    def finish(i, carry):
        here = pl.ds(mult(i * slot, slot), slot)
        total = acc[here, :] + nn(act_far[blocks - 1, here, :], wb[far, blocks - 1])
        scaled, _ = standard(total)
        acc[here, :] = scaled * g2
        obuf[0, here, :] = acc[here, pl.ds(m_col, half)].astype(BF)
        obuf[1, here, :] = acc[here, pl.ds(f_col, half)].astype(BF)
        @pl.when(i < own - 1)
        def _():
            out_copy(i, True).start()

        out_local(i).start()
        return carry

    lax.fori_loop(0, own, finish, 0)

    total = total + nn(act_all[far, blocks - 1], wb[far, blocks - 1])
    xh2, inverse2 = standard(total)
    cls = (xh2 * g2).astype(BF)
    similar = nt(cls, q_all[...])
    top = jnp.max(similar, axis=0, keepdims=True)
    log_sum = top + jnp.log(jnp.sum(jnp.exp(similar - top), axis=0, keepdims=True))
    q_count = query_total // nd
    from_q = lax.broadcasted_iota(jnp.int32, (query_total, q_pad), 0)
    to_q = lax.broadcasted_iota(jnp.int32, (query_total, q_pad), 1)
    spot = lax.div(from_q, q_count) * 16 + lax.rem(from_q, q_count)
    wanted = jnp.broadcast_to(row_of(positives[...]), (8, query_total)) + 1.0
    place = exact(wanted, (spot == to_q).astype(F32))[0:1, :] - 1.0
    target = lax.broadcasted_iota(jnp.int32, similar.shape, 0).astype(F32) == place
    picked = jnp.sum(jnp.where(target, similar, 0.0), axis=0, keepdims=True)
    o_loss[...] = jnp.broadcast_to(log_sum - picked, o_loss.shape)
    slopes = (jnp.exp(similar - log_sum) - target.astype(F32)) * (1.0 / query_total)
    slope_high = slopes.astype(BF)
    slope_low = (slopes - slope_high.astype(F32)).astype(BF)
    cls_grad = nn(slope_high, q_all[...]) + nn(slope_low, q_all[...])
    pick = (
        lax.broadcasted_iota(jnp.int32, (16, q_pad), 1)
        == lax.broadcasted_iota(jnp.int32, (16, q_pad), 0) + dp * 16
    ).astype(BF)
    o_qgrad[...] = nn(nt(pick, slope_high).astype(BF), cls) + nn(
        nt(pick, slope_low).astype(BF), cls
    )
    d_two = norm_back(g2 * cls_grad, xh2, inverse2)
    o_sums[0:1, :] = jnp.sum(cls_grad * xh2, axis=0, keepdims=True)
    o_sums[1:2, :] = jnp.sum(d_two, axis=0, keepdims=True)
    ffn_low = d_two.astype(BF)
    o_ffn[...] = ffn_low
    back = d_two
    for h in range(2):
        for u in range(blocks):
            d_active = nt(ffn_low, wb[h, u])
            d_inner = d_active * gelu_slope(inner_all[h, u])
            inner_all[h, u, 0:8, :] = jnp.broadcast_to(
                jnp.sum(d_inner, axis=0, keepdims=True), (8, unit)
            )
            inner_low = d_inner.astype(BF)
            low_all[h, u] = inner_low
            back = back + nt(inner_low, wi[h, u])
    for u in range(blocks):
        o_active[u] = act_all[mp, u]
        o_inner[u] = low_all[mp, u]
        o_sums_in[u : u + 1, :] = inner_all[mp, u, 0:1, :]
    xh1 = xh1_all[...]
    d_one = norm_back(g1 * back, xh1, inverse1)
    d1_all[...] = d_one
    o_sums[2:3, :] = jnp.sum(back * xh1, axis=0, keepdims=True)
    o_sums[3:4, :] = jnp.sum(back, axis=0, keepdims=True)
    o_sums[4:5, :] = jnp.sum(d_one, axis=0, keepdims=True)
    attn_low = d_one.astype(BF)
    o_attn[...] = attn_low
    o_norm[...] = norm_all[...]
    o_tok[...] = tok_all[...]
    d_ctx = nt(attn_low, wo[pl.ds(mult(mp * half, 128), half), :]).astype(BF)
    o_dctx[...] = d_ctx
    dc_all[...] = d_ctx.astype(F32)
    q_cls = (nn(tok_all[...], wq[:, 0:half]) + bias_q).astype(BF)
    o_qcls[...] = q_cls
    qc_all[...] = q_cls.astype(F32) * 0.125
    o_context[...] = ctx_all[:, pl.ds(m_col, half)]
    o_sums[5:6, 0:half] = jnp.sum(dc_all[...], axis=0, keepdims=True)

    def stored(src, dst, k):
        return pltpu.make_async_copy(src, dst, out_sem.at[k])

    early = [
        stored(src, dst, k)
        for k, (src, dst) in enumerate(
            (
                (o_active, h_active),
                (o_inner, h_inner),
                (o_context, h_context),
                (o_qcls, h_qcls),
                (o_dctx, h_dctx),
                (o_norm, h_norm),
                (o_ffn, h_ffn),
                (o_attn, h_attn),
                (o_tok, h_tok),
                (o_sums, h_sums),
                (o_sums_in, h_sums_in),
                (o_loss, h_loss),
                (o_qgrad, h_qgrad),
            )
        )
    ]
    for copy in early:
        copy.start()

    base = mult(dp * count, 8)
    fkind = count * 8

    mark = jnp.logical_or(row_place == heads, row_place == heads + 1)
    for p in range(count):
        d_row = dc_all[pl.ds(base + p, 1), :]
        q_row = qc_all[pl.ds(base + p, 1), :]
        rank_f[p * 16 : p * 16 + 8, 0:half] = jnp.where(head_mask, d_row, 0.0)
        rank_f[p * 16 + 8 : p * 16 + 16, 0:half] = jnp.where(head_mask, q_row, 0.0)
    kept = rank_f[:, 0:half].astype(BF)
    group = 4
    for first in range(0, count, group):
        d_scores = []
        for p in range(first, first + group):
            c = chance[p]
            d_chance = nt(kept[p * 16 : p * 16 + 16, :], valb[p * slot : (p + 1) * slot, :])[0:8, :]
            d_scores.append(c * (d_chance - jnp.sum(c * d_chance, axis=1, keepdims=True)))
        for p, d in zip(range(first, first + group), d_scores):
            s_low = d.astype(BF)
            at = slice(p * slot, (p + 1) * slot)
            coef_own[p * 16 + 8 : p * 16 + 16, :] = jnp.where(mark, first_key, d)
            factor[fkind + p * 8 : fkind + p * 8 + 8, :] = nn(s_low, tok[at, :])
            spread = nn(s_low, keyb[at, :])
            dq_rows[p : p + 1, :] = 0.125 * jnp.sum(
                jnp.where(head_mask, spread, 0.0), axis=0, keepdims=True
            )

    turned = jnp.transpose(factor[...]).astype(BF)
    dq = dq_rows[...]
    for b in range(half // 128):
        pack[b * 8 : b * 8 + 8, 0:128] = dq[:, b * 128 : b * 128 + 128]
    pack[half // 16 : 32, 0:128] = jnp.zeros((32 - half // 16, 128), F32)
    dq_low = pack[:, 0:128].astype(BF)
    share = width // nd
    for j in range(nd):
        fac_send[j, 0:share, :] = turned[j * share : (j + 1) * share, :]
        fac_send[j, share:, :] = dq_low
    o_factor[dp] = fac_send[dp]

    def factor_start(i, carry):
        there = lax.rem(dp + i, nd)
        remote(fac_send.at[there], o_factor.at[dp], f_send, f_recv, (there, mp)).start()
        return carry

    lax.fori_loop(1, nd, factor_start, 0)

    coef_low = coef_own[...].astype(BF)
    o_coef[0] = coef_low
    coef_far_copy = remote(o_coef.at[0], coef_far, m_send.at[0], m_recv.at[0], pair)
    coef_far_copy.start()
    dq_copy = remote(dq_rows, dq_far, m_send.at[1], m_recv.at[1], pair)
    dq_copy.start()
    out_copy(own - 1, True).start()
    kind = lax.rem(lax.div(lax.broadcasted_iota(jnp.int32, (count * 16, 1), 0), 8), 2)
    d1_rows = d1_all[pl.ds(base, count), :]
    d_far = nt(d1_rows.astype(BF), wo[pl.ds(mult(far * half, 128), half), :])
    q_far = (nn(tcls[...].astype(BF), wq_far[:, 0:half]) + bin_far[6:7, 0:half]) * 0.125
    for p in range(count):
        rank_f[p * 16 : p * 16 + 8, 0:half] = jnp.where(head_mask, d_far[p : p + 1, :], 0.0)
        rank_f[p * 16 + 8 : p * 16 + 16, 0:half] = jnp.where(head_mask, q_far[p : p + 1, :], 0.0)
    kept_far = rank_f[:, 0:half].astype(BF)
    my_rows = pl.ds(mult(mp * half, 128), half)

    def rank_rows(left, right):
        by_v = nt(left, right[my_rows, 2 * half :])
        by_k = nt(left, right[my_rows, half : 2 * half])
        return jnp.where(kind == 0, by_v, by_k)

    rank_f[:, 0:half] = rank_rows(kept, wq)
    rank_f[:, half:] = rank_rows(kept_far, wq_far)
    d1_mine = d1_all[pl.ds(base, count), pl.ds(m_col, half)]
    d1_high = d1_mine.astype(BF).astype(F32)
    d1_low = d1_mine - d1_high

    def first_rank(cols, back_q, high, low):
        for p in range(count):
            rank_f[p * 16 + heads : p * 16 + heads + 1, cols] = back_q[p : p + 1, :]
            rank_f[p * 16 + heads + 1 : p * 16 + 8, cols] = jnp.zeros((7 - heads, half), F32)
            rank_f[p * 16 + 8 + heads : p * 16 + 9 + heads, cols] = high[p : p + 1]
            rank_f[p * 16 + 9 + heads : p * 16 + 10 + heads, cols] = low[p : p + 1]

    mine = slice(0, half)
    theirs = slice(half, width)
    first_rank(mine, nt(dq.astype(BF), wq[my_rows, 0:half]), d1_high, d1_low)
    o_rank[0] = rank_f[:, mine].astype(BF)

    dq_copy.wait_recv()
    nothing = jnp.zeros((count, half), F32)
    first_rank(theirs, nt(dq_far[...].astype(BF), wq_far[my_rows, 0:half]), nothing, nothing)
    o_rank[1] = rank_f[:, theirs].astype(BF)
    coef_far_copy.wait_recv()
    o_coef[1] = coef_far[...]
    factor_window = fac_send.at[pl.ds(0, nd - 1)]
    spent(factor_window, f_recv)
    last = [stored(o_factor, h_factor, 15), stored(o_coef, h_coef, 13), stored(o_rank, h_rank, 14)]
    for copy in last:
        copy.start()
    spent(factor_window, f_send)
    coef_far_copy.wait_send()
    dq_copy.wait_send()
    bias_copy.wait_send()
    spent(gather_window, g_send)
    to_sibling.wait_send()
    to_pair.wait_send()
    for k in range(chunks):
        cross(k).wait_send()
        spent(sent_bytes(k), w_send.at[k])

    def drain(i, carry):
        out_copy(i, True).wait_send()
        out_copy(i, False).wait_recv()
        out_local(i).wait()
        return carry

    lax.fori_loop(0, own, drain, 0)
    for copy in early + last:
        copy.wait()


def gradients(
    nd,
    act_in,
    coef_in,
    rank_in,
    factor_in,
    active_in,
    inner_in,
    context_in,
    qcls_in,
    dctx_in,
    norm_in,
    ffn_in,
    attn_in,
    tok_in,
    sums_in,
    sums_units_in,
    loss_in,
    qgrad_in,
    act_out,
    query_loss,
    input_grad,
    query_grad,
    grad_qkv,
    grad_bias_qv,
    grad_out,
    grad_bias_out,
    grad_gain_one,
    grad_shift_one,
    grad_in,
    grad_bias_in,
    grad_back,
    grad_bias_back,
    grad_gain_two,
    coef,
    rank,
    factor,
    active,
    inner,
    context,
    qcls,
    dctx,
    norm,
    ffn,
    attn,
    tok,
    sums,
    sums_units,
    loss,
    qgrad,
    sems,
    act_sem,
    act_buf,
    in_buf,
    in_sems,
    rhs,
):
    dp = lax.axis_index("dp")
    act_load = pltpu.make_async_copy(act_in, act_buf, act_sem.at[0])
    act_store = pltpu.make_async_copy(act_buf, act_out, act_sem.at[1])
    act_load.start()
    pairs = (
        (coef_in, coef),
        (rank_in, rank),
        (factor_in, factor),
        (qcls_in, qcls),
        (dctx_in, dctx),
        (active_in, active),
        (inner_in, inner),
        (context_in, context),
        (norm_in, norm),
        (ffn_in, ffn),
        (attn_in, attn),
        (tok_in, tok),
        (sums_in, sums),
        (sums_units_in, sums_units),
        (loss_in, loss),
        (qgrad_in, qgrad),
    )
    loads = [pltpu.make_async_copy(src, dst, sems.at[i]) for i, (src, dst) in enumerate(pairs)]
    for load in loads:
        load.start()
    passages, width = ffn.shape
    half = width // 2
    share = width // nd
    count = passages // nd
    slot = coef.shape[2]
    for load in loads[:2]:
        load.wait()

    def input_copy(p):
        at = pl.ds(mult(p * slot, slot), slot)
        return pltpu.make_async_copy(in_buf.at[at, :], input_grad.at[at, :], in_sems.at[p])

    def input_rows(p, carry):
        rows16 = pl.ds(mult(p * 16, 16), 16)
        both = jnp.concatenate([coef[0, rows16, :], coef[1, rows16, :]], axis=0)
        right = jnp.concatenate([rank[0, rows16, :], rank[1, rows16, :]], axis=0)
        in_buf[pl.ds(mult(p * slot, slot), slot), :] = tn(both, right)
        input_copy(p).start()
        return carry

    lax.fori_loop(0, count, input_rows, 0)
    act_load.wait()
    act_store.start()
    for load in loads[2:]:
        load.wait()

    spread = lax.broadcasted_iota(jnp.int32, (8, half), 0) == lax.div(
        lax.broadcasted_iota(jnp.int32, (8, half), 1), HEAD
    )
    fkind = count * 8

    def build(s, carry):
        d_rows = dctx[pl.ds(mult(s * 2 * count, 16), 2 * count), :].astype(F32)
        q_rows = qcls[pl.ds(mult(s * 2 * count, 16), 2 * count), :].astype(F32) * 0.125
        k_blocks = [jnp.where(spread, q_rows[p : p + 1, :], 0.0) for p in range(2 * count)]
        v_blocks = [jnp.where(spread, d_rows[p : p + 1, :], 0.0) for p in range(2 * count)]
        here = pl.ds(mult(s * 2 * fkind, 16), 2 * fkind)
        rhs[here, 0:half] = jnp.concatenate(k_blocks, 0).astype(BF)
        rhs[here, half:] = jnp.concatenate(v_blocks, 0).astype(BF)
        return carry

    lax.fori_loop(0, nd // 2, build, 0)
    grad_k = jnp.zeros((share, half), F32)
    grad_v = jnp.zeros((share, half), F32)
    for s in range(0, nd, 4):
        left_v = jnp.concatenate([factor[s + t, 0:share, :][:, 0:fkind] for t in range(4)], axis=1)
        left_k = jnp.concatenate([factor[s + t, 0:share, :][:, fkind:] for t in range(4)], axis=1)
        grad_k = grad_k + nn(left_k, rhs[s * fkind : (s + 4) * fkind, 0:half])
        grad_v = grad_v + nn(left_v, rhs[s * fkind : (s + 4) * fkind, half:])
    grad_qkv[1] = grad_k
    grad_qkv[2] = grad_v

    pick = one_hot((width, share), dp * share)
    pick_low = pick.astype(BF)
    row = lax.broadcasted_iota(jnp.int32, (share, width), 0)
    column = lax.broadcasted_iota(jnp.int32, (share, width), 1)
    pick_t = (column == row + dp * share).astype(BF)
    ffn_own = nt(pick_t, ffn[...]).astype(BF)
    attn_own = nt(pick_t, attn[...]).astype(BF)
    norm_own = nt(pick_t, norm[...]).astype(BF)
    tok_own = nt(pick_t, tok[...]).astype(BF)
    grad_out[...] = nn(attn_own, context[...])
    unit = active.shape[2]
    blocks = active.shape[0]
    for u in range(blocks):
        cols = slice(u * unit, (u + 1) * unit)
        grad_back[:, cols] = nn(ffn_own, active[u])
        grad_in[:, cols] = nn(norm_own, inner[u])
    dq_sum = []
    for b in range(half // 128):
        cols = factor[:, share:, :].astype(F32)[:, b * 8 : b * 8 + 8, :].reshape(passages, 128)
        dq_sum.append(jnp.sum(cols, axis=0, keepdims=True))
        grad_qkv[0, :, b * 128 : b * 128 + 128] = nn(tok_own, cols.astype(BF))

    mine = exact(sums[...], pick)
    grad_gain_two[...] = mine[0:1, :].reshape(share)
    grad_bias_back[...] = mine[1:2, :].reshape(share)
    grad_gain_one[...] = mine[2:3, :].reshape(share)
    grad_shift_one[...] = mine[3:4, :].reshape(share)
    grad_bias_out[...] = mine[4:5, :].reshape(share)
    part = half // nd
    both = jnp.concatenate([jnp.concatenate(dq_sum, axis=1), sums[5:6, 0:half]], axis=0)
    wide = jnp.concatenate([both, jnp.zeros((6, half), F32)], axis=0)
    grad_bias_qv[...] = exact(wide, one_hot((half, part), dp * part))[0:2, :]
    in_share = grad_bias_in.shape[0]
    total = jnp.zeros((8, in_share), F32)
    for u in range(blocks):
        total = total + exact(
            jnp.broadcast_to(sums_units[u : u + 1, :], (8, unit)),
            one_hot((unit, in_share), dp * in_share - u * unit),
        )
    grad_bias_in[...] = total[0:1, :].reshape(in_share)
    q_rows = query_loss.shape[0]
    query_loss[...] = exact(loss[...], one_hot((loss.shape[1], q_rows), dp * 16))[0:1, :].reshape(q_rows)
    query_grad[...] = qgrad[0:q_rows, :]

    def input_wait(p, carry):
        input_copy(p).wait()
        return carry

    lax.fori_loop(0, count, input_wait, 0)
    act_store.wait()


def per_device(nd, *arrays):
    (
        tokens,
        lengths,
        queries,
        positives,
        w_qkv,
        b_qv,
        w_out,
        b_out,
        gain_one,
        shift_one,
        w_in,
        b_in,
        w_back,
        b_back,
        gain_two,
    ) = arrays
    rows, width = tokens.shape
    count = lengths.shape[0]
    slot = rows // count
    half = w_qkv.shape[2]
    units = w_in.shape[1]
    unit = 512
    blocks = units // unit
    chunks = 4 + 2 * blocks
    own_rows = rows // 2
    passages = nd * count
    chips = nd // 2
    q_rows = queries.shape[0]
    q_pad = nd * 16
    share = width // nd
    vmem = pl.BlockSpec(memory_space=pltpu.VMEM)
    hbm = pl.BlockSpec(memory_space=pl.ANY)
    smem = pl.BlockSpec(memory_space=pltpu.SMEM)
    in_specs = [smem, hbm, vmem, vmem, hbm, vmem, hbm, vmem, vmem, vmem, hbm, vmem, hbm, vmem, vmem]
    shape = jax.ShapeDtypeStruct
    outs = [
        (shape((rows, half), BF), hbm),
        (shape((2, count * 16, slot), BF), hbm),
        (shape((2, count * 16, half), BF), hbm),
        (shape((nd, share + 32, 128), BF), hbm),
        (shape((blocks, passages, unit), BF), hbm),
        (shape((blocks, passages, unit), BF), hbm),
        (shape((passages, half), BF), hbm),
        (shape((passages, half), BF), hbm),
        (shape((passages, half), BF), hbm),
        (shape((passages, width), BF), hbm),
        (shape((passages, width), BF), hbm),
        (shape((passages, width), BF), hbm),
        (shape((passages, width), BF), hbm),
        (shape((8, width), F32), hbm),
        (shape((8, unit), F32), hbm),
        (shape((8, q_pad), F32), hbm),
        (shape((16, width), F32), hbm),
    ]
    dma = pltpu.SemaphoreType.DMA
    scratch = [
        pltpu.VMEM((rows, width), BF),
        pltpu.VMEM((width, 3 * half), BF),
        pltpu.VMEM((width, 3 * half), BF),
        pltpu.VMEM((width, width), BF),
        pltpu.VMEM((2, blocks, width, unit), BF),
        pltpu.VMEM((2, blocks, unit, width), BF),
        pltpu.VMEM((rows, half), BF),
        pltpu.VMEM((rows, half), BF),
        pltpu.VMEM((own_rows, width), BF),
        pltpu.VMEM((own_rows, width), BF),
        pltpu.VMEM((own_rows, width), F32),
        pltpu.VMEM((blocks, own_rows, unit), BF),
        pltpu.VMEM((2, own_rows, half), BF),
        pltpu.VMEM((count, 8, slot), F32),
        pltpu.VMEM((2 * count * 8, width), F32),
        pltpu.VMEM((8, half), F32),
        pltpu.VMEM((8, width), F32),
        pltpu.VMEM((32, half), F32),
        pltpu.VMEM((chips, 2, 2, 32, half), BF),
        pltpu.VMEM((passages, width), BF),
        pltpu.VMEM((passages, width), BF),
        pltpu.VMEM((q_pad, width), BF),
        pltpu.VMEM((passages, width), F32),
        pltpu.VMEM((passages, width), BF),
        pltpu.VMEM((2, blocks, passages, unit), F32),
        pltpu.VMEM((2, blocks, passages, unit), BF),
        pltpu.VMEM((2, blocks, passages, unit), BF),
        pltpu.VMEM((passages, half), F32),
        pltpu.VMEM((passages, half), F32),
        pltpu.VMEM((passages, width), F32),
        pltpu.VMEM((8, half), F32),
        pltpu.VMEM((count * 16, width), F32),
        pltpu.VMEM((count * 16, slot), F32),
        pltpu.VMEM((count * 16, slot), BF),
        pltpu.VMEM((count, half), F32),
        pltpu.VMEM((nd, share + 32, 128), BF),
        dma((5 + 2 * blocks,)),
        dma((chunks,)),
        dma((chunks,)),
        dma((chunks,)),
        dma((chunks, 5)),
        dma((count // 2,)),
        dma((count // 2,)),
        dma((count // 2,)),
        dma,
        dma,
        dma((2,)),
        dma((2,)),
        dma,
        dma,
        dma((2,)),
        dma((2,)),
        dma,
        dma,
        pltpu.VMEM((8, unit), F32),
        pltpu.VMEM((8, unit), F32),
        dma((16,)),
    ] + [pltpu.VMEM(o[0].shape, o[0].dtype) for o in outs[1:]]
    made = pl.pallas_call(
        functools.partial(tower, nd, nd * q_rows),
        out_shape=[o[0] for o in outs],
        in_specs=in_specs,
        out_specs=[o[1] for o in outs],
        scratch_shapes=scratch,
        compiler_params=pltpu.CompilerParams(
            collective_id=0, has_side_effects=True, vmem_limit_bytes=60 * MIB
        ),
        name="tower",
    )(
        lengths,
        tokens,
        queries,
        positives,
        w_qkv,
        b_qv,
        w_out,
        b_out,
        gain_one,
        shift_one,
        w_in,
        b_in,
        w_back,
        b_back,
        gain_two,
    )
    g_outs = [
        (shape((rows, half), BF), hbm),
        (shape((q_rows,), F32), vmem),
        (shape((rows, half), F32), hbm),
        (shape((q_rows, width), F32), vmem),
        (shape((3, share, half), F32), vmem),
        (shape((2, half // nd), F32), vmem),
        (shape((share, half), F32), vmem),
        (shape((share,), F32), vmem),
        (shape((share,), F32), vmem),
        (shape((share,), F32), vmem),
        (shape((share, units), F32), vmem),
        (shape((units // nd,), F32), vmem),
        (shape((share, units), F32), vmem),
        (shape((share,), F32), vmem),
        (shape((share,), F32), vmem),
    ]
    grads = pl.pallas_call(
        functools.partial(gradients, nd),
        out_shape=[o[0] for o in g_outs],
        in_specs=[hbm] * len(outs),
        out_specs=[o[1] for o in g_outs],
        scratch_shapes=[pltpu.VMEM(o[0].shape, o[0].dtype) for o in outs[1:]]
        + [
            dma((len(outs) - 1,)),
            dma((2,)),
            pltpu.VMEM((rows, half), BF),
            pltpu.VMEM((rows, half), F32),
            dma((count,)),
            pltpu.VMEM((nd * count * 8, width), BF),
        ],
        compiler_params=pltpu.CompilerParams(vmem_limit_bytes=62 * MIB),
        name="gradients",
    )(*made)
    grads = list(grads)
    grads[6] = grads[6].T
    grads[12] = grads[12].T
    return tuple(grads)


def layer_norm(rows, gain, shift):
    center = jnp.mean(rows, axis=-1, keepdims=True)
    spread = rows - center
    second = jnp.mean(spread * spread, axis=-1, keepdims=True)
    return spread * lax.rsqrt(second + EPS) * gain + shift


def scaled_norm(rows, gain):
    center = jnp.mean(rows, axis=-1, keepdims=True)
    spread = rows - center
    second = jnp.mean(spread * spread, axis=-1, keepdims=True)
    return spread * lax.rsqrt(second + EPS) * gain


def gelu_exact(values):
    return jax.nn.gelu(values, approximate=False)


def first_rows(values, count):
    return values.reshape((count, values.shape[0] // count) + values.shape[1:])[:, 0]


def by_collectives(
    tokens,
    lengths,
    queries,
    positives,
    w_qkv,
    b_qv,
    w_out,
    b_out,
    gain_one,
    shift_one,
    w_in,
    b_in,
    w_back,
    b_back,
    gain_two,
):
    rows, width = tokens.shape
    count = lengths.shape[0]
    slot = rows // count
    local = w_qkv.shape[2]
    heads_here = local // HEAD
    scale = 1.0 / math.sqrt(HEAD)
    projected = jnp.einsum("rd,jdc->jrc", tokens, w_qkv, preferred_element_type=F32)
    bias_qv = b_qv.astype(F32)
    query = (projected[0] + bias_qv[0]).astype(BF)
    keyed = projected[1].astype(BF)
    value = (projected[2] + bias_qv[1]).astype(BF)
    block = min(count, max(1, 512 // slot))
    blocks = count // block
    valid = lax.broadcasted_iota(jnp.int32, (count, slot), 1) < lengths[:, None]
    split_shape = (blocks, block, slot, heads_here, HEAD)

    def attend(inputs):
        query_part, keyed_part, value_part, valid_part = inputs
        scores = (
            jnp.einsum(
                "pqhd,pkhd->phqk", query_part, keyed_part, preferred_element_type=F32
            )
            * scale
        )
        scores = jnp.where(valid_part[:, None, None, :], scores, MASKED)
        top = jnp.max(scores, axis=-1, keepdims=True)
        raised = jnp.exp(scores - top)
        total = jnp.sum(raised, axis=-1, keepdims=True)
        chance_low = (raised / total).astype(BF)
        mixed = jnp.einsum(
            "phqk,pkhd->pqhd", chance_low, value_part, preferred_element_type=F32
        )
        return (mixed.astype(BF), (top + jnp.log(total))[:, :, 0, 0])

    context, log_total = lax.map(
        attend,
        (
            query.reshape(split_shape),
            keyed.reshape(split_shape),
            value.reshape(split_shape),
            valid.reshape(blocks, block, slot),
        ),
    )
    context = context.reshape(rows, local)
    log_total = log_total.reshape(count, heads_here)
    partial_attn = jnp.dot(context, w_out, preferred_element_type=F32).astype(BF)
    attended = lax.psum(partial_attn, "mp").astype(F32) + b_out.astype(F32)
    resid_one = tokens.astype(F32) + attended
    gain_one_w = gain_one.astype(F32)
    shift_one_w = shift_one.astype(F32)
    gain_two_w = gain_two.astype(F32)
    norm_one = layer_norm(resid_one, gain_one_w, shift_one_w)
    norm_low = norm_one.astype(BF)
    inner = jnp.dot(norm_low, w_in, preferred_element_type=F32) + b_in.astype(F32)
    active = gelu_exact(inner).astype(BF)
    partial_ffn = jnp.dot(active, w_back, preferred_element_type=F32).astype(BF)
    resid_two = (
        norm_one + lax.psum(partial_ffn, "mp").astype(F32) + b_back.astype(F32)
    )
    output = scaled_norm(resid_two, gain_two_w)
    column = lax.axis_index("mp") * local
    activations = lax.dynamic_slice_in_dim(output, column, local, 1).astype(BF)
    cls_low = first_rows(output, count).astype(BF)
    query_rows = queries.shape[0]
    members = lax.axis_size("dp")
    query_total = query_rows * members
    own_query = lax.axis_index("dp") * query_rows
    gathered = lax.all_gather(cls_low, "dp", axis=0, tiled=True)
    similar = jnp.einsum("qd,pd->qp", queries, gathered, preferred_element_type=F32)
    mine = lax.dynamic_slice_in_dim(positives, own_query, query_rows)
    target = lax.broadcasted_iota(jnp.int32, similar.shape, 1) == mine[:, None]
    top = jnp.max(similar, axis=1, keepdims=True)
    log_sum = top[:, 0] + jnp.log(jnp.sum(jnp.exp(similar - top), axis=1))
    picked = jnp.sum(jnp.where(target, similar, 0.0), axis=1)
    query_loss = log_sum - picked
    slopes = (jnp.exp(similar - log_sum[:, None]) - target.astype(F32)) / query_total
    query_grad = jnp.dot(slopes, gathered.astype(F32), precision=lax.Precision.HIGHEST)
    queries_wide = queries.astype(F32)
    cls_grad = lax.psum_scatter(
        jnp.einsum("qp,qd->pd", slopes, queries_wide, precision=lax.Precision.HIGHEST),
        "dp",
        scatter_dimension=0,
        tiled=True,
    )
    _, norm_two_pull = jax.vjp(scaled_norm, first_rows(resid_two, count), gain_two_w)
    d_resid_two, grad_gain_two = norm_two_pull(cls_grad)
    grad_bias_back = jnp.sum(d_resid_two, axis=0)
    ffn_low = d_resid_two.astype(BF)
    grad_back = jnp.einsum(
        "pf,pd->fd", first_rows(active, count), ffn_low, preferred_element_type=F32
    )
    d_active = jnp.einsum("pd,fd->pf", ffn_low, w_back, preferred_element_type=F32)
    _, gelu_pull = jax.vjp(gelu_exact, first_rows(inner, count))
    d_inner = gelu_pull(d_active)[0]
    grad_bias_in = jnp.sum(d_inner, axis=0)
    inner_low = d_inner.astype(BF)
    grad_in = jnp.einsum(
        "pd,pf->df", first_rows(norm_low, count), inner_low, preferred_element_type=F32
    )
    back_norm = jnp.einsum("pf,df->pd", inner_low, w_in, preferred_element_type=F32)
    d_norm_one = d_resid_two + lax.psum(back_norm, "mp")
    _, norm_one_pull = jax.vjp(layer_norm, first_rows(resid_one, count), gain_one_w, shift_one_w)
    d_resid_one, grad_gain_one, grad_shift_one = norm_one_pull(d_norm_one)
    grad_bias_out = jnp.sum(d_resid_one, axis=0)
    attn_low = d_resid_one.astype(BF)
    grad_out = jnp.einsum(
        "pc,pd->cd", first_rows(context, count), attn_low, preferred_element_type=F32
    )
    d_context = jnp.einsum("pd,cd->pc", attn_low, w_out, preferred_element_type=F32).astype(
        BF
    )
    d_context = d_context.reshape(count, heads_here, HEAD)
    query_cls = first_rows(query, count).reshape(count, heads_here, HEAD)
    keyed_heads = keyed.reshape(count, slot, heads_here, HEAD)
    value_heads = value.reshape(count, slot, heads_here, HEAD)
    scores_cls = (
        jnp.einsum("phd,pkhd->phk", query_cls, keyed_heads, preferred_element_type=F32)
        * scale
    )
    scores_cls = jnp.where(valid[:, None, :], scores_cls, MASKED)
    chance = jnp.exp(scores_cls - log_total[:, :, None])
    d_chance = jnp.einsum(
        "phd,pkhd->phk", d_context, value_heads, preferred_element_type=F32
    )
    d_value = jnp.einsum(
        "phk,phd->pkhd", chance.astype(BF), d_context, preferred_element_type=F32
    )
    d_scores = chance * (d_chance - jnp.sum(chance * d_chance, axis=-1, keepdims=True))
    scores_low = d_scores.astype(BF)
    d_query = (
        jnp.einsum("phk,pkhd->phd", scores_low, keyed_heads, preferred_element_type=F32)
        * scale
    )
    d_keyed = (
        jnp.einsum("phk,phd->pkhd", scores_low, query_cls, preferred_element_type=F32)
        * scale
    )
    d_query = d_query.reshape(count, local)
    d_value = d_value.reshape(rows, local)
    query_low = d_query.astype(BF)
    keyed_value_low = jnp.stack(
        [d_keyed.reshape(rows, local).astype(BF), d_value.astype(BF)]
    )
    grad_bias_qv = jnp.stack([jnp.sum(d_query, axis=0), jnp.sum(d_value, axis=0)])
    grad_query_w = jnp.einsum(
        "pd,pc->dc", first_rows(tokens, count), query_low, preferred_element_type=F32
    )
    grad_kv = jnp.einsum("rd,jrc->jdc", tokens, keyed_value_low, preferred_element_type=F32)
    grad_qkv = jnp.concatenate([grad_query_w[None], grad_kv], axis=0)
    own_half = lax.dynamic_slice_in_dim(d_resid_one, column, local, 1)
    back_kv = jnp.einsum(
        "jrc,jdc->rd", keyed_value_low, w_qkv[1:], preferred_element_type=F32
    )
    back_query = jnp.einsum("pc,dc->pd", query_low, w_qkv[0], preferred_element_type=F32)
    back_all = back_kv.reshape(count, slot, width).at[:, 0].add(back_query).reshape(rows, width)
    input_grad = lax.psum_scatter(
        back_all.astype(BF), "mp", scatter_dimension=1, tiled=True
    ).astype(F32)
    input_grad = input_grad.reshape(count, slot, local).at[:, 0].add(own_half).reshape(rows, local)
    summed = (
        lax.psum_scatter(grad_qkv, "dp", scatter_dimension=1, tiled=True),
        lax.psum_scatter(grad_bias_qv, "dp", scatter_dimension=1, tiled=True),
        lax.psum_scatter(grad_out, "dp", scatter_dimension=1, tiled=True),
        lax.psum_scatter(grad_bias_out, "dp", scatter_dimension=0, tiled=True),
        lax.psum_scatter(grad_gain_one, "dp", scatter_dimension=0, tiled=True),
        lax.psum_scatter(grad_shift_one, "dp", scatter_dimension=0, tiled=True),
        lax.psum_scatter(grad_in, "dp", scatter_dimension=0, tiled=True),
        lax.psum_scatter(grad_bias_in, "dp", scatter_dimension=0, tiled=True),
        lax.psum_scatter(grad_back, "dp", scatter_dimension=1, tiled=True),
        lax.psum_scatter(grad_bias_back, "dp", scatter_dimension=0, tiled=True),
        lax.psum_scatter(grad_gain_two, "dp", scatter_dimension=0, tiled=True),
    )
    return (
        activations,
        query_loss,
        input_grad,
        query_grad,
        summed[0],
        summed[1],
        summed[2],
        summed[3],
        summed[4],
        summed[5],
        summed[6],
        summed[7],
        summed[8],
        summed[9],
        summed[10],
    )


def solution(mesh):
    in_specs = (
        P("dp", None),
        P("dp"),
        P("dp", None),
        P(),
        P(None, None, "mp"),
        P(None, "mp"),
        P("mp", None),
        P(),
        P(),
        P(),
        P(None, "mp"),
        P("mp"),
        P("mp", None),
        P(),
        P(),
    )
    out_specs = (
        P("dp", "mp"),
        P("dp"),
        P("dp", "mp"),
        P("dp", None),
        P(None, "dp", "mp"),
        P(None, ("mp", "dp")),
        P("mp", "dp"),
        P("dp"),
        P("dp"),
        P("dp"),
        P("dp", "mp"),
        P(("mp", "dp")),
        P("mp", "dp"),
        P("dp"),
        P("dp"),
    )
    groups = mesh.shape["dp"]
    fits = groups <= 16 and mesh.shape["mp"] == 2
    return jax.shard_map(
        functools.partial(per_device, groups) if fits else by_collectives,
        mesh=mesh,
        in_specs=in_specs,
        out_specs=out_specs,
        check_vma=False,
    )
```

```python
import functools
import math

import jax
import jax.numpy as jnp
from jax import lax
from jax.experimental import pallas as pl
from jax.experimental.pallas import tpu as pltpu
from jax.sharding import PartitionSpec as P

HEAD = 64
EPS = 1e-05
MASKED = -1e30
MESH = pl.DeviceIdType.MESH
BF = jnp.bfloat16
F32 = jnp.float32
MIB = 2**20


def nn(a, b):
    return jnp.dot(a, b, preferred_element_type=F32)


def nt(a, b):
    return lax.dot_general(a, b, (((1,), (1,)), ((), ())), preferred_element_type=F32)


def tn(a, b):
    return lax.dot_general(a, b, (((0,), (0,)), ((), ())), preferred_element_type=F32)


def gelu(h):
    return 0.5 * h * (1.0 + lax.erf(h * math.sqrt(0.5)))


def gelu_slope(h):
    bell = jnp.exp(-0.5 * h * h) * (1.0 / math.sqrt(2.0 * math.pi))
    return 0.5 * (1.0 + lax.erf(h * math.sqrt(0.5))) + h * bell


def row_of(vector):
    return vector[None, :].astype(F32)


def exact(a, b):
    return jnp.dot(a, b, preferred_element_type=F32, precision=lax.Precision.HIGHEST)


def one_hot(shape, shift, dtype=F32):
    row = lax.broadcasted_iota(jnp.int32, shape, 0)
    column = lax.broadcasted_iota(jnp.int32, shape, 1)
    return (row == column + shift).astype(dtype)


def standard(rows):
    center = jnp.mean(rows, axis=-1, keepdims=True)
    spread = rows - center
    second = jnp.mean(spread * spread, axis=-1, keepdims=True)
    inverse = lax.rsqrt(second + EPS)
    return spread * inverse, inverse


def norm_back(grad, scaled, inverse):
    first = jnp.mean(grad, axis=-1, keepdims=True)
    second = jnp.mean(grad * scaled, axis=-1, keepdims=True)
    return inverse * (grad - first - scaled * second)


def flip(index, bit):
    return index + bit * (1 - 2 * lax.rem(lax.div(index, bit), 2))


def mult(value, step):
    return pl.multiple_of(value, step)


def tower(
    nd,
    query_total,
    lengths,
    tokens,
    queries,
    positives,
    w_qkv,
    b_qv,
    w_out,
    b_out,
    gain_one,
    shift_one,
    w_in,
    b_in,
    w_back,
    b_back,
    gain_two,
    out_act,
    h_coef,
    h_rank,
    h_factor,
    h_active,
    h_inner,
    h_context,
    h_qcls,
    h_dctx,
    h_norm,
    h_ffn,
    h_attn,
    h_tok,
    h_sums,
    h_sums_in,
    h_loss,
    h_qgrad,
    tok,
    wq,
    wq_far,
    wo,
    wi,
    wb,
    keyb,
    valb,
    ctx,
    norm_low,
    acc,
    act_far,
    obuf,
    chance,
    factor,
    stage,
    tcls,
    pack,
    gath,
    ctx_all,
    tok_all,
    q_all,
    xh1_all,
    norm_all,
    inner_all,
    act_all,
    low_all,
    dc_all,
    qc_all,
    d1_all,
    dq_rows,
    rank_f,
    coef_own,
    coef_far,
    dq_far,
    fac_send,
    loc_sem,
    ysend,
    yrecv,
    w_send,
    w_recv,
    o_send,
    o_recv,
    o_loc,
    g_send,
    g_recv,
    gs_send,
    gs_recv,
    f_send,
    f_recv,
    m_send,
    m_recv,
    b_send,
    b_recv,
    bin_own,
    bin_far,
    out_sem,
    o_coef,
    o_rank,
    o_factor,
    o_active,
    o_inner,
    o_context,
    o_qcls,
    o_dctx,
    o_norm,
    o_ffn,
    o_attn,
    o_tok,
    o_sums,
    o_sums_in,
    o_loss,
    o_qgrad,
):
    dp = lax.axis_index("dp")
    mp = lax.axis_index("mp")
    far = 1 - mp
    chips = nd // 2
    core = lax.rem(dp, 2)
    chip = lax.div(dp, 2)
    bit_a = lax.rem(lax.div(dp, 2), 2)
    bit_b = lax.rem(lax.div(dp, 4), 2)
    quarter = bit_a + 2 * bit_b
    quarter_x = flip(quarter, 1)
    quarter_z = flip(quarter, 2)
    quarter_d = 3 - quarter
    pair = (dp, far)
    sibling = (flip(dp, 1), mp)
    near_x = (flip(dp, 2), mp)
    near_z = (flip(dp, 4), mp)

    rows, width = tok.shape
    count = lengths.shape[0]
    slot = rows // count
    own = count // 2
    half = width // 2
    own_rows = own * slot
    passages = nd * count
    blocks, unit = wi.shape[1], wi.shape[3]
    m_col = mult(mp * half, 128)
    f_col = mult(far * half, 128)

    barrier = pltpu.get_barrier_semaphore()

    def greet(i, carry):
        other = lax.rem(dp * 2 + mp + i, 2 * nd)
        pl.semaphore_signal(
            barrier,
            inc=1,
            device_id=(lax.div(other, 2), lax.rem(other, 2)),
            device_id_type=MESH,
        )
        return carry

    lax.fori_loop(1, 2 * nd, greet, 0)

    def local(src, dst, k):
        return pltpu.make_async_copy(src, dst, loc_sem.at[k])

    loads = [local(tokens, tok, 0)]
    loads += [local(w_qkv.at[j], wq.at[:, pl.ds(j * half, half)], 1 + j) for j in range(3)]
    loads.append(local(w_out, wo.at[pl.ds(mult(mp * half, 128), half), :], 4))
    loads += [
        local(w_in.at[:, pl.ds(u * unit, unit)], wi.at[mp, u], 5 + u) for u in range(blocks)
    ]
    loads += [
        local(w_back.at[pl.ds(u * unit, unit), :], wb.at[mp, u], 5 + blocks + u)
        for u in range(blocks)
    ]
    for copy in loads:
        copy.start()

    chunks = 7
    direct = (3, 6)
    lead = pl.ds(0, blocks - 1)

    def piece(k, q, c, which, side=None):
        cols = pl.ds(0, width) if side is None else pl.ds(side * half, half)
        if k in direct:
            size = half // 2 if k == 3 else unit // 2
            if k == 3:
                return wo.at[pl.ds(mult(which * half + c * size, 16), size), cols]
            return wb.at[which, blocks - 1, pl.ds(mult(c * size, 16), size), cols]
        size = unit // 8 if k == 5 else width // 8
        at = (c * 4 if q is None else c * 4 + q) * size
        size = 4 * size if q is None else size
        if k == 5:
            return wb.at[which, lead, pl.ds(mult(at, 16), size), cols]
        if side is not None:
            size = size // 2
            at = at + side * size
        here = pl.ds(mult(at, 16), size)
        return wq_far.at[here, pl.ds(k * half, half)] if k < 3 else wi.at[which, :, here, :]

    def sent_bytes(k):
        if k in direct:
            return piece(k, None, core, far)
        if k < 3:
            return wq_far.at[pl.ds(0, 7 * width // 8), pl.ds(k * half, half)]
        if k == 4:
            return wi.at[far, :, pl.ds(0, 7 * width // 8), :]
        return wb.at[far, lead, pl.ds(0, 7 * unit // 8), :]

    def source(k):
        if k < 3:
            return w_qkv.at[k, pl.ds(mult((core * 4 + quarter) * (width // 8), 16), width // 8), :]
        if k == 3:
            return w_out.at[pl.ds(mult(core * (half // 2), 16), half // 2), :]
        return piece(k, quarter, core, mp)

    def remote(src, dst, ss, rs, device):
        return pltpu.make_async_remote_copy(
            src_ref=src,
            dst_ref=dst,
            send_sem=ss,
            recv_sem=rs,
            device_id=device,
            device_id_type=MESH,
        )

    def cross(k):
        return remote(
            source(k), piece(k, quarter, core, mp), ysend.at[k], yrecv.at[k], pair
        )

    def send(k, lane, q, c, side, device):
        ref = piece(k, q, c, far, side)
        return remote(ref, ref, w_send.at[k], w_recv.at[k, lane], device)

    def lane(k, n):
        q = (quarter, quarter, quarter_z, quarter_x, None)[n]
        side = (None, None, 0, 1, None)[n]
        return send(k, n, q, core, side, (near_x, near_z, near_x, near_z, sibling)[n])

    def arrival(k, n):
        q = (quarter_x, quarter_z, quarter_d, quarter_d, None)[n]
        side = (None, None, 0, 1, None)[n]
        c = core if n < 4 else 1 - core
        return send(k, n, q, c, side, (near_x, near_z, near_x, near_z, sibling)[n])

    def step_one(k):
        remote(
            source(k), piece(k, quarter, core, far), ysend.at[k], yrecv.at[k], pair
        ).wait_recv()
        for n in (4,) if k in direct else (0, 1):
            lane(k, n).start()

    def step_two(k):
        arrival(k, 1).wait_recv()
        lane(k, 2).start()
        arrival(k, 0).wait_recv()
        lane(k, 3).start()

    def step_three(k):
        arrival(k, 2).wait_recv()
        arrival(k, 3).wait_recv()
        lane(k, 4).start()

    def complete(k):
        arrival(k, 4).wait_recv()

    def spent(window, sem):
        pltpu.make_async_copy(window, window, sem).wait()

    def advance(*steps):
        for stage_of, k in steps:
            (step_one, step_two, step_three)[stage_of - 1](k)

    for copy in loads[:4]:
        copy.wait()
    bin_own[...] = jnp.zeros_like(bin_own)
    for u in range(blocks):
        bin_own[u : u + 1, :] = row_of(b_in[pl.ds(u * unit, unit)])
    bin_own[6:8, 0:half] = b_qv[...].astype(F32)
    bias_copy = remote(bin_own, bin_far, b_send, b_recv, pair)

    lane_pair = lax.broadcasted_iota(jnp.int32, (slot, 128), 1)
    key_place = lax.broadcasted_iota(jnp.int32, (1, slot), 1)
    head_rows = lax.broadcasted_iota(jnp.int32, (8, half), 0)
    head_mask = head_rows == lax.div(lax.broadcasted_iota(jnp.int32, (8, half), 1), HEAD)
    heads = half // HEAD
    live = lax.broadcasted_iota(jnp.int32, (8, 1), 0) < heads
    bias_q = b_qv[0:1, :].astype(F32)
    bias_v = b_qv[1:2, :].astype(F32)
    ones = jnp.ones((slot, 128), BF)
    row_place = lax.broadcasted_iota(jnp.int32, (8, slot), 0)
    first_key = (lax.broadcasted_iota(jnp.int32, (8, slot), 1) == 0).astype(F32)

    def mix(query, keyed, value, bias):
        done = []
        for t in range(half // 128):
            q2 = query[:, 128 * t : 128 * t + 128]
            k2 = keyed[:, 128 * t : 128 * t + 128]
            v2 = jnp.concatenate([value[:, 128 * t : 128 * t + 128], ones], axis=1)
            parts = []
            for hx in range(2):
                mask = (lane_pair < HEAD) if hx == 0 else (lane_pair >= HEAD)
                s = nt(jnp.where(mask, q2, jnp.zeros_like(q2)), k2) + bias
                e = jnp.exp(s - jnp.max(s, axis=1, keepdims=True)).astype(BF)
                o = nn(e, v2)
                parts.append(o[:, :128] / o[:, 128:])
            done.append(jnp.where(lane_pair < HEAD, parts[0], parts[1]))
        return jnp.concatenate(done, axis=1).astype(BF)

    def first_row(p, x, query, keyed, value, bias):
        tcls[pl.ds(p, 1), :] = x[0:16, :].astype(F32)[0:1, :]
        q_heads = jnp.where(head_mask, query.astype(F32)[0:1, :], 0.0).astype(BF)
        s = nt(q_heads, keyed) + bias
        e = jnp.exp(s - jnp.max(s, axis=1, keepdims=True))
        c = jnp.where(live, e / jnp.sum(e, axis=1, keepdims=True), 0.0)
        chance[p] = c
        c_low = c.astype(BF)
        mixed = jnp.where(head_mask, nn(c_low, value), 0.0)
        stage[pl.ds(p, 1), :] = jnp.sum(mixed, axis=0, keepdims=True)
        coef_own[pl.ds(mult(p * 16, 16), 8), :] = jnp.where(row_place == heads, first_key, c)
        factor[pl.ds(mult(p * 8, 8), 8), :] = nn(c_low, x)

    theirs_plan = (((1, 0),), (), ((1, 1),), ())
    gap_plan = ((2, 0), (1, 2), (2, 1), (3, 0), (2, 2), (1, 4), (3, 1), (3, 2))
    far_plan = ((), (), (), ((1, 3),))
    feed_plan = (((2, 4),), ((1, 5),), (), ((3, 4),))
    in_plan = ((((2, 5), (1, 6)), ()), ((), ()), ((), ((3, 5),)))

    def move_on(i, plan):
        for j, steps in enumerate(plan):
            if steps:

                @pl.when(i == j)
                def _():
                    advance(*steps)

    def key_bias(p):
        return jnp.where(key_place < lengths[p], 0.0, MASKED)

    def attend_theirs(i, carry):
        move_on(i, theirs_plan)
        p = far * own + i
        at = mult(p * slot, slot)
        x = tok[pl.ds(at, slot), :]
        made = nn(x, wq[:, half:])
        keyed = made[:, :half].astype(BF)
        value = (made[:, half:] + bias_v).astype(BF)
        keyb[pl.ds(at, slot), :] = keyed
        valb[pl.ds(at, slot), :] = value
        query = ((nn(x[0:16, :], wq[:, :half]) + bias_q).astype(BF).astype(F32) * 0.125).astype(BF)
        first_row(p, x, query, keyed, value, key_bias(p))
        return carry

    def attend_own(i, carry):
        @pl.when(i == 1)
        def _():
            pl.semaphore_wait(barrier, 2 * nd - 1)
            for copy in loads[4:]:
                copy.wait()
            for k in (0, 1, 2, 4, 3):
                cross(k).start()
            bias_copy.start()

        p = mp * own + i
        at = mult(p * slot, slot)
        x = tok[pl.ds(at, slot), :]
        made = nn(x, wq[...])
        query = ((made[:, :half] + bias_q).astype(BF).astype(F32) * 0.125).astype(BF)
        keyed = made[:, half : 2 * half].astype(BF)
        value = (made[:, 2 * half :] + bias_v).astype(BF)
        keyb[pl.ds(at, slot), :] = keyed
        valb[pl.ds(at, slot), :] = value
        bias = key_bias(p)
        ctx[pl.ds(mult(i * slot, slot), slot), pl.ds(m_col, half)] = mix(query, keyed, value, bias)
        first_row(p, x, query[0:16, :], keyed, value, bias)
        return carry

    def attend_far(i, carry):
        move_on(i, far_plan)
        p = mp * own + i
        x = tok[pl.ds(mult(p * slot, slot), slot), :]
        made = nn(x, wq_far[...])
        bias_far = bin_far[6:8, 0:half]
        query = ((made[:, :half] + bias_far[0:1, :]).astype(BF).astype(F32) * 0.125).astype(BF)
        keyed = made[:, half : 2 * half].astype(BF)
        value = (made[:, 2 * half :] + bias_far[1:2, :]).astype(BF)
        ctx[pl.ds(mult(i * slot, slot), slot), pl.ds(f_col, half)] = mix(
            query, keyed, value, key_bias(p)
        )
        return carry

    lax.fori_loop(0, own, attend_own, 0)
    lax.fori_loop(0, own, attend_theirs, 0)

    pack[0:8, :] = stage[...]
    pack[8:16, :] = tcls[:, pl.ds(m_col, half)]
    pack[16:32, :] = jnp.zeros((16, half), F32)
    q_rows = queries.shape[0]
    pack[16 : 16 + q_rows, :] = queries[:, pl.ds(m_col, half)].astype(F32)
    gath[chip, core, mp] = pack[...].astype(BF)

    here = gath.at[chip, core, mp]
    to_pair = remote(here, here, gs_send.at[0], gs_recv.at[0], pair)
    to_pair.start()
    advance(*gap_plan)
    bias_copy.wait_recv()
    for k in range(3):
        complete(k)
    remote(
        here, gath.at[chip, core, far], gs_send.at[0], gs_recv.at[0], pair
    ).wait_recv()

    def gather_start(i, carry):
        both = gath.at[chip, core]
        there = lax.rem(chip + i, chips) * 2 + core
        remote(both, both, g_send, g_recv, (there, mp)).start()
        return carry

    lax.fori_loop(1, chips, gather_start, 0)
    gather_window = tok.at[pl.ds(0, (chips - 1) * 32), :]
    for k in (5, 6):
        cross(k).start()

    lax.fori_loop(0, own, attend_far, 0)

    complete(3)
    bo = row_of(b_out[...])
    g1 = row_of(gain_one[...])
    s1 = row_of(shift_one[...])
    g2 = row_of(gain_two[...])
    bb = row_of(b_back[...])

    def feed_own(i, carry):
        move_on(i, feed_plan)
        at = mult(i * slot, slot)
        here = pl.ds(at, slot)
        x = tok[pl.ds(mult(mp * own_rows + i * slot, slot), slot), :].astype(F32)
        resid = x + nn(ctx[here, :], wo[...]) + bo
        scaled, _ = standard(resid)
        norm = scaled * g1 + s1
        low = norm.astype(BF)
        norm_low[here, :] = low
        total = norm + bb
        for u in range(blocks):
            inner = nn(low, wi[mp, u]) + bin_own[u : u + 1, :]
            total = total + nn(gelu(inner).astype(BF), wb[mp, u])
        acc[here, :] = total

        return carry

    lax.fori_loop(0, own, feed_own, 0)

    complete(4)
    for u in range(blocks):

        def feed_far_in(i, carry, u=u):
            move_on(i, in_plan[u])
            here = pl.ds(mult(i * 2 * slot, slot), 2 * slot)
            inner = nn(norm_low[here, :], wi[far, u]) + bin_far[u : u + 1, :]
            act_far[u, here, :] = gelu(inner).astype(BF)
            return carry

        lax.fori_loop(0, own // 2, feed_far_in, 0)

    def feed_far_back(u):
        def feed(i, carry):
            here = pl.ds(mult(i * 2 * slot, slot), 2 * slot)
            acc[here, :] += nn(act_far[u, here, :], wb[far, u])
            return carry

        lax.fori_loop(0, own // 2, feed, 0)

    complete(5)
    feed_far_back(0)

    for u in range(1, blocks - 1):
        feed_far_back(u)
    spent(gather_window, g_recv)
    to_sibling = remote(
        gath.at[:, core], gath.at[:, core], gs_send.at[1], gs_recv.at[1], sibling
    )
    to_sibling.start()

    complete(chunks - 1)

    def out_copy(i, mine):
        side = mp if mine else far
        there = out_act.at[pl.ds(mult(side * own_rows + i * slot, 16), slot), :]
        return remote(
            obuf.at[1, pl.ds(mult(i * slot, 16), slot), :], there, o_send.at[i], o_recv.at[i], pair
        )

    def out_local(i):
        there = out_act.at[pl.ds(mult(mp * own_rows + i * slot, 16), slot), :]
        return pltpu.make_async_copy(
            obuf.at[0, pl.ds(mult(i * slot, 16), slot), :], there, o_loc.at[i]
        )

    def finish(i, carry):
        here = pl.ds(mult(i * slot, slot), slot)
        total = acc[here, :] + nn(act_far[blocks - 1, here, :], wb[far, blocks - 1])
        scaled, _ = standard(total)
        acc[here, :] = scaled * g2
        obuf[0, here, :] = acc[here, pl.ds(m_col, half)].astype(BF)
        obuf[1, here, :] = acc[here, pl.ds(f_col, half)].astype(BF)
        @pl.when(i < own - 1)
        def _():
            out_copy(i, True).start()

        out_local(i).start()
        return carry

    lax.fori_loop(0, own, finish, 0)

    remote(
        gath.at[:, 1 - core], gath.at[:, 1 - core], gs_send.at[1], gs_recv.at[1], sibling
    ).wait_recv()
    q_pad = nd * 16
    for h in range(2):
        cols = slice(h * half, (h + 1) * half)
        block = gath[:, :, h].astype(F32)
        ctx_all[:, cols] = block[:, :, 0:8].reshape(passages, half).astype(BF)
        tok_all[:, cols] = block[:, :, 8:16].reshape(passages, half).astype(BF)
        q_all[:, cols] = block[:, :, 16:32].reshape(q_pad, half).astype(BF)
    resid = tok_all[...].astype(F32) + nn(ctx_all[...], wo[...]) + bo
    scaled, inverse1 = standard(resid)
    xh1_all[...] = scaled
    norm = scaled * g1 + s1
    low = norm.astype(BF)
    norm_all[...] = low
    total = norm + bb
    for which, bias in ((mp, bin_own), (far, bin_far)):
        for u in range(blocks):
            inner = nn(low, wi[which, u]) + bias[u : u + 1, :]
            inner_all[which, u] = inner
            active = gelu(inner).astype(BF)
            act_all[which, u] = active
    for u in range(blocks):
        total = total + nn(act_all[mp, u], wb[mp, u])
    total = total + nn(act_all[far, 0], wb[far, 0])
    for u in range(1, blocks):
        total = total + nn(act_all[far, u], wb[far, u])

    xh2, inverse2 = standard(total)
    cls = (xh2 * g2).astype(BF)
    similar = nt(cls, q_all[...])
    top = jnp.max(similar, axis=0, keepdims=True)
    log_sum = top + jnp.log(jnp.sum(jnp.exp(similar - top), axis=0, keepdims=True))
    q_count = query_total // nd
    from_q = lax.broadcasted_iota(jnp.int32, (query_total, q_pad), 0)
    to_q = lax.broadcasted_iota(jnp.int32, (query_total, q_pad), 1)
    spot = lax.div(from_q, q_count) * 16 + lax.rem(from_q, q_count)
    wanted = jnp.broadcast_to(row_of(positives[...]), (8, query_total)) + 1.0
    place = exact(wanted, (spot == to_q).astype(F32))[0:1, :] - 1.0
    target = lax.broadcasted_iota(jnp.int32, similar.shape, 0).astype(F32) == place
    picked = jnp.sum(jnp.where(target, similar, 0.0), axis=0, keepdims=True)
    o_loss[...] = jnp.broadcast_to(log_sum - picked, o_loss.shape)
    slopes = (jnp.exp(similar - log_sum) - target.astype(F32)) * (1.0 / query_total)
    slope_high = slopes.astype(BF)
    slope_low = (slopes - slope_high.astype(F32)).astype(BF)
    cls_grad = nn(slope_high, q_all[...]) + nn(slope_low, q_all[...])
    pick = (
        lax.broadcasted_iota(jnp.int32, (16, q_pad), 1)
        == lax.broadcasted_iota(jnp.int32, (16, q_pad), 0) + dp * 16
    ).astype(BF)
    o_qgrad[...] = nn(nt(pick, slope_high).astype(BF), cls) + nn(
        nt(pick, slope_low).astype(BF), cls
    )
    d_two = norm_back(g2 * cls_grad, xh2, inverse2)
    o_sums[0:1, :] = jnp.sum(cls_grad * xh2, axis=0, keepdims=True)
    o_sums[1:2, :] = jnp.sum(d_two, axis=0, keepdims=True)
    ffn_low = d_two.astype(BF)
    o_ffn[...] = ffn_low
    back = d_two
    for h in range(2):
        for u in range(blocks):
            d_active = nt(ffn_low, wb[h, u])
            d_inner = d_active * gelu_slope(inner_all[h, u])
            inner_all[h, u, 0:8, :] = jnp.broadcast_to(
                jnp.sum(d_inner, axis=0, keepdims=True), (8, unit)
            )
            inner_low = d_inner.astype(BF)
            low_all[h, u] = inner_low
            back = back + nt(inner_low, wi[h, u])
    for u in range(blocks):
        o_active[u] = act_all[mp, u]
        o_inner[u] = low_all[mp, u]
        o_sums_in[u : u + 1, :] = inner_all[mp, u, 0:1, :]
    xh1 = xh1_all[...]
    d_one = norm_back(g1 * back, xh1, inverse1)
    d1_all[...] = d_one
    o_sums[2:3, :] = jnp.sum(back * xh1, axis=0, keepdims=True)
    o_sums[3:4, :] = jnp.sum(back, axis=0, keepdims=True)
    o_sums[4:5, :] = jnp.sum(d_one, axis=0, keepdims=True)
    attn_low = d_one.astype(BF)
    o_attn[...] = attn_low
    o_norm[...] = norm_all[...]
    o_tok[...] = tok_all[...]
    d_ctx = nt(attn_low, wo[pl.ds(mult(mp * half, 128), half), :]).astype(BF)
    o_dctx[...] = d_ctx
    dc_all[...] = d_ctx.astype(F32)
    q_cls = (nn(tok_all[...], wq[:, 0:half]) + bias_q).astype(BF)
    o_qcls[...] = q_cls
    qc_all[...] = q_cls.astype(F32) * 0.125
    o_context[...] = ctx_all[:, pl.ds(m_col, half)]
    o_sums[5:6, 0:half] = jnp.sum(dc_all[...], axis=0, keepdims=True)

    def stored(src, dst, k):
        return pltpu.make_async_copy(src, dst, out_sem.at[k])

    early = [
        stored(src, dst, k)
        for k, (src, dst) in enumerate(
            (
                (o_active, h_active),
                (o_inner, h_inner),
                (o_context, h_context),
                (o_qcls, h_qcls),
                (o_dctx, h_dctx),
                (o_norm, h_norm),
                (o_ffn, h_ffn),
                (o_attn, h_attn),
                (o_tok, h_tok),
                (o_sums, h_sums),
                (o_sums_in, h_sums_in),
                (o_loss, h_loss),
                (o_qgrad, h_qgrad),
            )
        )
    ]
    for copy in early:
        copy.start()

    base = mult(dp * count, 8)
    fkind = count * 8

    mark = jnp.logical_or(row_place == heads, row_place == heads + 1)
    for p in range(count):
        d_row = dc_all[pl.ds(base + p, 1), :]
        q_row = qc_all[pl.ds(base + p, 1), :]
        rank_f[p * 16 : p * 16 + 8, 0:half] = jnp.where(head_mask, d_row, 0.0)
        rank_f[p * 16 + 8 : p * 16 + 16, 0:half] = jnp.where(head_mask, q_row, 0.0)
    kept = rank_f[:, 0:half].astype(BF)
    group = 4
    for first in range(0, count, group):
        d_scores = []
        for p in range(first, first + group):
            c = chance[p]
            d_chance = nt(kept[p * 16 : p * 16 + 16, :], valb[p * slot : (p + 1) * slot, :])[0:8, :]
            d_scores.append(c * (d_chance - jnp.sum(c * d_chance, axis=1, keepdims=True)))
        for p, d in zip(range(first, first + group), d_scores):
            s_low = d.astype(BF)
            at = slice(p * slot, (p + 1) * slot)
            coef_own[p * 16 + 8 : p * 16 + 16, :] = jnp.where(mark, first_key, d)
            factor[fkind + p * 8 : fkind + p * 8 + 8, :] = nn(s_low, tok[at, :])
            spread = nn(s_low, keyb[at, :])
            dq_rows[p : p + 1, :] = 0.125 * jnp.sum(
                jnp.where(head_mask, spread, 0.0), axis=0, keepdims=True
            )

    turned = jnp.transpose(factor[...]).astype(BF)
    dq = dq_rows[...]
    for b in range(half // 128):
        pack[b * 8 : b * 8 + 8, 0:128] = dq[:, b * 128 : b * 128 + 128]
    pack[half // 16 : 32, 0:128] = jnp.zeros((32 - half // 16, 128), F32)
    dq_low = pack[:, 0:128].astype(BF)
    share = width // nd
    for j in range(nd):
        fac_send[j, 0:share, :] = turned[j * share : (j + 1) * share, :]
        fac_send[j, share:, :] = dq_low
    o_factor[dp] = fac_send[dp]

    def factor_start(i, carry):
        there = lax.rem(dp + i, nd)
        remote(fac_send.at[there], o_factor.at[dp], f_send, f_recv, (there, mp)).start()
        return carry

    lax.fori_loop(1, nd, factor_start, 0)

    coef_low = coef_own[...].astype(BF)
    o_coef[0] = coef_low
    coef_far_copy = remote(o_coef.at[0], coef_far, m_send.at[0], m_recv.at[0], pair)
    coef_far_copy.start()
    dq_copy = remote(dq_rows, dq_far, m_send.at[1], m_recv.at[1], pair)
    dq_copy.start()
    out_copy(own - 1, True).start()
    kind = lax.rem(lax.div(lax.broadcasted_iota(jnp.int32, (count * 16, 1), 0), 8), 2)
    d1_rows = d1_all[pl.ds(base, count), :]
    d_far = nt(d1_rows.astype(BF), wo[pl.ds(mult(far * half, 128), half), :])
    q_far = (nn(tcls[...].astype(BF), wq_far[:, 0:half]) + bin_far[6:7, 0:half]) * 0.125
    for p in range(count):
        rank_f[p * 16 : p * 16 + 8, 0:half] = jnp.where(head_mask, d_far[p : p + 1, :], 0.0)
        rank_f[p * 16 + 8 : p * 16 + 16, 0:half] = jnp.where(head_mask, q_far[p : p + 1, :], 0.0)
    kept_far = rank_f[:, 0:half].astype(BF)
    my_rows = pl.ds(mult(mp * half, 128), half)

    def rank_rows(left, right):
        by_v = nt(left, right[my_rows, 2 * half :])
        by_k = nt(left, right[my_rows, half : 2 * half])
        return jnp.where(kind == 0, by_v, by_k)

    rank_f[:, 0:half] = rank_rows(kept, wq)
    rank_f[:, half:] = rank_rows(kept_far, wq_far)
    d1_mine = d1_all[pl.ds(base, count), pl.ds(m_col, half)]
    d1_high = d1_mine.astype(BF).astype(F32)
    d1_low = d1_mine - d1_high

    def first_rank(cols, back_q, high, low):
        for p in range(count):
            rank_f[p * 16 + heads : p * 16 + heads + 1, cols] = back_q[p : p + 1, :]
            rank_f[p * 16 + heads + 1 : p * 16 + 8, cols] = jnp.zeros((7 - heads, half), F32)
            rank_f[p * 16 + 8 + heads : p * 16 + 9 + heads, cols] = high[p : p + 1]
            rank_f[p * 16 + 9 + heads : p * 16 + 10 + heads, cols] = low[p : p + 1]

    mine = slice(0, half)
    theirs = slice(half, width)
    first_rank(mine, nt(dq.astype(BF), wq[my_rows, 0:half]), d1_high, d1_low)
    o_rank[0] = rank_f[:, mine].astype(BF)

    dq_copy.wait_recv()
    nothing = jnp.zeros((count, half), F32)
    first_rank(theirs, nt(dq_far[...].astype(BF), wq_far[my_rows, 0:half]), nothing, nothing)
    o_rank[1] = rank_f[:, theirs].astype(BF)
    coef_far_copy.wait_recv()
    o_coef[1] = coef_far[...]
    factor_window = fac_send.at[pl.ds(0, nd - 1)]
    spent(factor_window, f_recv)
    last = [stored(o_factor, h_factor, 15), stored(o_coef, h_coef, 13), stored(o_rank, h_rank, 14)]
    for copy in last:
        copy.start()
    spent(factor_window, f_send)
    coef_far_copy.wait_send()
    dq_copy.wait_send()
    bias_copy.wait_send()
    spent(gather_window, g_send)
    to_sibling.wait_send()
    to_pair.wait_send()
    for k in range(chunks):
        cross(k).wait_send()
        spent(sent_bytes(k), w_send.at[k])

    def drain(i, carry):
        out_copy(i, True).wait_send()
        out_copy(i, False).wait_recv()
        out_local(i).wait()
        return carry

    lax.fori_loop(0, own, drain, 0)
    for copy in early + last:
        copy.wait()


def gradients(
    nd,
    act_in,
    coef_in,
    rank_in,
    factor_in,
    active_in,
    inner_in,
    context_in,
    qcls_in,
    dctx_in,
    norm_in,
    ffn_in,
    attn_in,
    tok_in,
    sums_in,
    sums_units_in,
    loss_in,
    qgrad_in,
    act_out,
    query_loss,
    input_grad,
    query_grad,
    grad_qkv,
    grad_bias_qv,
    grad_out,
    grad_bias_out,
    grad_gain_one,
    grad_shift_one,
    grad_in,
    grad_bias_in,
    grad_back,
    grad_bias_back,
    grad_gain_two,
    coef,
    rank,
    factor,
    active,
    inner,
    context,
    qcls,
    dctx,
    norm,
    ffn,
    attn,
    tok,
    sums,
    sums_units,
    loss,
    qgrad,
    sems,
    act_sem,
    act_buf,
    in_buf,
    in_sems,
    rhs,
):
    dp = lax.axis_index("dp")
    act_load = pltpu.make_async_copy(act_in, act_buf, act_sem.at[0])
    act_store = pltpu.make_async_copy(act_buf, act_out, act_sem.at[1])
    act_load.start()
    pairs = (
        (coef_in, coef),
        (rank_in, rank),
        (factor_in, factor),
        (qcls_in, qcls),
        (dctx_in, dctx),
        (active_in, active),
        (inner_in, inner),
        (context_in, context),
        (norm_in, norm),
        (ffn_in, ffn),
        (attn_in, attn),
        (tok_in, tok),
        (sums_in, sums),
        (sums_units_in, sums_units),
        (loss_in, loss),
        (qgrad_in, qgrad),
    )
    loads = [pltpu.make_async_copy(src, dst, sems.at[i]) for i, (src, dst) in enumerate(pairs)]
    for load in loads:
        load.start()
    passages, width = ffn.shape
    half = width // 2
    share = width // nd
    count = passages // nd
    slot = coef.shape[2]
    for load in loads[:2]:
        load.wait()

    def input_copy(p):
        at = pl.ds(mult(p * slot, slot), slot)
        return pltpu.make_async_copy(in_buf.at[at, :], input_grad.at[at, :], in_sems.at[p])

    def input_rows(p, carry):
        rows16 = pl.ds(mult(p * 16, 16), 16)
        both = jnp.concatenate([coef[0, rows16, :], coef[1, rows16, :]], axis=0)
        right = jnp.concatenate([rank[0, rows16, :], rank[1, rows16, :]], axis=0)
        in_buf[pl.ds(mult(p * slot, slot), slot), :] = tn(both, right)
        input_copy(p).start()
        return carry

    lax.fori_loop(0, count, input_rows, 0)
    act_load.wait()
    act_store.start()
    for load in loads[2:]:
        load.wait()

    spread = lax.broadcasted_iota(jnp.int32, (8, half), 0) == lax.div(
        lax.broadcasted_iota(jnp.int32, (8, half), 1), HEAD
    )
    fkind = count * 8

    def build(s, carry):
        d_rows = dctx[pl.ds(mult(s * 2 * count, 16), 2 * count), :].astype(F32)
        q_rows = qcls[pl.ds(mult(s * 2 * count, 16), 2 * count), :].astype(F32) * 0.125
        k_blocks = [jnp.where(spread, q_rows[p : p + 1, :], 0.0) for p in range(2 * count)]
        v_blocks = [jnp.where(spread, d_rows[p : p + 1, :], 0.0) for p in range(2 * count)]
        here = pl.ds(mult(s * 2 * fkind, 16), 2 * fkind)
        rhs[here, 0:half] = jnp.concatenate(k_blocks, 0).astype(BF)
        rhs[here, half:] = jnp.concatenate(v_blocks, 0).astype(BF)
        return carry

    lax.fori_loop(0, nd // 2, build, 0)
    grad_k = jnp.zeros((share, half), F32)
    grad_v = jnp.zeros((share, half), F32)
    for s in range(0, nd, 4):
        left_v = jnp.concatenate([factor[s + t, 0:share, :][:, 0:fkind] for t in range(4)], axis=1)
        left_k = jnp.concatenate([factor[s + t, 0:share, :][:, fkind:] for t in range(4)], axis=1)
        grad_k = grad_k + nn(left_k, rhs[s * fkind : (s + 4) * fkind, 0:half])
        grad_v = grad_v + nn(left_v, rhs[s * fkind : (s + 4) * fkind, half:])
    grad_qkv[1] = grad_k
    grad_qkv[2] = grad_v

    pick = one_hot((width, share), dp * share)
    pick_low = pick.astype(BF)
    row = lax.broadcasted_iota(jnp.int32, (share, width), 0)
    column = lax.broadcasted_iota(jnp.int32, (share, width), 1)
    pick_t = (column == row + dp * share).astype(BF)
    ffn_own = nt(pick_t, ffn[...]).astype(BF)
    attn_own = nt(pick_t, attn[...]).astype(BF)
    norm_own = nt(pick_t, norm[...]).astype(BF)
    tok_own = nt(pick_t, tok[...]).astype(BF)
    grad_out[...] = nn(attn_own, context[...])
    unit = active.shape[2]
    blocks = active.shape[0]
    for u in range(blocks):
        cols = slice(u * unit, (u + 1) * unit)
        grad_back[:, cols] = nn(ffn_own, active[u])
        grad_in[:, cols] = nn(norm_own, inner[u])
    dq_sum = []
    for b in range(half // 128):
        cols = factor[:, share:, :].astype(F32)[:, b * 8 : b * 8 + 8, :].reshape(passages, 128)
        dq_sum.append(jnp.sum(cols, axis=0, keepdims=True))
        grad_qkv[0, :, b * 128 : b * 128 + 128] = nn(tok_own, cols.astype(BF))

    mine = exact(sums[...], pick)
    grad_gain_two[...] = mine[0:1, :].reshape(share)
    grad_bias_back[...] = mine[1:2, :].reshape(share)
    grad_gain_one[...] = mine[2:3, :].reshape(share)
    grad_shift_one[...] = mine[3:4, :].reshape(share)
    grad_bias_out[...] = mine[4:5, :].reshape(share)
    part = half // nd
    both = jnp.concatenate([jnp.concatenate(dq_sum, axis=1), sums[5:6, 0:half]], axis=0)
    wide = jnp.concatenate([both, jnp.zeros((6, half), F32)], axis=0)
    grad_bias_qv[...] = exact(wide, one_hot((half, part), dp * part))[0:2, :]
    in_share = grad_bias_in.shape[0]
    total = jnp.zeros((8, in_share), F32)
    for u in range(blocks):
        total = total + exact(
            jnp.broadcast_to(sums_units[u : u + 1, :], (8, unit)),
            one_hot((unit, in_share), dp * in_share - u * unit),
        )
    grad_bias_in[...] = total[0:1, :].reshape(in_share)
    q_rows = query_loss.shape[0]
    query_loss[...] = exact(loss[...], one_hot((loss.shape[1], q_rows), dp * 16))[0:1, :].reshape(q_rows)
    query_grad[...] = qgrad[0:q_rows, :]

    def input_wait(p, carry):
        input_copy(p).wait()
        return carry

    lax.fori_loop(0, count, input_wait, 0)
    act_store.wait()


def per_device(nd, *arrays):
    (
        tokens,
        lengths,
        queries,
        positives,
        w_qkv,
        b_qv,
        w_out,
        b_out,
        gain_one,
        shift_one,
        w_in,
        b_in,
        w_back,
        b_back,
        gain_two,
    ) = arrays
    rows, width = tokens.shape
    count = lengths.shape[0]
    slot = rows // count
    half = w_qkv.shape[2]
    units = w_in.shape[1]
    unit = 512
    blocks = units // unit
    chunks = 7
    own_rows = rows // 2
    passages = nd * count
    chips = nd // 2
    q_rows = queries.shape[0]
    q_pad = nd * 16
    share = width // nd
    vmem = pl.BlockSpec(memory_space=pltpu.VMEM)
    hbm = pl.BlockSpec(memory_space=pl.ANY)
    smem = pl.BlockSpec(memory_space=pltpu.SMEM)
    in_specs = [smem, hbm, vmem, vmem, hbm, vmem, hbm, vmem, vmem, vmem, hbm, vmem, hbm, vmem, vmem]
    shape = jax.ShapeDtypeStruct
    outs = [
        (shape((rows, half), BF), hbm),
        (shape((2, count * 16, slot), BF), hbm),
        (shape((2, count * 16, half), BF), hbm),
        (shape((nd, share + 32, 128), BF), hbm),
        (shape((blocks, passages, unit), BF), hbm),
        (shape((blocks, passages, unit), BF), hbm),
        (shape((passages, half), BF), hbm),
        (shape((passages, half), BF), hbm),
        (shape((passages, half), BF), hbm),
        (shape((passages, width), BF), hbm),
        (shape((passages, width), BF), hbm),
        (shape((passages, width), BF), hbm),
        (shape((passages, width), BF), hbm),
        (shape((8, width), F32), hbm),
        (shape((8, unit), F32), hbm),
        (shape((8, q_pad), F32), hbm),
        (shape((16, width), F32), hbm),
    ]
    dma = pltpu.SemaphoreType.DMA
    scratch = [
        pltpu.VMEM((rows, width), BF),
        pltpu.VMEM((width, 3 * half), BF),
        pltpu.VMEM((width, 3 * half), BF),
        pltpu.VMEM((width, width), BF),
        pltpu.VMEM((2, blocks, width, unit), BF),
        pltpu.VMEM((2, blocks, unit, width), BF),
        pltpu.VMEM((rows, half), BF),
        pltpu.VMEM((rows, half), BF),
        pltpu.VMEM((own_rows, width), BF),
        pltpu.VMEM((own_rows, width), BF),
        pltpu.VMEM((own_rows, width), F32),
        pltpu.VMEM((blocks, own_rows, unit), BF),
        pltpu.VMEM((2, own_rows, half), BF),
        pltpu.VMEM((count, 8, slot), F32),
        pltpu.VMEM((2 * count * 8, width), F32),
        pltpu.VMEM((8, half), F32),
        pltpu.VMEM((8, width), F32),
        pltpu.VMEM((32, half), F32),
        pltpu.VMEM((chips, 2, 2, 32, half), BF),
        pltpu.VMEM((passages, width), BF),
        pltpu.VMEM((passages, width), BF),
        pltpu.VMEM((q_pad, width), BF),
        pltpu.VMEM((passages, width), F32),
        pltpu.VMEM((passages, width), BF),
        pltpu.VMEM((2, blocks, passages, unit), F32),
        pltpu.VMEM((2, blocks, passages, unit), BF),
        pltpu.VMEM((2, blocks, passages, unit), BF),
        pltpu.VMEM((passages, half), F32),
        pltpu.VMEM((passages, half), F32),
        pltpu.VMEM((passages, width), F32),
        pltpu.VMEM((8, half), F32),
        pltpu.VMEM((count * 16, width), F32),
        pltpu.VMEM((count * 16, slot), F32),
        pltpu.VMEM((count * 16, slot), BF),
        pltpu.VMEM((count, half), F32),
        pltpu.VMEM((nd, share + 32, 128), BF),
        dma((5 + 2 * blocks,)),
        dma((chunks,)),
        dma((chunks,)),
        dma((chunks,)),
        dma((chunks, 5)),
        dma((count // 2,)),
        dma((count // 2,)),
        dma((count // 2,)),
        dma,
        dma,
        dma((2,)),
        dma((2,)),
        dma,
        dma,
        dma((2,)),
        dma((2,)),
        dma,
        dma,
        pltpu.VMEM((8, unit), F32),
        pltpu.VMEM((8, unit), F32),
        dma((16,)),
    ] + [pltpu.VMEM(o[0].shape, o[0].dtype) for o in outs[1:]]
    made = pl.pallas_call(
        functools.partial(tower, nd, nd * q_rows),
        out_shape=[o[0] for o in outs],
        in_specs=in_specs,
        out_specs=[o[1] for o in outs],
        scratch_shapes=scratch,
        compiler_params=pltpu.CompilerParams(
            collective_id=0, has_side_effects=True, vmem_limit_bytes=60 * MIB
        ),
        name="tower",
    )(
        lengths,
        tokens,
        queries,
        positives,
        w_qkv,
        b_qv,
        w_out,
        b_out,
        gain_one,
        shift_one,
        w_in,
        b_in,
        w_back,
        b_back,
        gain_two,
    )
    g_outs = [
        (shape((rows, half), BF), hbm),
        (shape((q_rows,), F32), vmem),
        (shape((rows, half), F32), hbm),
        (shape((q_rows, width), F32), vmem),
        (shape((3, share, half), F32), vmem),
        (shape((2, half // nd), F32), vmem),
        (shape((share, half), F32), vmem),
        (shape((share,), F32), vmem),
        (shape((share,), F32), vmem),
        (shape((share,), F32), vmem),
        (shape((share, units), F32), vmem),
        (shape((units // nd,), F32), vmem),
        (shape((share, units), F32), vmem),
        (shape((share,), F32), vmem),
        (shape((share,), F32), vmem),
    ]
    grads = pl.pallas_call(
        functools.partial(gradients, nd),
        out_shape=[o[0] for o in g_outs],
        in_specs=[hbm] * len(outs),
        out_specs=[o[1] for o in g_outs],
        scratch_shapes=[pltpu.VMEM(o[0].shape, o[0].dtype) for o in outs[1:]]
        + [
            dma((len(outs) - 1,)),
            dma((2,)),
            pltpu.VMEM((rows, half), BF),
            pltpu.VMEM((rows, half), F32),
            dma((count,)),
            pltpu.VMEM((nd * count * 8, width), BF),
        ],
        compiler_params=pltpu.CompilerParams(vmem_limit_bytes=62 * MIB),
        name="gradients",
    )(*made)
    grads = list(grads)
    grads[6] = grads[6].T
    grads[12] = grads[12].T
    return tuple(grads)


def layer_norm(rows, gain, shift):
    center = jnp.mean(rows, axis=-1, keepdims=True)
    spread = rows - center
    second = jnp.mean(spread * spread, axis=-1, keepdims=True)
    return spread * lax.rsqrt(second + EPS) * gain + shift


def scaled_norm(rows, gain):
    center = jnp.mean(rows, axis=-1, keepdims=True)
    spread = rows - center
    second = jnp.mean(spread * spread, axis=-1, keepdims=True)
    return spread * lax.rsqrt(second + EPS) * gain


def gelu_exact(values):
    return jax.nn.gelu(values, approximate=False)


def first_rows(values, count):
    return values.reshape((count, values.shape[0] // count) + values.shape[1:])[:, 0]


def by_collectives(
    tokens,
    lengths,
    queries,
    positives,
    w_qkv,
    b_qv,
    w_out,
    b_out,
    gain_one,
    shift_one,
    w_in,
    b_in,
    w_back,
    b_back,
    gain_two,
):
    rows, width = tokens.shape
    count = lengths.shape[0]
    slot = rows // count
    local = w_qkv.shape[2]
    heads_here = local // HEAD
    scale = 1.0 / math.sqrt(HEAD)
    projected = jnp.einsum("rd,jdc->jrc", tokens, w_qkv, preferred_element_type=F32)
    bias_qv = b_qv.astype(F32)
    query = (projected[0] + bias_qv[0]).astype(BF)
    keyed = projected[1].astype(BF)
    value = (projected[2] + bias_qv[1]).astype(BF)
    block = min(count, max(1, 512 // slot))
    blocks = count // block
    valid = lax.broadcasted_iota(jnp.int32, (count, slot), 1) < lengths[:, None]
    split_shape = (blocks, block, slot, heads_here, HEAD)

    def attend(inputs):
        query_part, keyed_part, value_part, valid_part = inputs
        scores = (
            jnp.einsum(
                "pqhd,pkhd->phqk", query_part, keyed_part, preferred_element_type=F32
            )
            * scale
        )
        scores = jnp.where(valid_part[:, None, None, :], scores, MASKED)
        top = jnp.max(scores, axis=-1, keepdims=True)
        raised = jnp.exp(scores - top)
        total = jnp.sum(raised, axis=-1, keepdims=True)
        chance_low = (raised / total).astype(BF)
        mixed = jnp.einsum(
            "phqk,pkhd->pqhd", chance_low, value_part, preferred_element_type=F32
        )
        return (mixed.astype(BF), (top + jnp.log(total))[:, :, 0, 0])

    context, log_total = lax.map(
        attend,
        (
            query.reshape(split_shape),
            keyed.reshape(split_shape),
            value.reshape(split_shape),
            valid.reshape(blocks, block, slot),
        ),
    )
    context = context.reshape(rows, local)
    log_total = log_total.reshape(count, heads_here)
    partial_attn = jnp.dot(context, w_out, preferred_element_type=F32).astype(BF)
    attended = lax.psum(partial_attn, "mp").astype(F32) + b_out.astype(F32)
    resid_one = tokens.astype(F32) + attended
    gain_one_w = gain_one.astype(F32)
    shift_one_w = shift_one.astype(F32)
    gain_two_w = gain_two.astype(F32)
    norm_one = layer_norm(resid_one, gain_one_w, shift_one_w)
    norm_low = norm_one.astype(BF)
    inner = jnp.dot(norm_low, w_in, preferred_element_type=F32) + b_in.astype(F32)
    active = gelu_exact(inner).astype(BF)
    partial_ffn = jnp.dot(active, w_back, preferred_element_type=F32).astype(BF)
    resid_two = (
        norm_one + lax.psum(partial_ffn, "mp").astype(F32) + b_back.astype(F32)
    )
    output = scaled_norm(resid_two, gain_two_w)
    column = lax.axis_index("mp") * local
    activations = lax.dynamic_slice_in_dim(output, column, local, 1).astype(BF)
    cls_low = first_rows(output, count).astype(BF)
    query_rows = queries.shape[0]
    members = lax.axis_size("dp")
    query_total = query_rows * members
    own_query = lax.axis_index("dp") * query_rows
    gathered = lax.all_gather(cls_low, "dp", axis=0, tiled=True)
    similar = jnp.einsum("qd,pd->qp", queries, gathered, preferred_element_type=F32)
    mine = lax.dynamic_slice_in_dim(positives, own_query, query_rows)
    target = lax.broadcasted_iota(jnp.int32, similar.shape, 1) == mine[:, None]
    top = jnp.max(similar, axis=1, keepdims=True)
    log_sum = top[:, 0] + jnp.log(jnp.sum(jnp.exp(similar - top), axis=1))
    picked = jnp.sum(jnp.where(target, similar, 0.0), axis=1)
    query_loss = log_sum - picked
    slopes = (jnp.exp(similar - log_sum[:, None]) - target.astype(F32)) / query_total
    query_grad = jnp.dot(slopes, gathered.astype(F32), precision=lax.Precision.HIGHEST)
    queries_wide = queries.astype(F32)
    cls_grad = lax.psum_scatter(
        jnp.einsum("qp,qd->pd", slopes, queries_wide, precision=lax.Precision.HIGHEST),
        "dp",
        scatter_dimension=0,
        tiled=True,
    )
    _, norm_two_pull = jax.vjp(scaled_norm, first_rows(resid_two, count), gain_two_w)
    d_resid_two, grad_gain_two = norm_two_pull(cls_grad)
    grad_bias_back = jnp.sum(d_resid_two, axis=0)
    ffn_low = d_resid_two.astype(BF)
    grad_back = jnp.einsum(
        "pf,pd->fd", first_rows(active, count), ffn_low, preferred_element_type=F32
    )
    d_active = jnp.einsum("pd,fd->pf", ffn_low, w_back, preferred_element_type=F32)
    _, gelu_pull = jax.vjp(gelu_exact, first_rows(inner, count))
    d_inner = gelu_pull(d_active)[0]
    grad_bias_in = jnp.sum(d_inner, axis=0)
    inner_low = d_inner.astype(BF)
    grad_in = jnp.einsum(
        "pd,pf->df", first_rows(norm_low, count), inner_low, preferred_element_type=F32
    )
    back_norm = jnp.einsum("pf,df->pd", inner_low, w_in, preferred_element_type=F32)
    d_norm_one = d_resid_two + lax.psum(back_norm, "mp")
    _, norm_one_pull = jax.vjp(layer_norm, first_rows(resid_one, count), gain_one_w, shift_one_w)
    d_resid_one, grad_gain_one, grad_shift_one = norm_one_pull(d_norm_one)
    grad_bias_out = jnp.sum(d_resid_one, axis=0)
    attn_low = d_resid_one.astype(BF)
    grad_out = jnp.einsum(
        "pc,pd->cd", first_rows(context, count), attn_low, preferred_element_type=F32
    )
    d_context = jnp.einsum("pd,cd->pc", attn_low, w_out, preferred_element_type=F32).astype(
        BF
    )
    d_context = d_context.reshape(count, heads_here, HEAD)
    query_cls = first_rows(query, count).reshape(count, heads_here, HEAD)
    keyed_heads = keyed.reshape(count, slot, heads_here, HEAD)
    value_heads = value.reshape(count, slot, heads_here, HEAD)
    scores_cls = (
        jnp.einsum("phd,pkhd->phk", query_cls, keyed_heads, preferred_element_type=F32)
        * scale
    )
    scores_cls = jnp.where(valid[:, None, :], scores_cls, MASKED)
    chance = jnp.exp(scores_cls - log_total[:, :, None])
    d_chance = jnp.einsum(
        "phd,pkhd->phk", d_context, value_heads, preferred_element_type=F32
    )
    d_value = jnp.einsum(
        "phk,phd->pkhd", chance.astype(BF), d_context, preferred_element_type=F32
    )
    d_scores = chance * (d_chance - jnp.sum(chance * d_chance, axis=-1, keepdims=True))
    scores_low = d_scores.astype(BF)
    d_query = (
        jnp.einsum("phk,pkhd->phd", scores_low, keyed_heads, preferred_element_type=F32)
        * scale
    )
    d_keyed = (
        jnp.einsum("phk,phd->pkhd", scores_low, query_cls, preferred_element_type=F32)
        * scale
    )
    d_query = d_query.reshape(count, local)
    d_value = d_value.reshape(rows, local)
    query_low = d_query.astype(BF)
    keyed_value_low = jnp.stack(
        [d_keyed.reshape(rows, local).astype(BF), d_value.astype(BF)]
    )
    grad_bias_qv = jnp.stack([jnp.sum(d_query, axis=0), jnp.sum(d_value, axis=0)])
    grad_query_w = jnp.einsum(
        "pd,pc->dc", first_rows(tokens, count), query_low, preferred_element_type=F32
    )
    grad_kv = jnp.einsum("rd,jrc->jdc", tokens, keyed_value_low, preferred_element_type=F32)
    grad_qkv = jnp.concatenate([grad_query_w[None], grad_kv], axis=0)
    own_half = lax.dynamic_slice_in_dim(d_resid_one, column, local, 1)
    back_kv = jnp.einsum(
        "jrc,jdc->rd", keyed_value_low, w_qkv[1:], preferred_element_type=F32
    )
    back_query = jnp.einsum("pc,dc->pd", query_low, w_qkv[0], preferred_element_type=F32)
    back_all = back_kv.reshape(count, slot, width).at[:, 0].add(back_query).reshape(rows, width)
    input_grad = lax.psum_scatter(
        back_all.astype(BF), "mp", scatter_dimension=1, tiled=True
    ).astype(F32)
    input_grad = input_grad.reshape(count, slot, local).at[:, 0].add(own_half).reshape(rows, local)
    summed = (
        lax.psum_scatter(grad_qkv, "dp", scatter_dimension=1, tiled=True),
        lax.psum_scatter(grad_bias_qv, "dp", scatter_dimension=1, tiled=True),
        lax.psum_scatter(grad_out, "dp", scatter_dimension=1, tiled=True),
        lax.psum_scatter(grad_bias_out, "dp", scatter_dimension=0, tiled=True),
        lax.psum_scatter(grad_gain_one, "dp", scatter_dimension=0, tiled=True),
        lax.psum_scatter(grad_shift_one, "dp", scatter_dimension=0, tiled=True),
        lax.psum_scatter(grad_in, "dp", scatter_dimension=0, tiled=True),
        lax.psum_scatter(grad_bias_in, "dp", scatter_dimension=0, tiled=True),
        lax.psum_scatter(grad_back, "dp", scatter_dimension=1, tiled=True),
        lax.psum_scatter(grad_bias_back, "dp", scatter_dimension=0, tiled=True),
        lax.psum_scatter(grad_gain_two, "dp", scatter_dimension=0, tiled=True),
    )
    return (
        activations,
        query_loss,
        input_grad,
        query_grad,
        summed[0],
        summed[1],
        summed[2],
        summed[3],
        summed[4],
        summed[5],
        summed[6],
        summed[7],
        summed[8],
        summed[9],
        summed[10],
    )


def solution(mesh):
    in_specs = (
        P("dp", None),
        P("dp"),
        P("dp", None),
        P(),
        P(None, None, "mp"),
        P(None, "mp"),
        P("mp", None),
        P(),
        P(),
        P(),
        P(None, "mp"),
        P("mp"),
        P("mp", None),
        P(),
        P(),
    )
    out_specs = (
        P("dp", "mp"),
        P("dp"),
        P("dp", "mp"),
        P("dp", None),
        P(None, "dp", "mp"),
        P(None, ("mp", "dp")),
        P("mp", "dp"),
        P("dp"),
        P("dp"),
        P("dp"),
        P("dp", "mp"),
        P(("mp", "dp")),
        P("mp", "dp"),
        P("dp"),
        P("dp"),
    )
    groups = mesh.shape["dp"]
    fits = groups <= 16 and mesh.shape["mp"] == 2
    return jax.shard_map(
        functools.partial(per_device, groups) if fits else by_collectives,
        mesh=mesh,
        in_specs=in_specs,
        out_specs=out_specs,
        check_vma=False,
    )
```

```python
import functools
import math

import jax
import jax.numpy as jnp
from jax import lax
from jax.experimental import pallas as pl
from jax.experimental.pallas import tpu as pltpu
from jax.sharding import PartitionSpec as P

HEAD = 64
EPS = 1e-05
MASKED = -1e30
MESH = pl.DeviceIdType.MESH
BF = jnp.bfloat16
F32 = jnp.float32
MIB = 2**20


def nn(a, b):
    return jnp.dot(a, b, preferred_element_type=F32)


def nt(a, b):
    return lax.dot_general(a, b, (((1,), (1,)), ((), ())), preferred_element_type=F32)


def tn(a, b):
    return lax.dot_general(a, b, (((0,), (0,)), ((), ())), preferred_element_type=F32)


def gelu(h):
    return 0.5 * h * (1.0 + lax.erf(h * math.sqrt(0.5)))


def gelu_slope(h):
    bell = jnp.exp(-0.5 * h * h) * (1.0 / math.sqrt(2.0 * math.pi))
    return 0.5 * (1.0 + lax.erf(h * math.sqrt(0.5))) + h * bell


def row_of(vector):
    return vector[None, :].astype(F32)


def exact(a, b):
    return jnp.dot(a, b, preferred_element_type=F32, precision=lax.Precision.HIGHEST)


def one_hot(shape, shift, dtype=F32):
    row = lax.broadcasted_iota(jnp.int32, shape, 0)
    column = lax.broadcasted_iota(jnp.int32, shape, 1)
    return (row == column + shift).astype(dtype)


def standard(rows):
    center = jnp.mean(rows, axis=-1, keepdims=True)
    spread = rows - center
    second = jnp.mean(spread * spread, axis=-1, keepdims=True)
    inverse = lax.rsqrt(second + EPS)
    return spread * inverse, inverse


def norm_back(grad, scaled, inverse):
    first = jnp.mean(grad, axis=-1, keepdims=True)
    second = jnp.mean(grad * scaled, axis=-1, keepdims=True)
    return inverse * (grad - first - scaled * second)


def flip(index, bit):
    return index + bit * (1 - 2 * lax.rem(lax.div(index, bit), 2))


def mult(value, step):
    return pl.multiple_of(value, step)


def tower(
    nd,
    query_total,
    lengths,
    tokens,
    queries,
    positives,
    w_qkv,
    b_qv,
    w_out,
    b_out,
    gain_one,
    shift_one,
    w_in,
    b_in,
    w_back,
    b_back,
    gain_two,
    out_act,
    h_coef,
    h_rank,
    h_factor,
    h_active,
    h_inner,
    h_context,
    h_qcls,
    h_dctx,
    h_norm,
    h_ffn,
    h_attn,
    h_tok,
    h_sums,
    h_sums_in,
    h_loss,
    h_qgrad,
    tok,
    wq,
    wq_far,
    wo,
    wi,
    wb,
    keyb,
    valb,
    ctx,
    norm_low,
    acc,
    act_far,
    obuf,
    chance,
    factor,
    stage,
    tcls,
    pack,
    gath,
    ctx_all,
    tok_all,
    q_all,
    xh1_all,
    norm_all,
    inner_all,
    act_all,
    low_all,
    dc_all,
    qc_all,
    d1_all,
    dq_rows,
    rank_f,
    coef_own,
    coef_far,
    dq_far,
    fac_send,
    loc_sem,
    ysend,
    yrecv,
    w_send,
    w_recv,
    o_send,
    o_recv,
    o_loc,
    g_send,
    g_recv,
    gs_send,
    gs_recv,
    f_send,
    f_recv,
    m_send,
    m_recv,
    b_send,
    b_recv,
    bin_own,
    bin_far,
    out_sem,
    o_coef,
    o_rank,
    o_factor,
    o_active,
    o_inner,
    o_context,
    o_qcls,
    o_dctx,
    o_norm,
    o_ffn,
    o_attn,
    o_tok,
    o_sums,
    o_sums_in,
    o_loss,
    o_qgrad,
):
    dp = lax.axis_index("dp")
    mp = lax.axis_index("mp")
    far = 1 - mp
    chips = nd // 2
    core = lax.rem(dp, 2)
    chip = lax.div(dp, 2)
    bit_a = lax.rem(lax.div(dp, 2), 2)
    bit_b = lax.rem(lax.div(dp, 4), 2)
    quarter = bit_a + 2 * bit_b
    quarter_x = flip(quarter, 1)
    quarter_z = flip(quarter, 2)
    quarter_d = 3 - quarter
    pair = (dp, far)
    sibling = (flip(dp, 1), mp)
    near_x = (flip(dp, 2), mp)
    near_z = (flip(dp, 4), mp)

    rows, width = tok.shape
    count = lengths.shape[0]
    slot = rows // count
    own = count // 2
    half = width // 2
    own_rows = own * slot
    passages = nd * count
    blocks, unit = wi.shape[1], wi.shape[3]
    m_col = mult(mp * half, 128)
    f_col = mult(far * half, 128)

    barrier = pltpu.get_barrier_semaphore()

    def greet(i, carry):
        other = lax.rem(dp * 2 + mp + i, 2 * nd)
        pl.semaphore_signal(
            barrier,
            inc=1,
            device_id=(lax.div(other, 2), lax.rem(other, 2)),
            device_id_type=MESH,
        )
        return carry

    lax.fori_loop(1, 2 * nd, greet, 0)

    def local(src, dst, k):
        return pltpu.make_async_copy(src, dst, loc_sem.at[k])

    loads = [local(tokens, tok, 0)]
    loads += [local(w_qkv.at[j], wq.at[:, pl.ds(j * half, half)], 1 + j) for j in range(3)]
    loads.append(local(w_out, wo.at[pl.ds(mult(mp * half, 128), half), :], 4))
    loads += [
        local(w_in.at[:, pl.ds(u * unit, unit)], wi.at[mp, u], 5 + u) for u in range(blocks)
    ]
    loads += [
        local(w_back.at[pl.ds(u * unit, unit), :], wb.at[mp, u], 5 + blocks + u)
        for u in range(blocks)
    ]
    for copy in loads:
        copy.start()

    chunks = 7
    direct = (3, 6)
    lead = pl.ds(0, blocks - 1)

    def piece(k, q, c, which, side=None):
        cols = pl.ds(0, width) if side is None else pl.ds(side * half, half)
        if k in direct:
            size = half // 2 if k == 3 else unit // 2
            if k == 3:
                return wo.at[pl.ds(mult(which * half + c * size, 16), size), cols]
            return wb.at[which, blocks - 1, pl.ds(mult(c * size, 16), size), cols]
        size = unit // 8 if k == 5 else width // 8
        at = (c * 4 if q is None else c * 4 + q) * size
        size = 4 * size if q is None else size
        if k == 5:
            return wb.at[which, lead, pl.ds(mult(at, 16), size), cols]
        if side is not None:
            size = size // 2
            at = at + side * size
        here = pl.ds(mult(at, 16), size)
        return wq_far.at[here, pl.ds(k * half, half)] if k < 3 else wi.at[which, :, here, :]

    def sent_bytes(k):
        if k in direct:
            return piece(k, None, core, far)
        if k < 3:
            return wq_far.at[pl.ds(0, 7 * width // 8), pl.ds(k * half, half)]
        if k == 4:
            return wi.at[far, :, pl.ds(0, 7 * width // 8), :]
        return wb.at[far, lead, pl.ds(0, 7 * unit // 8), :]

    def source(k):
        if k < 3:
            return w_qkv.at[k, pl.ds(mult((core * 4 + quarter) * (width // 8), 16), width // 8), :]
        if k == 3:
            return w_out.at[pl.ds(mult(core * (half // 2), 16), half // 2), :]
        return piece(k, quarter, core, mp)

    def remote(src, dst, ss, rs, device):
        return pltpu.make_async_remote_copy(
            src_ref=src,
            dst_ref=dst,
            send_sem=ss,
            recv_sem=rs,
            device_id=device,
            device_id_type=MESH,
        )

    def cross(k):
        return remote(
            source(k), piece(k, quarter, core, mp), ysend.at[k], yrecv.at[k], pair
        )

    def send(k, lane, q, c, side, device):
        ref = piece(k, q, c, far, side)
        return remote(ref, ref, w_send.at[k], w_recv.at[k, lane], device)

    def lane(k, n):
        q = (quarter, quarter, quarter_z, quarter_x, None)[n]
        side = (None, None, 0, 1, None)[n]
        return send(k, n, q, core, side, (near_x, near_z, near_x, near_z, sibling)[n])

    def arrival(k, n):
        q = (quarter_x, quarter_z, quarter_d, quarter_d, None)[n]
        side = (None, None, 0, 1, None)[n]
        c = core if n < 4 else 1 - core
        return send(k, n, q, c, side, (near_x, near_z, near_x, near_z, sibling)[n])

    def step_one(k):
        remote(
            source(k), piece(k, quarter, core, far), ysend.at[k], yrecv.at[k], pair
        ).wait_recv()
        for n in (4,) if k in direct else (0, 1):
            lane(k, n).start()

    def step_two(k):
        arrival(k, 1).wait_recv()
        lane(k, 2).start()
        arrival(k, 0).wait_recv()
        lane(k, 3).start()

    def step_three(k):
        arrival(k, 2).wait_recv()
        arrival(k, 3).wait_recv()
        lane(k, 4).start()

    def complete(k):
        arrival(k, 4).wait_recv()

    def spent(window, sem):
        pltpu.make_async_copy(window, window, sem).wait()

    def advance(*steps):
        for stage_of, k in steps:
            (step_one, step_two, step_three)[stage_of - 1](k)

    for copy in loads[:4]:
        copy.wait()
    bin_own[...] = jnp.zeros_like(bin_own)
    for u in range(blocks):
        bin_own[u : u + 1, :] = row_of(b_in[pl.ds(u * unit, unit)])
    bin_own[6:8, 0:half] = b_qv[...].astype(F32)
    bias_copy = remote(bin_own, bin_far, b_send, b_recv, pair)

    lane_pair = lax.broadcasted_iota(jnp.int32, (slot, 128), 1)
    key_place = lax.broadcasted_iota(jnp.int32, (1, slot), 1)
    head_rows = lax.broadcasted_iota(jnp.int32, (8, half), 0)
    head_mask = head_rows == lax.div(lax.broadcasted_iota(jnp.int32, (8, half), 1), HEAD)
    heads = half // HEAD
    live = lax.broadcasted_iota(jnp.int32, (8, 1), 0) < heads
    bias_q = b_qv[0:1, :].astype(F32)
    bias_v = b_qv[1:2, :].astype(F32)
    ones = jnp.ones((slot, 128), BF)
    row_place = lax.broadcasted_iota(jnp.int32, (8, slot), 0)
    first_key = (lax.broadcasted_iota(jnp.int32, (8, slot), 1) == 0).astype(F32)

    def mix(query, keyed, value, bias):
        done = []
        for t in range(half // 128):
            q2 = query[:, 128 * t : 128 * t + 128]
            k2 = keyed[:, 128 * t : 128 * t + 128]
            v2 = jnp.concatenate([value[:, 128 * t : 128 * t + 128], ones], axis=1)
            parts = []
            for hx in range(2):
                mask = (lane_pair < HEAD) if hx == 0 else (lane_pair >= HEAD)
                s = nt(jnp.where(mask, q2, jnp.zeros_like(q2)), k2) + bias
                e = jnp.exp(s - jnp.max(s, axis=1, keepdims=True)).astype(BF)
                o = nn(e, v2)
                parts.append(o[:, :128] / o[:, 128:])
            done.append(jnp.where(lane_pair < HEAD, parts[0], parts[1]))
        return jnp.concatenate(done, axis=1).astype(BF)

    def first_row(p, x, query, keyed, value, bias):
        tcls[pl.ds(p, 1), :] = x[0:16, :].astype(F32)[0:1, :]
        q_heads = jnp.where(head_mask, query.astype(F32)[0:1, :], 0.0).astype(BF)
        s = nt(q_heads, keyed) + bias
        e = jnp.exp(s - jnp.max(s, axis=1, keepdims=True))
        c = jnp.where(live, e / jnp.sum(e, axis=1, keepdims=True), 0.0)
        chance[p] = c
        c_low = c.astype(BF)
        mixed = jnp.where(head_mask, nn(c_low, value), 0.0)
        stage[pl.ds(p, 1), :] = jnp.sum(mixed, axis=0, keepdims=True)
        coef_own[pl.ds(mult(p * 16, 16), 8), :] = jnp.where(row_place == heads, first_key, c)
        factor[pl.ds(mult(p * 8, 8), 8), :] = nn(c_low, x)

    theirs_plan = (((1, 0),), (), ((1, 1),), ())
    gap_plan = ((2, 0), (1, 2), (2, 1), (3, 0), (2, 2), (1, 4), (3, 1), (3, 2))
    far_plan = ((), (), (), ((1, 3),))
    feed_plan = (((2, 4),), ((1, 5),), (), ((3, 4),))
    in_plan = ((((2, 5), (1, 6)), ()), ((), ()), ((), ((3, 5),)))

    def move_on(i, plan):
        for j, steps in enumerate(plan):
            if steps:

                @pl.when(i == j)
                def _():
                    advance(*steps)

    def key_bias(p):
        return jnp.where(key_place < lengths[p], 0.0, MASKED)

    def attend_theirs(i, carry):
        move_on(i, theirs_plan)
        p = far * own + i
        at = mult(p * slot, slot)
        x = tok[pl.ds(at, slot), :]
        made = nn(x, wq[:, half:])
        keyed = made[:, :half].astype(BF)
        value = (made[:, half:] + bias_v).astype(BF)
        keyb[pl.ds(at, slot), :] = keyed
        valb[pl.ds(at, slot), :] = value
        query = ((nn(x[0:16, :], wq[:, :half]) + bias_q).astype(BF).astype(F32) * 0.125).astype(BF)
        first_row(p, x, query, keyed, value, key_bias(p))
        return carry

    def attend_own(i, carry):
        @pl.when(i == 1)
        def _():
            pl.semaphore_wait(barrier, 2 * nd - 1)
            for copy in loads[4:]:
                copy.wait()
            bias_copy.start()
            for k in (0, 1, 2, 4, 3):
                cross(k).start()

        p = mp * own + i
        at = mult(p * slot, slot)
        x = tok[pl.ds(at, slot), :]
        made = nn(x, wq[...])
        query = ((made[:, :half] + bias_q).astype(BF).astype(F32) * 0.125).astype(BF)
        keyed = made[:, half : 2 * half].astype(BF)
        value = (made[:, 2 * half :] + bias_v).astype(BF)
        keyb[pl.ds(at, slot), :] = keyed
        valb[pl.ds(at, slot), :] = value
        bias = key_bias(p)
        ctx[pl.ds(mult(i * slot, slot), slot), pl.ds(m_col, half)] = mix(query, keyed, value, bias)
        first_row(p, x, query[0:16, :], keyed, value, bias)
        return carry

    def attend_far(i, carry):
        move_on(i, far_plan)
        p = mp * own + i
        x = tok[pl.ds(mult(p * slot, slot), slot), :]
        made = nn(x, wq_far[...])
        bias_far = bin_far[6:8, 0:half]
        query = ((made[:, :half] + bias_far[0:1, :]).astype(BF).astype(F32) * 0.125).astype(BF)
        keyed = made[:, half : 2 * half].astype(BF)
        value = (made[:, 2 * half :] + bias_far[1:2, :]).astype(BF)
        ctx[pl.ds(mult(i * slot, slot), slot), pl.ds(f_col, half)] = mix(
            query, keyed, value, key_bias(p)
        )
        return carry

    lax.fori_loop(0, own, attend_own, 0)
    lax.fori_loop(0, own, attend_theirs, 0)

    pack[0:8, :] = stage[...]
    pack[8:16, :] = tcls[:, pl.ds(m_col, half)]
    pack[16:32, :] = jnp.zeros((16, half), F32)
    q_rows = queries.shape[0]
    pack[16 : 16 + q_rows, :] = queries[:, pl.ds(m_col, half)].astype(F32)
    gath[chip, core, mp] = pack[...].astype(BF)

    here = gath.at[chip, core, mp]
    to_pair = remote(here, here, gs_send.at[0], gs_recv.at[0], pair)
    to_pair.start()
    advance(*gap_plan)
    bias_copy.wait_recv()
    for k in range(3):
        complete(k)

    def gather_start(i, carry):
        both = gath.at[chip, core]
        there = lax.rem(chip + i, chips) * 2 + core
        remote(both, both, g_send, g_recv, (there, mp)).start()
        return carry

    gather_window = tok.at[pl.ds(0, (chips - 1) * 32), :]
    for k in (5, 6):
        cross(k).start()

    lax.fori_loop(0, own, attend_far, 0)
    remote(
        here, gath.at[chip, core, far], gs_send.at[0], gs_recv.at[0], pair
    ).wait_recv()
    lax.fori_loop(1, chips, gather_start, 0)

    complete(3)
    bo = row_of(b_out[...])
    g1 = row_of(gain_one[...])
    s1 = row_of(shift_one[...])
    g2 = row_of(gain_two[...])
    bb = row_of(b_back[...])

    def feed_own(i, carry):
        move_on(i, feed_plan)
        at = mult(i * slot, slot)
        here = pl.ds(at, slot)
        x = tok[pl.ds(mult(mp * own_rows + i * slot, slot), slot), :].astype(F32)
        resid = x + nn(ctx[here, :], wo[...]) + bo
        scaled, _ = standard(resid)
        norm = scaled * g1 + s1
        low = norm.astype(BF)
        norm_low[here, :] = low
        total = norm + bb
        for u in range(blocks):
            inner = nn(low, wi[mp, u]) + bin_own[u : u + 1, :]
            total = total + nn(gelu(inner).astype(BF), wb[mp, u])
        acc[here, :] = total

        return carry

    lax.fori_loop(0, own, feed_own, 0)

    complete(4)
    for u in range(blocks):

        def feed_far_in(i, carry, u=u):
            move_on(i, in_plan[u])
            here = pl.ds(mult(i * 2 * slot, slot), 2 * slot)
            inner = nn(norm_low[here, :], wi[far, u]) + bin_far[u : u + 1, :]
            act_far[u, here, :] = gelu(inner).astype(BF)
            return carry

        lax.fori_loop(0, own // 2, feed_far_in, 0)

    def feed_far_back(u):
        def feed(i, carry):
            here = pl.ds(mult(i * 2 * slot, slot), 2 * slot)
            acc[here, :] += nn(act_far[u, here, :], wb[far, u])
            return carry

        lax.fori_loop(0, own // 2, feed, 0)

    complete(5)
    feed_far_back(0)

    for u in range(1, blocks - 1):
        feed_far_back(u)
    spent(gather_window, g_recv)
    to_sibling = remote(
        gath.at[:, core], gath.at[:, core], gs_send.at[1], gs_recv.at[1], sibling
    )
    to_sibling.start()

    complete(chunks - 1)

    def out_copy(i, mine):
        side = mp if mine else far
        there = out_act.at[pl.ds(mult(side * own_rows + i * slot, 16), slot), :]
        return remote(
            obuf.at[1, pl.ds(mult(i * slot, 16), slot), :], there, o_send.at[i], o_recv.at[i], pair
        )

    def out_local(i):
        there = out_act.at[pl.ds(mult(mp * own_rows + i * slot, 16), slot), :]
        return pltpu.make_async_copy(
            obuf.at[0, pl.ds(mult(i * slot, 16), slot), :], there, o_loc.at[i]
        )

    def finish(i, carry):
        here = pl.ds(mult(i * slot, slot), slot)
        total = acc[here, :] + nn(act_far[blocks - 1, here, :], wb[far, blocks - 1])
        scaled, _ = standard(total)
        acc[here, :] = scaled * g2
        obuf[0, here, :] = acc[here, pl.ds(m_col, half)].astype(BF)
        obuf[1, here, :] = acc[here, pl.ds(f_col, half)].astype(BF)
        @pl.when(i < own - 1)
        def _():
            out_copy(i, True).start()

        out_local(i).start()
        return carry

    lax.fori_loop(0, own, finish, 0)

    remote(
        gath.at[:, 1 - core], gath.at[:, 1 - core], gs_send.at[1], gs_recv.at[1], sibling
    ).wait_recv()
    q_pad = nd * 16
    for h in range(2):
        cols = slice(h * half, (h + 1) * half)
        block = gath[:, :, h].astype(F32)
        ctx_all[:, cols] = block[:, :, 0:8].reshape(passages, half).astype(BF)
        tok_all[:, cols] = block[:, :, 8:16].reshape(passages, half).astype(BF)
        q_all[:, cols] = block[:, :, 16:32].reshape(q_pad, half).astype(BF)
    resid = tok_all[...].astype(F32) + nn(ctx_all[...], wo[...]) + bo
    scaled, inverse1 = standard(resid)
    xh1_all[...] = scaled
    norm = scaled * g1 + s1
    low = norm.astype(BF)
    norm_all[...] = low
    total = norm + bb
    for which, bias in ((mp, bin_own), (far, bin_far)):
        for u in range(blocks):
            inner = nn(low, wi[which, u]) + bias[u : u + 1, :]
            inner_all[which, u] = inner
            active = gelu(inner).astype(BF)
            act_all[which, u] = active
    for u in range(blocks):
        total = total + nn(act_all[mp, u], wb[mp, u])
    total = total + nn(act_all[far, 0], wb[far, 0])
    for u in range(1, blocks):
        total = total + nn(act_all[far, u], wb[far, u])

    xh2, inverse2 = standard(total)
    cls = (xh2 * g2).astype(BF)
    similar = nt(cls, q_all[...])
    top = jnp.max(similar, axis=0, keepdims=True)
    log_sum = top + jnp.log(jnp.sum(jnp.exp(similar - top), axis=0, keepdims=True))
    q_count = query_total // nd
    from_q = lax.broadcasted_iota(jnp.int32, (query_total, q_pad), 0)
    to_q = lax.broadcasted_iota(jnp.int32, (query_total, q_pad), 1)
    spot = lax.div(from_q, q_count) * 16 + lax.rem(from_q, q_count)
    wanted = jnp.broadcast_to(row_of(positives[...]), (8, query_total)) + 1.0
    place = exact(wanted, (spot == to_q).astype(F32))[0:1, :] - 1.0
    target = lax.broadcasted_iota(jnp.int32, similar.shape, 0).astype(F32) == place
    picked = jnp.sum(jnp.where(target, similar, 0.0), axis=0, keepdims=True)
    o_loss[...] = jnp.broadcast_to(log_sum - picked, o_loss.shape)
    slopes = (jnp.exp(similar - log_sum) - target.astype(F32)) * (1.0 / query_total)
    slope_high = slopes.astype(BF)
    slope_low = (slopes - slope_high.astype(F32)).astype(BF)
    cls_grad = nn(slope_high, q_all[...]) + nn(slope_low, q_all[...])
    pick = (
        lax.broadcasted_iota(jnp.int32, (16, q_pad), 1)
        == lax.broadcasted_iota(jnp.int32, (16, q_pad), 0) + dp * 16
    ).astype(BF)
    o_qgrad[...] = nn(nt(pick, slope_high).astype(BF), cls) + nn(
        nt(pick, slope_low).astype(BF), cls
    )
    d_two = norm_back(g2 * cls_grad, xh2, inverse2)
    o_sums[0:1, :] = jnp.sum(cls_grad * xh2, axis=0, keepdims=True)
    o_sums[1:2, :] = jnp.sum(d_two, axis=0, keepdims=True)
    ffn_low = d_two.astype(BF)
    o_ffn[...] = ffn_low
    back = d_two
    for h in range(2):
        for u in range(blocks):
            d_active = nt(ffn_low, wb[h, u])
            d_inner = d_active * gelu_slope(inner_all[h, u])
            inner_all[h, u, 0:8, :] = jnp.broadcast_to(
                jnp.sum(d_inner, axis=0, keepdims=True), (8, unit)
            )
            inner_low = d_inner.astype(BF)
            low_all[h, u] = inner_low
            back = back + nt(inner_low, wi[h, u])
    for u in range(blocks):
        o_active[u] = act_all[mp, u]
        o_inner[u] = low_all[mp, u]
        o_sums_in[u : u + 1, :] = inner_all[mp, u, 0:1, :]
    xh1 = xh1_all[...]
    d_one = norm_back(g1 * back, xh1, inverse1)
    d1_all[...] = d_one
    o_sums[2:3, :] = jnp.sum(back * xh1, axis=0, keepdims=True)
    o_sums[3:4, :] = jnp.sum(back, axis=0, keepdims=True)
    o_sums[4:5, :] = jnp.sum(d_one, axis=0, keepdims=True)
    attn_low = d_one.astype(BF)
    o_attn[...] = attn_low
    o_norm[...] = norm_all[...]
    o_tok[...] = tok_all[...]
    d_ctx = nt(attn_low, wo[pl.ds(mult(mp * half, 128), half), :]).astype(BF)
    o_dctx[...] = d_ctx
    dc_all[...] = d_ctx.astype(F32)
    q_cls = (nn(tok_all[...], wq[:, 0:half]) + bias_q).astype(BF)
    o_qcls[...] = q_cls
    qc_all[...] = q_cls.astype(F32) * 0.125
    o_context[...] = ctx_all[:, pl.ds(m_col, half)]
    o_sums[5:6, 0:half] = jnp.sum(dc_all[...], axis=0, keepdims=True)

    def stored(src, dst, k):
        return pltpu.make_async_copy(src, dst, out_sem.at[k])

    early = [
        stored(src, dst, k)
        for k, (src, dst) in enumerate(
            (
                (o_active, h_active),
                (o_inner, h_inner),
                (o_context, h_context),
                (o_qcls, h_qcls),
                (o_dctx, h_dctx),
                (o_norm, h_norm),
                (o_ffn, h_ffn),
                (o_attn, h_attn),
                (o_tok, h_tok),
                (o_sums, h_sums),
                (o_sums_in, h_sums_in),
                (o_loss, h_loss),
                (o_qgrad, h_qgrad),
            )
        )
    ]
    for copy in early:
        copy.start()

    base = mult(dp * count, 8)
    fkind = count * 8

    mark = jnp.logical_or(row_place == heads, row_place == heads + 1)
    for p in range(count):
        d_row = dc_all[pl.ds(base + p, 1), :]
        q_row = qc_all[pl.ds(base + p, 1), :]
        rank_f[p * 16 : p * 16 + 8, 0:half] = jnp.where(head_mask, d_row, 0.0)
        rank_f[p * 16 + 8 : p * 16 + 16, 0:half] = jnp.where(head_mask, q_row, 0.0)
    kept = rank_f[:, 0:half].astype(BF)
    group = 4
    for first in range(0, count, group):
        d_scores = []
        for p in range(first, first + group):
            c = chance[p]
            d_chance = nt(kept[p * 16 : p * 16 + 16, :], valb[p * slot : (p + 1) * slot, :])[0:8, :]
            d_scores.append(c * (d_chance - jnp.sum(c * d_chance, axis=1, keepdims=True)))
        for p, d in zip(range(first, first + group), d_scores):
            s_low = d.astype(BF)
            at = slice(p * slot, (p + 1) * slot)
            coef_own[p * 16 + 8 : p * 16 + 16, :] = jnp.where(mark, first_key, d)
            factor[fkind + p * 8 : fkind + p * 8 + 8, :] = nn(s_low, tok[at, :])
            spread = nn(s_low, keyb[at, :])
            dq_rows[p : p + 1, :] = 0.125 * jnp.sum(
                jnp.where(head_mask, spread, 0.0), axis=0, keepdims=True
            )

    turned = jnp.transpose(factor[...]).astype(BF)
    dq = dq_rows[...]
    for b in range(half // 128):
        pack[b * 8 : b * 8 + 8, 0:128] = dq[:, b * 128 : b * 128 + 128]
    pack[half // 16 : 32, 0:128] = jnp.zeros((32 - half // 16, 128), F32)
    dq_low = pack[:, 0:128].astype(BF)
    share = width // nd
    for j in range(nd):
        fac_send[j, 0:share, :] = turned[j * share : (j + 1) * share, :]
        fac_send[j, share:, :] = dq_low
    o_factor[dp] = fac_send[dp]

    def factor_start(i, carry):
        there = lax.rem(dp + i, nd)
        remote(fac_send.at[there], o_factor.at[dp], f_send, f_recv, (there, mp)).start()
        return carry

    lax.fori_loop(1, nd, factor_start, 0)

    coef_low = coef_own[...].astype(BF)
    o_coef[0] = coef_low
    coef_far_copy = remote(o_coef.at[0], coef_far, m_send.at[0], m_recv.at[0], pair)
    coef_far_copy.start()
    dq_copy = remote(dq_rows, dq_far, m_send.at[1], m_recv.at[1], pair)
    dq_copy.start()
    out_copy(own - 1, True).start()
    kind = lax.rem(lax.div(lax.broadcasted_iota(jnp.int32, (count * 16, 1), 0), 8), 2)
    d1_rows = d1_all[pl.ds(base, count), :]
    d_far = nt(d1_rows.astype(BF), wo[pl.ds(mult(far * half, 128), half), :])
    q_far = (nn(tcls[...].astype(BF), wq_far[:, 0:half]) + bin_far[6:7, 0:half]) * 0.125
    for p in range(count):
        rank_f[p * 16 : p * 16 + 8, 0:half] = jnp.where(head_mask, d_far[p : p + 1, :], 0.0)
        rank_f[p * 16 + 8 : p * 16 + 16, 0:half] = jnp.where(head_mask, q_far[p : p + 1, :], 0.0)
    kept_far = rank_f[:, 0:half].astype(BF)
    my_rows = pl.ds(mult(mp * half, 128), half)

    def rank_rows(left, right):
        by_v = nt(left, right[my_rows, 2 * half :])
        by_k = nt(left, right[my_rows, half : 2 * half])
        return jnp.where(kind == 0, by_v, by_k)

    rank_f[:, 0:half] = rank_rows(kept, wq)
    rank_f[:, half:] = rank_rows(kept_far, wq_far)
    d1_mine = d1_all[pl.ds(base, count), pl.ds(m_col, half)]
    d1_high = d1_mine.astype(BF).astype(F32)
    d1_low = d1_mine - d1_high

    def first_rank(cols, back_q, high, low):
        for p in range(count):
            rank_f[p * 16 + heads : p * 16 + heads + 1, cols] = back_q[p : p + 1, :]
            rank_f[p * 16 + heads + 1 : p * 16 + 8, cols] = jnp.zeros((7 - heads, half), F32)
            rank_f[p * 16 + 8 + heads : p * 16 + 9 + heads, cols] = high[p : p + 1]
            rank_f[p * 16 + 9 + heads : p * 16 + 10 + heads, cols] = low[p : p + 1]

    mine = slice(0, half)
    theirs = slice(half, width)
    first_rank(mine, nt(dq.astype(BF), wq[my_rows, 0:half]), d1_high, d1_low)
    o_rank[0] = rank_f[:, mine].astype(BF)

    dq_copy.wait_recv()
    nothing = jnp.zeros((count, half), F32)
    first_rank(theirs, nt(dq_far[...].astype(BF), wq_far[my_rows, 0:half]), nothing, nothing)
    o_rank[1] = rank_f[:, theirs].astype(BF)
    coef_far_copy.wait_recv()
    o_coef[1] = coef_far[...]
    factor_window = fac_send.at[pl.ds(0, nd - 1)]
    spent(factor_window, f_recv)
    last = [stored(o_factor, h_factor, 15), stored(o_coef, h_coef, 13), stored(o_rank, h_rank, 14)]
    for copy in last:
        copy.start()
    spent(factor_window, f_send)
    coef_far_copy.wait_send()
    dq_copy.wait_send()
    bias_copy.wait_send()
    spent(gather_window, g_send)
    to_sibling.wait_send()
    to_pair.wait_send()
    for k in range(chunks):
        cross(k).wait_send()
        spent(sent_bytes(k), w_send.at[k])

    def drain(i, carry):
        out_copy(i, True).wait_send()
        out_copy(i, False).wait_recv()
        out_local(i).wait()
        return carry

    lax.fori_loop(0, own, drain, 0)
    for copy in early + last:
        copy.wait()


def gradients(
    nd,
    act_in,
    coef_in,
    rank_in,
    factor_in,
    active_in,
    inner_in,
    context_in,
    qcls_in,
    dctx_in,
    norm_in,
    ffn_in,
    attn_in,
    tok_in,
    sums_in,
    sums_units_in,
    loss_in,
    qgrad_in,
    act_out,
    query_loss,
    input_grad,
    query_grad,
    grad_qkv,
    grad_bias_qv,
    grad_out,
    grad_bias_out,
    grad_gain_one,
    grad_shift_one,
    grad_in,
    grad_bias_in,
    grad_back,
    grad_bias_back,
    grad_gain_two,
    coef,
    rank,
    factor,
    active,
    inner,
    context,
    qcls,
    dctx,
    norm,
    ffn,
    attn,
    tok,
    sums,
    sums_units,
    loss,
    qgrad,
    sems,
    act_sem,
    act_buf,
    in_buf,
    in_sems,
    rhs,
):
    dp = lax.axis_index("dp")
    act_load = pltpu.make_async_copy(act_in, act_buf, act_sem.at[0])
    act_store = pltpu.make_async_copy(act_buf, act_out, act_sem.at[1])
    act_load.start()
    pairs = (
        (coef_in, coef),
        (rank_in, rank),
        (factor_in, factor),
        (qcls_in, qcls),
        (dctx_in, dctx),
        (active_in, active),
        (inner_in, inner),
        (context_in, context),
        (norm_in, norm),
        (ffn_in, ffn),
        (attn_in, attn),
        (tok_in, tok),
        (sums_in, sums),
        (sums_units_in, sums_units),
        (loss_in, loss),
        (qgrad_in, qgrad),
    )
    loads = [pltpu.make_async_copy(src, dst, sems.at[i]) for i, (src, dst) in enumerate(pairs)]
    for load in loads:
        load.start()
    passages, width = ffn.shape
    half = width // 2
    share = width // nd
    count = passages // nd
    slot = coef.shape[2]
    for load in loads[:2]:
        load.wait()

    def input_copy(p):
        at = pl.ds(mult(p * slot, slot), slot)
        return pltpu.make_async_copy(in_buf.at[at, :], input_grad.at[at, :], in_sems.at[p])

    def input_rows(p, carry):
        rows16 = pl.ds(mult(p * 16, 16), 16)
        both = jnp.concatenate([coef[0, rows16, :], coef[1, rows16, :]], axis=0)
        right = jnp.concatenate([rank[0, rows16, :], rank[1, rows16, :]], axis=0)
        in_buf[pl.ds(mult(p * slot, slot), slot), :] = tn(both, right)
        input_copy(p).start()
        return carry

    lax.fori_loop(0, count, input_rows, 0)
    act_load.wait()
    act_store.start()
    for load in loads[2:]:
        load.wait()

    spread = lax.broadcasted_iota(jnp.int32, (8, half), 0) == lax.div(
        lax.broadcasted_iota(jnp.int32, (8, half), 1), HEAD
    )
    fkind = count * 8

    def build(s, carry):
        d_rows = dctx[pl.ds(mult(s * 2 * count, 16), 2 * count), :].astype(F32)
        q_rows = qcls[pl.ds(mult(s * 2 * count, 16), 2 * count), :].astype(F32) * 0.125
        k_blocks = [jnp.where(spread, q_rows[p : p + 1, :], 0.0) for p in range(2 * count)]
        v_blocks = [jnp.where(spread, d_rows[p : p + 1, :], 0.0) for p in range(2 * count)]
        here = pl.ds(mult(s * 2 * fkind, 16), 2 * fkind)
        rhs[here, 0:half] = jnp.concatenate(k_blocks, 0).astype(BF)
        rhs[here, half:] = jnp.concatenate(v_blocks, 0).astype(BF)
        return carry

    lax.fori_loop(0, nd // 2, build, 0)
    grad_k = jnp.zeros((share, half), F32)
    grad_v = jnp.zeros((share, half), F32)
    for s in range(0, nd, 4):
        left_v = jnp.concatenate([factor[s + t, 0:share, :][:, 0:fkind] for t in range(4)], axis=1)
        left_k = jnp.concatenate([factor[s + t, 0:share, :][:, fkind:] for t in range(4)], axis=1)
        grad_k = grad_k + nn(left_k, rhs[s * fkind : (s + 4) * fkind, 0:half])
        grad_v = grad_v + nn(left_v, rhs[s * fkind : (s + 4) * fkind, half:])
    grad_qkv[1] = grad_k
    grad_qkv[2] = grad_v

    pick = one_hot((width, share), dp * share)
    pick_low = pick.astype(BF)
    row = lax.broadcasted_iota(jnp.int32, (share, width), 0)
    column = lax.broadcasted_iota(jnp.int32, (share, width), 1)
    pick_t = (column == row + dp * share).astype(BF)
    ffn_own = nt(pick_t, ffn[...]).astype(BF)
    attn_own = nt(pick_t, attn[...]).astype(BF)
    norm_own = nt(pick_t, norm[...]).astype(BF)
    tok_own = nt(pick_t, tok[...]).astype(BF)
    grad_out[...] = nn(attn_own, context[...])
    unit = active.shape[2]
    blocks = active.shape[0]
    for u in range(blocks):
        cols = slice(u * unit, (u + 1) * unit)
        grad_back[:, cols] = nn(ffn_own, active[u])
        grad_in[:, cols] = nn(norm_own, inner[u])
    dq_sum = []
    for b in range(half // 128):
        cols = factor[:, share:, :].astype(F32)[:, b * 8 : b * 8 + 8, :].reshape(passages, 128)
        dq_sum.append(jnp.sum(cols, axis=0, keepdims=True))
        grad_qkv[0, :, b * 128 : b * 128 + 128] = nn(tok_own, cols.astype(BF))

    mine = exact(sums[...], pick)
    grad_gain_two[...] = mine[0:1, :].reshape(share)
    grad_bias_back[...] = mine[1:2, :].reshape(share)
    grad_gain_one[...] = mine[2:3, :].reshape(share)
    grad_shift_one[...] = mine[3:4, :].reshape(share)
    grad_bias_out[...] = mine[4:5, :].reshape(share)
    part = half // nd
    both = jnp.concatenate([jnp.concatenate(dq_sum, axis=1), sums[5:6, 0:half]], axis=0)
    wide = jnp.concatenate([both, jnp.zeros((6, half), F32)], axis=0)
    grad_bias_qv[...] = exact(wide, one_hot((half, part), dp * part))[0:2, :]
    in_share = grad_bias_in.shape[0]
    total = jnp.zeros((8, in_share), F32)
    for u in range(blocks):
        total = total + exact(
            jnp.broadcast_to(sums_units[u : u + 1, :], (8, unit)),
            one_hot((unit, in_share), dp * in_share - u * unit),
        )
    grad_bias_in[...] = total[0:1, :].reshape(in_share)
    q_rows = query_loss.shape[0]
    query_loss[...] = exact(loss[...], one_hot((loss.shape[1], q_rows), dp * 16))[0:1, :].reshape(q_rows)
    query_grad[...] = qgrad[0:q_rows, :]

    def input_wait(p, carry):
        input_copy(p).wait()
        return carry

    lax.fori_loop(0, count, input_wait, 0)
    act_store.wait()


def per_device(nd, *arrays):
    (
        tokens,
        lengths,
        queries,
        positives,
        w_qkv,
        b_qv,
        w_out,
        b_out,
        gain_one,
        shift_one,
        w_in,
        b_in,
        w_back,
        b_back,
        gain_two,
    ) = arrays
    rows, width = tokens.shape
    count = lengths.shape[0]
    slot = rows // count
    half = w_qkv.shape[2]
    units = w_in.shape[1]
    unit = 512
    blocks = units // unit
    chunks = 7
    own_rows = rows // 2
    passages = nd * count
    chips = nd // 2
    q_rows = queries.shape[0]
    q_pad = nd * 16
    share = width // nd
    vmem = pl.BlockSpec(memory_space=pltpu.VMEM)
    hbm = pl.BlockSpec(memory_space=pl.ANY)
    smem = pl.BlockSpec(memory_space=pltpu.SMEM)
    in_specs = [smem, hbm, vmem, vmem, hbm, vmem, hbm, vmem, vmem, vmem, hbm, vmem, hbm, vmem, vmem]
    shape = jax.ShapeDtypeStruct
    outs = [
        (shape((rows, half), BF), hbm),
        (shape((2, count * 16, slot), BF), hbm),
        (shape((2, count * 16, half), BF), hbm),
        (shape((nd, share + 32, 128), BF), hbm),
        (shape((blocks, passages, unit), BF), hbm),
        (shape((blocks, passages, unit), BF), hbm),
        (shape((passages, half), BF), hbm),
        (shape((passages, half), BF), hbm),
        (shape((passages, half), BF), hbm),
        (shape((passages, width), BF), hbm),
        (shape((passages, width), BF), hbm),
        (shape((passages, width), BF), hbm),
        (shape((passages, width), BF), hbm),
        (shape((8, width), F32), hbm),
        (shape((8, unit), F32), hbm),
        (shape((8, q_pad), F32), hbm),
        (shape((16, width), F32), hbm),
    ]
    dma = pltpu.SemaphoreType.DMA
    scratch = [
        pltpu.VMEM((rows, width), BF),
        pltpu.VMEM((width, 3 * half), BF),
        pltpu.VMEM((width, 3 * half), BF),
        pltpu.VMEM((width, width), BF),
        pltpu.VMEM((2, blocks, width, unit), BF),
        pltpu.VMEM((2, blocks, unit, width), BF),
        pltpu.VMEM((rows, half), BF),
        pltpu.VMEM((rows, half), BF),
        pltpu.VMEM((own_rows, width), BF),
        pltpu.VMEM((own_rows, width), BF),
        pltpu.VMEM((own_rows, width), F32),
        pltpu.VMEM((blocks, own_rows, unit), BF),
        pltpu.VMEM((2, own_rows, half), BF),
        pltpu.VMEM((count, 8, slot), F32),
        pltpu.VMEM((2 * count * 8, width), F32),
        pltpu.VMEM((8, half), F32),
        pltpu.VMEM((8, width), F32),
        pltpu.VMEM((32, half), F32),
        pltpu.VMEM((chips, 2, 2, 32, half), BF),
        pltpu.VMEM((passages, width), BF),
        pltpu.VMEM((passages, width), BF),
        pltpu.VMEM((q_pad, width), BF),
        pltpu.VMEM((passages, width), F32),
        pltpu.VMEM((passages, width), BF),
        pltpu.VMEM((2, blocks, passages, unit), F32),
        pltpu.VMEM((2, blocks, passages, unit), BF),
        pltpu.VMEM((2, blocks, passages, unit), BF),
        pltpu.VMEM((passages, half), F32),
        pltpu.VMEM((passages, half), F32),
        pltpu.VMEM((passages, width), F32),
        pltpu.VMEM((8, half), F32),
        pltpu.VMEM((count * 16, width), F32),
        pltpu.VMEM((count * 16, slot), F32),
        pltpu.VMEM((count * 16, slot), BF),
        pltpu.VMEM((count, half), F32),
        pltpu.VMEM((nd, share + 32, 128), BF),
        dma((5 + 2 * blocks,)),
        dma((chunks,)),
        dma((chunks,)),
        dma((chunks,)),
        dma((chunks, 5)),
        dma((count // 2,)),
        dma((count // 2,)),
        dma((count // 2,)),
        dma,
        dma,
        dma((2,)),
        dma((2,)),
        dma,
        dma,
        dma((2,)),
        dma((2,)),
        dma,
        dma,
        pltpu.VMEM((8, unit), F32),
        pltpu.VMEM((8, unit), F32),
        dma((16,)),
    ] + [pltpu.VMEM(o[0].shape, o[0].dtype) for o in outs[1:]]
    made = pl.pallas_call(
        functools.partial(tower, nd, nd * q_rows),
        out_shape=[o[0] for o in outs],
        in_specs=in_specs,
        out_specs=[o[1] for o in outs],
        scratch_shapes=scratch,
        compiler_params=pltpu.CompilerParams(
            collective_id=0, has_side_effects=True, vmem_limit_bytes=60 * MIB
        ),
        name="tower",
    )(
        lengths,
        tokens,
        queries,
        positives,
        w_qkv,
        b_qv,
        w_out,
        b_out,
        gain_one,
        shift_one,
        w_in,
        b_in,
        w_back,
        b_back,
        gain_two,
    )
    g_outs = [
        (shape((rows, half), BF), hbm),
        (shape((q_rows,), F32), vmem),
        (shape((rows, half), F32), hbm),
        (shape((q_rows, width), F32), vmem),
        (shape((3, share, half), F32), vmem),
        (shape((2, half // nd), F32), vmem),
        (shape((share, half), F32), vmem),
        (shape((share,), F32), vmem),
        (shape((share,), F32), vmem),
        (shape((share,), F32), vmem),
        (shape((share, units), F32), vmem),
        (shape((units // nd,), F32), vmem),
        (shape((share, units), F32), vmem),
        (shape((share,), F32), vmem),
        (shape((share,), F32), vmem),
    ]
    grads = pl.pallas_call(
        functools.partial(gradients, nd),
        out_shape=[o[0] for o in g_outs],
        in_specs=[hbm] * len(outs),
        out_specs=[o[1] for o in g_outs],
        scratch_shapes=[pltpu.VMEM(o[0].shape, o[0].dtype) for o in outs[1:]]
        + [
            dma((len(outs) - 1,)),
            dma((2,)),
            pltpu.VMEM((rows, half), BF),
            pltpu.VMEM((rows, half), F32),
            dma((count,)),
            pltpu.VMEM((nd * count * 8, width), BF),
        ],
        compiler_params=pltpu.CompilerParams(vmem_limit_bytes=62 * MIB),
        name="gradients",
    )(*made)
    grads = list(grads)
    grads[6] = grads[6].T
    grads[12] = grads[12].T
    return tuple(grads)


def layer_norm(rows, gain, shift):
    center = jnp.mean(rows, axis=-1, keepdims=True)
    spread = rows - center
    second = jnp.mean(spread * spread, axis=-1, keepdims=True)
    return spread * lax.rsqrt(second + EPS) * gain + shift


def scaled_norm(rows, gain):
    center = jnp.mean(rows, axis=-1, keepdims=True)
    spread = rows - center
    second = jnp.mean(spread * spread, axis=-1, keepdims=True)
    return spread * lax.rsqrt(second + EPS) * gain


def gelu_exact(values):
    return jax.nn.gelu(values, approximate=False)


def first_rows(values, count):
    return values.reshape((count, values.shape[0] // count) + values.shape[1:])[:, 0]


def by_collectives(
    tokens,
    lengths,
    queries,
    positives,
    w_qkv,
    b_qv,
    w_out,
    b_out,
    gain_one,
    shift_one,
    w_in,
    b_in,
    w_back,
    b_back,
    gain_two,
):
    rows, width = tokens.shape
    count = lengths.shape[0]
    slot = rows // count
    local = w_qkv.shape[2]
    heads_here = local // HEAD
    scale = 1.0 / math.sqrt(HEAD)
    projected = jnp.einsum("rd,jdc->jrc", tokens, w_qkv, preferred_element_type=F32)
    bias_qv = b_qv.astype(F32)
    query = (projected[0] + bias_qv[0]).astype(BF)
    keyed = projected[1].astype(BF)
    value = (projected[2] + bias_qv[1]).astype(BF)
    block = min(count, max(1, 512 // slot))
    blocks = count // block
    valid = lax.broadcasted_iota(jnp.int32, (count, slot), 1) < lengths[:, None]
    split_shape = (blocks, block, slot, heads_here, HEAD)

    def attend(inputs):
        query_part, keyed_part, value_part, valid_part = inputs
        scores = (
            jnp.einsum(
                "pqhd,pkhd->phqk", query_part, keyed_part, preferred_element_type=F32
            )
            * scale
        )
        scores = jnp.where(valid_part[:, None, None, :], scores, MASKED)
        top = jnp.max(scores, axis=-1, keepdims=True)
        raised = jnp.exp(scores - top)
        total = jnp.sum(raised, axis=-1, keepdims=True)
        chance_low = (raised / total).astype(BF)
        mixed = jnp.einsum(
            "phqk,pkhd->pqhd", chance_low, value_part, preferred_element_type=F32
        )
        return (mixed.astype(BF), (top + jnp.log(total))[:, :, 0, 0])

    context, log_total = lax.map(
        attend,
        (
            query.reshape(split_shape),
            keyed.reshape(split_shape),
            value.reshape(split_shape),
            valid.reshape(blocks, block, slot),
        ),
    )
    context = context.reshape(rows, local)
    log_total = log_total.reshape(count, heads_here)
    partial_attn = jnp.dot(context, w_out, preferred_element_type=F32).astype(BF)
    attended = lax.psum(partial_attn, "mp").astype(F32) + b_out.astype(F32)
    resid_one = tokens.astype(F32) + attended
    gain_one_w = gain_one.astype(F32)
    shift_one_w = shift_one.astype(F32)
    gain_two_w = gain_two.astype(F32)
    norm_one = layer_norm(resid_one, gain_one_w, shift_one_w)
    norm_low = norm_one.astype(BF)
    inner = jnp.dot(norm_low, w_in, preferred_element_type=F32) + b_in.astype(F32)
    active = gelu_exact(inner).astype(BF)
    partial_ffn = jnp.dot(active, w_back, preferred_element_type=F32).astype(BF)
    resid_two = (
        norm_one + lax.psum(partial_ffn, "mp").astype(F32) + b_back.astype(F32)
    )
    output = scaled_norm(resid_two, gain_two_w)
    column = lax.axis_index("mp") * local
    activations = lax.dynamic_slice_in_dim(output, column, local, 1).astype(BF)
    cls_low = first_rows(output, count).astype(BF)
    query_rows = queries.shape[0]
    members = lax.axis_size("dp")
    query_total = query_rows * members
    own_query = lax.axis_index("dp") * query_rows
    gathered = lax.all_gather(cls_low, "dp", axis=0, tiled=True)
    similar = jnp.einsum("qd,pd->qp", queries, gathered, preferred_element_type=F32)
    mine = lax.dynamic_slice_in_dim(positives, own_query, query_rows)
    target = lax.broadcasted_iota(jnp.int32, similar.shape, 1) == mine[:, None]
    top = jnp.max(similar, axis=1, keepdims=True)
    log_sum = top[:, 0] + jnp.log(jnp.sum(jnp.exp(similar - top), axis=1))
    picked = jnp.sum(jnp.where(target, similar, 0.0), axis=1)
    query_loss = log_sum - picked
    slopes = (jnp.exp(similar - log_sum[:, None]) - target.astype(F32)) / query_total
    query_grad = jnp.dot(slopes, gathered.astype(F32), precision=lax.Precision.HIGHEST)
    queries_wide = queries.astype(F32)
    cls_grad = lax.psum_scatter(
        jnp.einsum("qp,qd->pd", slopes, queries_wide, precision=lax.Precision.HIGHEST),
        "dp",
        scatter_dimension=0,
        tiled=True,
    )
    _, norm_two_pull = jax.vjp(scaled_norm, first_rows(resid_two, count), gain_two_w)
    d_resid_two, grad_gain_two = norm_two_pull(cls_grad)
    grad_bias_back = jnp.sum(d_resid_two, axis=0)
    ffn_low = d_resid_two.astype(BF)
    grad_back = jnp.einsum(
        "pf,pd->fd", first_rows(active, count), ffn_low, preferred_element_type=F32
    )
    d_active = jnp.einsum("pd,fd->pf", ffn_low, w_back, preferred_element_type=F32)
    _, gelu_pull = jax.vjp(gelu_exact, first_rows(inner, count))
    d_inner = gelu_pull(d_active)[0]
    grad_bias_in = jnp.sum(d_inner, axis=0)
    inner_low = d_inner.astype(BF)
    grad_in = jnp.einsum(
        "pd,pf->df", first_rows(norm_low, count), inner_low, preferred_element_type=F32
    )
    back_norm = jnp.einsum("pf,df->pd", inner_low, w_in, preferred_element_type=F32)
    d_norm_one = d_resid_two + lax.psum(back_norm, "mp")
    _, norm_one_pull = jax.vjp(layer_norm, first_rows(resid_one, count), gain_one_w, shift_one_w)
    d_resid_one, grad_gain_one, grad_shift_one = norm_one_pull(d_norm_one)
    grad_bias_out = jnp.sum(d_resid_one, axis=0)
    attn_low = d_resid_one.astype(BF)
    grad_out = jnp.einsum(
        "pc,pd->cd", first_rows(context, count), attn_low, preferred_element_type=F32
    )
    d_context = jnp.einsum("pd,cd->pc", attn_low, w_out, preferred_element_type=F32).astype(
        BF
    )
    d_context = d_context.reshape(count, heads_here, HEAD)
    query_cls = first_rows(query, count).reshape(count, heads_here, HEAD)
    keyed_heads = keyed.reshape(count, slot, heads_here, HEAD)
    value_heads = value.reshape(count, slot, heads_here, HEAD)
    scores_cls = (
        jnp.einsum("phd,pkhd->phk", query_cls, keyed_heads, preferred_element_type=F32)
        * scale
    )
    scores_cls = jnp.where(valid[:, None, :], scores_cls, MASKED)
    chance = jnp.exp(scores_cls - log_total[:, :, None])
    d_chance = jnp.einsum(
        "phd,pkhd->phk", d_context, value_heads, preferred_element_type=F32
    )
    d_value = jnp.einsum(
        "phk,phd->pkhd", chance.astype(BF), d_context, preferred_element_type=F32
    )
    d_scores = chance * (d_chance - jnp.sum(chance * d_chance, axis=-1, keepdims=True))
    scores_low = d_scores.astype(BF)
    d_query = (
        jnp.einsum("phk,pkhd->phd", scores_low, keyed_heads, preferred_element_type=F32)
        * scale
    )
    d_keyed = (
        jnp.einsum("phk,phd->pkhd", scores_low, query_cls, preferred_element_type=F32)
        * scale
    )
    d_query = d_query.reshape(count, local)
    d_value = d_value.reshape(rows, local)
    query_low = d_query.astype(BF)
    keyed_value_low = jnp.stack(
        [d_keyed.reshape(rows, local).astype(BF), d_value.astype(BF)]
    )
    grad_bias_qv = jnp.stack([jnp.sum(d_query, axis=0), jnp.sum(d_value, axis=0)])
    grad_query_w = jnp.einsum(
        "pd,pc->dc", first_rows(tokens, count), query_low, preferred_element_type=F32
    )
    grad_kv = jnp.einsum("rd,jrc->jdc", tokens, keyed_value_low, preferred_element_type=F32)
    grad_qkv = jnp.concatenate([grad_query_w[None], grad_kv], axis=0)
    own_half = lax.dynamic_slice_in_dim(d_resid_one, column, local, 1)
    back_kv = jnp.einsum(
        "jrc,jdc->rd", keyed_value_low, w_qkv[1:], preferred_element_type=F32
    )
    back_query = jnp.einsum("pc,dc->pd", query_low, w_qkv[0], preferred_element_type=F32)
    back_all = back_kv.reshape(count, slot, width).at[:, 0].add(back_query).reshape(rows, width)
    input_grad = lax.psum_scatter(
        back_all.astype(BF), "mp", scatter_dimension=1, tiled=True
    ).astype(F32)
    input_grad = input_grad.reshape(count, slot, local).at[:, 0].add(own_half).reshape(rows, local)
    summed = (
        lax.psum_scatter(grad_qkv, "dp", scatter_dimension=1, tiled=True),
        lax.psum_scatter(grad_bias_qv, "dp", scatter_dimension=1, tiled=True),
        lax.psum_scatter(grad_out, "dp", scatter_dimension=1, tiled=True),
        lax.psum_scatter(grad_bias_out, "dp", scatter_dimension=0, tiled=True),
        lax.psum_scatter(grad_gain_one, "dp", scatter_dimension=0, tiled=True),
        lax.psum_scatter(grad_shift_one, "dp", scatter_dimension=0, tiled=True),
        lax.psum_scatter(grad_in, "dp", scatter_dimension=0, tiled=True),
        lax.psum_scatter(grad_bias_in, "dp", scatter_dimension=0, tiled=True),
        lax.psum_scatter(grad_back, "dp", scatter_dimension=1, tiled=True),
        lax.psum_scatter(grad_bias_back, "dp", scatter_dimension=0, tiled=True),
        lax.psum_scatter(grad_gain_two, "dp", scatter_dimension=0, tiled=True),
    )
    return (
        activations,
        query_loss,
        input_grad,
        query_grad,
        summed[0],
        summed[1],
        summed[2],
        summed[3],
        summed[4],
        summed[5],
        summed[6],
        summed[7],
        summed[8],
        summed[9],
        summed[10],
    )


def solution(mesh):
    in_specs = (
        P("dp", None),
        P("dp"),
        P("dp", None),
        P(),
        P(None, None, "mp"),
        P(None, "mp"),
        P("mp", None),
        P(),
        P(),
        P(),
        P(None, "mp"),
        P("mp"),
        P("mp", None),
        P(),
        P(),
    )
    out_specs = (
        P("dp", "mp"),
        P("dp"),
        P("dp", "mp"),
        P("dp", None),
        P(None, "dp", "mp"),
        P(None, ("mp", "dp")),
        P("mp", "dp"),
        P("dp"),
        P("dp"),
        P("dp"),
        P("dp", "mp"),
        P(("mp", "dp")),
        P("mp", "dp"),
        P("dp"),
        P("dp"),
    )
    groups = mesh.shape["dp"]
    fits = groups <= 16 and mesh.shape["mp"] == 2
    return jax.shard_map(
        functools.partial(per_device, groups) if fits else by_collectives,
        mesh=mesh,
        in_specs=in_specs,
        out_specs=out_specs,
        check_vma=False,
    )
```

```python
import functools
import math

import jax
import jax.numpy as jnp
from jax import lax
from jax.experimental import pallas as pl
from jax.experimental.pallas import tpu as pltpu
from jax.sharding import PartitionSpec as P

HEAD = 64
EPS = 1e-05
MASKED = -1e30
MESH = pl.DeviceIdType.MESH
BF = jnp.bfloat16
F32 = jnp.float32
MIB = 2**20


def nn(a, b):
    return jnp.dot(a, b, preferred_element_type=F32)


def nt(a, b):
    return lax.dot_general(a, b, (((1,), (1,)), ((), ())), preferred_element_type=F32)


def tn(a, b):
    return lax.dot_general(a, b, (((0,), (0,)), ((), ())), preferred_element_type=F32)


def gelu(h):
    return 0.5 * h * (1.0 + lax.erf(h * math.sqrt(0.5)))


def gelu_slope(h):
    bell = jnp.exp(-0.5 * h * h) * (1.0 / math.sqrt(2.0 * math.pi))
    return 0.5 * (1.0 + lax.erf(h * math.sqrt(0.5))) + h * bell


def row_of(vector):
    return vector[None, :].astype(F32)


def exact(a, b):
    return jnp.dot(a, b, preferred_element_type=F32, precision=lax.Precision.HIGHEST)


def one_hot(shape, shift, dtype=F32):
    row = lax.broadcasted_iota(jnp.int32, shape, 0)
    column = lax.broadcasted_iota(jnp.int32, shape, 1)
    return (row == column + shift).astype(dtype)


def standard(rows):
    center = jnp.mean(rows, axis=-1, keepdims=True)
    spread = rows - center
    second = jnp.mean(spread * spread, axis=-1, keepdims=True)
    inverse = lax.rsqrt(second + EPS)
    return spread * inverse, inverse


def norm_back(grad, scaled, inverse):
    first = jnp.mean(grad, axis=-1, keepdims=True)
    second = jnp.mean(grad * scaled, axis=-1, keepdims=True)
    return inverse * (grad - first - scaled * second)


def flip(index, bit):
    return index + bit * (1 - 2 * lax.rem(lax.div(index, bit), 2))


def mult(value, step):
    return pl.multiple_of(value, step)


def tower(
    nd,
    query_total,
    lengths,
    tokens,
    queries,
    positives,
    w_qkv,
    b_qv,
    w_out,
    b_out,
    gain_one,
    shift_one,
    w_in,
    b_in,
    w_back,
    b_back,
    gain_two,
    out_act,
    h_coef,
    h_rank,
    h_factor,
    h_active,
    h_inner,
    h_context,
    h_qcls,
    h_dctx,
    h_norm,
    h_ffn,
    h_attn,
    h_tok,
    h_sums,
    h_sums_in,
    h_loss,
    h_qgrad,
    tok,
    wq,
    wq_far,
    wo,
    wi,
    wb,
    keyb,
    valb,
    ctx,
    norm_low,
    acc,
    act_far,
    obuf,
    chance,
    factor,
    stage,
    tcls,
    pack,
    gath,
    ctx_all,
    tok_all,
    q_all,
    xh1_all,
    norm_all,
    inner_all,
    act_all,
    low_all,
    dc_all,
    qc_all,
    d1_all,
    dq_rows,
    rank_f,
    coef_own,
    coef_far,
    dq_far,
    fac_send,
    loc_sem,
    ysend,
    yrecv,
    w_send,
    w_recv,
    o_send,
    o_recv,
    o_loc,
    g_send,
    g_recv,
    gs_send,
    gs_recv,
    f_send,
    f_recv,
    m_send,
    m_recv,
    b_send,
    b_recv,
    bin_own,
    bin_far,
    out_sem,
    o_coef,
    o_rank,
    o_factor,
    o_active,
    o_inner,
    o_context,
    o_qcls,
    o_dctx,
    o_norm,
    o_ffn,
    o_attn,
    o_tok,
    o_sums,
    o_sums_in,
    o_loss,
    o_qgrad,
):
    dp = lax.axis_index("dp")
    mp = lax.axis_index("mp")
    far = 1 - mp
    chips = nd // 2
    core = lax.rem(dp, 2)
    chip = lax.div(dp, 2)
    bit_a = lax.rem(lax.div(dp, 2), 2)
    bit_b = lax.rem(lax.div(dp, 4), 2)
    quarter = bit_a + 2 * bit_b
    quarter_x = flip(quarter, 1)
    quarter_z = flip(quarter, 2)
    quarter_d = 3 - quarter
    pair = (dp, far)
    sibling = (flip(dp, 1), mp)
    near_x = (flip(dp, 2), mp)
    near_z = (flip(dp, 4), mp)

    rows, width = tok.shape
    count = lengths.shape[0]
    slot = rows // count
    own = count // 2
    half = width // 2
    own_rows = own * slot
    passages = nd * count
    blocks, unit = wi.shape[1], wi.shape[3]
    m_col = mult(mp * half, 128)
    f_col = mult(far * half, 128)

    barrier = pltpu.get_barrier_semaphore()

    def greet(i, carry):
        other = lax.rem(dp * 2 + mp + i, 2 * nd)
        pl.semaphore_signal(
            barrier,
            inc=1,
            device_id=(lax.div(other, 2), lax.rem(other, 2)),
            device_id_type=MESH,
        )
        return carry

    lax.fori_loop(1, 2 * nd, greet, 0)

    def local(src, dst, k):
        return pltpu.make_async_copy(src, dst, loc_sem.at[k])

    loads = [local(tokens, tok, 0)]
    loads += [local(w_qkv.at[j], wq.at[:, pl.ds(j * half, half)], 1 + j) for j in range(3)]
    loads.append(local(w_out, wo.at[pl.ds(mult(mp * half, 128), half), :], 4))
    loads += [
        local(w_in.at[:, pl.ds(u * unit, unit)], wi.at[mp, u], 5 + u) for u in range(blocks)
    ]
    loads += [
        local(w_back.at[pl.ds(u * unit, unit), :], wb.at[mp, u], 5 + blocks + u)
        for u in range(blocks)
    ]
    for copy in loads:
        copy.start()

    chunks = 7
    direct = (3, 6)
    lead = pl.ds(0, blocks - 1)

    def piece(k, q, c, which, side=None):
        cols = pl.ds(0, width) if side is None else pl.ds(side * half, half)
        if k in direct:
            size = half // 2 if k == 3 else unit // 2
            if k == 3:
                return wo.at[pl.ds(mult(which * half + c * size, 16), size), cols]
            return wb.at[which, blocks - 1, pl.ds(mult(c * size, 16), size), cols]
        size = unit // 8 if k == 5 else width // 8
        at = (c * 4 if q is None else c * 4 + q) * size
        size = 4 * size if q is None else size
        if k == 5:
            return wb.at[which, lead, pl.ds(mult(at, 16), size), cols]
        if side is not None:
            size = size // 2
            at = at + side * size
        here = pl.ds(mult(at, 16), size)
        return wq_far.at[here, pl.ds(k * half, half)] if k < 3 else wi.at[which, :, here, :]

    def sent_bytes(k):
        if k in direct:
            return piece(k, None, core, far)
        if k < 3:
            return wq_far.at[pl.ds(0, 7 * width // 8), pl.ds(k * half, half)]
        if k == 4:
            return wi.at[far, :, pl.ds(0, 7 * width // 8), :]
        return wb.at[far, lead, pl.ds(0, 7 * unit // 8), :]

    def source(k):
        if k < 3:
            return w_qkv.at[k, pl.ds(mult((core * 4 + quarter) * (width // 8), 16), width // 8), :]
        if k == 3:
            return w_out.at[pl.ds(mult(core * (half // 2), 16), half // 2), :]
        return piece(k, quarter, core, mp)

    def remote(src, dst, ss, rs, device):
        return pltpu.make_async_remote_copy(
            src_ref=src,
            dst_ref=dst,
            send_sem=ss,
            recv_sem=rs,
            device_id=device,
            device_id_type=MESH,
        )

    def cross(k):
        return remote(
            source(k), piece(k, quarter, core, mp), ysend.at[k], yrecv.at[k], pair
        )

    def send(k, lane, q, c, side, device):
        ref = piece(k, q, c, far, side)
        return remote(ref, ref, w_send.at[k], w_recv.at[k, lane], device)

    def lane(k, n):
        q = (quarter, quarter, quarter_z, quarter_x, None)[n]
        side = (None, None, 0, 1, None)[n]
        return send(k, n, q, core, side, (near_x, near_z, near_x, near_z, sibling)[n])

    def arrival(k, n):
        q = (quarter_x, quarter_z, quarter_d, quarter_d, None)[n]
        side = (None, None, 0, 1, None)[n]
        c = core if n < 4 else 1 - core
        return send(k, n, q, c, side, (near_x, near_z, near_x, near_z, sibling)[n])

    def step_one(k):
        remote(
            source(k), piece(k, quarter, core, far), ysend.at[k], yrecv.at[k], pair
        ).wait_recv()
        for n in (4,) if k in direct else (0, 1):
            lane(k, n).start()

    def step_two(k):
        arrival(k, 1).wait_recv()
        lane(k, 2).start()
        arrival(k, 0).wait_recv()
        lane(k, 3).start()

    def step_three(k):
        arrival(k, 2).wait_recv()
        arrival(k, 3).wait_recv()
        lane(k, 4).start()

    def complete(k):
        arrival(k, 4).wait_recv()

    def spent(window, sem):
        pltpu.make_async_copy(window, window, sem).wait()

    def advance(*steps):
        for stage_of, k in steps:
            (step_one, step_two, step_three)[stage_of - 1](k)

    for copy in loads[:4]:
        copy.wait()
    bin_own[...] = jnp.zeros_like(bin_own)
    for u in range(blocks):
        bin_own[u : u + 1, :] = row_of(b_in[pl.ds(u * unit, unit)])
    bin_own[6:8, 0:half] = b_qv[...].astype(F32)
    bias_copy = remote(bin_own, bin_far, b_send, b_recv, pair)

    lane_pair = lax.broadcasted_iota(jnp.int32, (slot, 128), 1)
    key_place = lax.broadcasted_iota(jnp.int32, (1, slot), 1)
    head_rows = lax.broadcasted_iota(jnp.int32, (8, half), 0)
    head_mask = head_rows == lax.div(lax.broadcasted_iota(jnp.int32, (8, half), 1), HEAD)
    heads = half // HEAD
    live = lax.broadcasted_iota(jnp.int32, (8, 1), 0) < heads
    bias_q = b_qv[0:1, :].astype(F32)
    bias_v = b_qv[1:2, :].astype(F32)
    ones = jnp.ones((slot, 128), BF)
    row_place = lax.broadcasted_iota(jnp.int32, (8, slot), 0)
    first_key = (lax.broadcasted_iota(jnp.int32, (8, slot), 1) == 0).astype(F32)

    def mix(query, keyed, value, bias):
        done = []
        for t in range(half // 128):
            q2 = query[:, 128 * t : 128 * t + 128]
            k2 = keyed[:, 128 * t : 128 * t + 128]
            v2 = jnp.concatenate([value[:, 128 * t : 128 * t + 128], ones], axis=1)
            parts = []
            for hx in range(2):
                mask = (lane_pair < HEAD) if hx == 0 else (lane_pair >= HEAD)
                s = nt(jnp.where(mask, q2, jnp.zeros_like(q2)), k2) + bias
                e = jnp.exp(s - jnp.max(s, axis=1, keepdims=True)).astype(BF)
                o = nn(e, v2)
                parts.append(o[:, :128] / o[:, 128:])
            done.append(jnp.where(lane_pair < HEAD, parts[0], parts[1]))
        return jnp.concatenate(done, axis=1).astype(BF)

    def first_row(p, x, query, keyed, value, bias):
        tcls[pl.ds(p, 1), :] = x[0:16, :].astype(F32)[0:1, :]
        q_heads = jnp.where(head_mask, query.astype(F32)[0:1, :], 0.0).astype(BF)
        s = nt(q_heads, keyed) + bias
        e = jnp.exp(s - jnp.max(s, axis=1, keepdims=True))
        c = jnp.where(live, e / jnp.sum(e, axis=1, keepdims=True), 0.0)
        chance[p] = c
        c_low = c.astype(BF)
        mixed = jnp.where(head_mask, nn(c_low, value), 0.0)
        stage[pl.ds(p, 1), :] = jnp.sum(mixed, axis=0, keepdims=True)
        coef_own[pl.ds(mult(p * 16, 16), 8), :] = jnp.where(row_place == heads, first_key, c)
        factor[pl.ds(mult(p * 8, 8), 8), :] = nn(c_low, x)

    theirs_plan = (((1, 0),), (), ((1, 1),), ())
    gap_plan = ((2, 0), (1, 2), (2, 1), (3, 0), (2, 2), (1, 4), (3, 1), (3, 2))
    far_plan = ((), (), (), ((1, 3),))
    feed_plan = (((2, 4),), ((1, 5),), (), ((3, 4),))
    in_plan = ((((2, 5), (1, 6)), ()), ((), ()), ((), ((3, 5),)))

    def move_on(i, plan):
        for j, steps in enumerate(plan):
            if steps:

                @pl.when(i == j)
                def _():
                    advance(*steps)

    def key_bias(p):
        return jnp.where(key_place < lengths[p], 0.0, MASKED)

    def attend_theirs(i, carry):
        move_on(i, theirs_plan)
        p = far * own + i
        at = mult(p * slot, slot)
        x = tok[pl.ds(at, slot), :]
        made = nn(x, wq[:, half:])
        keyed = made[:, :half].astype(BF)
        value = (made[:, half:] + bias_v).astype(BF)
        keyb[pl.ds(at, slot), :] = keyed
        valb[pl.ds(at, slot), :] = value
        query = ((nn(x[0:16, :], wq[:, :half]) + bias_q).astype(BF).astype(F32) * 0.125).astype(BF)
        first_row(p, x, query, keyed, value, key_bias(p))
        return carry

    def attend_own(i, carry):
        @pl.when(i == 1)
        def _():
            pl.semaphore_wait(barrier, 2 * nd - 1)
            for copy in loads[4:]:
                copy.wait()
            for k in (0, 1, 2, 4, 3):
                cross(k).start()
            bias_copy.start()

        p = mp * own + i
        at = mult(p * slot, slot)
        x = tok[pl.ds(at, slot), :]
        made = nn(x, wq[...])
        query = ((made[:, :half] + bias_q).astype(BF).astype(F32) * 0.125).astype(BF)
        keyed = made[:, half : 2 * half].astype(BF)
        value = (made[:, 2 * half :] + bias_v).astype(BF)
        keyb[pl.ds(at, slot), :] = keyed
        valb[pl.ds(at, slot), :] = value
        bias = key_bias(p)
        ctx[pl.ds(mult(i * slot, slot), slot), pl.ds(m_col, half)] = mix(query, keyed, value, bias)
        first_row(p, x, query[0:16, :], keyed, value, bias)
        return carry

    def attend_far(i, carry):
        move_on(i, far_plan)
        p = mp * own + i
        x = tok[pl.ds(mult(p * slot, slot), slot), :]
        made = nn(x, wq_far[...])
        bias_far = bin_far[6:8, 0:half]
        query = ((made[:, :half] + bias_far[0:1, :]).astype(BF).astype(F32) * 0.125).astype(BF)
        keyed = made[:, half : 2 * half].astype(BF)
        value = (made[:, 2 * half :] + bias_far[1:2, :]).astype(BF)
        ctx[pl.ds(mult(i * slot, slot), slot), pl.ds(f_col, half)] = mix(
            query, keyed, value, key_bias(p)
        )
        return carry

    lax.fori_loop(0, own, attend_own, 0)
    lax.fori_loop(0, own, attend_theirs, 0)

    pack[0:8, :] = stage[...]
    pack[8:16, :] = tcls[:, pl.ds(m_col, half)]
    pack[16:32, :] = jnp.zeros((16, half), F32)
    q_rows = queries.shape[0]
    pack[16 : 16 + q_rows, :] = queries[:, pl.ds(m_col, half)].astype(F32)
    gath[chip, core, mp] = pack[...].astype(BF)

    here = gath.at[chip, core, mp]
    to_pair = remote(here, here, gs_send.at[0], gs_recv.at[0], pair)
    to_pair.start()
    advance(*gap_plan)
    bias_copy.wait_recv()
    for k in range(3):
        complete(k)
    remote(
        here, gath.at[chip, core, far], gs_send.at[0], gs_recv.at[0], pair
    ).wait_recv()

    def gather_start(i, carry):
        both = gath.at[chip, core]
        there = lax.rem(chip + i, chips) * 2 + core
        remote(both, both, g_send, g_recv, (there, mp)).start()
        return carry

    lax.fori_loop(1, chips, gather_start, 0)
    gather_window = tok.at[pl.ds(0, (chips - 1) * 32), :]
    for k in (5, 6):
        cross(k).start()

    lax.fori_loop(0, own, attend_far, 0)

    complete(3)
    bo = row_of(b_out[...])
    g1 = row_of(gain_one[...])
    s1 = row_of(shift_one[...])
    g2 = row_of(gain_two[...])
    bb = row_of(b_back[...])

    def feed_own(i, carry):
        move_on(i, feed_plan)
        at = mult(i * slot, slot)
        here = pl.ds(at, slot)
        x = tok[pl.ds(mult(mp * own_rows + i * slot, slot), slot), :].astype(F32)
        resid = x + nn(ctx[here, :], wo[...]) + bo
        scaled, _ = standard(resid)
        norm = scaled * g1 + s1
        low = norm.astype(BF)
        norm_low[here, :] = low
        total = norm + bb
        for u in range(blocks):
            inner = nn(low, wi[mp, u]) + bin_own[u : u + 1, :]
            total = total + nn(gelu(inner).astype(BF), wb[mp, u])
        acc[here, :] = total

        return carry

    lax.fori_loop(0, own, feed_own, 0)

    complete(4)
    for u in range(blocks):

        def feed_far_in(i, carry, u=u):
            move_on(i, in_plan[u])
            here = pl.ds(mult(i * 2 * slot, slot), 2 * slot)
            inner = nn(norm_low[here, :], wi[far, u]) + bin_far[u : u + 1, :]
            act_far[u, here, :] = gelu(inner).astype(BF)
            return carry

        lax.fori_loop(0, own // 2, feed_far_in, 0)

    def feed_far_back(u):
        def feed(i, carry):
            here = pl.ds(mult(i * 2 * slot, slot), 2 * slot)
            acc[here, :] += nn(act_far[u, here, :], wb[far, u])
            return carry

        lax.fori_loop(0, own // 2, feed, 0)

    complete(5)
    feed_far_back(0)

    for u in range(1, blocks - 1):
        feed_far_back(u)
    to_sibling = remote(
        gath.at[:, core], gath.at[:, core], gs_send.at[1], gs_recv.at[1], sibling
    )
    complete(chunks - 1)

    def out_copy(i, mine):
        side = mp if mine else far
        there = out_act.at[pl.ds(mult(side * own_rows + i * slot, 16), slot), :]
        return remote(
            obuf.at[1, pl.ds(mult(i * slot, 16), slot), :], there, o_send.at[i], o_recv.at[i], pair
        )

    def out_local(i):
        there = out_act.at[pl.ds(mult(mp * own_rows + i * slot, 16), slot), :]
        return pltpu.make_async_copy(
            obuf.at[0, pl.ds(mult(i * slot, 16), slot), :], there, o_loc.at[i]
        )

    def finish(i, carry):
        @pl.when(i == 1)
        def _():
            spent(gather_window, g_recv)
            to_sibling.start()

        here = pl.ds(mult(i * slot, slot), slot)
        total = acc[here, :] + nn(act_far[blocks - 1, here, :], wb[far, blocks - 1])
        scaled, _ = standard(total)
        acc[here, :] = scaled * g2
        obuf[0, here, :] = acc[here, pl.ds(m_col, half)].astype(BF)
        obuf[1, here, :] = acc[here, pl.ds(f_col, half)].astype(BF)
        @pl.when(i < own - 1)
        def _():
            out_copy(i, True).start()

        out_local(i).start()
        return carry

    lax.fori_loop(0, own, finish, 0)

    remote(
        gath.at[:, 1 - core], gath.at[:, 1 - core], gs_send.at[1], gs_recv.at[1], sibling
    ).wait_recv()
    q_pad = nd * 16
    for h in range(2):
        cols = slice(h * half, (h + 1) * half)
        block = gath[:, :, h].astype(F32)
        ctx_all[:, cols] = block[:, :, 0:8].reshape(passages, half).astype(BF)
        tok_all[:, cols] = block[:, :, 8:16].reshape(passages, half).astype(BF)
        q_all[:, cols] = block[:, :, 16:32].reshape(q_pad, half).astype(BF)
    resid = tok_all[...].astype(F32) + nn(ctx_all[...], wo[...]) + bo
    scaled, inverse1 = standard(resid)
    xh1_all[...] = scaled
    norm = scaled * g1 + s1
    low = norm.astype(BF)
    norm_all[...] = low
    total = norm + bb
    for which, bias in ((mp, bin_own), (far, bin_far)):
        for u in range(blocks):
            inner = nn(low, wi[which, u]) + bias[u : u + 1, :]
            inner_all[which, u] = inner
            active = gelu(inner).astype(BF)
            act_all[which, u] = active
    for u in range(blocks):
        total = total + nn(act_all[mp, u], wb[mp, u])
    total = total + nn(act_all[far, 0], wb[far, 0])
    for u in range(1, blocks):
        total = total + nn(act_all[far, u], wb[far, u])

    xh2, inverse2 = standard(total)
    cls = (xh2 * g2).astype(BF)
    similar = nt(cls, q_all[...])
    top = jnp.max(similar, axis=0, keepdims=True)
    log_sum = top + jnp.log(jnp.sum(jnp.exp(similar - top), axis=0, keepdims=True))
    q_count = query_total // nd
    from_q = lax.broadcasted_iota(jnp.int32, (query_total, q_pad), 0)
    to_q = lax.broadcasted_iota(jnp.int32, (query_total, q_pad), 1)
    spot = lax.div(from_q, q_count) * 16 + lax.rem(from_q, q_count)
    wanted = jnp.broadcast_to(row_of(positives[...]), (8, query_total)) + 1.0
    place = exact(wanted, (spot == to_q).astype(F32))[0:1, :] - 1.0
    target = lax.broadcasted_iota(jnp.int32, similar.shape, 0).astype(F32) == place
    picked = jnp.sum(jnp.where(target, similar, 0.0), axis=0, keepdims=True)
    o_loss[...] = jnp.broadcast_to(log_sum - picked, o_loss.shape)
    slopes = (jnp.exp(similar - log_sum) - target.astype(F32)) * (1.0 / query_total)
    slope_high = slopes.astype(BF)
    slope_low = (slopes - slope_high.astype(F32)).astype(BF)
    cls_grad = nn(slope_high, q_all[...]) + nn(slope_low, q_all[...])
    pick = (
        lax.broadcasted_iota(jnp.int32, (16, q_pad), 1)
        == lax.broadcasted_iota(jnp.int32, (16, q_pad), 0) + dp * 16
    ).astype(BF)
    o_qgrad[...] = nn(nt(pick, slope_high).astype(BF), cls) + nn(
        nt(pick, slope_low).astype(BF), cls
    )
    d_two = norm_back(g2 * cls_grad, xh2, inverse2)
    o_sums[0:1, :] = jnp.sum(cls_grad * xh2, axis=0, keepdims=True)
    o_sums[1:2, :] = jnp.sum(d_two, axis=0, keepdims=True)
    ffn_low = d_two.astype(BF)
    o_ffn[...] = ffn_low
    back = d_two
    for h in range(2):
        for u in range(blocks):
            d_active = nt(ffn_low, wb[h, u])
            d_inner = d_active * gelu_slope(inner_all[h, u])
            inner_all[h, u, 0:8, :] = jnp.broadcast_to(
                jnp.sum(d_inner, axis=0, keepdims=True), (8, unit)
            )
            inner_low = d_inner.astype(BF)
            low_all[h, u] = inner_low
            back = back + nt(inner_low, wi[h, u])
    for u in range(blocks):
        o_active[u] = act_all[mp, u]
        o_inner[u] = low_all[mp, u]
        o_sums_in[u : u + 1, :] = inner_all[mp, u, 0:1, :]
    xh1 = xh1_all[...]
    d_one = norm_back(g1 * back, xh1, inverse1)
    d1_all[...] = d_one
    o_sums[2:3, :] = jnp.sum(back * xh1, axis=0, keepdims=True)
    o_sums[3:4, :] = jnp.sum(back, axis=0, keepdims=True)
    o_sums[4:5, :] = jnp.sum(d_one, axis=0, keepdims=True)
    attn_low = d_one.astype(BF)
    o_attn[...] = attn_low
    o_norm[...] = norm_all[...]
    o_tok[...] = tok_all[...]
    d_ctx = nt(attn_low, wo[pl.ds(mult(mp * half, 128), half), :]).astype(BF)
    o_dctx[...] = d_ctx
    dc_all[...] = d_ctx.astype(F32)
    q_cls = (nn(tok_all[...], wq[:, 0:half]) + bias_q).astype(BF)
    o_qcls[...] = q_cls
    qc_all[...] = q_cls.astype(F32) * 0.125
    o_context[...] = ctx_all[:, pl.ds(m_col, half)]
    o_sums[5:6, 0:half] = jnp.sum(dc_all[...], axis=0, keepdims=True)

    def stored(src, dst, k):
        return pltpu.make_async_copy(src, dst, out_sem.at[k])

    early = [
        stored(src, dst, k)
        for k, (src, dst) in enumerate(
            (
                (o_active, h_active),
                (o_inner, h_inner),
                (o_context, h_context),
                (o_qcls, h_qcls),
                (o_dctx, h_dctx),
                (o_norm, h_norm),
                (o_ffn, h_ffn),
                (o_attn, h_attn),
                (o_tok, h_tok),
                (o_sums, h_sums),
                (o_sums_in, h_sums_in),
                (o_loss, h_loss),
                (o_qgrad, h_qgrad),
            )
        )
    ]
    for copy in early:
        copy.start()

    base = mult(dp * count, 8)
    fkind = count * 8

    mark = jnp.logical_or(row_place == heads, row_place == heads + 1)
    for p in range(count):
        d_row = dc_all[pl.ds(base + p, 1), :]
        q_row = qc_all[pl.ds(base + p, 1), :]
        rank_f[p * 16 : p * 16 + 8, 0:half] = jnp.where(head_mask, d_row, 0.0)
        rank_f[p * 16 + 8 : p * 16 + 16, 0:half] = jnp.where(head_mask, q_row, 0.0)
    kept = rank_f[:, 0:half].astype(BF)
    group = 4
    for first in range(0, count, group):
        d_scores = []
        for p in range(first, first + group):
            c = chance[p]
            d_chance = nt(kept[p * 16 : p * 16 + 16, :], valb[p * slot : (p + 1) * slot, :])[0:8, :]
            d_scores.append(c * (d_chance - jnp.sum(c * d_chance, axis=1, keepdims=True)))
        for p, d in zip(range(first, first + group), d_scores):
            s_low = d.astype(BF)
            at = slice(p * slot, (p + 1) * slot)
            coef_own[p * 16 + 8 : p * 16 + 16, :] = jnp.where(mark, first_key, d)
            factor[fkind + p * 8 : fkind + p * 8 + 8, :] = nn(s_low, tok[at, :])
            spread = nn(s_low, keyb[at, :])
            dq_rows[p : p + 1, :] = 0.125 * jnp.sum(
                jnp.where(head_mask, spread, 0.0), axis=0, keepdims=True
            )

    turned = jnp.transpose(factor[...]).astype(BF)
    dq = dq_rows[...]
    for b in range(half // 128):
        pack[b * 8 : b * 8 + 8, 0:128] = dq[:, b * 128 : b * 128 + 128]
    pack[half // 16 : 32, 0:128] = jnp.zeros((32 - half // 16, 128), F32)
    dq_low = pack[:, 0:128].astype(BF)
    share = width // nd
    for j in range(nd):
        fac_send[j, 0:share, :] = turned[j * share : (j + 1) * share, :]
        fac_send[j, share:, :] = dq_low
    o_factor[dp] = fac_send[dp]

    def factor_start(i, carry):
        there = lax.rem(dp + i, nd)
        remote(fac_send.at[there], o_factor.at[dp], f_send, f_recv, (there, mp)).start()
        return carry

    lax.fori_loop(1, nd, factor_start, 0)

    coef_low = coef_own[...].astype(BF)
    o_coef[0] = coef_low
    coef_far_copy = remote(o_coef.at[0], coef_far, m_send.at[0], m_recv.at[0], pair)
    coef_far_copy.start()
    dq_copy = remote(dq_rows, dq_far, m_send.at[1], m_recv.at[1], pair)
    dq_copy.start()
    out_copy(own - 1, True).start()
    kind = lax.rem(lax.div(lax.broadcasted_iota(jnp.int32, (count * 16, 1), 0), 8), 2)
    d1_rows = d1_all[pl.ds(base, count), :]
    d_far = nt(d1_rows.astype(BF), wo[pl.ds(mult(far * half, 128), half), :])
    q_far = (nn(tcls[...].astype(BF), wq_far[:, 0:half]) + bin_far[6:7, 0:half]) * 0.125
    for p in range(count):
        rank_f[p * 16 : p * 16 + 8, 0:half] = jnp.where(head_mask, d_far[p : p + 1, :], 0.0)
        rank_f[p * 16 + 8 : p * 16 + 16, 0:half] = jnp.where(head_mask, q_far[p : p + 1, :], 0.0)
    kept_far = rank_f[:, 0:half].astype(BF)
    my_rows = pl.ds(mult(mp * half, 128), half)

    def rank_rows(left, right):
        by_v = nt(left, right[my_rows, 2 * half :])
        by_k = nt(left, right[my_rows, half : 2 * half])
        return jnp.where(kind == 0, by_v, by_k)

    rank_f[:, 0:half] = rank_rows(kept, wq)
    rank_f[:, half:] = rank_rows(kept_far, wq_far)
    d1_mine = d1_all[pl.ds(base, count), pl.ds(m_col, half)]
    d1_high = d1_mine.astype(BF).astype(F32)
    d1_low = d1_mine - d1_high

    def first_rank(cols, back_q, high, low):
        for p in range(count):
            rank_f[p * 16 + heads : p * 16 + heads + 1, cols] = back_q[p : p + 1, :]
            rank_f[p * 16 + heads + 1 : p * 16 + 8, cols] = jnp.zeros((7 - heads, half), F32)
            rank_f[p * 16 + 8 + heads : p * 16 + 9 + heads, cols] = high[p : p + 1]
            rank_f[p * 16 + 9 + heads : p * 16 + 10 + heads, cols] = low[p : p + 1]

    mine = slice(0, half)
    theirs = slice(half, width)
    first_rank(mine, nt(dq.astype(BF), wq[my_rows, 0:half]), d1_high, d1_low)
    o_rank[0] = rank_f[:, mine].astype(BF)

    dq_copy.wait_recv()
    nothing = jnp.zeros((count, half), F32)
    first_rank(theirs, nt(dq_far[...].astype(BF), wq_far[my_rows, 0:half]), nothing, nothing)
    o_rank[1] = rank_f[:, theirs].astype(BF)
    coef_far_copy.wait_recv()
    o_coef[1] = coef_far[...]
    factor_window = fac_send.at[pl.ds(0, nd - 1)]
    spent(factor_window, f_recv)
    last = [stored(o_factor, h_factor, 15), stored(o_coef, h_coef, 13), stored(o_rank, h_rank, 14)]
    for copy in last:
        copy.start()
    spent(factor_window, f_send)
    coef_far_copy.wait_send()
    dq_copy.wait_send()
    bias_copy.wait_send()
    spent(gather_window, g_send)
    to_sibling.wait_send()
    to_pair.wait_send()
    for k in range(chunks):
        cross(k).wait_send()
        spent(sent_bytes(k), w_send.at[k])

    def drain(i, carry):
        out_copy(i, True).wait_send()
        out_copy(i, False).wait_recv()
        out_local(i).wait()
        return carry

    lax.fori_loop(0, own, drain, 0)
    for copy in early + last:
        copy.wait()


def gradients(
    nd,
    act_in,
    coef_in,
    rank_in,
    factor_in,
    active_in,
    inner_in,
    context_in,
    qcls_in,
    dctx_in,
    norm_in,
    ffn_in,
    attn_in,
    tok_in,
    sums_in,
    sums_units_in,
    loss_in,
    qgrad_in,
    act_out,
    query_loss,
    input_grad,
    query_grad,
    grad_qkv,
    grad_bias_qv,
    grad_out,
    grad_bias_out,
    grad_gain_one,
    grad_shift_one,
    grad_in,
    grad_bias_in,
    grad_back,
    grad_bias_back,
    grad_gain_two,
    coef,
    rank,
    factor,
    active,
    inner,
    context,
    qcls,
    dctx,
    norm,
    ffn,
    attn,
    tok,
    sums,
    sums_units,
    loss,
    qgrad,
    sems,
    act_sem,
    act_buf,
    in_buf,
    in_sems,
    rhs,
):
    dp = lax.axis_index("dp")
    act_load = pltpu.make_async_copy(act_in, act_buf, act_sem.at[0])
    act_store = pltpu.make_async_copy(act_buf, act_out, act_sem.at[1])
    act_load.start()
    pairs = (
        (coef_in, coef),
        (rank_in, rank),
        (factor_in, factor),
        (qcls_in, qcls),
        (dctx_in, dctx),
        (active_in, active),
        (inner_in, inner),
        (context_in, context),
        (norm_in, norm),
        (ffn_in, ffn),
        (attn_in, attn),
        (tok_in, tok),
        (sums_in, sums),
        (sums_units_in, sums_units),
        (loss_in, loss),
        (qgrad_in, qgrad),
    )
    loads = [pltpu.make_async_copy(src, dst, sems.at[i]) for i, (src, dst) in enumerate(pairs)]
    for load in loads:
        load.start()
    passages, width = ffn.shape
    half = width // 2
    share = width // nd
    count = passages // nd
    slot = coef.shape[2]
    for load in loads[:2]:
        load.wait()

    def input_copy(p):
        at = pl.ds(mult(p * slot, slot), slot)
        return pltpu.make_async_copy(in_buf.at[at, :], input_grad.at[at, :], in_sems.at[p])

    def input_rows(p, carry):
        rows16 = pl.ds(mult(p * 16, 16), 16)
        both = jnp.concatenate([coef[0, rows16, :], coef[1, rows16, :]], axis=0)
        right = jnp.concatenate([rank[0, rows16, :], rank[1, rows16, :]], axis=0)
        in_buf[pl.ds(mult(p * slot, slot), slot), :] = tn(both, right)
        input_copy(p).start()
        return carry

    lax.fori_loop(0, count, input_rows, 0)
    act_load.wait()
    act_store.start()
    for load in loads[2:]:
        load.wait()

    spread = lax.broadcasted_iota(jnp.int32, (8, half), 0) == lax.div(
        lax.broadcasted_iota(jnp.int32, (8, half), 1), HEAD
    )
    fkind = count * 8

    def build(s, carry):
        d_rows = dctx[pl.ds(mult(s * 2 * count, 16), 2 * count), :].astype(F32)
        q_rows = qcls[pl.ds(mult(s * 2 * count, 16), 2 * count), :].astype(F32) * 0.125
        k_blocks = [jnp.where(spread, q_rows[p : p + 1, :], 0.0) for p in range(2 * count)]
        v_blocks = [jnp.where(spread, d_rows[p : p + 1, :], 0.0) for p in range(2 * count)]
        here = pl.ds(mult(s * 2 * fkind, 16), 2 * fkind)
        rhs[here, 0:half] = jnp.concatenate(k_blocks, 0).astype(BF)
        rhs[here, half:] = jnp.concatenate(v_blocks, 0).astype(BF)
        return carry

    lax.fori_loop(0, nd // 2, build, 0)
    grad_k = jnp.zeros((share, half), F32)
    grad_v = jnp.zeros((share, half), F32)
    for s in range(0, nd, 4):
        left_v = jnp.concatenate([factor[s + t, 0:share, :][:, 0:fkind] for t in range(4)], axis=1)
        left_k = jnp.concatenate([factor[s + t, 0:share, :][:, fkind:] for t in range(4)], axis=1)
        grad_k = grad_k + nn(left_k, rhs[s * fkind : (s + 4) * fkind, 0:half])
        grad_v = grad_v + nn(left_v, rhs[s * fkind : (s + 4) * fkind, half:])
    grad_qkv[1] = grad_k
    grad_qkv[2] = grad_v

    pick = one_hot((width, share), dp * share)
    pick_low = pick.astype(BF)
    row = lax.broadcasted_iota(jnp.int32, (share, width), 0)
    column = lax.broadcasted_iota(jnp.int32, (share, width), 1)
    pick_t = (column == row + dp * share).astype(BF)
    ffn_own = nt(pick_t, ffn[...]).astype(BF)
    attn_own = nt(pick_t, attn[...]).astype(BF)
    norm_own = nt(pick_t, norm[...]).astype(BF)
    tok_own = nt(pick_t, tok[...]).astype(BF)
    grad_out[...] = nn(attn_own, context[...])
    unit = active.shape[2]
    blocks = active.shape[0]
    for u in range(blocks):
        cols = slice(u * unit, (u + 1) * unit)
        grad_back[:, cols] = nn(ffn_own, active[u])
        grad_in[:, cols] = nn(norm_own, inner[u])
    dq_sum = []
    for b in range(half // 128):
        cols = factor[:, share:, :].astype(F32)[:, b * 8 : b * 8 + 8, :].reshape(passages, 128)
        dq_sum.append(jnp.sum(cols, axis=0, keepdims=True))
        grad_qkv[0, :, b * 128 : b * 128 + 128] = nn(tok_own, cols.astype(BF))

    mine = exact(sums[...], pick)
    grad_gain_two[...] = mine[0:1, :].reshape(share)
    grad_bias_back[...] = mine[1:2, :].reshape(share)
    grad_gain_one[...] = mine[2:3, :].reshape(share)
    grad_shift_one[...] = mine[3:4, :].reshape(share)
    grad_bias_out[...] = mine[4:5, :].reshape(share)
    part = half // nd
    both = jnp.concatenate([jnp.concatenate(dq_sum, axis=1), sums[5:6, 0:half]], axis=0)
    wide = jnp.concatenate([both, jnp.zeros((6, half), F32)], axis=0)
    grad_bias_qv[...] = exact(wide, one_hot((half, part), dp * part))[0:2, :]
    in_share = grad_bias_in.shape[0]
    total = jnp.zeros((8, in_share), F32)
    for u in range(blocks):
        total = total + exact(
            jnp.broadcast_to(sums_units[u : u + 1, :], (8, unit)),
            one_hot((unit, in_share), dp * in_share - u * unit),
        )
    grad_bias_in[...] = total[0:1, :].reshape(in_share)
    q_rows = query_loss.shape[0]
    query_loss[...] = exact(loss[...], one_hot((loss.shape[1], q_rows), dp * 16))[0:1, :].reshape(q_rows)
    query_grad[...] = qgrad[0:q_rows, :]

    def input_wait(p, carry):
        input_copy(p).wait()
        return carry

    lax.fori_loop(0, count, input_wait, 0)
    act_store.wait()


def per_device(nd, *arrays):
    (
        tokens,
        lengths,
        queries,
        positives,
        w_qkv,
        b_qv,
        w_out,
        b_out,
        gain_one,
        shift_one,
        w_in,
        b_in,
        w_back,
        b_back,
        gain_two,
    ) = arrays
    rows, width = tokens.shape
    count = lengths.shape[0]
    slot = rows // count
    half = w_qkv.shape[2]
    units = w_in.shape[1]
    unit = 512
    blocks = units // unit
    chunks = 7
    own_rows = rows // 2
    passages = nd * count
    chips = nd // 2
    q_rows = queries.shape[0]
    q_pad = nd * 16
    share = width // nd
    vmem = pl.BlockSpec(memory_space=pltpu.VMEM)
    hbm = pl.BlockSpec(memory_space=pl.ANY)
    smem = pl.BlockSpec(memory_space=pltpu.SMEM)
    in_specs = [smem, hbm, vmem, vmem, hbm, vmem, hbm, vmem, vmem, vmem, hbm, vmem, hbm, vmem, vmem]
    shape = jax.ShapeDtypeStruct
    outs = [
        (shape((rows, half), BF), hbm),
        (shape((2, count * 16, slot), BF), hbm),
        (shape((2, count * 16, half), BF), hbm),
        (shape((nd, share + 32, 128), BF), hbm),
        (shape((blocks, passages, unit), BF), hbm),
        (shape((blocks, passages, unit), BF), hbm),
        (shape((passages, half), BF), hbm),
        (shape((passages, half), BF), hbm),
        (shape((passages, half), BF), hbm),
        (shape((passages, width), BF), hbm),
        (shape((passages, width), BF), hbm),
        (shape((passages, width), BF), hbm),
        (shape((passages, width), BF), hbm),
        (shape((8, width), F32), hbm),
        (shape((8, unit), F32), hbm),
        (shape((8, q_pad), F32), hbm),
        (shape((16, width), F32), hbm),
    ]
    dma = pltpu.SemaphoreType.DMA
    scratch = [
        pltpu.VMEM((rows, width), BF),
        pltpu.VMEM((width, 3 * half), BF),
        pltpu.VMEM((width, 3 * half), BF),
        pltpu.VMEM((width, width), BF),
        pltpu.VMEM((2, blocks, width, unit), BF),
        pltpu.VMEM((2, blocks, unit, width), BF),
        pltpu.VMEM((rows, half), BF),
        pltpu.VMEM((rows, half), BF),
        pltpu.VMEM((own_rows, width), BF),
        pltpu.VMEM((own_rows, width), BF),
        pltpu.VMEM((own_rows, width), F32),
        pltpu.VMEM((blocks, own_rows, unit), BF),
        pltpu.VMEM((2, own_rows, half), BF),
        pltpu.VMEM((count, 8, slot), F32),
        pltpu.VMEM((2 * count * 8, width), F32),
        pltpu.VMEM((8, half), F32),
        pltpu.VMEM((8, width), F32),
        pltpu.VMEM((32, half), F32),
        pltpu.VMEM((chips, 2, 2, 32, half), BF),
        pltpu.VMEM((passages, width), BF),
        pltpu.VMEM((passages, width), BF),
        pltpu.VMEM((q_pad, width), BF),
        pltpu.VMEM((passages, width), F32),
        pltpu.VMEM((passages, width), BF),
        pltpu.VMEM((2, blocks, passages, unit), F32),
        pltpu.VMEM((2, blocks, passages, unit), BF),
        pltpu.VMEM((2, blocks, passages, unit), BF),
        pltpu.VMEM((passages, half), F32),
        pltpu.VMEM((passages, half), F32),
        pltpu.VMEM((passages, width), F32),
        pltpu.VMEM((8, half), F32),
        pltpu.VMEM((count * 16, width), F32),
        pltpu.VMEM((count * 16, slot), F32),
        pltpu.VMEM((count * 16, slot), BF),
        pltpu.VMEM((count, half), F32),
        pltpu.VMEM((nd, share + 32, 128), BF),
        dma((5 + 2 * blocks,)),
        dma((chunks,)),
        dma((chunks,)),
        dma((chunks,)),
        dma((chunks, 5)),
        dma((count // 2,)),
        dma((count // 2,)),
        dma((count // 2,)),
        dma,
        dma,
        dma((2,)),
        dma((2,)),
        dma,
        dma,
        dma((2,)),
        dma((2,)),
        dma,
        dma,
        pltpu.VMEM((8, unit), F32),
        pltpu.VMEM((8, unit), F32),
        dma((16,)),
    ] + [pltpu.VMEM(o[0].shape, o[0].dtype) for o in outs[1:]]
    made = pl.pallas_call(
        functools.partial(tower, nd, nd * q_rows),
        out_shape=[o[0] for o in outs],
        in_specs=in_specs,
        out_specs=[o[1] for o in outs],
        scratch_shapes=scratch,
        compiler_params=pltpu.CompilerParams(
            collective_id=0, has_side_effects=True, vmem_limit_bytes=60 * MIB
        ),
        name="tower",
    )(
        lengths,
        tokens,
        queries,
        positives,
        w_qkv,
        b_qv,
        w_out,
        b_out,
        gain_one,
        shift_one,
        w_in,
        b_in,
        w_back,
        b_back,
        gain_two,
    )
    g_outs = [
        (shape((rows, half), BF), hbm),
        (shape((q_rows,), F32), vmem),
        (shape((rows, half), F32), hbm),
        (shape((q_rows, width), F32), vmem),
        (shape((3, share, half), F32), vmem),
        (shape((2, half // nd), F32), vmem),
        (shape((share, half), F32), vmem),
        (shape((share,), F32), vmem),
        (shape((share,), F32), vmem),
        (shape((share,), F32), vmem),
        (shape((share, units), F32), vmem),
        (shape((units // nd,), F32), vmem),
        (shape((share, units), F32), vmem),
        (shape((share,), F32), vmem),
        (shape((share,), F32), vmem),
    ]
    grads = pl.pallas_call(
        functools.partial(gradients, nd),
        out_shape=[o[0] for o in g_outs],
        in_specs=[hbm] * len(outs),
        out_specs=[o[1] for o in g_outs],
        scratch_shapes=[pltpu.VMEM(o[0].shape, o[0].dtype) for o in outs[1:]]
        + [
            dma((len(outs) - 1,)),
            dma((2,)),
            pltpu.VMEM((rows, half), BF),
            pltpu.VMEM((rows, half), F32),
            dma((count,)),
            pltpu.VMEM((nd * count * 8, width), BF),
        ],
        compiler_params=pltpu.CompilerParams(vmem_limit_bytes=62 * MIB),
        name="gradients",
    )(*made)
    grads = list(grads)
    grads[6] = grads[6].T
    grads[12] = grads[12].T
    return tuple(grads)


def layer_norm(rows, gain, shift):
    center = jnp.mean(rows, axis=-1, keepdims=True)
    spread = rows - center
    second = jnp.mean(spread * spread, axis=-1, keepdims=True)
    return spread * lax.rsqrt(second + EPS) * gain + shift


def scaled_norm(rows, gain):
    center = jnp.mean(rows, axis=-1, keepdims=True)
    spread = rows - center
    second = jnp.mean(spread * spread, axis=-1, keepdims=True)
    return spread * lax.rsqrt(second + EPS) * gain


def gelu_exact(values):
    return jax.nn.gelu(values, approximate=False)


def first_rows(values, count):
    return values.reshape((count, values.shape[0] // count) + values.shape[1:])[:, 0]


def by_collectives(
    tokens,
    lengths,
    queries,
    positives,
    w_qkv,
    b_qv,
    w_out,
    b_out,
    gain_one,
    shift_one,
    w_in,
    b_in,
    w_back,
    b_back,
    gain_two,
):
    rows, width = tokens.shape
    count = lengths.shape[0]
    slot = rows // count
    local = w_qkv.shape[2]
    heads_here = local // HEAD
    scale = 1.0 / math.sqrt(HEAD)
    projected = jnp.einsum("rd,jdc->jrc", tokens, w_qkv, preferred_element_type=F32)
    bias_qv = b_qv.astype(F32)
    query = (projected[0] + bias_qv[0]).astype(BF)
    keyed = projected[1].astype(BF)
    value = (projected[2] + bias_qv[1]).astype(BF)
    block = min(count, max(1, 512 // slot))
    blocks = count // block
    valid = lax.broadcasted_iota(jnp.int32, (count, slot), 1) < lengths[:, None]
    split_shape = (blocks, block, slot, heads_here, HEAD)

    def attend(inputs):
        query_part, keyed_part, value_part, valid_part = inputs
        scores = (
            jnp.einsum(
                "pqhd,pkhd->phqk", query_part, keyed_part, preferred_element_type=F32
            )
            * scale
        )
        scores = jnp.where(valid_part[:, None, None, :], scores, MASKED)
        top = jnp.max(scores, axis=-1, keepdims=True)
        raised = jnp.exp(scores - top)
        total = jnp.sum(raised, axis=-1, keepdims=True)
        chance_low = (raised / total).astype(BF)
        mixed = jnp.einsum(
            "phqk,pkhd->pqhd", chance_low, value_part, preferred_element_type=F32
        )
        return (mixed.astype(BF), (top + jnp.log(total))[:, :, 0, 0])

    context, log_total = lax.map(
        attend,
        (
            query.reshape(split_shape),
            keyed.reshape(split_shape),
            value.reshape(split_shape),
            valid.reshape(blocks, block, slot),
        ),
    )
    context = context.reshape(rows, local)
    log_total = log_total.reshape(count, heads_here)
    partial_attn = jnp.dot(context, w_out, preferred_element_type=F32).astype(BF)
    attended = lax.psum(partial_attn, "mp").astype(F32) + b_out.astype(F32)
    resid_one = tokens.astype(F32) + attended
    gain_one_w = gain_one.astype(F32)
    shift_one_w = shift_one.astype(F32)
    gain_two_w = gain_two.astype(F32)
    norm_one = layer_norm(resid_one, gain_one_w, shift_one_w)
    norm_low = norm_one.astype(BF)
    inner = jnp.dot(norm_low, w_in, preferred_element_type=F32) + b_in.astype(F32)
    active = gelu_exact(inner).astype(BF)
    partial_ffn = jnp.dot(active, w_back, preferred_element_type=F32).astype(BF)
    resid_two = (
        norm_one + lax.psum(partial_ffn, "mp").astype(F32) + b_back.astype(F32)
    )
    output = scaled_norm(resid_two, gain_two_w)
    column = lax.axis_index("mp") * local
    activations = lax.dynamic_slice_in_dim(output, column, local, 1).astype(BF)
    cls_low = first_rows(output, count).astype(BF)
    query_rows = queries.shape[0]
    members = lax.axis_size("dp")
    query_total = query_rows * members
    own_query = lax.axis_index("dp") * query_rows
    gathered = lax.all_gather(cls_low, "dp", axis=0, tiled=True)
    similar = jnp.einsum("qd,pd->qp", queries, gathered, preferred_element_type=F32)
    mine = lax.dynamic_slice_in_dim(positives, own_query, query_rows)
    target = lax.broadcasted_iota(jnp.int32, similar.shape, 1) == mine[:, None]
    top = jnp.max(similar, axis=1, keepdims=True)
    log_sum = top[:, 0] + jnp.log(jnp.sum(jnp.exp(similar - top), axis=1))
    picked = jnp.sum(jnp.where(target, similar, 0.0), axis=1)
    query_loss = log_sum - picked
    slopes = (jnp.exp(similar - log_sum[:, None]) - target.astype(F32)) / query_total
    query_grad = jnp.dot(slopes, gathered.astype(F32), precision=lax.Precision.HIGHEST)
    queries_wide = queries.astype(F32)
    cls_grad = lax.psum_scatter(
        jnp.einsum("qp,qd->pd", slopes, queries_wide, precision=lax.Precision.HIGHEST),
        "dp",
        scatter_dimension=0,
        tiled=True,
    )
    _, norm_two_pull = jax.vjp(scaled_norm, first_rows(resid_two, count), gain_two_w)
    d_resid_two, grad_gain_two = norm_two_pull(cls_grad)
    grad_bias_back = jnp.sum(d_resid_two, axis=0)
    ffn_low = d_resid_two.astype(BF)
    grad_back = jnp.einsum(
        "pf,pd->fd", first_rows(active, count), ffn_low, preferred_element_type=F32
    )
    d_active = jnp.einsum("pd,fd->pf", ffn_low, w_back, preferred_element_type=F32)
    _, gelu_pull = jax.vjp(gelu_exact, first_rows(inner, count))
    d_inner = gelu_pull(d_active)[0]
    grad_bias_in = jnp.sum(d_inner, axis=0)
    inner_low = d_inner.astype(BF)
    grad_in = jnp.einsum(
        "pd,pf->df", first_rows(norm_low, count), inner_low, preferred_element_type=F32
    )
    back_norm = jnp.einsum("pf,df->pd", inner_low, w_in, preferred_element_type=F32)
    d_norm_one = d_resid_two + lax.psum(back_norm, "mp")
    _, norm_one_pull = jax.vjp(layer_norm, first_rows(resid_one, count), gain_one_w, shift_one_w)
    d_resid_one, grad_gain_one, grad_shift_one = norm_one_pull(d_norm_one)
    grad_bias_out = jnp.sum(d_resid_one, axis=0)
    attn_low = d_resid_one.astype(BF)
    grad_out = jnp.einsum(
        "pc,pd->cd", first_rows(context, count), attn_low, preferred_element_type=F32
    )
    d_context = jnp.einsum("pd,cd->pc", attn_low, w_out, preferred_element_type=F32).astype(
        BF
    )
    d_context = d_context.reshape(count, heads_here, HEAD)
    query_cls = first_rows(query, count).reshape(count, heads_here, HEAD)
    keyed_heads = keyed.reshape(count, slot, heads_here, HEAD)
    value_heads = value.reshape(count, slot, heads_here, HEAD)
    scores_cls = (
        jnp.einsum("phd,pkhd->phk", query_cls, keyed_heads, preferred_element_type=F32)
        * scale
    )
    scores_cls = jnp.where(valid[:, None, :], scores_cls, MASKED)
    chance = jnp.exp(scores_cls - log_total[:, :, None])
    d_chance = jnp.einsum(
        "phd,pkhd->phk", d_context, value_heads, preferred_element_type=F32
    )
    d_value = jnp.einsum(
        "phk,phd->pkhd", chance.astype(BF), d_context, preferred_element_type=F32
    )
    d_scores = chance * (d_chance - jnp.sum(chance * d_chance, axis=-1, keepdims=True))
    scores_low = d_scores.astype(BF)
    d_query = (
        jnp.einsum("phk,pkhd->phd", scores_low, keyed_heads, preferred_element_type=F32)
        * scale
    )
    d_keyed = (
        jnp.einsum("phk,phd->pkhd", scores_low, query_cls, preferred_element_type=F32)
        * scale
    )
    d_query = d_query.reshape(count, local)
    d_value = d_value.reshape(rows, local)
    query_low = d_query.astype(BF)
    keyed_value_low = jnp.stack(
        [d_keyed.reshape(rows, local).astype(BF), d_value.astype(BF)]
    )
    grad_bias_qv = jnp.stack([jnp.sum(d_query, axis=0), jnp.sum(d_value, axis=0)])
    grad_query_w = jnp.einsum(
        "pd,pc->dc", first_rows(tokens, count), query_low, preferred_element_type=F32
    )
    grad_kv = jnp.einsum("rd,jrc->jdc", tokens, keyed_value_low, preferred_element_type=F32)
    grad_qkv = jnp.concatenate([grad_query_w[None], grad_kv], axis=0)
    own_half = lax.dynamic_slice_in_dim(d_resid_one, column, local, 1)
    back_kv = jnp.einsum(
        "jrc,jdc->rd", keyed_value_low, w_qkv[1:], preferred_element_type=F32
    )
    back_query = jnp.einsum("pc,dc->pd", query_low, w_qkv[0], preferred_element_type=F32)
    back_all = back_kv.reshape(count, slot, width).at[:, 0].add(back_query).reshape(rows, width)
    input_grad = lax.psum_scatter(
        back_all.astype(BF), "mp", scatter_dimension=1, tiled=True
    ).astype(F32)
    input_grad = input_grad.reshape(count, slot, local).at[:, 0].add(own_half).reshape(rows, local)
    summed = (
        lax.psum_scatter(grad_qkv, "dp", scatter_dimension=1, tiled=True),
        lax.psum_scatter(grad_bias_qv, "dp", scatter_dimension=1, tiled=True),
        lax.psum_scatter(grad_out, "dp", scatter_dimension=1, tiled=True),
        lax.psum_scatter(grad_bias_out, "dp", scatter_dimension=0, tiled=True),
        lax.psum_scatter(grad_gain_one, "dp", scatter_dimension=0, tiled=True),
        lax.psum_scatter(grad_shift_one, "dp", scatter_dimension=0, tiled=True),
        lax.psum_scatter(grad_in, "dp", scatter_dimension=0, tiled=True),
        lax.psum_scatter(grad_bias_in, "dp", scatter_dimension=0, tiled=True),
        lax.psum_scatter(grad_back, "dp", scatter_dimension=1, tiled=True),
        lax.psum_scatter(grad_bias_back, "dp", scatter_dimension=0, tiled=True),
        lax.psum_scatter(grad_gain_two, "dp", scatter_dimension=0, tiled=True),
    )
    return (
        activations,
        query_loss,
        input_grad,
        query_grad,
        summed[0],
        summed[1],
        summed[2],
        summed[3],
        summed[4],
        summed[5],
        summed[6],
        summed[7],
        summed[8],
        summed[9],
        summed[10],
    )


def solution(mesh):
    in_specs = (
        P("dp", None),
        P("dp"),
        P("dp", None),
        P(),
        P(None, None, "mp"),
        P(None, "mp"),
        P("mp", None),
        P(),
        P(),
        P(),
        P(None, "mp"),
        P("mp"),
        P("mp", None),
        P(),
        P(),
    )
    out_specs = (
        P("dp", "mp"),
        P("dp"),
        P("dp", "mp"),
        P("dp", None),
        P(None, "dp", "mp"),
        P(None, ("mp", "dp")),
        P("mp", "dp"),
        P("dp"),
        P("dp"),
        P("dp"),
        P("dp", "mp"),
        P(("mp", "dp")),
        P("mp", "dp"),
        P("dp"),
        P("dp"),
    )
    groups = mesh.shape["dp"]
    fits = groups <= 16 and mesh.shape["mp"] == 2
    return jax.shard_map(
        functools.partial(per_device, groups) if fits else by_collectives,
        mesh=mesh,
        in_specs=in_specs,
        out_specs=out_specs,
        check_vma=False,
    )
```
